32 devices in a mesh: dp: 4 (over z), mp: 8 (over y, x, core).
Axes of the slice: x: 2, y: 2, z: 4, core: 2. Of those that a mesh axis runs over, the one named last changes fastest.
Arguments:
- layer_input: bfloat16 [8192, 2048], P(('dp', 'mp')), may hold values from -6 to 6
- cotangent: bfloat16 [8192, 2048], P(('dp', 'mp')), may hold values from -6 to 6
- norm_in: float32 [2048], P(('dp', 'mp')), may hold values from 0.5 to 1.5
- norm_mid: float32 [2048], P(('dp', 'mp')), may hold values from 0.5 to 1.5
- w_rnn_in: float32 [2048, 2560], P('dp', 'mp'), may hold values from -0.125 to 0.125
- w_rnn_gate: float32 [2048, 2560], P('dp', 'mp'), may hold values from -0.125 to 0.125
- w_rnn_out: float32 [2560, 2048], P('mp', 'dp'), may hold values from -0.3125 to 0.3125
- gate_in_blocks: float32 [16, 160, 160], P('mp', 'dp'), may hold values from -0.5 to 0.5
- gate_a_blocks: float32 [16, 160, 160], P('mp', 'dp'), may hold values from -0.5 to 0.5
- channel_params: float32 [8, 2560], P('dp', 'mp')
- w_mlp_gate: float32 [2048, 6144], P('dp', 'mp'), may hold values from -0.125 to 0.125
- w_mlp_up: float32 [2048, 6144], P('dp', 'mp'), may hold values from -0.125 to 0.125
- w_mlp_down: float32 [6144, 2048], P('mp', 'dp'), may hold values from -0.15625 to 0.15625
- lengths: int32 [4, 3], P('dp'), may hold values from 1 to 2046, as said below
Outputs:
- layer_output: bfloat16 [8192, 2048], P(('dp', 'mp'))
- grad_input: float32 [8192, 2048], P(('dp', 'mp'))
- grad_norm_in: float32 [2048], P(('dp', 'mp'))
- grad_norm_mid: float32 [2048], P(('dp', 'mp'))
- grad_rnn_in: float32 [2048, 2560], P('dp', 'mp')
- grad_rnn_gate: float32 [2048, 2560], P('dp', 'mp')
- grad_rnn_out: float32 [2560, 2048], P('mp', 'dp')
- grad_gate_in: float32 [16, 160, 160], P('mp', 'dp')
- grad_gate_a: float32 [16, 160, 160], P('mp', 'dp')
- grad_channel: float32 [8, 2560], P('dp', 'mp')
- grad_mlp_gate: float32 [2048, 6144], P('dp', 'mp')
- grad_mlp_up: float32 [2048, 6144], P('dp', 'mp')
- grad_mlp_down: float32 [6144, 2048], P('mp', 'dp')
The draws below stay inside these ranges and needn't reach their ends.
Inputs may be any that keep to these rules, and one draw needn't show every extreme that they name: The lengths of each pack sum to at most 2048, exactly that in some pack of every draw; the positions after them are padding.
All inputs are finite; a program needn't handle non-finite values.
Results may differ from the reference program's by a relative error of at most 0.019.
Values may be sent and summed in bfloat16 or wider, within the bound.
A program may use at most 320 MiB of HBM per device.

```python
import jax
import jax.numpy as jnp
from jax import lax

D = 2048
NB = 16
BW = 160
FF = 6144
CONV = 4
TOK_DEV = 256
SEQS = 3
R = 2560
TOKENS = 8192
N_DP = 4
N_MP = 8


def draw_channel_params(key, part):
    key = jax.random.fold_in(key, 5)
    keys = jax.random.split(key, 4)
    width = NB * BW
    taps = 0.5 * jax.random.normal(keys[0], (CONV, width), jnp.float32)
    biases = 0.5 * jax.random.normal(keys[2], (2, width), jnp.float32)
    decay_param = jax.random.uniform(keys[3], (1, width), jnp.float32, 2.2, 6.9)
    conv_bias = jax.random.uniform(keys[1], (1, width), jnp.float32, -0.5, 0.5)
    return jnp.concatenate([taps, conv_bias, biases, decay_param], axis=0)


def draw_lengths(key, part):
    key = jax.random.fold_in(key, 11)
    keys = jax.random.split(key, 4)
    group_len = N_MP * TOK_DEV
    short_top = TOK_DEV // (2 * (SEQS - 1))
    shorts = jax.random.randint(keys[0], (N_DP, SEQS), 1, short_top + 1)
    padding = jax.random.randint(keys[1], (N_DP, 1), 0, TOK_DEV // 2)
    full_pack = jax.random.randint(keys[2], (), 0, N_DP)
    is_full = jnp.arange(N_DP)[:, None] == full_pack
    padding = jnp.where(is_full, 0, padding)
    shorts = jnp.where(is_full, 1, shorts)
    long_slot = jax.random.randint(keys[3], (N_DP, 1), 0, SEQS)
    is_long = jnp.arange(SEQS)[None, :] == long_slot
    short_sum = jnp.sum(jnp.where(is_long, 0, shorts), axis=1, keepdims=True)
    long_len = group_len - padding - short_sum
    return jnp.where(is_long, long_len, shorts).astype(jnp.int32)


def spiked(result, stream_key, source, target, parts, factor):
    def block_of(dim):
        return (jnp.arange(result.shape[dim]) // (result.shape[dim] // parts)).reshape((-1,) + (1,) * (result.ndim - 1 - dim))

    near = jax.random.permutation(stream_key, parts)[block_of(target)]
    far = (block_of(target) + parts // 2) % parts
    return jnp.where((block_of(source) == near) | (block_of(source) == far), factor * result, result)


def steps_of(own_key, extent, pieces, least, high):
    level, own = 1.0, jax.random.fold_in(own_key, 6)
    for position, shards_of in pieces:
        heights = jnp.exp(jax.random.uniform(jax.random.fold_in(own, position), (shards_of,), jnp.float32, least / len(pieces), high / len(pieces)))
        level = level * jnp.repeat(heights, extent[position] // shards_of).reshape([-1 if axis == position else 1 for axis in range(len(extent))])
    return level


def scatter_about(own_key, dims, scale, limit, shards=(), held_as=jnp.bfloat16):
    factor_of = steps_of(own_key, dims, shards, -0.22, 0.18) if shards else 1.0
    result = jax.random.normal(own_key, dims, jnp.float32) * scale * factor_of
    return jnp.minimum(jnp.maximum(result, -limit), limit).astype(held_as)


def gaussian_with(stream_key, shape, deviation, most, cuts, heavy, kind=jnp.bfloat16):
    drawn = deviation * jax.random.normal(stream_key, shape, jnp.float32)
    if cuts:
        drawn = drawn * steps_of(stream_key, shape, cuts, -0.22, 0.18)
    return jnp.clip(spiked(drawn, jax.random.fold_in(stream_key, 3), *heavy), -most, most).astype(kind)


def setup_inputs(seed: int = 0) -> dict:
    arg_keys = jax.random.split(jax.random.key(seed), 15)
    return {
        "layer_input": gaussian_with(arg_keys[0], (TOKENS, D), 1.0, 6.0, ((0, 32),), (0, 1, 32, 2.75)),
        "cotangent": scatter_about(arg_keys[1], (TOKENS, D), 1.0, 6.0, ((0, 32),)),
        "norm_in": jnp.clip(1.0 + 0.1 * jax.random.normal(arg_keys[2], (D,), jnp.float32), 0.5, 1.5),
        "norm_mid": jnp.clip(1.0 + 0.1 * jax.random.normal(arg_keys[3], (D,), jnp.float32), 0.5, 1.5),
        "w_rnn_in": scatter_about(arg_keys[4], (D, R), D ** -0.5, 0.125, ((0, 4), (1, 8)), jnp.float32),
        "w_rnn_gate": scatter_about(arg_keys[5], (D, R), D ** -0.5, 0.125, ((0, 4), (1, 8)), jnp.float32),
        "w_rnn_out": scatter_about(arg_keys[6], (R, D), (R // 8) ** -0.5, 0.3125, ((0, 8), (1, 4)), jnp.float32),
        "gate_in_blocks": scatter_about(arg_keys[7], (NB, BW, BW), BW ** -0.5, 0.5, ((0, 8), (1, 4)), jnp.float32),
        "gate_a_blocks": scatter_about(arg_keys[8], (NB, BW, BW), BW ** -0.5, 0.5, ((0, 8), (1, 4)), jnp.float32),
        "channel_params": draw_channel_params(jax.random.fold_in(arg_keys[14], 71), 0),
        "w_mlp_gate": scatter_about(arg_keys[10], (D, FF), D ** -0.5, 0.125, ((0, 4), (1, 8)), jnp.float32),
        "w_mlp_up": scatter_about(arg_keys[11], (D, FF), D ** -0.5, 0.125, ((0, 4), (1, 8)), jnp.float32),
        "w_mlp_down": scatter_about(arg_keys[12], (FF, D), (FF // 4) ** -0.5, 0.15625, ((0, 8), (1, 4)), jnp.float32),
        "lengths": draw_lengths(jax.random.fold_in(arg_keys[14], 71), 0),
    }


@jax.custom_vjp
def low(v):
    return lax.optimization_barrier(v.astype(jnp.bfloat16)).astype(jnp.float32)

@jax.custom_vjp
def low_back(v):
    return v

def low_keep(v):
    return (low(v), None)

def low_pass(kept, grad):
    return (grad,)

def back_keep(v):
    return (v, None)

def back_low(kept, grad):
    return (low(grad),)
low.defvjp(low_keep, low_pass)
low_back.defvjp(back_keep, back_low)
EPS = 1e-06
DECAY = 8.0

def product(left, right):
    return jnp.dot(left, right, precision=lax.Precision.HIGHEST, preferred_element_type=jnp.float32)

def layout(lens):
    group_len = N_MP * TOK_DEV
    places = jnp.arange(group_len, dtype=jnp.int32)
    finish = jnp.cumsum(lens).astype(jnp.int32)
    bounds = jnp.concatenate([(finish - lens).astype(jnp.int32), finish[-1:]])
    resets = jnp.any(places[:, None] == bounds[None, :], axis=1)
    begins = lax.optimization_barrier(jnp.max(jnp.where(bounds[None, :] <= places[:, None], bounds[None, :], 0), axis=1))
    living = places < finish[-1]
    return (places, resets, begins, living)

def rms_norm(values, gain):
    return values * lax.rsqrt(lax.optimization_barrier(jnp.mean(values * values, axis=-1, keepdims=True)) + EPS) * gain

def combine(left, right):
    return (left[0] * right[0], right[0] * left[1] + right[1])

def group_layer(rows_in, lens, weights):
    gain_in, gain_mid, rnn_in, rnn_gate, rnn_out, blocks_in, blocks_a, channel, mlp_gate, mlp_up, mlp_down = weights
    places, resets, begins, living = layout(lens)
    group_len = rows_in.shape[0]
    width = rnn_in.shape[1]
    normed = low(rms_norm(rows_in, gain_in))
    branch = low_back(low(product(normed, rnn_in)))
    side_gate = jax.nn.gelu(low_back(product(normed, rnn_gate)))
    convolved = jnp.zeros_like(branch) + channel[CONV]
    for offset in range(CONV):
        moved_rows = jnp.concatenate([jnp.zeros((offset, width), branch.dtype), branch[:group_len - offset]], axis=0)
        convolved = convolved + jnp.where((places - offset >= begins)[:, None], moved_rows * channel[offset], 0.0)
    blocked = convolved.reshape(group_len, NB, BW)
    logit_in = jnp.einsum('gnb,nbc->gnc', blocked, blocks_in, precision=lax.Precision.HIGHEST).reshape(group_len, width) + channel[CONV + 1]
    logit_a = jnp.einsum('gnb,nbc->gnc', blocked, blocks_a, precision=lax.Precision.HIGHEST).reshape(group_len, width) + channel[CONV + 2]
    gate_in = jax.nn.sigmoid(logit_in)
    gate_a = jax.nn.sigmoid(logit_a)
    decays = jnp.exp(-DECAY * gate_a * jax.nn.softplus(-channel[CONV + 3]))
    drives = gate_in * convolved * jnp.sqrt(1.0 - decays * decays)
    coeffs = jnp.where(resets[:, None], 0.0, decays)
    states = lax.associative_scan(combine, (coeffs, drives), axis=0)[1]
    mixed_state = low_back(low(states))
    branch_out = low(side_gate * mixed_state * living.astype(rows_in.dtype)[:, None])
    residual = rows_in + low_back(product(branch_out, rnn_out))
    normed_mid = low(rms_norm(residual, gain_mid))
    gate_pre = low_back(product(normed_mid, mlp_gate))
    up_pre = low_back(product(normed_mid, mlp_up))
    hidden = low(jax.nn.gelu(gate_pre) * up_pre)
    return residual + low_back(product(hidden, mlp_down))

def reference(layer_input, cotangent, norm_in, norm_mid, w_rnn_in, w_rnn_gate, w_rnn_out, gate_in_blocks, gate_a_blocks, channel_params, w_mlp_gate, w_mlp_up, w_mlp_down, lengths):
    floats = tuple((entry.astype(jnp.float32) for entry in (layer_input, norm_in, norm_mid, w_rnn_in, w_rnn_gate, w_rnn_out, gate_in_blocks, gate_a_blocks, channel_params, w_mlp_gate, w_mlp_up, w_mlp_down)))

    def forward(inputs, *masters):
        weights = tuple((low(master) for master in masters))
        groups = inputs.reshape(N_DP, N_MP * TOK_DEV, inputs.shape[1])

        def single_group(entry):
            return group_layer(entry[0], entry[1], weights)
        results = lax.map(jax.checkpoint(single_group), (groups, lengths))
        return results.reshape(inputs.shape)
    outcome, pullback = jax.vjp(forward, *floats)
    gradients = pullback(cotangent.astype(jnp.float32))
    return (outcome.astype(jnp.bfloat16), gradients[0], gradients[1], gradients[2], gradients[3], gradients[4], gradients[5], gradients[6], gradients[7], gradients[8], gradients[9], gradients[10], gradients[11])
```

```python
import functools

import jax
import jax.numpy as jnp
from jax import lax
from jax.experimental import pallas as pl
from jax.experimental.pallas import tpu as pltpu
from jax.sharding import PartitionSpec as P

CONV = 4
EPS = 1e-06
DECAY = 8.0
HALF = jnp.bfloat16
SINGLE = jnp.float32
MESH = pl.DeviceIdType.MESH
VMEM_BYTES = 56 * 1024 * 1024
GELU_C = 0.7978845608028654
GELU_K = 0.044715


def dot_nn(left, right):
    return lax.dot_general(
        left, right, (((1,), (0,)), ((), ())), preferred_element_type=SINGLE
    )


def dot_nt(left, right):
    return lax.dot_general(
        left, right, (((1,), (1,)), ((), ())), preferred_element_type=SINGLE
    )


def dot_tn(left, right):
    return lax.dot_general(
        left, right, (((0,), (0,)), ((), ())), preferred_element_type=SINGLE
    )


def gelu(v):
    return 0.5 * v * (1.0 + jnp.tanh(GELU_C * (v + GELU_K * v * v * v)))


def gelu_both(v):
    square = v * v
    t = jnp.tanh(GELU_C * (v + GELU_K * v * square))
    value = 0.5 * v * (1.0 + t)
    slope = 0.5 * (1.0 + t) + 0.5 * v * (1.0 - t * t) * (GELU_C * (1.0 + 3.0 * GELU_K * square))
    return value, slope


def flip(me, mask, count):
    place = me
    bit = 1
    while bit < count:
        if mask & bit:
            place = place + (1 - 2 * ((me // bit) % 2)) * bit
        bit *= 2
    return place


def gather_plan(count):
    bits = [1 << b for b in range(count.bit_length() - 1)]
    outer = bits[1:]
    orders = (outer + bits[:1], outer[::-1] + bits[:1])
    sends = []
    for half, order in enumerate(orders):
        for stage, bit in enumerate(order):
            for pick in range(1 << stage):
                mask = sum(order[j] for j in range(stage) if pick >> j & 1)
                sends.append((bin(mask).count("1"), half, mask, bit))
    sends.sort(key=lambda s: s[0])
    return bits, [s[1:] for s in sends]


def start_barrier(masks, count):
    me = lax.axis_index("mp")
    barrier = pltpu.get_barrier_semaphore()
    for mask in masks:
        pl.semaphore_signal(
            barrier, inc=1, device_id={"mp": flip(me, mask, count)}, device_id_type=MESH
        )
    pl.semaphore_wait(barrier, len(masks))


def gather_kernel(count, x_ref, o_ref, own_sem, send, recv):
    me = lax.axis_index("mp")
    rows = x_ref.shape[0]
    bits, plan = gather_plan(count)
    own = pltpu.make_async_copy(x_ref, o_ref.at[me], own_sem)
    own.start()
    start_barrier(bits, count)
    copies = {}
    landed = set()
    for half, mask, bit in plan:
        span = pl.ds(half * (rows // 2), rows // 2)
        slot = flip(me, mask, count)
        if mask and (half, mask) not in landed:
            copies[(half, mask)].wait_recv()
            landed.add((half, mask))
        source = o_ref.at[slot, span] if mask else x_ref.at[span]
        copy = pltpu.make_async_remote_copy(
            src_ref=source,
            dst_ref=o_ref.at[slot, span],
            send_sem=send.at[half, mask | bit],
            recv_sem=recv.at[half, mask | bit],
            device_id={"mp": flip(me, bit, count)},
            device_id_type=MESH,
        )
        copy.start()
        copies[(half, mask | bit)] = copy
    for key, copy in copies.items():
        if key not in landed:
            copy.wait_recv()
    for copy in copies.values():
        copy.wait_send()
    own.wait()


def gather_rows(x, collective_id):
    count = lax.axis_size("mp")
    if count != 8:
        return lax.all_gather(x, "mp", axis=0, tiled=False)
    rows, width = x.shape
    return pl.pallas_call(
        functools.partial(gather_kernel, count),
        out_shape=jax.ShapeDtypeStruct((count, rows, width), x.dtype),
        in_specs=[pl.BlockSpec(memory_space=pl.ANY)],
        out_specs=pl.BlockSpec(memory_space=pl.ANY),
        scratch_shapes=[
            pltpu.SemaphoreType.DMA,
            pltpu.SemaphoreType.DMA((2, count)),
            pltpu.SemaphoreType.DMA((2, count)),
        ],
        compiler_params=pltpu.CompilerParams(
            collective_id=collective_id, has_side_effects=True, vmem_limit_bytes=VMEM_BYTES
        ),
        cost_estimate=pl.CostEstimate(
            flops=0, bytes_accessed=2 * count * rows * width * 2 * 4, transcendentals=0
        ),
        name="gather_rows",
    )(x)


def scatter_kernel(products, tile, *refs):
    count = 8
    pairs = len(products)
    lefts, rights = refs[:pairs], refs[pairs : 2 * pairs]
    out_ref = refs[2 * pairs]
    acc, core_out, core_in, link_out, link_in = refs[2 * pairs + 1 : 2 * pairs + 6]
    core_send, core_recv, link_send, link_recv = refs[2 * pairs + 6 :]
    rows, width = out_ref.shape
    me = lax.axis_index("mp")
    start_barrier((1, 2, 4), count)

    def partial(slot, store):
        first = pl.multiple_of(slot * rows, rows)

        def step(t, carry):
            columns = pl.ds(pl.multiple_of(t * tile, tile), tile)
            total = None
            for left, right, product in zip(lefts, rights, products):
                term = product(left[pl.ds(first, rows), :], right, t, columns)
                total = term if total is None else total + term
            store(columns, total)
            return carry

        lax.fori_loop(0, width // tile, step, 0)

    def into_core(c):
        def store(columns, total):
            core_out[c, :, columns] = total.astype(HALF)

        return store

    def into_acc(c):
        def store(columns, total):
            acc[c, :, columns] = total

        return store

    core_copies = {}
    link_copies = {}
    middle = rows // 2

    def core_half(c):
        partial(flip(me, 2 * c + 1, count), into_core(c))
        copy = pltpu.make_async_remote_copy(
            src_ref=core_out.at[c],
            dst_ref=core_in.at[c],
            send_sem=core_send.at[c],
            recv_sem=core_recv.at[c],
            device_id={"mp": flip(me, 1, count)},
            device_id_type=MESH,
        )
        copy.start()
        core_copies[c] = copy

    def core_sum(c):
        core_copies[c].wait_recv()

        def step(t, carry):
            columns = pl.ds(pl.multiple_of(t * tile, tile), tile)
            acc[c, :, columns] = acc[c, :, columns] + core_in[c, :, columns].astype(SINGLE)
            return carry

        lax.fori_loop(0, width // tile, step, 0)

    def link(index, c, half, axis):
        span = pl.ds(half * middle, middle)

        def step(t, carry):
            columns = pl.ds(pl.multiple_of(t * tile, tile), tile)
            link_out[index, :, columns] = acc[c, span, columns].astype(HALF)
            return carry

        lax.fori_loop(0, width // tile, step, 0)
        copy = pltpu.make_async_remote_copy(
            src_ref=link_out.at[index],
            dst_ref=link_in.at[index],
            send_sem=link_send.at[index],
            recv_sem=link_recv.at[index],
            device_id={"mp": flip(me, 2 * axis, count)},
            device_id_type=MESH,
        )
        copy.start()
        link_copies[index] = copy

    def link_sum(index, c, half):
        link_copies[index].wait_recv()
        span = pl.ds(half * middle, middle)

        def step(t, carry):
            columns = pl.ds(pl.multiple_of(t * tile, tile), tile)
            acc[c, span, columns] = acc[c, span, columns] + link_in[index, :, columns].astype(
                SINGLE
            )
            return carry

        lax.fori_loop(0, width // tile, step, 0)

    core_half(3)
    partial(flip(me, 6, count), into_acc(3))
    core_half(1)
    core_sum(3)
    link(0, 3, 0, 2)
    link(1, 3, 1, 1)
    partial(flip(me, 2, count), into_acc(1))
    core_half(2)
    core_sum(1)
    link(2, 1, 1, 1)
    partial(flip(me, 4, count), into_acc(2))
    core_half(0)
    core_sum(2)
    link(3, 2, 0, 2)
    partial(me, into_acc(0))
    core_sum(0)
    link_sum(0, 1, 0)
    link(4, 1, 0, 1)
    link_sum(1, 2, 1)
    link(5, 2, 1, 2)
    link_sum(2, 0, 1)
    link_sum(3, 0, 0)
    link_sum(4, 0, 0)
    link_sum(5, 0, 1)
    out_ref[...] = acc[0]
    for copy in core_copies.values():
        copy.wait_send()
    for copy in link_copies.values():
        copy.wait_send()


def scatter_products(lefts, rights, products, fallback, width, tile, collective_id, flops):
    count = lax.axis_size("mp")
    tokens = lefts[0].shape[0]
    rows = tokens // count
    if count != 8:
        return lax.psum_scatter(
            fallback().astype(HALF), "mp", scatter_dimension=0, tiled=True
        ).astype(SINGLE)
    return pl.pallas_call(
        functools.partial(scatter_kernel, products, tile),
        out_shape=jax.ShapeDtypeStruct((rows, width), SINGLE),
        in_specs=[pl.BlockSpec(memory_space=pltpu.VMEM)] * (len(lefts) + len(rights)),
        out_specs=pl.BlockSpec(memory_space=pltpu.VMEM),
        scratch_shapes=[
            pltpu.VMEM((4, rows, width), SINGLE),
            pltpu.VMEM((4, rows, width), HALF),
            pltpu.VMEM((4, rows, width), HALF),
            pltpu.VMEM((6, rows // 2, width), HALF),
            pltpu.VMEM((6, rows // 2, width), HALF),
            pltpu.SemaphoreType.DMA((4,)),
            pltpu.SemaphoreType.DMA((4,)),
            pltpu.SemaphoreType.DMA((6,)),
            pltpu.SemaphoreType.DMA((6,)),
        ],
        compiler_params=pltpu.CompilerParams(
            collective_id=collective_id, has_side_effects=True, vmem_limit_bytes=VMEM_BYTES
        ),
        cost_estimate=pl.CostEstimate(
            flops=flops, bytes_accessed=tokens * width * 2 * 8, transcendentals=0
        ),
        name="scatter_products",
    )(*lefts, *rights)


def positions(lens_ref, first, shape):
    place = lax.broadcasted_iota(jnp.int32, shape, 0) + first
    begin = jnp.zeros(shape, jnp.int32)
    total = 0
    for j in range(lens_ref.shape[1]):
        total = total + lens_ref[0, j]
        begin = jnp.where(place >= total, total, begin)
    return place - begin, place < total


def split_dot(dot, left, right):
    high = left.astype(HALF)
    low = (left - high.astype(SINGLE)).astype(HALF)
    return dot(high, right) + dot(low, right)


def lane_tiles(width):
    return [(t, t * 128, min(128, width - t * 128)) for t in range(-(-width // 128))]


def put_tiles(ref, value):
    for t, first, lanes in lane_tiles(value.shape[1]):
        ref[t, :, :lanes] = value[:, first : first + lanes]


def scan_start(tiles, lanes):
    return [(jnp.zeros((lanes, 128), SINGLE), jnp.ones((lanes, 128), SINGLE)) for _ in tiles]


def sigmoid(v):
    return 1.0 / (1.0 + jnp.exp(-v))


def forward_kernel(
    lens_ref,
    x_ref,
    gain_ref,
    pack_ref,
    bin_ref,
    ba_ref,
    chan_ref,
    n1_ref,
    bx_ref,
    by_ref,
    conv_ref,
    gi_ref,
    ra_ref,
    h_ref,
    ob_ref,
    taps,
    coef,
    drive,
    carry,
):
    step = pl.program_id(0)
    rows, width = bx_ref.shape
    depth = pack_ref.shape[2]
    lanes = 8
    span = rows // lanes

    @pl.when(step == 0)
    def _():
        taps[...] = jnp.zeros_like(taps)
        carry[...] = jnp.zeros_like(carry)
        coef[...] = jnp.zeros_like(coef)
        drive[...] = jnp.zeros_like(drive)

    x = x_ref[0].astype(SINGLE)
    scale = lax.rsqrt(jnp.mean(x * x, axis=-1, keepdims=True) + EPS)
    normed = (x * scale * gain_ref[...]).astype(HALF)
    n1_ref[...] = normed
    total = None
    for d in range(pack_ref.shape[0]):
        term = dot_nt(normed[:, d * depth : (d + 1) * depth], pack_ref[d, : 2 * width, :])
        total = term if total is None else total + term
    bx = total[:, :width].astype(HALF)
    by = total[:, width:]
    bx_ref[...] = bx
    by_ref[...] = by
    pos, live = positions(lens_ref, step * rows, (rows, width))
    taps[0:8, :] = taps[rows : rows + 8, :]
    taps[8 : rows + 8, :] = bx.astype(SINGLE)
    conv = jnp.zeros((rows, width), SINGLE) + chan_ref[CONV : CONV + 1, :]
    for k in range(CONV):
        moved = taps[8 - k : 8 - k + rows, :]
        conv = conv + jnp.where(pos >= k, moved * chan_ref[k : k + 1, :], 0.0)
    conv_ref[...] = conv
    high = conv.astype(HALF)
    low = (conv - high.astype(SINGLE)).astype(HALF)
    gate_in = sigmoid(
        dot_nn(high, bin_ref[...]) + dot_nn(low, bin_ref[...]) + chan_ref[CONV + 1 : CONV + 2, :]
    )
    gate_a = sigmoid(
        dot_nn(high, ba_ref[...]) + dot_nn(low, ba_ref[...]) + chan_ref[CONV + 2 : CONV + 3, :]
    )
    gi_ref[...] = gate_in
    ra_ref[...] = gate_a
    decay = jnp.exp(-DECAY * gate_a * chan_ref[CONV + 4 : CONV + 5, :])
    root = jnp.sqrt(1.0 - decay * decay)
    put_tiles(coef, jnp.where(pos == 0, 0.0, decay))
    put_tiles(drive, gate_in * conv * root)
    tiles = lane_tiles(width)

    def scan(i, state):
        at = pl.ds(i, lanes, stride=span)
        result = []
        for (t, _, _), (h, prod) in zip(tiles, state):
            a = coef[t, at, :]
            h = a * h + drive[t, at, :]
            prod = prod * a
            drive[t, at, :] = h
            coef[t, at, :] = prod
            result.append((h, prod))
        return result

    state = lax.fori_loop(0, span, scan, scan_start(tiles, lanes), unroll=4)
    for (t, first, used), (h, prod) in zip(tiles, state):
        running = carry[t, 0:1, :]
        for s in range(lanes):
            at = slice(s * span, (s + 1) * span)
            value = drive[t, at, :] + coef[t, at, :] * running
            h_ref[at, first : first + used] = value[:, :used]
            running = h[s : s + 1, :] + prod[s : s + 1, :] * running
        carry[t, 0:1, :] = running
    mixed = h_ref[...].astype(HALF).astype(SINGLE)
    ob_ref[...] = jnp.where(live, gelu(by) * mixed, 0.0).astype(HALF)


def forward_channels(lens, x_all, gain, pack, blocks_in, blocks_a, chan):
    count, rows, model = x_all.shape
    width = chan.shape[1]
    tokens = count * rows
    whole = lambda shape: pl.BlockSpec(shape, lambda i: (0,) * len(shape))
    part = pl.BlockSpec((rows, width), lambda i: (i, 0))
    full = lambda kind: jax.ShapeDtypeStruct((tokens, width), kind)
    return pl.pallas_call(
        forward_kernel,
        grid=(count,),
        out_shape=(
            jax.ShapeDtypeStruct((tokens, model), HALF),
            full(HALF),
            full(SINGLE),
            full(SINGLE),
            full(SINGLE),
            full(SINGLE),
            full(SINGLE),
            full(HALF),
        ),
        in_specs=[
            pl.BlockSpec(memory_space=pltpu.SMEM),
            pl.BlockSpec((1, rows, model), lambda i: (i, 0, 0)),
            whole(gain.shape),
            whole(pack.shape),
            whole(blocks_in.shape),
            whole(blocks_a.shape),
            whole(chan.shape),
        ],
        out_specs=(pl.BlockSpec((rows, model), lambda i: (i, 0)),) + (part,) * 7,
        scratch_shapes=[
            pltpu.VMEM((rows + 8, width), SINGLE),
            pltpu.VMEM((len(lane_tiles(width)), rows, 128), SINGLE),
            pltpu.VMEM((len(lane_tiles(width)), rows, 128), SINGLE),
            pltpu.VMEM((len(lane_tiles(width)), 8, 128), SINGLE),
        ],
        compiler_params=pltpu.CompilerParams(vmem_limit_bytes=VMEM_BYTES),
        cost_estimate=pl.CostEstimate(
            flops=2 * tokens * model * 2 * width,
            bytes_accessed=tokens * (model * 4 + width * 24),
            transcendentals=8 * tokens * width,
        ),
        name="forward_channels",
    )(lens, x_all, gain, pack, blocks_in, blocks_a, chan)


def backward_kernel(
    lens_ref,
    dt_ref,
    pack_ref,
    bin_ref,
    ba_ref,
    chan_ref,
    bx_ref,
    by_ref,
    conv_ref,
    gi_ref,
    ra_ref,
    h_ref,
    hprev_ref,
    dbx_ref,
    dby_ref,
    gin_ref,
    ga_ref,
    gchan_ref,
    lift,
    coef,
    drive,
    carry,
):
    step = pl.program_id(0)
    chunk = pl.num_programs(0) - 1 - step
    rows, width = bx_ref.shape
    depth = pack_ref.shape[2]
    lanes = 8
    span = rows // lanes

    @pl.when(step == 0)
    def _():
        lift[...] = jnp.zeros_like(lift)
        carry[...] = jnp.zeros_like(carry)
        coef[...] = jnp.zeros_like(coef)
        drive[...] = jnp.zeros_like(drive)
        gin_ref[...] = jnp.zeros_like(gin_ref)
        ga_ref[...] = jnp.zeros_like(ga_ref)
        gchan_ref[...] = jnp.zeros_like(gchan_ref)

    d_out = None
    for d in range(pack_ref.shape[0]):
        term = dot_nt(
            dt_ref[0, :, d * depth : (d + 1) * depth], pack_ref[d, 2 * width : 3 * width, :]
        )
        d_out = term if d_out is None else d_out + term
    pos, live = positions(lens_ref, chunk * rows, (rows, width))
    by = by_ref[...]
    h = h_ref[...]
    side, slope = gelu_both(by)
    d_out = jnp.where(live, d_out, 0.0)
    dby_ref[...] = (d_out * h.astype(HALF).astype(SINGLE) * slope).astype(HALF)
    gate_a = ra_ref[...]
    soft = chan_ref[CONV + 4 : CONV + 5, :]
    decay = jnp.exp(-DECAY * gate_a * soft)
    put_tiles(coef, jnp.where(pos == 0, 0.0, decay))
    put_tiles(drive, (d_out * side).astype(HALF).astype(SINGLE))
    tiles = lane_tiles(width)

    def scan(j, state):
        at = pl.ds(span - 1 - j, lanes, stride=span)
        result = []
        for (t, _, _), (after, prod) in zip(tiles, state):
            a = coef[t, at, :]
            lam = drive[t, at, :] + after
            drive[t, at, :] = lam
            coef[t, at, :] = prod
            result.append((a * lam, prod * a))
        return result

    state = lax.fori_loop(0, span, scan, scan_start(tiles, lanes), unroll=4)
    for (t, first, used), (after, prod) in zip(tiles, state):
        running = carry[t, 0:1, :]
        for s in reversed(range(lanes)):
            at = slice(s * span, (s + 1) * span)
            value = drive[t, at, :] + coef[t, at, :] * running
            lift[at, first : first + used] = value[:, :used]
            running = after[s : s + 1, :] + prod[s : s + 1, :] * running
        carry[t, 0:1, :] = running
    lam = lift[0:rows, :]
    last = jnp.where(chunk > 0, hprev_ref[7:8, :], 0.0)
    before = jnp.concatenate([last, h[: rows - 1, :]], axis=0)
    before = jnp.where(pos == 0, 0.0, before)
    conv = conv_ref[...]
    gate_in = gi_ref[...]
    root = jnp.sqrt(1.0 - decay * decay)
    d_decay = lam * before - lam * gate_in * conv * decay / root
    d_log = d_decay * decay
    d_a = d_log * (-DECAY * soft)
    d_in = lam * conv * root
    d_logit_in = d_in * gate_in * (1.0 - gate_in)
    d_logit_a = d_a * gate_a * (1.0 - gate_a)
    d_conv = (
        lam * gate_in * root
        + split_dot(dot_nt, d_logit_in, bin_ref[...])
        + split_dot(dot_nt, d_logit_a, ba_ref[...])
    )
    low = conv.astype(HALF)
    gin_ref[...] += dot_tn(low, d_logit_in.astype(HALF))
    ga_ref[...] += dot_tn(low, d_logit_a.astype(HALF))
    lift[0:rows, :] = d_conv
    bx = bx_ref[...].astype(SINGLE)
    d_bx = jnp.zeros((rows, width), SINGLE)
    for k in range(CONV):
        if k:
            ahead, _ = positions(lens_ref, chunk * rows + k, (rows, width))
            moved = jnp.where(ahead >= k, lift[k : k + rows, :], 0.0)
        else:
            moved = d_conv
        d_bx = d_bx + moved * chan_ref[k : k + 1, :]
        gchan_ref[k : k + 1, :] += jnp.sum(moved * bx, axis=0, keepdims=True)
    dbx_ref[...] = d_bx.astype(HALF)
    lift[rows : rows + 8, :] = d_conv[0:8, :]
    sums = (d_conv, d_logit_in, d_logit_a, d_log * gate_a)
    for j, value in enumerate(sums):
        gchan_ref[CONV + j : CONV + j + 1, :] += jnp.sum(value, axis=0, keepdims=True)


def backward_channels(lens, dt_all, pack, blocks_in, blocks_a, chan, saved):
    bx, by, conv, gate_in, gate_a, h = saved
    count, rows, model = dt_all.shape
    width = chan.shape[1]
    tokens = count * rows
    last = count - 1
    whole = lambda shape: pl.BlockSpec(shape, lambda i: (0,) * len(shape))
    part = pl.BlockSpec((rows, width), lambda i: (last - i, 0))
    before = pl.BlockSpec(
        (8, width), lambda i: (jnp.maximum((last - i) * (rows // 8) - 1, 0), 0)
    )
    full = lambda kind: jax.ShapeDtypeStruct((tokens, width), kind)
    square = jax.ShapeDtypeStruct((width, width), SINGLE)
    return pl.pallas_call(
        backward_kernel,
        grid=(count,),
        out_shape=(full(HALF), full(HALF), square, square, jax.ShapeDtypeStruct((8, width), SINGLE)),
        in_specs=[
            pl.BlockSpec(memory_space=pltpu.SMEM),
            pl.BlockSpec((1, rows, model), lambda i: (last - i, 0, 0)),
            whole(pack.shape),
            whole(blocks_in.shape),
            whole(blocks_a.shape),
            whole(chan.shape),
            part,
            part,
            part,
            part,
            part,
            part,
            before,
        ],
        out_specs=(part, part, whole((width, width)), whole((width, width)), whole((8, width))),
        scratch_shapes=[
            pltpu.VMEM((rows + 8, width), SINGLE),
            pltpu.VMEM((len(lane_tiles(width)), rows, 128), SINGLE),
            pltpu.VMEM((len(lane_tiles(width)), rows, 128), SINGLE),
            pltpu.VMEM((len(lane_tiles(width)), 8, 128), SINGLE),
        ],
        compiler_params=pltpu.CompilerParams(vmem_limit_bytes=VMEM_BYTES),
        cost_estimate=pl.CostEstimate(
            flops=2 * tokens * model * width,
            bytes_accessed=tokens * (model * 2 + width * 28),
            transcendentals=8 * tokens * width,
        ),
        name="backward_channels",
    )(lens, dt_all, pack, blocks_in, blocks_a, chan, bx, by, conv, gate_in, gate_a, h, h)


def diagonal(blocks):
    count, size, _ = blocks.shape
    spread = blocks[:, :, None, :] * jnp.eye(count, dtype=blocks.dtype)[:, None, :, None]
    return spread.reshape(count * size, count * size)


def on_device(
    layer_input,
    cotangent,
    norm_in,
    norm_mid,
    w_rnn_in,
    w_rnn_gate,
    w_rnn_out,
    gate_in_blocks,
    gate_a_blocks,
    channel_params,
    w_mlp_gate,
    w_mlp_up,
    w_mlp_down,
    lengths,
):
    parts = lax.axis_size("dp")
    rows, model = layer_input.shape
    depth, width = w_rnn_in.shape
    heads, bite, block = gate_in_blocks.shape
    tokens = rows * lax.axis_size("mp")

    flat = jnp.concatenate(
        [
            gate_in_blocks.astype(HALF).reshape(-1),
            gate_a_blocks.astype(HALF).reshape(-1),
            channel_params.astype(HALF).reshape(-1),
        ]
    )
    used = flat.shape[0]
    small_rows = -(-used // (16 * depth)) * 16
    flat = jnp.pad(flat, (0, small_rows * depth - used)).reshape(small_rows, depth)
    mine = jnp.concatenate(
        [
            w_rnn_in.astype(HALF).T,
            w_rnn_gate.astype(HALF).T,
            w_rnn_out.astype(HALF),
            flat,
        ],
        axis=0,
    )
    pack = lax.all_gather(mine, "dp", axis=0, tiled=False)
    down = lax.all_gather(w_mlp_down.astype(HALF), "dp", axis=1, tiled=True)
    gate_w = lax.all_gather(w_mlp_gate.astype(HALF), "dp", axis=0, tiled=True)
    up_w = lax.all_gather(w_mlp_up.astype(HALF), "dp", axis=0, tiled=True)
    gains = lax.all_gather(
        jnp.stack([norm_in, norm_mid]).astype(HALF), ("dp", "mp"), axis=1, tiled=True
    ).astype(SINGLE)
    gain_first, gain_second = gains[0:1], gains[1:2]

    small = pack[:, 3 * width :, :].reshape(parts, -1)
    size = heads * bite * block
    whole_block = lambda v: diagonal(
        v.reshape(parts, heads, bite, block).transpose(1, 0, 2, 3).reshape(heads, block, block)
    )
    blocks_in = whole_block(small[:, :size])
    blocks_a = whole_block(small[:, size : 2 * size])
    channel = small[:, 2 * size : used].reshape(2 * CONV, width).astype(SINGLE)
    soft = jax.nn.softplus(-channel[2 * CONV - 1 :])
    chan = jnp.concatenate([channel, soft, jnp.zeros((7, width), SINGLE)], axis=0)

    x_all = gather_rows(layer_input, 0)
    c_all = gather_rows(cotangent, 1).reshape(tokens, model)
    n1, bx, by, conv, gate_in, gate_a, h, ob = forward_channels(
        lengths, x_all, gain_first, pack, blocks_in, blocks_a, chan
    )
    inputs = layer_input.astype(SINGLE)
    out = scatter_products(
        [ob],
        [pack],
        [lambda l, r, t, cols: dot_nn(l, r[t, 2 * width : 3 * width, :])],
        lambda: jnp.einsum(
            "tc,dcm->tdm", ob, pack[:, 2 * width : 3 * width], preferred_element_type=SINGLE
        ).reshape(tokens, model),
        model,
        depth,
        2,
        2 * tokens * width * model,
    )
    residual = inputs + out
    scale_second = lax.rsqrt(jnp.mean(residual * residual, axis=-1, keepdims=True) + EPS)
    normed_mid = (residual * scale_second * gain_second).astype(HALF)
    n2 = gather_rows(normed_mid, 3).reshape(tokens, model)

    gate_pre = dot_nn(n2, gate_w)
    d_hidden = dot_nt(c_all, down)
    act, slope = gelu_both(gate_pre)
    d_up = (d_hidden * act).astype(HALF)
    up_pre = dot_nn(n2, up_w)
    hidden = (act * up_pre).astype(HALF)
    d_gate = (d_hidden * up_pre * slope).astype(HALF)
    tile = 512
    by_rows = lambda l, r, t, cols: dot_nt(l, r[cols, :])
    d_normed_mid = scatter_products(
        [d_gate, d_up],
        [gate_w, up_w],
        [by_rows, by_rows],
        lambda: dot_nt(d_gate, gate_w) + dot_nt(d_up, up_w),
        model,
        tile,
        4,
        4 * tokens * model * up_w.shape[1],
    )
    grad_up = dot_tn(n2, d_up)
    grad_gate = dot_tn(n2, d_gate)
    grad_down = dot_tn(hidden, c_all)
    mlp_out = scatter_products(
        [hidden],
        [down],
        [lambda l, r, t, cols: dot_nn(l, r[:, cols])],
        lambda: dot_nn(hidden, down),
        model,
        tile,
        5,
        2 * tokens * model * up_w.shape[1],
    )
    layer_output = (residual + mlp_out).astype(HALF)

    weighted_second = gain_second * d_normed_mid
    grad_gain_second = jnp.sum(d_normed_mid * residual * scale_second, axis=0)
    cube_second = scale_second * scale_second * scale_second
    d_residual = (
        cotangent.astype(SINGLE)
        + scale_second * weighted_second
        - residual * cube_second * jnp.mean(weighted_second * residual, axis=-1, keepdims=True)
    )
    dt_all = gather_rows(d_residual.astype(HALF), 6)

    d_bx, d_by, gin, ga, gchan = backward_channels(
        lengths, dt_all, pack, blocks_in, blocks_a, chan, (bx, by, conv, gate_in, gate_a, h)
    )
    d_normed = scatter_products(
        [d_bx, d_by],
        [pack, pack],
        [
            lambda l, r, t, cols: dot_nn(l, r[t, :width, :]),
            lambda l, r, t, cols: dot_nn(l, r[t, width : 2 * width, :]),
        ],
        lambda: jnp.einsum(
            "tc,dcm->tdm",
            jnp.concatenate([d_bx, d_by], axis=1),
            pack[:, : 2 * width],
            preferred_element_type=SINGLE,
        ).reshape(tokens, model),
        model,
        depth,
        7,
        4 * tokens * width * model,
    )
    dt_flat = dt_all.reshape(tokens, model)
    grad_out = dot_tn(ob, dt_flat)
    grad_in = dot_tn(d_bx, n1)
    grad_side = dot_tn(d_by, n1)

    scale_first = lax.rsqrt(jnp.mean(inputs * inputs, axis=-1, keepdims=True) + EPS)
    weighted_first = gain_first * d_normed
    grad_gain_first = jnp.sum(d_normed * inputs * scale_first, axis=0)
    cube_first = scale_first * scale_first * scale_first
    grad_input = (
        d_residual
        + scale_first * weighted_first
        - inputs * cube_first * jnp.mean(weighted_first * inputs, axis=-1, keepdims=True)
    )

    def over_dp(value, dimension):
        return lax.psum_scatter(
            value.astype(HALF), "dp", scatter_dimension=dimension, tiled=True
        )

    own = lambda full: jnp.stack(
        [full[j * block : (j + 1) * block, j * block : (j + 1) * block] for j in range(heads)]
    )
    decay_row = DECAY * jax.nn.sigmoid(-channel[2 * CONV - 1 :]) * gchan[2 * CONV - 1 :]
    grad_channel = jnp.concatenate([gchan[: 2 * CONV - 1], decay_row], axis=0)
    split = lambda v: v.reshape(heads, parts, bite, block).transpose(1, 0, 2, 3).reshape(parts, -1)
    small_grads = jnp.concatenate(
        [split(own(gin)), split(own(ga)), grad_channel.reshape(parts, -1)], axis=1
    )
    small_grads = jnp.pad(small_grads, ((0, 0), (0, small_rows * depth - used)))
    small_grads = small_grads.reshape(parts, small_rows, depth)
    by_part = lambda v: v.reshape(width, parts, depth).transpose(1, 0, 2)
    rnn_grads = jnp.concatenate(
        [by_part(grad_in), by_part(grad_side), by_part(grad_out), small_grads], axis=1
    )
    grad_up = over_dp(grad_up, 0).astype(SINGLE)
    grad_gate = over_dp(grad_gate, 0).astype(SINGLE)
    grad_down = over_dp(grad_down, 1).astype(SINGLE)
    rnn_grads = over_dp(rnn_grads, 0)[0].astype(SINGLE)
    flat_grads = rnn_grads[3 * width :].reshape(-1)
    gain_grads = lax.psum_scatter(
        jnp.stack([grad_gain_first, grad_gain_second]).astype(HALF),
        ("dp", "mp"),
        scatter_dimension=1,
        tiled=True,
    ).astype(SINGLE)
    return (
        layer_output,
        grad_input,
        gain_grads[0],
        gain_grads[1],
        rnn_grads[:width].T,
        rnn_grads[width : 2 * width].T,
        rnn_grads[2 * width : 3 * width],
        flat_grads[:size].reshape(heads, bite, block),
        flat_grads[size : 2 * size].reshape(heads, bite, block),
        flat_grads[2 * size : used].reshape(channel_params.shape),
        grad_gate,
        grad_up,
        grad_down,
    )


def solution(mesh):
    rows = P(("dp", "mp"), None)
    return jax.shard_map(
        on_device,
        mesh=mesh,
        in_specs=(
            rows,
            rows,
            P(("dp", "mp")),
            P(("dp", "mp")),
            P("dp", "mp"),
            P("dp", "mp"),
            P("mp", "dp"),
            P("mp", "dp", None),
            P("mp", "dp", None),
            P("dp", "mp"),
            P("dp", "mp"),
            P("dp", "mp"),
            P("mp", "dp"),
            P("dp", None),
        ),
        out_specs=(
            rows,
            rows,
            P(("dp", "mp")),
            P(("dp", "mp")),
            P("dp", "mp"),
            P("dp", "mp"),
            P("mp", "dp"),
            P("mp", "dp", None),
            P("mp", "dp", None),
            P("dp", "mp"),
            P("dp", "mp"),
            P("dp", "mp"),
            P("mp", "dp"),
        ),
        check_vma=False,
    )
```

```python
import functools

import jax
import jax.numpy as jnp
from jax import lax
from jax.experimental import pallas as pl
from jax.experimental.pallas import tpu as pltpu
from jax.sharding import PartitionSpec as P

CONV = 4
EPS = 1e-06
DECAY = 8.0
HALF = jnp.bfloat16
SINGLE = jnp.float32
MESH = pl.DeviceIdType.MESH
VMEM_BYTES = 56 * 1024 * 1024
GELU_C = 0.7978845608028654
GELU_K = 0.044715


def dot_nn(left, right):
    return lax.dot_general(
        left, right, (((1,), (0,)), ((), ())), preferred_element_type=SINGLE
    )


def dot_nt(left, right):
    return lax.dot_general(
        left, right, (((1,), (1,)), ((), ())), preferred_element_type=SINGLE
    )


def dot_tn(left, right):
    return lax.dot_general(
        left, right, (((0,), (0,)), ((), ())), preferred_element_type=SINGLE
    )


def gelu(v):
    return 0.5 * v * (1.0 + jnp.tanh(GELU_C * (v + GELU_K * v * v * v)))


def gelu_both(v):
    square = v * v
    t = jnp.tanh(GELU_C * (v + GELU_K * v * square))
    value = 0.5 * v * (1.0 + t)
    slope = 0.5 * (1.0 + t) + 0.5 * v * (1.0 - t * t) * (GELU_C * (1.0 + 3.0 * GELU_K * square))
    return value, slope


def flip(me, mask, count):
    place = me
    bit = 1
    while bit < count:
        if mask & bit:
            place = place + (1 - 2 * ((me // bit) % 2)) * bit
        bit *= 2
    return place


def all_bits():
    inner, outer = lax.axis_size("mp"), lax.axis_size("dp")
    bits = [(1 << b, "mp", 1 << b) for b in range(inner.bit_length() - 1)]
    return bits + [(inner << b, "dp", 1 << b) for b in range(outer.bit_length() - 1)]


def across(axis, bit):
    return {axis: flip(lax.axis_index(axis), bit, 2 * bit)}


def greet(bits):
    barrier = pltpu.get_barrier_semaphore()
    for _, axis, bit in bits:
        pl.semaphore_signal(barrier, inc=1, device_id=across(axis, bit), device_id_type=MESH)
    pl.semaphore_wait(barrier, len(bits))


def share_kernel(x_ref, o_ref, send, recv):
    bits = all_bits()
    place = lax.axis_index("dp") * lax.axis_size("mp") + lax.axis_index("mp")
    o_ref[place] = x_ref[...]
    greet(bits)
    copies = []
    for j, (size, axis, bit) in enumerate(bits):
        window = o_ref.at[pl.ds(place // size * size, size)]
        copy = pltpu.make_async_remote_copy(
            src_ref=window,
            dst_ref=window,
            send_sem=send.at[j],
            recv_sem=recv.at[j],
            device_id=across(axis, bit),
            device_id_type=MESH,
        )
        copy.start()
        copy.wait_recv()
        copies.append(copy)
    for copy in copies:
        copy.wait_send()


def share(x, collective_id):
    bits = all_bits()
    return pl.pallas_call(
        share_kernel,
        out_shape=jax.ShapeDtypeStruct((1 << len(bits),) + x.shape, x.dtype),
        in_specs=[pl.BlockSpec(memory_space=pltpu.VMEM)],
        out_specs=pl.BlockSpec(memory_space=pltpu.VMEM),
        scratch_shapes=[
            pltpu.SemaphoreType.DMA((len(bits),)),
            pltpu.SemaphoreType.DMA((len(bits),)),
        ],
        compiler_params=pltpu.CompilerParams(
            collective_id=collective_id, has_side_effects=True
        ),
        name="share",
    )(x)


def total_kernel(x_ref, o_ref, kept, landed, send, recv):
    bits = all_bits()
    place = lax.axis_index("dp") * lax.axis_size("mp") + lax.axis_index("mp")
    kept[...] = x_ref[...]
    greet(bits)
    copies = []
    for j, (size, axis, bit) in reversed(list(enumerate(bits))):
        first = place // size * size
        other = first + (1 - 2 * ((place // size) % 2)) * size
        copy = pltpu.make_async_remote_copy(
            src_ref=kept.at[pl.ds(other, size)],
            dst_ref=landed.at[pl.ds(size, size)],
            send_sem=send.at[j],
            recv_sem=recv.at[j],
            device_id=across(axis, bit),
            device_id_type=MESH,
        )
        copy.start()
        copy.wait_recv()
        mine = pl.ds(first, size)
        kept[mine] = kept[mine] + landed[size : 2 * size]
        copies.append(copy)
    o_ref[...] = kept[place]
    for copy in copies:
        copy.wait_send()


def total(x, collective_id):
    bits = all_bits()
    return pl.pallas_call(
        total_kernel,
        out_shape=jax.ShapeDtypeStruct(x.shape[1:], x.dtype),
        in_specs=[pl.BlockSpec(memory_space=pltpu.VMEM)],
        out_specs=pl.BlockSpec(memory_space=pltpu.VMEM),
        scratch_shapes=[
            pltpu.VMEM(x.shape, x.dtype),
            pltpu.VMEM(x.shape, x.dtype),
            pltpu.SemaphoreType.DMA((len(bits),)),
            pltpu.SemaphoreType.DMA((len(bits),)),
        ],
        compiler_params=pltpu.CompilerParams(
            collective_id=collective_id, has_side_effects=True
        ),
        name="total",
    )(x)


def gather_plan(count):
    bits = [1 << b for b in range(count.bit_length() - 1)]
    outer = bits[1:]
    orders = (outer + bits[:1], outer[::-1] + bits[:1])
    sends = []
    for half, order in enumerate(orders):
        for stage, bit in enumerate(order):
            for pick in range(1 << stage):
                mask = sum(order[j] for j in range(stage) if pick >> j & 1)
                sends.append((bin(mask).count("1"), half, mask, bit))
    sends.sort(key=lambda s: s[0])
    return bits, [s[1:] for s in sends]


def start_barrier(masks, count):
    me = lax.axis_index("mp")
    barrier = pltpu.get_barrier_semaphore()
    for mask in masks:
        pl.semaphore_signal(
            barrier, inc=1, device_id={"mp": flip(me, mask, count)}, device_id_type=MESH
        )
    pl.semaphore_wait(barrier, len(masks))


def gather_kernel(count, x_ref, o_ref, own_sem, send, recv):
    me = lax.axis_index("mp")
    rows = x_ref.shape[0]
    bits, plan = gather_plan(count)
    own = pltpu.make_async_copy(x_ref, o_ref.at[me], own_sem)
    own.start()
    start_barrier(bits, count)
    copies = {}
    landed = set()
    for half, mask, bit in plan:
        span = pl.ds(half * (rows // 2), rows // 2)
        slot = flip(me, mask, count)
        if mask and (half, mask) not in landed:
            copies[(half, mask)].wait_recv()
            landed.add((half, mask))
        source = o_ref.at[slot, span] if mask else x_ref.at[span]
        copy = pltpu.make_async_remote_copy(
            src_ref=source,
            dst_ref=o_ref.at[slot, span],
            send_sem=send.at[half, mask | bit],
            recv_sem=recv.at[half, mask | bit],
            device_id={"mp": flip(me, bit, count)},
            device_id_type=MESH,
        )
        copy.start()
        copies[(half, mask | bit)] = copy
    for key, copy in copies.items():
        if key not in landed:
            copy.wait_recv()
    for copy in copies.values():
        copy.wait_send()
    own.wait()


def gather_rows(x, collective_id):
    count = lax.axis_size("mp")
    if count != 8:
        return lax.all_gather(x, "mp", axis=0, tiled=False)
    rows, width = x.shape
    return pl.pallas_call(
        functools.partial(gather_kernel, count),
        out_shape=jax.ShapeDtypeStruct((count, rows, width), x.dtype),
        in_specs=[pl.BlockSpec(memory_space=pl.ANY)],
        out_specs=pl.BlockSpec(memory_space=pl.ANY),
        scratch_shapes=[
            pltpu.SemaphoreType.DMA,
            pltpu.SemaphoreType.DMA((2, count)),
            pltpu.SemaphoreType.DMA((2, count)),
        ],
        compiler_params=pltpu.CompilerParams(
            collective_id=collective_id, has_side_effects=True, vmem_limit_bytes=VMEM_BYTES
        ),
        cost_estimate=pl.CostEstimate(
            flops=0, bytes_accessed=2 * count * rows * width * 2 * 4, transcendentals=0
        ),
        name="gather_rows",
    )(x)


def scatter_kernel(products, tile, *refs):
    count = 8
    pairs = len(products)
    lefts, rights = refs[:pairs], refs[pairs : 2 * pairs]
    out_ref = refs[2 * pairs]
    acc, core_out, core_in, link_out, link_in = refs[2 * pairs + 1 : 2 * pairs + 6]
    core_send, core_recv, link_send, link_recv = refs[2 * pairs + 6 :]
    rows, width = out_ref.shape
    me = lax.axis_index("mp")
    start_barrier((1, 2, 4), count)

    def partial(slot, store):
        first = pl.multiple_of(slot * rows, rows)

        def step(t, carry):
            columns = pl.ds(pl.multiple_of(t * tile, tile), tile)
            total = None
            for left, right, product in zip(lefts, rights, products):
                term = product(left[pl.ds(first, rows), :], right, t, columns)
                total = term if total is None else total + term
            store(columns, total)
            return carry

        lax.fori_loop(0, width // tile, step, 0)

    def into_core(c):
        def store(columns, total):
            core_out[c, :, columns] = total.astype(HALF)

        return store

    def into_acc(c):
        def store(columns, total):
            acc[c, :, columns] = total

        return store

    core_copies = {}
    link_copies = {}
    middle = rows // 2

    def core_half(c):
        partial(flip(me, 2 * c + 1, count), into_core(c))
        copy = pltpu.make_async_remote_copy(
            src_ref=core_out.at[c],
            dst_ref=core_in.at[c],
            send_sem=core_send.at[c],
            recv_sem=core_recv.at[c],
            device_id={"mp": flip(me, 1, count)},
            device_id_type=MESH,
        )
        copy.start()
        core_copies[c] = copy

    def core_sum(c):
        core_copies[c].wait_recv()

        def step(t, carry):
            columns = pl.ds(pl.multiple_of(t * tile, tile), tile)
            acc[c, :, columns] = acc[c, :, columns] + core_in[c, :, columns].astype(SINGLE)
            return carry

        lax.fori_loop(0, width // tile, step, 0)

    def link(index, c, half, axis):
        span = pl.ds(half * middle, middle)

        def step(t, carry):
            columns = pl.ds(pl.multiple_of(t * tile, tile), tile)
            link_out[index, :, columns] = acc[c, span, columns].astype(HALF)
            return carry

        lax.fori_loop(0, width // tile, step, 0)
        copy = pltpu.make_async_remote_copy(
            src_ref=link_out.at[index],
            dst_ref=link_in.at[index],
            send_sem=link_send.at[index],
            recv_sem=link_recv.at[index],
            device_id={"mp": flip(me, 2 * axis, count)},
            device_id_type=MESH,
        )
        copy.start()
        link_copies[index] = copy

    def link_sum(index, c, half):
        link_copies[index].wait_recv()
        span = pl.ds(half * middle, middle)

        def step(t, carry):
            columns = pl.ds(pl.multiple_of(t * tile, tile), tile)
            acc[c, span, columns] = acc[c, span, columns] + link_in[index, :, columns].astype(
                SINGLE
            )
            return carry

        lax.fori_loop(0, width // tile, step, 0)

    core_half(3)
    partial(flip(me, 6, count), into_acc(3))
    core_half(1)
    core_sum(3)
    link(0, 3, 0, 2)
    link(1, 3, 1, 1)
    partial(flip(me, 2, count), into_acc(1))
    core_half(2)
    core_sum(1)
    link(2, 1, 1, 1)
    partial(flip(me, 4, count), into_acc(2))
    core_half(0)
    core_sum(2)
    link(3, 2, 0, 2)
    partial(me, into_acc(0))
    core_sum(0)
    link_sum(0, 1, 0)
    link(4, 1, 0, 1)
    link_sum(1, 2, 1)
    link(5, 2, 1, 2)
    link_sum(2, 0, 1)
    link_sum(3, 0, 0)
    link_sum(4, 0, 0)
    link_sum(5, 0, 1)
    out_ref[...] = acc[0]
    for copy in core_copies.values():
        copy.wait_send()
    for copy in link_copies.values():
        copy.wait_send()


def scatter_products(lefts, rights, products, fallback, width, tile, collective_id, flops):
    count = lax.axis_size("mp")
    tokens = lefts[0].shape[0]
    rows = tokens // count
    if count != 8:
        return lax.psum_scatter(
            fallback().astype(HALF), "mp", scatter_dimension=0, tiled=True
        ).astype(SINGLE)
    return pl.pallas_call(
        functools.partial(scatter_kernel, products, tile),
        out_shape=jax.ShapeDtypeStruct((rows, width), SINGLE),
        in_specs=[pl.BlockSpec(memory_space=pltpu.VMEM)] * (len(lefts) + len(rights)),
        out_specs=pl.BlockSpec(memory_space=pltpu.VMEM),
        scratch_shapes=[
            pltpu.VMEM((4, rows, width), SINGLE),
            pltpu.VMEM((4, rows, width), HALF),
            pltpu.VMEM((4, rows, width), HALF),
            pltpu.VMEM((6, rows // 2, width), HALF),
            pltpu.VMEM((6, rows // 2, width), HALF),
            pltpu.SemaphoreType.DMA((4,)),
            pltpu.SemaphoreType.DMA((4,)),
            pltpu.SemaphoreType.DMA((6,)),
            pltpu.SemaphoreType.DMA((6,)),
        ],
        compiler_params=pltpu.CompilerParams(
            collective_id=collective_id, has_side_effects=True, vmem_limit_bytes=VMEM_BYTES
        ),
        cost_estimate=pl.CostEstimate(
            flops=flops, bytes_accessed=tokens * width * 2 * 8, transcendentals=0
        ),
        name="scatter_products",
    )(*lefts, *rights)


def positions(lens_ref, first, shape):
    place = lax.broadcasted_iota(jnp.int32, shape, 0) + first
    begin = jnp.zeros(shape, jnp.int32)
    total = 0
    for j in range(lens_ref.shape[1]):
        total = total + lens_ref[0, j]
        begin = jnp.where(place >= total, total, begin)
    return place - begin, place < total


def split_dot(dot, left, right):
    high = left.astype(HALF)
    low = (left - high.astype(SINGLE)).astype(HALF)
    return dot(high, right) + dot(low, right)


def lane_tiles(width):
    return [(t, t * 128, min(128, width - t * 128)) for t in range(-(-width // 128))]


def put_tiles(ref, value):
    for t, first, lanes in lane_tiles(value.shape[1]):
        ref[t, :, :lanes] = value[:, first : first + lanes]


def scan_start(tiles, lanes):
    return [(jnp.zeros((lanes, 128), SINGLE), jnp.ones((lanes, 128), SINGLE)) for _ in tiles]


def sigmoid(v):
    return 1.0 / (1.0 + jnp.exp(-v))


def forward_kernel(
    lens_ref,
    x_ref,
    gain_ref,
    pack_ref,
    bin_ref,
    ba_ref,
    chan_ref,
    n1_ref,
    bx_ref,
    by_ref,
    conv_ref,
    gi_ref,
    ra_ref,
    h_ref,
    ob_ref,
    taps,
    coef,
    drive,
    carry,
):
    step = pl.program_id(0)
    rows, width = bx_ref.shape
    depth = pack_ref.shape[2]
    lanes = 8
    span = rows // lanes

    @pl.when(step == 0)
    def _():
        taps[...] = jnp.zeros_like(taps)
        carry[...] = jnp.zeros_like(carry)
        coef[...] = jnp.zeros_like(coef)
        drive[...] = jnp.zeros_like(drive)

    x = x_ref[0].astype(SINGLE)
    scale = lax.rsqrt(jnp.mean(x * x, axis=-1, keepdims=True) + EPS)
    normed = (x * scale * gain_ref[...]).astype(HALF)
    n1_ref[...] = normed
    total = None
    for d in range(pack_ref.shape[0]):
        term = dot_nt(normed[:, d * depth : (d + 1) * depth], pack_ref[d, : 2 * width, :])
        total = term if total is None else total + term
    bx = total[:, :width].astype(HALF)
    by = total[:, width:]
    bx_ref[...] = bx
    by_ref[...] = by
    pos, live = positions(lens_ref, step * rows, (rows, width))
    taps[0:8, :] = taps[rows : rows + 8, :]
    taps[8 : rows + 8, :] = bx.astype(SINGLE)
    conv = jnp.zeros((rows, width), SINGLE) + chan_ref[CONV : CONV + 1, :]
    for k in range(CONV):
        moved = taps[8 - k : 8 - k + rows, :]
        conv = conv + jnp.where(pos >= k, moved * chan_ref[k : k + 1, :], 0.0)
    conv_ref[...] = conv
    high = conv.astype(HALF)
    low = (conv - high.astype(SINGLE)).astype(HALF)
    gate_in = sigmoid(
        dot_nn(high, bin_ref[...]) + dot_nn(low, bin_ref[...]) + chan_ref[CONV + 1 : CONV + 2, :]
    )
    gate_a = sigmoid(
        dot_nn(high, ba_ref[...]) + dot_nn(low, ba_ref[...]) + chan_ref[CONV + 2 : CONV + 3, :]
    )
    gi_ref[...] = gate_in
    ra_ref[...] = gate_a
    decay = jnp.exp(-DECAY * gate_a * chan_ref[CONV + 4 : CONV + 5, :])
    root = jnp.sqrt(1.0 - decay * decay)
    put_tiles(coef, jnp.where(pos == 0, 0.0, decay))
    put_tiles(drive, gate_in * conv * root)
    tiles = lane_tiles(width)

    def scan(i, state):
        at = pl.ds(i, lanes, stride=span)
        result = []
        for (t, _, _), (h, prod) in zip(tiles, state):
            a = coef[t, at, :]
            h = a * h + drive[t, at, :]
            prod = prod * a
            drive[t, at, :] = h
            coef[t, at, :] = prod
            result.append((h, prod))
        return result

    state = lax.fori_loop(0, span, scan, scan_start(tiles, lanes), unroll=4)
    for (t, first, used), (h, prod) in zip(tiles, state):
        running = carry[t, 0:1, :]
        for s in range(lanes):
            at = slice(s * span, (s + 1) * span)
            value = drive[t, at, :] + coef[t, at, :] * running
            h_ref[at, first : first + used] = value[:, :used]
            running = h[s : s + 1, :] + prod[s : s + 1, :] * running
        carry[t, 0:1, :] = running
    mixed = h_ref[...].astype(HALF).astype(SINGLE)
    ob_ref[...] = jnp.where(live, gelu(by) * mixed, 0.0).astype(HALF)


def forward_channels(lens, x_all, gain, pack, blocks_in, blocks_a, chan):
    count, rows, model = x_all.shape
    width = chan.shape[1]
    tokens = count * rows
    whole = lambda shape: pl.BlockSpec(shape, lambda i: (0,) * len(shape))
    part = pl.BlockSpec((rows, width), lambda i: (i, 0))
    full = lambda kind: jax.ShapeDtypeStruct((tokens, width), kind)
    return pl.pallas_call(
        forward_kernel,
        grid=(count,),
        out_shape=(
            jax.ShapeDtypeStruct((tokens, model), HALF),
            full(HALF),
            full(SINGLE),
            full(SINGLE),
            full(SINGLE),
            full(SINGLE),
            full(SINGLE),
            full(HALF),
        ),
        in_specs=[
            pl.BlockSpec(memory_space=pltpu.SMEM),
            pl.BlockSpec((1, rows, model), lambda i: (i, 0, 0)),
            whole(gain.shape),
            whole(pack.shape),
            whole(blocks_in.shape),
            whole(blocks_a.shape),
            whole(chan.shape),
        ],
        out_specs=(pl.BlockSpec((rows, model), lambda i: (i, 0)),) + (part,) * 7,
        scratch_shapes=[
            pltpu.VMEM((rows + 8, width), SINGLE),
            pltpu.VMEM((len(lane_tiles(width)), rows, 128), SINGLE),
            pltpu.VMEM((len(lane_tiles(width)), rows, 128), SINGLE),
            pltpu.VMEM((len(lane_tiles(width)), 8, 128), SINGLE),
        ],
        compiler_params=pltpu.CompilerParams(vmem_limit_bytes=VMEM_BYTES),
        cost_estimate=pl.CostEstimate(
            flops=2 * tokens * model * 2 * width,
            bytes_accessed=tokens * (model * 4 + width * 24),
            transcendentals=8 * tokens * width,
        ),
        name="forward_channels",
    )(lens, x_all, gain, pack, blocks_in, blocks_a, chan)


def backward_kernel(
    lens_ref,
    dt_ref,
    pack_ref,
    bin_ref,
    ba_ref,
    chan_ref,
    bx_ref,
    by_ref,
    conv_ref,
    gi_ref,
    ra_ref,
    h_ref,
    hprev_ref,
    ob_ref,
    n1_ref,
    dbx_ref,
    dby_ref,
    gin_ref,
    ga_ref,
    gchan_ref,
    grads_ref,
    grads,
    lift,
    coef,
    drive,
    carry,
):
    step = pl.program_id(0)
    chunk = pl.num_programs(0) - 1 - step
    rows, width = bx_ref.shape
    depth = pack_ref.shape[2]
    lanes = 8
    span = rows // lanes

    @pl.when(step == 0)
    def _():
        lift[...] = jnp.zeros_like(lift)
        carry[...] = jnp.zeros_like(carry)
        coef[...] = jnp.zeros_like(coef)
        drive[...] = jnp.zeros_like(drive)
        gin_ref[...] = jnp.zeros_like(gin_ref)
        ga_ref[...] = jnp.zeros_like(ga_ref)
        gchan_ref[...] = jnp.zeros_like(gchan_ref)
        grads[...] = jnp.zeros_like(grads)

    d_out = None
    for d in range(pack_ref.shape[0]):
        term = dot_nt(
            dt_ref[0, :, d * depth : (d + 1) * depth], pack_ref[d, 2 * width : 3 * width, :]
        )
        d_out = term if d_out is None else d_out + term
    pos, live = positions(lens_ref, chunk * rows, (rows, width))
    by = by_ref[...]
    h = h_ref[...]
    side, slope = gelu_both(by)
    d_out = jnp.where(live, d_out, 0.0)
    dby_ref[...] = (d_out * h.astype(HALF).astype(SINGLE) * slope).astype(HALF)
    gate_a = ra_ref[...]
    soft = chan_ref[CONV + 4 : CONV + 5, :]
    decay = jnp.exp(-DECAY * gate_a * soft)
    put_tiles(coef, jnp.where(pos == 0, 0.0, decay))
    put_tiles(drive, (d_out * side).astype(HALF).astype(SINGLE))
    tiles = lane_tiles(width)

    def scan(j, state):
        at = pl.ds(span - 1 - j, lanes, stride=span)
        result = []
        for (t, _, _), (after, prod) in zip(tiles, state):
            a = coef[t, at, :]
            lam = drive[t, at, :] + after
            drive[t, at, :] = lam
            coef[t, at, :] = prod
            result.append((a * lam, prod * a))
        return result

    state = lax.fori_loop(0, span, scan, scan_start(tiles, lanes), unroll=4)
    for (t, first, used), (after, prod) in zip(tiles, state):
        running = carry[t, 0:1, :]
        for s in reversed(range(lanes)):
            at = slice(s * span, (s + 1) * span)
            value = drive[t, at, :] + coef[t, at, :] * running
            lift[at, first : first + used] = value[:, :used]
            running = after[s : s + 1, :] + prod[s : s + 1, :] * running
        carry[t, 0:1, :] = running
    lam = lift[0:rows, :]
    last = jnp.where(chunk > 0, hprev_ref[7:8, :], 0.0)
    before = jnp.concatenate([last, h[: rows - 1, :]], axis=0)
    before = jnp.where(pos == 0, 0.0, before)
    conv = conv_ref[...]
    gate_in = gi_ref[...]
    root = jnp.sqrt(1.0 - decay * decay)
    d_decay = lam * before - lam * gate_in * conv * decay / root
    d_log = d_decay * decay
    d_a = d_log * (-DECAY * soft)
    d_in = lam * conv * root
    d_logit_in = d_in * gate_in * (1.0 - gate_in)
    d_logit_a = d_a * gate_a * (1.0 - gate_a)
    d_conv = (
        lam * gate_in * root
        + split_dot(dot_nt, d_logit_in, bin_ref[...])
        + split_dot(dot_nt, d_logit_a, ba_ref[...])
    )
    low = conv.astype(HALF)
    gin_ref[...] += dot_tn(low, d_logit_in.astype(HALF))
    ga_ref[...] += dot_tn(low, d_logit_a.astype(HALF))
    lift[0:rows, :] = d_conv
    bx = bx_ref[...].astype(SINGLE)
    d_bx = jnp.zeros((rows, width), SINGLE)
    for k in range(CONV):
        if k:
            ahead, _ = positions(lens_ref, chunk * rows + k, (rows, width))
            moved = jnp.where(ahead >= k, lift[k : k + rows, :], 0.0)
        else:
            moved = d_conv
        d_bx = d_bx + moved * chan_ref[k : k + 1, :]
        gchan_ref[k : k + 1, :] += jnp.sum(moved * bx, axis=0, keepdims=True)
    dbx_ref[...] = d_bx.astype(HALF)
    lift[rows : rows + 8, :] = d_conv[0:8, :]
    sums = (d_conv, d_logit_in, d_logit_a, d_log * gate_a)
    for j, value in enumerate(sums):
        gchan_ref[CONV + j : CONV + j + 1, :] += jnp.sum(value, axis=0, keepdims=True)
    lefts = (dbx_ref[...], dby_ref[...], ob_ref[...])
    for d in range(grads.shape[0]):
        columns = slice(d * depth, (d + 1) * depth)
        rights = (n1_ref[:, columns], n1_ref[:, columns], dt_ref[0, :, columns])
        for j, (left, right) in enumerate(zip(lefts, rights)):
            grads[d, j * width : (j + 1) * width, :] += dot_tn(left, right)

    @pl.when(chunk == 0)
    def _():
        grads_ref[...] = grads[...].astype(HALF)


def backward_channels(lens, dt_all, pack, blocks_in, blocks_a, chan, saved):
    bx, by, conv, gate_in, gate_a, h, ob, n1 = saved
    count, rows, model = dt_all.shape
    width = chan.shape[1]
    tokens = count * rows
    last = count - 1
    whole = lambda shape: pl.BlockSpec(shape, lambda i: (0,) * len(shape))
    part = pl.BlockSpec((rows, width), lambda i: (last - i, 0))
    before = pl.BlockSpec(
        (8, width), lambda i: (jnp.maximum((last - i) * (rows // 8) - 1, 0), 0)
    )
    full = lambda kind: jax.ShapeDtypeStruct((tokens, width), kind)
    square = jax.ShapeDtypeStruct((width, width), SINGLE)
    grads = (pack.shape[0], 3 * width, pack.shape[2])
    return pl.pallas_call(
        backward_kernel,
        grid=(count,),
        out_shape=(
            full(HALF),
            full(HALF),
            square,
            square,
            jax.ShapeDtypeStruct((8, width), SINGLE),
            jax.ShapeDtypeStruct(grads, HALF),
        ),
        in_specs=[
            pl.BlockSpec(memory_space=pltpu.SMEM),
            pl.BlockSpec((1, rows, model), lambda i: (last - i, 0, 0)),
            whole(pack.shape),
            whole(blocks_in.shape),
            whole(blocks_a.shape),
            whole(chan.shape),
            part,
            part,
            part,
            part,
            part,
            part,
            before,
            part,
            pl.BlockSpec((rows, model), lambda i: (last - i, 0)),
        ],
        out_specs=(
            part,
            part,
            whole((width, width)),
            whole((width, width)),
            whole((8, width)),
            whole(grads),
        ),
        scratch_shapes=[
            pltpu.VMEM(grads, SINGLE),
            pltpu.VMEM((rows + 8, width), SINGLE),
            pltpu.VMEM((len(lane_tiles(width)), rows, 128), SINGLE),
            pltpu.VMEM((len(lane_tiles(width)), rows, 128), SINGLE),
            pltpu.VMEM((len(lane_tiles(width)), 8, 128), SINGLE),
        ],
        compiler_params=pltpu.CompilerParams(vmem_limit_bytes=VMEM_BYTES),
        cost_estimate=pl.CostEstimate(
            flops=2 * tokens * model * width,
            bytes_accessed=tokens * (model * 2 + width * 28),
            transcendentals=8 * tokens * width,
        ),
        name="backward_channels",
    )(lens, dt_all, pack, blocks_in, blocks_a, chan, bx, by, conv, gate_in, gate_a, h, h, ob, n1)


def diagonal(blocks):
    count, size, _ = blocks.shape
    spread = blocks[:, :, None, :] * jnp.eye(count, dtype=blocks.dtype)[:, None, :, None]
    return spread.reshape(count * size, count * size)


def on_device(
    layer_input,
    cotangent,
    norm_in,
    norm_mid,
    w_rnn_in,
    w_rnn_gate,
    w_rnn_out,
    gate_in_blocks,
    gate_a_blocks,
    channel_params,
    w_mlp_gate,
    w_mlp_up,
    w_mlp_down,
    lengths,
):
    parts = lax.axis_size("dp")
    rows, model = layer_input.shape
    depth, width = w_rnn_in.shape
    heads, bite, block = gate_in_blocks.shape
    tokens = rows * lax.axis_size("mp")

    flat = jnp.concatenate(
        [
            gate_in_blocks.astype(HALF).reshape(-1),
            gate_a_blocks.astype(HALF).reshape(-1),
            channel_params.astype(HALF).reshape(-1),
        ]
    )
    used = flat.shape[0]
    small_rows = -(-used // (16 * depth)) * 16
    flat = jnp.pad(flat, (0, small_rows * depth - used)).reshape(small_rows, depth)
    mine = jnp.concatenate(
        [
            w_rnn_in.astype(HALF).T,
            w_rnn_gate.astype(HALF).T,
            w_rnn_out.astype(HALF),
            flat,
        ],
        axis=0,
    )
    pack = lax.all_gather(mine, "dp", axis=0, tiled=False)
    down = lax.all_gather(w_mlp_down.astype(HALF), "dp", axis=1, tiled=True)
    gate_w = lax.all_gather(w_mlp_gate.astype(HALF), "dp", axis=0, tiled=True)
    up_w = lax.all_gather(w_mlp_up.astype(HALF), "dp", axis=0, tiled=True)
    bite_gain = norm_in.shape[0]
    gains = jnp.stack([norm_in, norm_mid]).astype(HALF).astype(SINGLE)
    gains = share(jnp.pad(gains, ((0, 6), (0, 128 - bite_gain))), 8)
    gain_first = gains[:, 0, :bite_gain].reshape(1, model)
    gain_second = gains[:, 1, :bite_gain].reshape(1, model)

    small = pack[:, 3 * width :, :].reshape(parts, -1)
    size = heads * bite * block
    whole_block = lambda v: diagonal(
        v.reshape(parts, heads, bite, block).transpose(1, 0, 2, 3).reshape(heads, block, block)
    )
    blocks_in = whole_block(small[:, :size])
    blocks_a = whole_block(small[:, size : 2 * size])
    channel = small[:, 2 * size : used].reshape(2 * CONV, width).astype(SINGLE)
    soft = jax.nn.softplus(-channel[2 * CONV - 1 :])
    chan = jnp.concatenate([channel, soft, jnp.zeros((7, width), SINGLE)], axis=0)

    x_all = gather_rows(layer_input, 0)
    c_all = gather_rows(cotangent, 1).reshape(tokens, model)
    n1, bx, by, conv, gate_in, gate_a, h, ob = forward_channels(
        lengths, x_all, gain_first, pack, blocks_in, blocks_a, chan
    )
    inputs = layer_input.astype(SINGLE)
    out = scatter_products(
        [ob],
        [pack],
        [lambda l, r, t, cols: dot_nn(l, r[t, 2 * width : 3 * width, :])],
        lambda: jnp.einsum(
            "tc,dcm->tdm", ob, pack[:, 2 * width : 3 * width], preferred_element_type=SINGLE
        ).reshape(tokens, model),
        model,
        depth,
        2,
        2 * tokens * width * model,
    )
    residual = inputs + out
    scale_second = lax.rsqrt(jnp.mean(residual * residual, axis=-1, keepdims=True) + EPS)
    normed_mid = (residual * scale_second * gain_second).astype(HALF)
    n2 = gather_rows(normed_mid, 3).reshape(tokens, model)

    def over_dp(value, dimension):
        return lax.psum_scatter(
            value.astype(HALF), "dp", scatter_dimension=dimension, tiled=True
        )

    d_hidden = dot_nt(c_all, down)
    gate_pre = dot_nn(n2, gate_w)
    act, slope = gelu_both(gate_pre)
    d_up = (d_hidden * act).astype(HALF)
    grad_up = over_dp(dot_tn(n2, d_up), 0)
    up_pre = dot_nn(n2, up_w)
    hidden = (act * up_pre).astype(HALF)
    d_gate = (d_hidden * up_pre * slope).astype(HALF)
    grad_gate = dot_tn(n2, d_gate).astype(HALF)
    d_gate, grad_gate = lax.optimization_barrier((d_gate, grad_gate))
    grad_gate = over_dp(grad_gate, 0)
    tile = 512
    by_rows = lambda l, r, t, cols: dot_nt(l, r[cols, :])
    d_normed_mid = scatter_products(
        [d_gate, d_up],
        [gate_w, up_w],
        [by_rows, by_rows],
        lambda: dot_nt(d_gate, gate_w) + dot_nt(d_up, up_w),
        model,
        tile,
        4,
        4 * tokens * model * up_w.shape[1],
    )
    hidden, d_normed_mid = lax.optimization_barrier((hidden, d_normed_mid))
    grad_down = dot_tn(c_all, hidden).astype(HALF)
    d_normed_mid, grad_down = lax.optimization_barrier((d_normed_mid, grad_down))
    grad_down = over_dp(grad_down, 0)

    weighted_second = gain_second * d_normed_mid
    grad_gain_second = jnp.sum(d_normed_mid * residual * scale_second, axis=0)
    cube_second = scale_second * scale_second * scale_second
    d_residual = (
        cotangent.astype(SINGLE)
        + scale_second * weighted_second
        - residual * cube_second * jnp.mean(weighted_second * residual, axis=-1, keepdims=True)
    )
    d_resid_low, grad_up = lax.optimization_barrier((d_residual.astype(HALF), grad_up))
    dt_all = gather_rows(d_resid_low, 6)
    dt_all, grad_gate = lax.optimization_barrier((dt_all, grad_gate))

    saved = (bx, by, conv, gate_in, gate_a, h, ob, n1)
    d_bx, d_by, gin, ga, gchan, rnn_grads = backward_channels(
        lengths, dt_all, pack, blocks_in, blocks_a, chan, saved
    )
    d_bx, grad_down = lax.optimization_barrier((d_bx, grad_down))
    d_normed = scatter_products(
        [d_bx, d_by],
        [pack, pack],
        [
            lambda l, r, t, cols: dot_nn(l, r[t, :width, :]),
            lambda l, r, t, cols: dot_nn(l, r[t, width : 2 * width, :]),
        ],
        lambda: jnp.einsum(
            "tc,dcm->tdm",
            jnp.concatenate([d_bx, d_by], axis=1),
            pack[:, : 2 * width],
            preferred_element_type=SINGLE,
        ).reshape(tokens, model),
        model,
        depth,
        7,
        4 * tokens * width * model,
    )
    rnn_grads = over_dp(rnn_grads, 0)
    hidden, d_normed = lax.optimization_barrier((hidden, d_normed))
    mlp_out = scatter_products(
        [hidden],
        [down],
        [lambda l, r, t, cols: dot_nn(l, r[:, cols])],
        lambda: dot_nn(hidden, down),
        model,
        tile,
        5,
        2 * tokens * model * up_w.shape[1],
    )
    mlp_out, rnn_grads = lax.optimization_barrier((mlp_out, rnn_grads))
    layer_output = (residual + mlp_out).astype(HALF)

    scale_first = lax.rsqrt(jnp.mean(inputs * inputs, axis=-1, keepdims=True) + EPS)
    weighted_first = gain_first * d_normed
    grad_gain_first = jnp.sum(d_normed * inputs * scale_first, axis=0)
    cube_first = scale_first * scale_first * scale_first
    grad_input = (
        d_residual
        + scale_first * weighted_first
        - inputs * cube_first * jnp.mean(weighted_first * inputs, axis=-1, keepdims=True)
    )

    own = lambda full: jnp.stack(
        [full[j * block : (j + 1) * block, j * block : (j + 1) * block] for j in range(heads)]
    )
    decay_row = DECAY * jax.nn.sigmoid(-channel[2 * CONV - 1 :]) * gchan[2 * CONV - 1 :]
    grad_channel = jnp.concatenate([gchan[: 2 * CONV - 1], decay_row], axis=0)
    split = lambda v: v.reshape(heads, parts, bite, block).transpose(1, 0, 2, 3).reshape(parts, -1)
    small_grads = jnp.concatenate(
        [split(own(gin)), split(own(ga)), grad_channel.reshape(parts, -1)], axis=1
    )
    small_grads = jnp.pad(small_grads, ((0, 0), (0, small_rows * depth - used)))
    small_grads = small_grads.reshape(parts, small_rows, depth)
    rnn_grads = rnn_grads[0].astype(SINGLE)
    flat_grads = over_dp(small_grads, 0).astype(SINGLE).reshape(-1)
    gain_grads = jnp.stack([grad_gain_first, grad_gain_second]).reshape(2, -1, bite_gain)
    gain_grads = jnp.pad(gain_grads.transpose(1, 0, 2), ((0, 0), (0, 6), (0, 128 - bite_gain)))
    gain_grads = total(gain_grads, 9)
    return (
        layer_output,
        grad_input,
        gain_grads[0, :bite_gain],
        gain_grads[1, :bite_gain],
        rnn_grads[:width].T,
        rnn_grads[width : 2 * width].T,
        rnn_grads[2 * width : 3 * width],
        flat_grads[:size].reshape(heads, bite, block),
        flat_grads[size : 2 * size].reshape(heads, bite, block),
        flat_grads[2 * size : used].reshape(channel_params.shape),
        grad_gate.astype(SINGLE),
        grad_up.astype(SINGLE),
        grad_down.T.astype(SINGLE),
    )


def solution(mesh):
    rows = P(("dp", "mp"), None)
    return jax.shard_map(
        on_device,
        mesh=mesh,
        in_specs=(
            rows,
            rows,
            P(("dp", "mp")),
            P(("dp", "mp")),
            P("dp", "mp"),
            P("dp", "mp"),
            P("mp", "dp"),
            P("mp", "dp", None),
            P("mp", "dp", None),
            P("dp", "mp"),
            P("dp", "mp"),
            P("dp", "mp"),
            P("mp", "dp"),
            P("dp", None),
        ),
        out_specs=(
            rows,
            rows,
            P(("dp", "mp")),
            P(("dp", "mp")),
            P("dp", "mp"),
            P("dp", "mp"),
            P("mp", "dp"),
            P("mp", "dp", None),
            P("mp", "dp", None),
            P("dp", "mp"),
            P("dp", "mp"),
            P("dp", "mp"),
            P("mp", "dp"),
        ),
        check_vma=False,
    )
```

```python
import functools

import jax
import jax.numpy as jnp
from jax import lax
from jax.experimental import pallas as pl
from jax.experimental.pallas import tpu as pltpu
from jax.sharding import PartitionSpec as P

CONV = 4
EPS = 1e-06
DECAY = 8.0
HALF = jnp.bfloat16
SINGLE = jnp.float32
MESH = pl.DeviceIdType.MESH
VMEM_BYTES = 56 * 1024 * 1024
GELU_C = 0.7978845608028654
GELU_K = 0.044715


def dot_nn(left, right):
    return lax.dot_general(
        left, right, (((1,), (0,)), ((), ())), preferred_element_type=SINGLE
    )


def dot_nt(left, right):
    return lax.dot_general(
        left, right, (((1,), (1,)), ((), ())), preferred_element_type=SINGLE
    )


def dot_tn(left, right):
    return lax.dot_general(
        left, right, (((0,), (0,)), ((), ())), preferred_element_type=SINGLE
    )


def gelu(v):
    return 0.5 * v * (1.0 + jnp.tanh(GELU_C * (v + GELU_K * v * v * v)))


def gelu_both(v):
    square = v * v
    t = jnp.tanh(GELU_C * (v + GELU_K * v * square))
    value = 0.5 * v * (1.0 + t)
    slope = 0.5 * (1.0 + t) + 0.5 * v * (1.0 - t * t) * (GELU_C * (1.0 + 3.0 * GELU_K * square))
    return value, slope


def flip(me, mask, count):
    place = me
    bit = 1
    while bit < count:
        if mask & bit:
            place = place + (1 - 2 * ((me // bit) % 2)) * bit
        bit *= 2
    return place


def ring_peers(axis):
    me, count = lax.axis_index(axis), lax.axis_size(axis)
    return [(k, {axis: (me + k) % count}) for k in range(1, count)]


def greet(peers):
    barrier = pltpu.get_barrier_semaphore()
    for _, peer in peers:
        pl.semaphore_signal(barrier, inc=1, device_id=peer, device_id_type=MESH)
    pl.semaphore_wait(barrier, len(peers))


def exchange(peers, source, target, send, recv):
    copies = []
    for k, peer in peers:
        copy = pltpu.make_async_remote_copy(
            src_ref=source(k),
            dst_ref=target(k),
            send_sem=send.at[k],
            recv_sem=recv.at[k],
            device_id=peer,
            device_id_type=MESH,
        )
        copy.start()
        copies.append(copy)
    for copy in copies:
        copy.wait_recv()
    return copies


def share_kernel(x_ref, o_ref, send_mp, recv_mp, send_dp, recv_dp):
    inner, outer = ring_peers("mp"), ring_peers("dp")
    count = len(inner) + 1
    first = lax.axis_index("dp") * count
    place = first + lax.axis_index("mp")
    o_ref[place] = x_ref[...]
    greet(inner + outer)
    mine = lambda k: o_ref.at[place]
    plane = lambda k: o_ref.at[pl.ds(first, count)]
    copies = exchange(inner, mine, mine, send_mp, recv_mp)
    copies += exchange(outer, plane, plane, send_dp, recv_dp)
    for copy in copies:
        copy.wait_send()


def small_call(kernel, x, out_shape, scratch, collective_id, name):
    inner, outer = lax.axis_size("mp"), lax.axis_size("dp")
    sems = [pltpu.SemaphoreType.DMA((c,)) for c in (inner, inner, outer, outer)]
    return pl.pallas_call(
        kernel,
        out_shape=jax.ShapeDtypeStruct(out_shape, x.dtype),
        in_specs=[pl.BlockSpec(memory_space=pltpu.VMEM)],
        out_specs=pl.BlockSpec(memory_space=pltpu.VMEM),
        scratch_shapes=scratch + sems,
        compiler_params=pltpu.CompilerParams(
            collective_id=collective_id, has_side_effects=True
        ),
        name=name,
    )(x)


def share(x, collective_id):
    devices = lax.axis_size("mp") * lax.axis_size("dp")
    return small_call(share_kernel, x, (devices,) + x.shape, [], collective_id, "share")


def total_kernel(x_ref, o_ref, plane, landed_mp, landed_dp, send_mp, recv_mp, send_dp, recv_dp):
    inner, outer = ring_peers("mp"), ring_peers("dp")
    across, count = len(outer) + 1, len(inner) + 1
    me, level = lax.axis_index("mp"), lax.axis_index("dp")
    greet(inner + outer)
    copies = exchange(
        outer,
        lambda k: x_ref.at[pl.ds((level + k) % across * count, count)],
        lambda k: landed_dp.at[k],
        send_dp,
        recv_dp,
    )
    plane[...] = x_ref[pl.ds(level * count, count)]
    for k, _ in outer:
        plane[...] = plane[...] + landed_dp[k]
    copies += exchange(
        inner,
        lambda k: plane.at[(me + k) % count],
        lambda k: landed_mp.at[k],
        send_mp,
        recv_mp,
    )
    value = plane[me]
    for k, _ in inner:
        value = value + landed_mp[k]
    o_ref[...] = value
    for copy in copies:
        copy.wait_send()


def total(x, collective_id):
    inner, outer = lax.axis_size("mp"), lax.axis_size("dp")
    tile = x.shape[1:]
    scratch = [
        pltpu.VMEM((inner,) + tile, x.dtype),
        pltpu.VMEM((inner,) + tile, x.dtype),
        pltpu.VMEM((outer, inner) + tile, x.dtype),
    ]
    return small_call(total_kernel, x, tile, scratch, collective_id, "total")


def gather_plan(count):
    bits = [1 << b for b in range(count.bit_length() - 1)]
    outer = bits[1:]
    orders = (outer + bits[:1], outer[::-1] + bits[:1])
    sends = []
    for half, order in enumerate(orders):
        for stage, bit in enumerate(order):
            for pick in range(1 << stage):
                mask = sum(order[j] for j in range(stage) if pick >> j & 1)
                sends.append((bin(mask).count("1"), half, mask, bit))
    sends.sort(key=lambda s: s[0])
    return bits, [s[1:] for s in sends]


def start_barrier(masks, count):
    me = lax.axis_index("mp")
    barrier = pltpu.get_barrier_semaphore()
    for mask in masks:
        pl.semaphore_signal(
            barrier, inc=1, device_id={"mp": flip(me, mask, count)}, device_id_type=MESH
        )
    pl.semaphore_wait(barrier, len(masks))


def gather_kernel(count, x_ref, o_ref, own_sem, send, recv):
    me = lax.axis_index("mp")
    rows = x_ref.shape[0]
    bits, plan = gather_plan(count)
    own = pltpu.make_async_copy(x_ref, o_ref.at[me], own_sem)
    own.start()
    start_barrier(bits, count)
    copies = {}
    landed = set()
    for half, mask, bit in plan:
        span = pl.ds(half * (rows // 2), rows // 2)
        slot = flip(me, mask, count)
        if mask and (half, mask) not in landed:
            copies[(half, mask)].wait_recv()
            landed.add((half, mask))
        source = o_ref.at[slot, span] if mask else x_ref.at[span]
        copy = pltpu.make_async_remote_copy(
            src_ref=source,
            dst_ref=o_ref.at[slot, span],
            send_sem=send.at[half, mask | bit],
            recv_sem=recv.at[half, mask | bit],
            device_id={"mp": flip(me, bit, count)},
            device_id_type=MESH,
        )
        copy.start()
        copies[(half, mask | bit)] = copy
    for key, copy in copies.items():
        if key not in landed:
            copy.wait_recv()
    for copy in copies.values():
        copy.wait_send()
    own.wait()


def gather_rows(x, collective_id):
    count = lax.axis_size("mp")
    if count != 8:
        return lax.all_gather(x, "mp", axis=0, tiled=False)
    rows, width = x.shape
    return pl.pallas_call(
        functools.partial(gather_kernel, count),
        out_shape=jax.ShapeDtypeStruct((count, rows, width), x.dtype),
        in_specs=[pl.BlockSpec(memory_space=pl.ANY)],
        out_specs=pl.BlockSpec(memory_space=pl.ANY),
        scratch_shapes=[
            pltpu.SemaphoreType.DMA,
            pltpu.SemaphoreType.DMA((2, count)),
            pltpu.SemaphoreType.DMA((2, count)),
        ],
        compiler_params=pltpu.CompilerParams(
            collective_id=collective_id, has_side_effects=True, vmem_limit_bytes=VMEM_BYTES
        ),
        cost_estimate=pl.CostEstimate(
            flops=0, bytes_accessed=2 * count * rows * width * 2 * 4, transcendentals=0
        ),
        name="gather_rows",
    )(x)


def beside_products(pairs):
    for left, right, out in pairs:
        tokens, rows = left.shape
        tile = min(256, rows)

        def body(left_tile, out_tile):
            out_tile[...] = dot_tn(left_tile[...], right[...]).astype(out_tile.dtype)

        pltpu.emit_pipeline(
            body,
            grid=(rows // tile,),
            in_specs=[pl.BlockSpec((tokens, tile), lambda i: (0, i))],
            out_specs=[pl.BlockSpec((tile, right.shape[1]), lambda i: (i, 0))],
        )(left, out)


def scatter_kernel(products, tile, extra, *refs):
    count = 8
    pairs = len(products)
    refs = list(refs)
    take = lambda n: [refs.pop(0) for _ in range(n)]
    lefts, rights = take(pairs), take(pairs)
    beside = take(2 * extra)
    (out_ref,) = take(1)
    beside_out = take(extra)
    acc, core_out, core_in, link_out, link_in = take(5)
    core_send, core_recv, link_send, link_recv = refs
    rows, width = out_ref.shape
    me = lax.axis_index("mp")
    start_barrier((1, 2, 4), count)

    def partial(slot, store):
        first = pl.multiple_of(slot * rows, rows)

        def step(t, carry):
            columns = pl.ds(pl.multiple_of(t * tile, tile), tile)
            total = None
            for left, right, product in zip(lefts, rights, products):
                term = product(left[pl.ds(first, rows), :], right, t, columns)
                total = term if total is None else total + term
            store(columns, total)
            return carry

        lax.fori_loop(0, width // tile, step, 0)

    def into_core(c):
        def store(columns, total):
            core_out[c, :, columns] = total.astype(HALF)

        return store

    def into_acc(c):
        def store(columns, total):
            acc[c, :, columns] = total

        return store

    core_copies = {}
    link_copies = {}
    middle = rows // 2

    def core_half(c):
        partial(flip(me, 2 * c + 1, count), into_core(c))
        copy = pltpu.make_async_remote_copy(
            src_ref=core_out.at[c],
            dst_ref=core_in.at[c],
            send_sem=core_send.at[c],
            recv_sem=core_recv.at[c],
            device_id={"mp": flip(me, 1, count)},
            device_id_type=MESH,
        )
        copy.start()
        core_copies[c] = copy

    def core_sum(c):
        core_copies[c].wait_recv()

        def step(t, carry):
            columns = pl.ds(pl.multiple_of(t * tile, tile), tile)
            acc[c, :, columns] = acc[c, :, columns] + core_in[c, :, columns].astype(SINGLE)
            return carry

        lax.fori_loop(0, width // tile, step, 0)

    def link(index, c, half, axis):
        span = pl.ds(half * middle, middle)

        def step(t, carry):
            columns = pl.ds(pl.multiple_of(t * tile, tile), tile)
            link_out[index, :, columns] = acc[c, span, columns].astype(HALF)
            return carry

        lax.fori_loop(0, width // tile, step, 0)
        copy = pltpu.make_async_remote_copy(
            src_ref=link_out.at[index],
            dst_ref=link_in.at[index],
            send_sem=link_send.at[index],
            recv_sem=link_recv.at[index],
            device_id={"mp": flip(me, 2 * axis, count)},
            device_id_type=MESH,
        )
        copy.start()
        link_copies[index] = copy

    def link_sum(index, c, half):
        link_copies[index].wait_recv()
        span = pl.ds(half * middle, middle)

        def step(t, carry):
            columns = pl.ds(pl.multiple_of(t * tile, tile), tile)
            acc[c, span, columns] = acc[c, span, columns] + link_in[index, :, columns].astype(
                SINGLE
            )
            return carry

        lax.fori_loop(0, width // tile, step, 0)

    core_half(3)
    partial(flip(me, 6, count), into_acc(3))
    core_half(1)
    core_sum(3)
    link(0, 3, 0, 2)
    link(1, 3, 1, 1)
    partial(flip(me, 2, count), into_acc(1))
    core_half(2)
    core_sum(1)
    link(2, 1, 1, 1)
    partial(flip(me, 4, count), into_acc(2))
    core_half(0)
    core_sum(2)
    link(3, 2, 0, 2)
    partial(me, into_acc(0))
    core_sum(0)
    link_sum(0, 1, 0)
    link(4, 1, 0, 1)
    link_sum(1, 2, 1)
    link(5, 2, 1, 2)
    beside_products(list(zip(beside[:extra], beside[extra:], beside_out)))
    link_sum(2, 0, 1)
    link_sum(3, 0, 0)
    link_sum(4, 0, 0)
    link_sum(5, 0, 1)
    out_ref[...] = acc[0]
    for copy in core_copies.values():
        copy.wait_send()
    for copy in link_copies.values():
        copy.wait_send()


def scatter_products(
    lefts, rights, products, fallback, width, tile, collective_id, flops, beside=()
):
    count = lax.axis_size("mp")
    tokens = lefts[0].shape[0]
    rows = tokens // count
    if count != 8:
        summed = lax.psum_scatter(
            fallback().astype(HALF), "mp", scatter_dimension=0, tiled=True
        ).astype(SINGLE)
        return [summed] + [dot_tn(left, right).astype(HALF) for left, right in beside]
    extra = len(beside)
    in_vmem, in_hbm = pl.BlockSpec(memory_space=pltpu.VMEM), pl.BlockSpec(memory_space=pl.ANY)
    return pl.pallas_call(
        functools.partial(scatter_kernel, products, tile, extra),
        out_shape=[jax.ShapeDtypeStruct((rows, width), SINGLE)]
        + [
            jax.ShapeDtypeStruct((left.shape[1], right.shape[1]), HALF) for left, right in beside
        ],
        in_specs=[in_vmem] * (len(lefts) + len(rights)) + [in_hbm] * extra + [in_vmem] * extra,
        out_specs=[in_vmem] + [in_hbm] * extra,
        scratch_shapes=[
            pltpu.VMEM((4, rows, width), SINGLE),
            pltpu.VMEM((4, rows, width), HALF),
            pltpu.VMEM((4, rows, width), HALF),
            pltpu.VMEM((6, rows // 2, width), HALF),
            pltpu.VMEM((6, rows // 2, width), HALF),
            pltpu.SemaphoreType.DMA((4,)),
            pltpu.SemaphoreType.DMA((4,)),
            pltpu.SemaphoreType.DMA((6,)),
            pltpu.SemaphoreType.DMA((6,)),
        ],
        compiler_params=pltpu.CompilerParams(
            collective_id=collective_id, has_side_effects=True, vmem_limit_bytes=VMEM_BYTES
        ),
        cost_estimate=pl.CostEstimate(
            flops=flops, bytes_accessed=tokens * width * 2 * 8, transcendentals=0
        ),
        name="scatter_products",
    )(*lefts, *rights, *[pair[0] for pair in beside], *[pair[1] for pair in beside])


def positions(lens_ref, first, shape):
    place = lax.broadcasted_iota(jnp.int32, shape, 0) + first
    begin = jnp.zeros(shape, jnp.int32)
    total = 0
    for j in range(lens_ref.shape[1]):
        total = total + lens_ref[0, j]
        begin = jnp.where(place >= total, total, begin)
    return place - begin, place < total


def split_dot(dot, left, right):
    high = left.astype(HALF)
    low = (left - high.astype(SINGLE)).astype(HALF)
    return dot(high, right) + dot(low, right)


def lane_tiles(width):
    return [(t, t * 128, min(128, width - t * 128)) for t in range(-(-width // 128))]


def put_tiles(ref, value):
    for t, first, lanes in lane_tiles(value.shape[1]):
        ref[t, :, :lanes] = value[:, first : first + lanes]


def scan_start(tiles, lanes):
    return [(jnp.zeros((lanes, 128), SINGLE), jnp.ones((lanes, 128), SINGLE)) for _ in tiles]


def sigmoid(v):
    return 1.0 / (1.0 + jnp.exp(-v))


def forward_kernel(
    lens_ref,
    x_ref,
    gain_ref,
    pack_ref,
    bin_ref,
    ba_ref,
    chan_ref,
    n1_ref,
    bx_ref,
    by_ref,
    conv_ref,
    gi_ref,
    ra_ref,
    h_ref,
    ob_ref,
    taps,
    coef,
    drive,
    carry,
):
    step = pl.program_id(0)
    rows, width = bx_ref.shape
    depth = pack_ref.shape[2]
    lanes = 8
    span = rows // lanes

    @pl.when(step == 0)
    def _():
        taps[...] = jnp.zeros_like(taps)
        carry[...] = jnp.zeros_like(carry)
        coef[...] = jnp.zeros_like(coef)
        drive[...] = jnp.zeros_like(drive)

    x = x_ref[0].astype(SINGLE)
    scale = lax.rsqrt(jnp.mean(x * x, axis=-1, keepdims=True) + EPS)
    normed = (x * scale * gain_ref[...]).astype(HALF)
    n1_ref[...] = normed
    total = None
    for d in range(pack_ref.shape[0]):
        term = dot_nt(normed[:, d * depth : (d + 1) * depth], pack_ref[d, : 2 * width, :])
        total = term if total is None else total + term
    bx = total[:, :width].astype(HALF)
    by = total[:, width:]
    bx_ref[...] = bx
    by_ref[...] = by
    pos, live = positions(lens_ref, step * rows, (rows, width))
    taps[0:8, :] = taps[rows : rows + 8, :]
    taps[8 : rows + 8, :] = bx.astype(SINGLE)
    conv = jnp.zeros((rows, width), SINGLE) + chan_ref[CONV : CONV + 1, :]
    for k in range(CONV):
        moved = taps[8 - k : 8 - k + rows, :]
        conv = conv + jnp.where(pos >= k, moved * chan_ref[k : k + 1, :], 0.0)
    conv_ref[...] = conv
    high = conv.astype(HALF)
    low = (conv - high.astype(SINGLE)).astype(HALF)
    gate_in = sigmoid(
        dot_nn(high, bin_ref[...]) + dot_nn(low, bin_ref[...]) + chan_ref[CONV + 1 : CONV + 2, :]
    )
    gate_a = sigmoid(
        dot_nn(high, ba_ref[...]) + dot_nn(low, ba_ref[...]) + chan_ref[CONV + 2 : CONV + 3, :]
    )
    gi_ref[...] = gate_in
    ra_ref[...] = gate_a
    decay = jnp.exp(-DECAY * gate_a * chan_ref[CONV + 4 : CONV + 5, :])
    root = jnp.sqrt(1.0 - decay * decay)
    put_tiles(coef, jnp.where(pos == 0, 0.0, decay))
    put_tiles(drive, gate_in * conv * root)
    tiles = lane_tiles(width)

    def scan(i, state):
        at = pl.ds(i, lanes, stride=span)
        result = []
        for (t, _, _), (h, prod) in zip(tiles, state):
            a = coef[t, at, :]
            h = a * h + drive[t, at, :]
            prod = prod * a
            drive[t, at, :] = h
            coef[t, at, :] = prod
            result.append((h, prod))
        return result

    state = lax.fori_loop(0, span, scan, scan_start(tiles, lanes), unroll=4)
    for (t, first, used), (h, prod) in zip(tiles, state):
        running = carry[t, 0:1, :]
        for s in range(lanes):
            at = slice(s * span, (s + 1) * span)
            value = drive[t, at, :] + coef[t, at, :] * running
            h_ref[at, first : first + used] = value[:, :used]
            running = h[s : s + 1, :] + prod[s : s + 1, :] * running
        carry[t, 0:1, :] = running
    mixed = h_ref[...].astype(HALF).astype(SINGLE)
    ob_ref[...] = jnp.where(live, gelu(by) * mixed, 0.0).astype(HALF)


def forward_channels(lens, x_all, gain, pack, blocks_in, blocks_a, chan):
    count, rows, model = x_all.shape
    width = chan.shape[1]
    tokens = count * rows
    whole = lambda shape: pl.BlockSpec(shape, lambda i: (0,) * len(shape))
    part = pl.BlockSpec((rows, width), lambda i: (i, 0))
    full = lambda kind: jax.ShapeDtypeStruct((tokens, width), kind)
    return pl.pallas_call(
        forward_kernel,
        grid=(count,),
        out_shape=(
            jax.ShapeDtypeStruct((tokens, model), HALF),
            full(HALF),
            full(SINGLE),
            full(SINGLE),
            full(SINGLE),
            full(SINGLE),
            full(SINGLE),
            full(HALF),
        ),
        in_specs=[
            pl.BlockSpec(memory_space=pltpu.SMEM),
            pl.BlockSpec((1, rows, model), lambda i: (i, 0, 0)),
            whole(gain.shape),
            whole(pack.shape),
            whole(blocks_in.shape),
            whole(blocks_a.shape),
            whole(chan.shape),
        ],
        out_specs=(pl.BlockSpec((rows, model), lambda i: (i, 0)),) + (part,) * 7,
        scratch_shapes=[
            pltpu.VMEM((rows + 8, width), SINGLE),
            pltpu.VMEM((len(lane_tiles(width)), rows, 128), SINGLE),
            pltpu.VMEM((len(lane_tiles(width)), rows, 128), SINGLE),
            pltpu.VMEM((len(lane_tiles(width)), 8, 128), SINGLE),
        ],
        compiler_params=pltpu.CompilerParams(vmem_limit_bytes=VMEM_BYTES),
        cost_estimate=pl.CostEstimate(
            flops=2 * tokens * model * 2 * width,
            bytes_accessed=tokens * (model * 4 + width * 24),
            transcendentals=8 * tokens * width,
        ),
        name="forward_channels",
    )(lens, x_all, gain, pack, blocks_in, blocks_a, chan)


def backward_kernel(
    lens_ref,
    dt_ref,
    pack_ref,
    bin_ref,
    ba_ref,
    chan_ref,
    bx_ref,
    by_ref,
    conv_ref,
    gi_ref,
    ra_ref,
    h_ref,
    hprev_ref,
    ob_ref,
    n1_ref,
    dbx_ref,
    dby_ref,
    gin_ref,
    ga_ref,
    gchan_ref,
    grads_ref,
    grads,
    lift,
    coef,
    drive,
    carry,
):
    step = pl.program_id(0)
    chunk = pl.num_programs(0) - 1 - step
    rows, width = bx_ref.shape
    depth = pack_ref.shape[2]
    lanes = 8
    span = rows // lanes

    @pl.when(step == 0)
    def _():
        lift[...] = jnp.zeros_like(lift)
        carry[...] = jnp.zeros_like(carry)
        coef[...] = jnp.zeros_like(coef)
        drive[...] = jnp.zeros_like(drive)
        gin_ref[...] = jnp.zeros_like(gin_ref)
        ga_ref[...] = jnp.zeros_like(ga_ref)
        gchan_ref[...] = jnp.zeros_like(gchan_ref)
        grads[...] = jnp.zeros_like(grads)

    d_out = None
    for d in range(pack_ref.shape[0]):
        term = dot_nt(
            dt_ref[0, :, d * depth : (d + 1) * depth], pack_ref[d, 2 * width : 3 * width, :]
        )
        d_out = term if d_out is None else d_out + term
    pos, live = positions(lens_ref, chunk * rows, (rows, width))
    by = by_ref[...]
    h = h_ref[...]
    side, slope = gelu_both(by)
    d_out = jnp.where(live, d_out, 0.0)
    dby_ref[...] = (d_out * h.astype(HALF).astype(SINGLE) * slope).astype(HALF)
    gate_a = ra_ref[...]
    soft = chan_ref[CONV + 4 : CONV + 5, :]
    decay = jnp.exp(-DECAY * gate_a * soft)
    put_tiles(coef, jnp.where(pos == 0, 0.0, decay))
    put_tiles(drive, (d_out * side).astype(HALF).astype(SINGLE))
    tiles = lane_tiles(width)

    def scan(j, state):
        at = pl.ds(span - 1 - j, lanes, stride=span)
        result = []
        for (t, _, _), (after, prod) in zip(tiles, state):
            a = coef[t, at, :]
            lam = drive[t, at, :] + after
            drive[t, at, :] = lam
            coef[t, at, :] = prod
            result.append((a * lam, prod * a))
        return result

    state = lax.fori_loop(0, span, scan, scan_start(tiles, lanes), unroll=4)
    for (t, first, used), (after, prod) in zip(tiles, state):
        running = carry[t, 0:1, :]
        for s in reversed(range(lanes)):
            at = slice(s * span, (s + 1) * span)
            value = drive[t, at, :] + coef[t, at, :] * running
            lift[at, first : first + used] = value[:, :used]
            running = after[s : s + 1, :] + prod[s : s + 1, :] * running
        carry[t, 0:1, :] = running
    lam = lift[0:rows, :]
    last = jnp.where(chunk > 0, hprev_ref[7:8, :], 0.0)
    before = jnp.concatenate([last, h[: rows - 1, :]], axis=0)
    before = jnp.where(pos == 0, 0.0, before)
    conv = conv_ref[...]
    gate_in = gi_ref[...]
    root = jnp.sqrt(1.0 - decay * decay)
    d_decay = lam * before - lam * gate_in * conv * decay / root
    d_log = d_decay * decay
    d_a = d_log * (-DECAY * soft)
    d_in = lam * conv * root
    d_logit_in = d_in * gate_in * (1.0 - gate_in)
    d_logit_a = d_a * gate_a * (1.0 - gate_a)
    d_conv = (
        lam * gate_in * root
        + split_dot(dot_nt, d_logit_in, bin_ref[...])
        + split_dot(dot_nt, d_logit_a, ba_ref[...])
    )
    low = conv.astype(HALF)
    gin_ref[...] += dot_tn(low, d_logit_in.astype(HALF))
    ga_ref[...] += dot_tn(low, d_logit_a.astype(HALF))
    lift[0:rows, :] = d_conv
    bx = bx_ref[...].astype(SINGLE)
    d_bx = jnp.zeros((rows, width), SINGLE)
    for k in range(CONV):
        if k:
            ahead, _ = positions(lens_ref, chunk * rows + k, (rows, width))
            moved = jnp.where(ahead >= k, lift[k : k + rows, :], 0.0)
        else:
            moved = d_conv
        d_bx = d_bx + moved * chan_ref[k : k + 1, :]
        gchan_ref[k : k + 1, :] += jnp.sum(moved * bx, axis=0, keepdims=True)
    dbx_ref[...] = d_bx.astype(HALF)
    lift[rows : rows + 8, :] = d_conv[0:8, :]
    sums = (d_conv, d_logit_in, d_logit_a, d_log * gate_a)
    for j, value in enumerate(sums):
        gchan_ref[CONV + j : CONV + j + 1, :] += jnp.sum(value, axis=0, keepdims=True)
    lefts = (dbx_ref[...], dby_ref[...], ob_ref[...])
    for d in range(grads.shape[0]):
        columns = slice(d * depth, (d + 1) * depth)
        rights = (n1_ref[:, columns], n1_ref[:, columns], dt_ref[0, :, columns])
        for j, (left, right) in enumerate(zip(lefts, rights)):
            grads[d, j * width : (j + 1) * width, :] += dot_tn(left, right)

    @pl.when(chunk == 0)
    def _():
        grads_ref[...] = grads[...].astype(HALF)


def backward_channels(lens, dt_all, pack, blocks_in, blocks_a, chan, saved):
    bx, by, conv, gate_in, gate_a, h, ob, n1 = saved
    count, rows, model = dt_all.shape
    width = chan.shape[1]
    tokens = count * rows
    last = count - 1
    whole = lambda shape: pl.BlockSpec(shape, lambda i: (0,) * len(shape))
    part = pl.BlockSpec((rows, width), lambda i: (last - i, 0))
    before = pl.BlockSpec(
        (8, width), lambda i: (jnp.maximum((last - i) * (rows // 8) - 1, 0), 0)
    )
    full = lambda kind: jax.ShapeDtypeStruct((tokens, width), kind)
    square = jax.ShapeDtypeStruct((width, width), SINGLE)
    grads = (pack.shape[0], 3 * width, pack.shape[2])
    return pl.pallas_call(
        backward_kernel,
        grid=(count,),
        out_shape=(
            full(HALF),
            full(HALF),
            square,
            square,
            jax.ShapeDtypeStruct((8, width), SINGLE),
            jax.ShapeDtypeStruct(grads, HALF),
        ),
        in_specs=[
            pl.BlockSpec(memory_space=pltpu.SMEM),
            pl.BlockSpec((1, rows, model), lambda i: (last - i, 0, 0)),
            whole(pack.shape),
            whole(blocks_in.shape),
            whole(blocks_a.shape),
            whole(chan.shape),
            part,
            part,
            part,
            part,
            part,
            part,
            before,
            part,
            pl.BlockSpec((rows, model), lambda i: (last - i, 0)),
        ],
        out_specs=(
            part,
            part,
            whole((width, width)),
            whole((width, width)),
            whole((8, width)),
            whole(grads),
        ),
        scratch_shapes=[
            pltpu.VMEM(grads, SINGLE),
            pltpu.VMEM((rows + 8, width), SINGLE),
            pltpu.VMEM((len(lane_tiles(width)), rows, 128), SINGLE),
            pltpu.VMEM((len(lane_tiles(width)), rows, 128), SINGLE),
            pltpu.VMEM((len(lane_tiles(width)), 8, 128), SINGLE),
        ],
        compiler_params=pltpu.CompilerParams(vmem_limit_bytes=VMEM_BYTES),
        cost_estimate=pl.CostEstimate(
            flops=2 * tokens * model * width,
            bytes_accessed=tokens * (model * 2 + width * 28),
            transcendentals=8 * tokens * width,
        ),
        name="backward_channels",
    )(lens, dt_all, pack, blocks_in, blocks_a, chan, bx, by, conv, gate_in, gate_a, h, h, ob, n1)


def diagonal(blocks):
    count, size, _ = blocks.shape
    spread = blocks[:, :, None, :] * jnp.eye(count, dtype=blocks.dtype)[:, None, :, None]
    return spread.reshape(count * size, count * size)


def on_device(
    layer_input,
    cotangent,
    norm_in,
    norm_mid,
    w_rnn_in,
    w_rnn_gate,
    w_rnn_out,
    gate_in_blocks,
    gate_a_blocks,
    channel_params,
    w_mlp_gate,
    w_mlp_up,
    w_mlp_down,
    lengths,
):
    parts = lax.axis_size("dp")
    rows, model = layer_input.shape
    depth, width = w_rnn_in.shape
    heads, bite, block = gate_in_blocks.shape
    tokens = rows * lax.axis_size("mp")

    flat = jnp.concatenate(
        [
            gate_in_blocks.astype(HALF).reshape(-1),
            gate_a_blocks.astype(HALF).reshape(-1),
            channel_params.astype(HALF).reshape(-1),
        ]
    )
    used = flat.shape[0]
    small_rows = -(-used // (16 * depth)) * 16
    flat = jnp.pad(flat, (0, small_rows * depth - used)).reshape(small_rows, depth)
    mine = jnp.concatenate(
        [
            w_rnn_in.astype(HALF).T,
            w_rnn_gate.astype(HALF).T,
            w_rnn_out.astype(HALF),
            flat,
        ],
        axis=0,
    )
    pack = lax.all_gather(mine, "dp", axis=0, tiled=False)
    down = lax.all_gather(w_mlp_down.astype(HALF), "dp", axis=1, tiled=True)
    gate_w = lax.all_gather(w_mlp_gate.astype(HALF), "dp", axis=0, tiled=True)
    up_w = lax.all_gather(w_mlp_up.astype(HALF), "dp", axis=0, tiled=True)
    bite_gain = norm_in.shape[0]
    gains = jnp.stack([norm_in, norm_mid]).astype(HALF).astype(SINGLE)
    gains = share(jnp.pad(gains, ((0, 6), (0, 128 - bite_gain))), 8)
    gain_first = gains[:, 0, :bite_gain].reshape(1, model)
    gain_second = gains[:, 1, :bite_gain].reshape(1, model)

    small = pack[:, 3 * width :, :].reshape(parts, -1)
    size = heads * bite * block
    whole_block = lambda v: diagonal(
        v.reshape(parts, heads, bite, block).transpose(1, 0, 2, 3).reshape(heads, block, block)
    )
    blocks_in = whole_block(small[:, :size])
    blocks_a = whole_block(small[:, size : 2 * size])
    channel = small[:, 2 * size : used].reshape(2 * CONV, width).astype(SINGLE)
    soft = jax.nn.softplus(-channel[2 * CONV - 1 :])
    chan = jnp.concatenate([channel, soft, jnp.zeros((7, width), SINGLE)], axis=0)

    x_all = gather_rows(layer_input, 0)
    c_all = gather_rows(cotangent, 1).reshape(tokens, model)
    n1, bx, by, conv, gate_in, gate_a, h, ob = forward_channels(
        lengths, x_all, gain_first, pack, blocks_in, blocks_a, chan
    )
    inputs = layer_input.astype(SINGLE)
    (out,) = scatter_products(
        [ob],
        [pack],
        [lambda l, r, t, cols: dot_nn(l, r[t, 2 * width : 3 * width, :])],
        lambda: jnp.einsum(
            "tc,dcm->tdm", ob, pack[:, 2 * width : 3 * width], preferred_element_type=SINGLE
        ).reshape(tokens, model),
        model,
        depth,
        2,
        2 * tokens * width * model,
    )
    residual = inputs + out
    scale_second = lax.rsqrt(jnp.mean(residual * residual, axis=-1, keepdims=True) + EPS)
    normed_mid = (residual * scale_second * gain_second).astype(HALF)
    n2 = gather_rows(normed_mid, 3).reshape(tokens, model)

    def over_dp(value, dimension):
        return lax.psum_scatter(
            value.astype(HALF), "dp", scatter_dimension=dimension, tiled=True
        )

    d_hidden = dot_nt(c_all, down)
    gate_pre = dot_nn(n2, gate_w)
    act, slope = gelu_both(gate_pre)
    d_up = (d_hidden * act).astype(HALF)
    grad_up = dot_tn(n2, d_up).astype(HALF)
    up_w, grad_up = lax.optimization_barrier((up_w, grad_up))
    grad_up = over_dp(grad_up, 0)
    up_pre = dot_nn(n2, up_w)
    hidden = (act * up_pre).astype(HALF)
    d_gate = (d_hidden * up_pre * slope).astype(HALF)
    tile = 512
    by_rows = lambda l, r, t, cols: dot_nt(l, r[cols, :])
    d_normed_mid, grad_gate, grad_down = scatter_products(
        [d_gate, d_up],
        [gate_w, up_w],
        [by_rows, by_rows],
        lambda: dot_nt(d_gate, gate_w) + dot_nt(d_up, up_w),
        model,
        tile,
        4,
        4 * tokens * model * up_w.shape[1],
        [(n2, d_gate), (c_all, hidden)],
    )
    grad_gate = over_dp(grad_gate, 0)
    grad_down = over_dp(grad_down, 0)

    weighted_second = gain_second * d_normed_mid
    grad_gain_second = jnp.sum(d_normed_mid * residual * scale_second, axis=0)
    cube_second = scale_second * scale_second * scale_second
    d_residual = (
        cotangent.astype(SINGLE)
        + scale_second * weighted_second
        - residual * cube_second * jnp.mean(weighted_second * residual, axis=-1, keepdims=True)
    )
    d_resid_low, grad_up = lax.optimization_barrier((d_residual.astype(HALF), grad_up))
    dt_all = gather_rows(d_resid_low, 6)
    dt_all, grad_gate = lax.optimization_barrier((dt_all, grad_gate))

    saved = (bx, by, conv, gate_in, gate_a, h, ob, n1)
    d_bx, d_by, gin, ga, gchan, rnn_grads = backward_channels(
        lengths, dt_all, pack, blocks_in, blocks_a, chan, saved
    )
    d_bx, grad_down = lax.optimization_barrier((d_bx, grad_down))
    (d_normed,) = scatter_products(
        [d_bx, d_by],
        [pack, pack],
        [
            lambda l, r, t, cols: dot_nn(l, r[t, :width, :]),
            lambda l, r, t, cols: dot_nn(l, r[t, width : 2 * width, :]),
        ],
        lambda: jnp.einsum(
            "tc,dcm->tdm",
            jnp.concatenate([d_bx, d_by], axis=1),
            pack[:, : 2 * width],
            preferred_element_type=SINGLE,
        ).reshape(tokens, model),
        model,
        depth,
        7,
        4 * tokens * width * model,
    )
    own = lambda full: jnp.stack(
        [full[j * block : (j + 1) * block, j * block : (j + 1) * block] for j in range(heads)]
    )
    decay_row = DECAY * jax.nn.sigmoid(-channel[2 * CONV - 1 :]) * gchan[2 * CONV - 1 :]
    grad_channel = jnp.concatenate([gchan[: 2 * CONV - 1], decay_row], axis=0)
    split = lambda v: v.reshape(heads, parts, bite, block).transpose(1, 0, 2, 3).reshape(parts, -1)
    small_grads = jnp.concatenate(
        [split(own(gin)), split(own(ga)), grad_channel.reshape(parts, -1)], axis=1
    )
    small_grads = jnp.pad(small_grads, ((0, 0), (0, small_rows * depth - used)))
    small_grads = small_grads.reshape(parts, small_rows, depth).astype(HALF)
    rnn_grads = over_dp(jnp.concatenate([rnn_grads, small_grads], axis=1), 0)
    hidden, d_normed = lax.optimization_barrier((hidden, d_normed))
    (mlp_out,) = scatter_products(
        [hidden],
        [down],
        [lambda l, r, t, cols: dot_nn(l, r[:, cols])],
        lambda: dot_nn(hidden, down),
        model,
        tile,
        5,
        2 * tokens * model * up_w.shape[1],
    )
    mlp_out, rnn_grads = lax.optimization_barrier((mlp_out, rnn_grads))
    layer_output = (residual + mlp_out).astype(HALF)

    scale_first = lax.rsqrt(jnp.mean(inputs * inputs, axis=-1, keepdims=True) + EPS)
    weighted_first = gain_first * d_normed
    grad_gain_first = jnp.sum(d_normed * inputs * scale_first, axis=0)
    cube_first = scale_first * scale_first * scale_first
    grad_input = (
        d_residual
        + scale_first * weighted_first
        - inputs * cube_first * jnp.mean(weighted_first * inputs, axis=-1, keepdims=True)
    )

    rnn_grads = rnn_grads[0].astype(SINGLE)
    flat_grads = rnn_grads[3 * width :].reshape(-1)
    gain_grads = jnp.stack([grad_gain_first, grad_gain_second]).reshape(2, -1, bite_gain)
    gain_grads = jnp.pad(gain_grads.transpose(1, 0, 2), ((0, 0), (0, 6), (0, 128 - bite_gain)))
    gain_grads = total(gain_grads, 9)
    return (
        layer_output,
        grad_input,
        gain_grads[0, :bite_gain],
        gain_grads[1, :bite_gain],
        rnn_grads[:width].T,
        rnn_grads[width : 2 * width].T,
        rnn_grads[2 * width : 3 * width],
        flat_grads[:size].reshape(heads, bite, block),
        flat_grads[size : 2 * size].reshape(heads, bite, block),
        flat_grads[2 * size : used].reshape(channel_params.shape),
        grad_gate.astype(SINGLE),
        grad_up.astype(SINGLE),
        grad_down.T.astype(SINGLE),
    )


def solution(mesh):
    rows = P(("dp", "mp"), None)
    return jax.shard_map(
        on_device,
        mesh=mesh,
        in_specs=(
            rows,
            rows,
            P(("dp", "mp")),
            P(("dp", "mp")),
            P("dp", "mp"),
            P("dp", "mp"),
            P("mp", "dp"),
            P("mp", "dp", None),
            P("mp", "dp", None),
            P("dp", "mp"),
            P("dp", "mp"),
            P("dp", "mp"),
            P("mp", "dp"),
            P("dp", None),
        ),
        out_specs=(
            rows,
            rows,
            P(("dp", "mp")),
            P(("dp", "mp")),
            P("dp", "mp"),
            P("dp", "mp"),
            P("mp", "dp"),
            P("mp", "dp", None),
            P("mp", "dp", None),
            P("dp", "mp"),
            P("dp", "mp"),
            P("dp", "mp"),
            P("mp", "dp"),
        ),
        check_vma=False,
    )
```

```python
import functools

import jax
import jax.numpy as jnp
from jax import lax
from jax.experimental import pallas as pl
from jax.experimental.pallas import tpu as pltpu
from jax.sharding import PartitionSpec as P

CONV = 4
EPS = 1e-06
DECAY = 8.0
HALF = jnp.bfloat16
SINGLE = jnp.float32
MESH = pl.DeviceIdType.MESH
VMEM_BYTES = 56 * 1024 * 1024
GELU_C = 0.7978845608028654
GELU_K = 0.044715


def dot_nn(left, right):
    return lax.dot_general(
        left, right, (((1,), (0,)), ((), ())), preferred_element_type=SINGLE
    )


def dot_nt(left, right):
    return lax.dot_general(
        left, right, (((1,), (1,)), ((), ())), preferred_element_type=SINGLE
    )


def dot_tn(left, right):
    return lax.dot_general(
        left, right, (((0,), (0,)), ((), ())), preferred_element_type=SINGLE
    )


def gelu(v):
    return 0.5 * v * (1.0 + jnp.tanh(GELU_C * (v + GELU_K * v * v * v)))


def gelu_both(v):
    square = v * v
    t = jnp.tanh(GELU_C * (v + GELU_K * v * square))
    value = 0.5 * v * (1.0 + t)
    slope = 0.5 * (1.0 + t) + 0.5 * v * (1.0 - t * t) * (GELU_C * (1.0 + 3.0 * GELU_K * square))
    return value, slope


def flip(me, mask, count):
    place = me
    bit = 1
    while bit < count:
        if mask & bit:
            place = place + (1 - 2 * ((me // bit) % 2)) * bit
        bit *= 2
    return place


def ring_peers(axis):
    me, count = lax.axis_index(axis), lax.axis_size(axis)
    return [(k, {axis: (me + k) % count}) for k in range(1, count)]


def greet(peers):
    barrier = pltpu.get_barrier_semaphore()
    for _, peer in peers:
        pl.semaphore_signal(barrier, inc=1, device_id=peer, device_id_type=MESH)
    pl.semaphore_wait(barrier, len(peers))


def exchange(peers, source, target, send, recv):
    copies = []
    for k, peer in peers:
        copy = pltpu.make_async_remote_copy(
            src_ref=source(k),
            dst_ref=target(k),
            send_sem=send.at[k],
            recv_sem=recv.at[k],
            device_id=peer,
            device_id_type=MESH,
        )
        copy.start()
        copies.append(copy)
    for copy in copies:
        copy.wait_recv()
    return copies


def share_kernel(x_ref, o_ref, send_mp, recv_mp, send_dp, recv_dp):
    inner, outer = ring_peers("mp"), ring_peers("dp")
    count = len(inner) + 1
    first = lax.axis_index("dp") * count
    place = first + lax.axis_index("mp")
    o_ref[place] = x_ref[...]
    greet(inner + outer)
    mine = lambda k: o_ref.at[place]
    plane = lambda k: o_ref.at[pl.ds(first, count)]
    copies = exchange(inner, mine, mine, send_mp, recv_mp)
    copies += exchange(outer, plane, plane, send_dp, recv_dp)
    for copy in copies:
        copy.wait_send()


def small_call(kernel, x, out_shape, scratch, collective_id, name):
    inner, outer = lax.axis_size("mp"), lax.axis_size("dp")
    sems = [pltpu.SemaphoreType.DMA((c,)) for c in (inner, inner, outer, outer)]
    return pl.pallas_call(
        kernel,
        out_shape=jax.ShapeDtypeStruct(out_shape, x.dtype),
        in_specs=[pl.BlockSpec(memory_space=pltpu.VMEM)],
        out_specs=pl.BlockSpec(memory_space=pltpu.VMEM),
        scratch_shapes=scratch + sems,
        compiler_params=pltpu.CompilerParams(
            collective_id=collective_id, has_side_effects=True
        ),
        name=name,
    )(x)


def share(x, collective_id):
    devices = lax.axis_size("mp") * lax.axis_size("dp")
    return small_call(share_kernel, x, (devices,) + x.shape, [], collective_id, "share")


def total_kernel(x_ref, o_ref, plane, landed_mp, landed_dp, send_mp, recv_mp, send_dp, recv_dp):
    inner, outer = ring_peers("mp"), ring_peers("dp")
    across, count = len(outer) + 1, len(inner) + 1
    me, level = lax.axis_index("mp"), lax.axis_index("dp")
    greet(inner + outer)
    copies = exchange(
        outer,
        lambda k: x_ref.at[pl.ds((level + k) % across * count, count)],
        lambda k: landed_dp.at[k],
        send_dp,
        recv_dp,
    )
    plane[...] = x_ref[pl.ds(level * count, count)]
    for k, _ in outer:
        plane[...] = plane[...] + landed_dp[k]
    copies += exchange(
        inner,
        lambda k: plane.at[(me + k) % count],
        lambda k: landed_mp.at[k],
        send_mp,
        recv_mp,
    )
    value = plane[me]
    for k, _ in inner:
        value = value + landed_mp[k]
    o_ref[...] = value
    for copy in copies:
        copy.wait_send()


def total(x, collective_id):
    inner, outer = lax.axis_size("mp"), lax.axis_size("dp")
    tile = x.shape[1:]
    scratch = [
        pltpu.VMEM((inner,) + tile, x.dtype),
        pltpu.VMEM((inner,) + tile, x.dtype),
        pltpu.VMEM((outer, inner) + tile, x.dtype),
    ]
    return small_call(total_kernel, x, tile, scratch, collective_id, "total")


def gather_plan(count):
    bits = [1 << b for b in range(count.bit_length() - 1)]
    outer = bits[1:]
    orders = (outer + bits[:1], outer[::-1] + bits[:1])
    sends = []
    for half, order in enumerate(orders):
        for stage, bit in enumerate(order):
            for pick in range(1 << stage):
                mask = sum(order[j] for j in range(stage) if pick >> j & 1)
                sends.append((bin(mask).count("1"), half, mask, bit))
    sends.sort(key=lambda s: s[0])
    return bits, [s[1:] for s in sends]


def start_barrier(masks, count):
    me = lax.axis_index("mp")
    barrier = pltpu.get_barrier_semaphore()
    for mask in masks:
        pl.semaphore_signal(
            barrier, inc=1, device_id={"mp": flip(me, mask, count)}, device_id_type=MESH
        )
    pl.semaphore_wait(barrier, len(masks))


def gather_kernel(count, x_ref, o_ref, own_sem, send, recv):
    me = lax.axis_index("mp")
    rows = x_ref.shape[0]
    bits, plan = gather_plan(count)
    own = pltpu.make_async_copy(x_ref, o_ref.at[me], own_sem)
    own.start()
    start_barrier(bits, count)
    copies = {}
    landed = set()
    for half, mask, bit in plan:
        span = pl.ds(half * (rows // 2), rows // 2)
        slot = flip(me, mask, count)
        if mask and (half, mask) not in landed:
            copies[(half, mask)].wait_recv()
            landed.add((half, mask))
        source = o_ref.at[slot, span] if mask else x_ref.at[span]
        copy = pltpu.make_async_remote_copy(
            src_ref=source,
            dst_ref=o_ref.at[slot, span],
            send_sem=send.at[half, mask | bit],
            recv_sem=recv.at[half, mask | bit],
            device_id={"mp": flip(me, bit, count)},
            device_id_type=MESH,
        )
        copy.start()
        copies[(half, mask | bit)] = copy
    for key, copy in copies.items():
        if key not in landed:
            copy.wait_recv()
    for copy in copies.values():
        copy.wait_send()
    own.wait()


def gather_rows(x, collective_id):
    count = lax.axis_size("mp")
    if count != 8:
        return lax.all_gather(x, "mp", axis=0, tiled=False)
    rows, width = x.shape
    return pl.pallas_call(
        functools.partial(gather_kernel, count),
        out_shape=jax.ShapeDtypeStruct((count, rows, width), x.dtype),
        in_specs=[pl.BlockSpec(memory_space=pl.ANY)],
        out_specs=pl.BlockSpec(memory_space=pl.ANY),
        scratch_shapes=[
            pltpu.SemaphoreType.DMA,
            pltpu.SemaphoreType.DMA((2, count)),
            pltpu.SemaphoreType.DMA((2, count)),
        ],
        compiler_params=pltpu.CompilerParams(
            collective_id=collective_id, has_side_effects=True, vmem_limit_bytes=VMEM_BYTES
        ),
        cost_estimate=pl.CostEstimate(
            flops=0, bytes_accessed=2 * count * rows * width * 2 * 4, transcendentals=0
        ),
        name="gather_rows",
    )(x)


def beside_products(pairs):
    for left, right, out in pairs:
        tokens, rows = left.shape
        tile = min(256, rows)

        def body(left_tile, out_tile):
            out_tile[...] = dot_tn(left_tile[...], right[...]).astype(out_tile.dtype)

        pltpu.emit_pipeline(
            body,
            grid=(rows // tile,),
            in_specs=[pl.BlockSpec((tokens, tile), lambda i: (0, i))],
            out_specs=[pl.BlockSpec((tile, right.shape[1]), lambda i: (i, 0))],
        )(left, out)


class PlaneSum:
    COUNT = 8
    ORDER = (3, 1, 2, 0)
    LINKS = ((3, 0, 2), (3, 1, 1), (1, 1, 1), (2, 0, 2), (1, 0, 1), (2, 1, 2))

    @staticmethod
    def scratch(rows, width):
        middle = rows // 2
        return [
            pltpu.VMEM((rows, width), SINGLE),
            pltpu.VMEM((2, middle, width), SINGLE),
            pltpu.VMEM((2, rows, width), HALF),
            pltpu.VMEM((4, rows, width), HALF),
            pltpu.VMEM((6, middle, width), HALF),
            pltpu.VMEM((6, middle, width), HALF),
            pltpu.SemaphoreType.DMA((4,)),
            pltpu.SemaphoreType.DMA((4,)),
            pltpu.SemaphoreType.DMA((6,)),
            pltpu.SemaphoreType.DMA((6,)),
        ]

    def __init__(self, products, tile, lefts, rights, scratch):
        self.terms = list(zip(lefts, rights, products))
        self.tile = tile
        self.acc, self.side, self.core_out, self.core_in = scratch[:4]
        self.link_out, self.link_in = scratch[4:6]
        self.core_send, self.core_recv, self.link_send, self.link_recv = scratch[6:]
        self.rows, self.width = self.acc.shape
        self.halves = (slice(0, self.rows // 2), slice(self.rows // 2, self.rows))
        self.me = lax.axis_index("mp")

    def tiles(self, step):
        def body(t, carry):
            step(t, pl.ds(pl.multiple_of(t * self.tile, self.tile), self.tile))
            return carry

        lax.fori_loop(0, self.width // self.tile, body, 0)

    def partial(self, slot, t, columns):
        span = pl.ds(pl.multiple_of(slot * self.rows, self.rows), self.rows)
        value = None
        for left, right, product in self.terms:
            term = product(left[span, :], right, t, columns)
            value = term if value is None else value + term
        return value

    def core_copy(self, c):
        return pltpu.make_async_remote_copy(
            src_ref=self.core_out.at[self.ORDER.index(c) % 2],
            dst_ref=self.core_in.at[c],
            send_sem=self.core_send.at[c],
            recv_sem=self.core_recv.at[c],
            device_id={"mp": flip(self.me, 1, self.COUNT)},
            device_id_type=MESH,
        )

    def link_copy(self, index):
        return pltpu.make_async_remote_copy(
            src_ref=self.link_out.at[index],
            dst_ref=self.link_in.at[index],
            send_sem=self.link_send.at[index],
            recv_sem=self.link_recv.at[index],
            device_id={"mp": flip(self.me, 2 * self.LINKS[index][2], self.COUNT)},
            device_id_type=MESH,
        )

    def greet(self):
        start_barrier((1, 2, 4), self.COUNT)

    def send(self, c):
        place = self.ORDER.index(c)
        if place >= 2:
            self.core_copy(self.ORDER[place - 2]).wait_send()
        slot = flip(self.me, 2 * c + 1, self.COUNT)

        def step(t, columns):
            self.core_out[place % 2, :, columns] = self.partial(slot, t, columns).astype(HALF)

        self.tiles(step)
        self.core_copy(c).start()

    def take(self, c):
        self.core_copy(c).wait_recv()
        slot = flip(self.me, 2 * c, self.COUNT)
        ways = [i for i in range(4) if self.LINKS[i][0] == c]
        kept = [h for h in (0, 1) if c and h not in [self.LINKS[i][1] for i in ways]]

        def step(t, columns):
            value = self.partial(slot, t, columns) + self.core_in[c, :, columns].astype(SINGLE)
            if c == 0:
                self.acc[:, columns] = value
            for i in ways:
                self.link_out[i, :, columns] = value[self.halves[self.LINKS[i][1]]].astype(HALF)
            for h in kept:
                self.side[h, :, columns] = value[self.halves[h]]

        self.tiles(step)
        for i in ways:
            self.link_copy(i).start()

    def relay(self):
        for index, landed, half in ((4, 0, 0), (5, 1, 1)):
            self.link_copy(landed).wait_recv()

            def step(t, columns):
                value = self.side[half, :, columns]
                value = value + self.link_in[landed, :, columns].astype(SINGLE)
                self.link_out[index, :, columns] = value.astype(HALF)

            self.tiles(step)
            self.link_copy(index).start()

    def finish(self, out_ref):
        for index in (2, 3, 4, 5):
            self.link_copy(index).wait_recv()

        def step(t, columns):
            for half, (one, two) in enumerate(((3, 4), (2, 5))):
                value = self.acc[self.halves[half], columns]
                value = value + self.link_in[one, :, columns].astype(SINGLE)
                value = value + self.link_in[two, :, columns].astype(SINGLE)
                out_ref[self.halves[half], columns] = value

        self.tiles(step)
        for c in self.ORDER[2:]:
            self.core_copy(c).wait_send()
        for index in range(6):
            self.link_copy(index).wait_send()


def scatter_kernel(products, tile, extra, *refs):
    pairs = len(products)
    refs = list(refs)
    take = lambda n: [refs.pop(0) for _ in range(n)]
    lefts, rights = take(pairs), take(pairs)
    beside = take(2 * extra)
    (out_ref,) = take(1)
    beside_out = take(extra)
    plane = PlaneSum(products, tile, lefts, rights, refs)
    plane.greet()
    plane.send(3)
    plane.send(1)
    plane.take(3)
    plane.send(2)
    plane.take(1)
    plane.send(0)
    plane.take(2)
    plane.take(0)
    plane.relay()
    beside_products(list(zip(beside[:extra], beside[extra:], beside_out)))
    plane.finish(out_ref)


def scatter_products(
    lefts, rights, products, fallback, width, tile, collective_id, flops, beside=()
):
    count = lax.axis_size("mp")
    tokens = lefts[0].shape[0]
    rows = tokens // count
    if count != 8:
        summed = lax.psum_scatter(
            fallback().astype(HALF), "mp", scatter_dimension=0, tiled=True
        ).astype(SINGLE)
        return [summed] + [dot_tn(left, right).astype(HALF) for left, right in beside]
    extra = len(beside)
    in_vmem, in_hbm = pl.BlockSpec(memory_space=pltpu.VMEM), pl.BlockSpec(memory_space=pl.ANY)
    return pl.pallas_call(
        functools.partial(scatter_kernel, products, tile, extra),
        out_shape=[jax.ShapeDtypeStruct((rows, width), SINGLE)]
        + [
            jax.ShapeDtypeStruct((left.shape[1], right.shape[1]), HALF) for left, right in beside
        ],
        in_specs=[in_vmem] * (len(lefts) + len(rights)) + [in_hbm] * extra + [in_vmem] * extra,
        out_specs=[in_vmem] + [in_hbm] * extra,
        scratch_shapes=PlaneSum.scratch(rows, width),
        compiler_params=pltpu.CompilerParams(
            collective_id=collective_id, has_side_effects=True, vmem_limit_bytes=VMEM_BYTES
        ),
        cost_estimate=pl.CostEstimate(
            flops=flops, bytes_accessed=tokens * width * 2 * 8, transcendentals=0
        ),
        name="scatter_products",
    )(*lefts, *rights, *[pair[0] for pair in beside], *[pair[1] for pair in beside])


def positions(lens_ref, first, shape):
    place = lax.broadcasted_iota(jnp.int32, shape, 0) + first
    begin = jnp.zeros(shape, jnp.int32)
    total = 0
    for j in range(lens_ref.shape[1]):
        total = total + lens_ref[0, j]
        begin = jnp.where(place >= total, total, begin)
    return place - begin, place < total


def split_dot(dot, left, right):
    high = left.astype(HALF)
    low = (left - high.astype(SINGLE)).astype(HALF)
    return dot(high, right) + dot(low, right)


def lane_tiles(width):
    return [(t, t * 128, min(128, width - t * 128)) for t in range(-(-width // 128))]


def put_tiles(ref, value):
    for t, first, lanes in lane_tiles(value.shape[1]):
        ref[t, :, :lanes] = value[:, first : first + lanes]


def scan_start(tiles, lanes):
    return [(jnp.zeros((lanes, 128), SINGLE), jnp.ones((lanes, 128), SINGLE)) for _ in tiles]


def sigmoid(v):
    return 1.0 / (1.0 + jnp.exp(-v))


def forward_kernel(
    lens_ref,
    x_ref,
    gain_ref,
    pack_ref,
    bin_ref,
    ba_ref,
    chan_ref,
    n1_ref,
    bx_ref,
    by_ref,
    conv_ref,
    gi_ref,
    ra_ref,
    h_ref,
    ob_ref,
    taps,
    coef,
    drive,
    carry,
):
    step = pl.program_id(0)
    rows, width = bx_ref.shape
    depth = pack_ref.shape[2]
    lanes = 8
    span = rows // lanes

    @pl.when(step == 0)
    def _():
        taps[...] = jnp.zeros_like(taps)
        carry[...] = jnp.zeros_like(carry)
        coef[...] = jnp.zeros_like(coef)
        drive[...] = jnp.zeros_like(drive)

    x = x_ref[0].astype(SINGLE)
    scale = lax.rsqrt(jnp.mean(x * x, axis=-1, keepdims=True) + EPS)
    normed = (x * scale * gain_ref[...]).astype(HALF)
    n1_ref[...] = normed
    total = None
    for d in range(pack_ref.shape[0]):
        term = dot_nt(normed[:, d * depth : (d + 1) * depth], pack_ref[d, : 2 * width, :])
        total = term if total is None else total + term
    bx = total[:, :width].astype(HALF)
    by = total[:, width:]
    bx_ref[...] = bx
    by_ref[...] = by
    pos, live = positions(lens_ref, step * rows, (rows, width))
    taps[0:8, :] = taps[rows : rows + 8, :]
    taps[8 : rows + 8, :] = bx.astype(SINGLE)
    conv = jnp.zeros((rows, width), SINGLE) + chan_ref[CONV : CONV + 1, :]
    for k in range(CONV):
        moved = taps[8 - k : 8 - k + rows, :]
        conv = conv + jnp.where(pos >= k, moved * chan_ref[k : k + 1, :], 0.0)
    conv_ref[...] = conv
    high = conv.astype(HALF)
    low = (conv - high.astype(SINGLE)).astype(HALF)
    gate_in = sigmoid(
        dot_nn(high, bin_ref[...]) + dot_nn(low, bin_ref[...]) + chan_ref[CONV + 1 : CONV + 2, :]
    )
    gate_a = sigmoid(
        dot_nn(high, ba_ref[...]) + dot_nn(low, ba_ref[...]) + chan_ref[CONV + 2 : CONV + 3, :]
    )
    gi_ref[...] = gate_in
    ra_ref[...] = gate_a
    decay = jnp.exp(-DECAY * gate_a * chan_ref[CONV + 4 : CONV + 5, :])
    root = jnp.sqrt(1.0 - decay * decay)
    put_tiles(coef, jnp.where(pos == 0, 0.0, decay))
    put_tiles(drive, gate_in * conv * root)
    tiles = lane_tiles(width)

    def scan(i, state):
        at = pl.ds(i, lanes, stride=span)
        result = []
        for (t, _, _), (h, prod) in zip(tiles, state):
            a = coef[t, at, :]
            h = a * h + drive[t, at, :]
            prod = prod * a
            drive[t, at, :] = h
            coef[t, at, :] = prod
            result.append((h, prod))
        return result

    state = lax.fori_loop(0, span, scan, scan_start(tiles, lanes), unroll=4)
    for (t, first, used), (h, prod) in zip(tiles, state):
        running = carry[t, 0:1, :]
        for s in range(lanes):
            at = slice(s * span, (s + 1) * span)
            value = drive[t, at, :] + coef[t, at, :] * running
            h_ref[at, first : first + used] = value[:, :used]
            running = h[s : s + 1, :] + prod[s : s + 1, :] * running
        carry[t, 0:1, :] = running
    mixed = h_ref[...].astype(HALF).astype(SINGLE)
    ob_ref[...] = jnp.where(live, gelu(by) * mixed, 0.0).astype(HALF)


def forward_channels(lens, x_all, gain, pack, blocks_in, blocks_a, chan):
    count, rows, model = x_all.shape
    width = chan.shape[1]
    tokens = count * rows
    whole = lambda shape: pl.BlockSpec(shape, lambda i: (0,) * len(shape))
    part = pl.BlockSpec((rows, width), lambda i: (i, 0))
    full = lambda kind: jax.ShapeDtypeStruct((tokens, width), kind)
    return pl.pallas_call(
        forward_kernel,
        grid=(count,),
        out_shape=(
            jax.ShapeDtypeStruct((tokens, model), HALF),
            full(HALF),
            full(SINGLE),
            full(SINGLE),
            full(SINGLE),
            full(SINGLE),
            full(SINGLE),
            full(HALF),
        ),
        in_specs=[
            pl.BlockSpec(memory_space=pltpu.SMEM),
            pl.BlockSpec((1, rows, model), lambda i: (i, 0, 0)),
            whole(gain.shape),
            whole(pack.shape),
            whole(blocks_in.shape),
            whole(blocks_a.shape),
            whole(chan.shape),
        ],
        out_specs=(pl.BlockSpec((rows, model), lambda i: (i, 0)),) + (part,) * 7,
        scratch_shapes=[
            pltpu.VMEM((rows + 8, width), SINGLE),
            pltpu.VMEM((len(lane_tiles(width)), rows, 128), SINGLE),
            pltpu.VMEM((len(lane_tiles(width)), rows, 128), SINGLE),
            pltpu.VMEM((len(lane_tiles(width)), 8, 128), SINGLE),
        ],
        compiler_params=pltpu.CompilerParams(vmem_limit_bytes=VMEM_BYTES),
        cost_estimate=pl.CostEstimate(
            flops=2 * tokens * model * 2 * width,
            bytes_accessed=tokens * (model * 4 + width * 24),
            transcendentals=8 * tokens * width,
        ),
        name="forward_channels",
    )(lens, x_all, gain, pack, blocks_in, blocks_a, chan)


def by_columns(left, right, t, columns):
    return dot_nn(left, right[:, columns])


def backward_kernel(
    plane_tile,
    lens_ref,
    dt_ref,
    pack_ref,
    bin_ref,
    ba_ref,
    chan_ref,
    bx_ref,
    by_ref,
    conv_ref,
    gi_ref,
    ra_ref,
    h_ref,
    hprev_ref,
    ob_ref,
    n1_ref,
    hidden_ref,
    down_ref,
    dbx_ref,
    dby_ref,
    gin_ref,
    ga_ref,
    gchan_ref,
    grads_ref,
    mlp_ref,
    grads,
    lift,
    coef,
    drive,
    carry,
    *plane_scratch,
):
    if plane_scratch:
        plane = PlaneSum([by_columns], plane_tile, [hidden_ref], [down_ref], plane_scratch)
        schedule = {
            0: lambda: (plane.greet(), plane.send(3), plane.send(1)),
            1: lambda: (plane.take(3), plane.send(2)),
            2: lambda: (plane.take(1), plane.send(0)),
            3: lambda: (plane.take(2), plane.take(0)),
            5: plane.relay,
            7: lambda: plane.finish(mlp_ref),
        }
        for when, act in schedule.items():
            pl.when(pl.program_id(0) == when)(lambda act=act: (act(), None)[1])
    step = pl.program_id(0)
    chunk = pl.num_programs(0) - 1 - step
    rows, width = bx_ref.shape
    depth = pack_ref.shape[2]
    lanes = 8
    span = rows // lanes

    @pl.when(step == 0)
    def _():
        lift[...] = jnp.zeros_like(lift)
        carry[...] = jnp.zeros_like(carry)
        coef[...] = jnp.zeros_like(coef)
        drive[...] = jnp.zeros_like(drive)
        gin_ref[...] = jnp.zeros_like(gin_ref)
        ga_ref[...] = jnp.zeros_like(ga_ref)
        gchan_ref[...] = jnp.zeros_like(gchan_ref)
        grads[...] = jnp.zeros_like(grads)

    d_out = None
    for d in range(pack_ref.shape[0]):
        term = dot_nt(
            dt_ref[0, :, d * depth : (d + 1) * depth], pack_ref[d]
        )
        d_out = term if d_out is None else d_out + term
    pos, live = positions(lens_ref, chunk * rows, (rows, width))
    by = by_ref[...]
    h = h_ref[...]
    side, slope = gelu_both(by)
    d_out = jnp.where(live, d_out, 0.0)
    dby_ref[...] = (d_out * h.astype(HALF).astype(SINGLE) * slope).astype(HALF)
    gate_a = ra_ref[...]
    soft = chan_ref[CONV + 4 : CONV + 5, :]
    decay = jnp.exp(-DECAY * gate_a * soft)
    put_tiles(coef, jnp.where(pos == 0, 0.0, decay))
    put_tiles(drive, (d_out * side).astype(HALF).astype(SINGLE))
    tiles = lane_tiles(width)

    def scan(j, state):
        at = pl.ds(span - 1 - j, lanes, stride=span)
        result = []
        for (t, _, _), (after, prod) in zip(tiles, state):
            a = coef[t, at, :]
            lam = drive[t, at, :] + after
            drive[t, at, :] = lam
            coef[t, at, :] = prod
            result.append((a * lam, prod * a))
        return result

    state = lax.fori_loop(0, span, scan, scan_start(tiles, lanes), unroll=4)
    for (t, first, used), (after, prod) in zip(tiles, state):
        running = carry[t, 0:1, :]
        for s in reversed(range(lanes)):
            at = slice(s * span, (s + 1) * span)
            value = drive[t, at, :] + coef[t, at, :] * running
            lift[at, first : first + used] = value[:, :used]
            running = after[s : s + 1, :] + prod[s : s + 1, :] * running
        carry[t, 0:1, :] = running
    lam = lift[0:rows, :]
    last = jnp.where(chunk > 0, hprev_ref[7:8, :], 0.0)
    before = jnp.concatenate([last, h[: rows - 1, :]], axis=0)
    before = jnp.where(pos == 0, 0.0, before)
    conv = conv_ref[...]
    gate_in = gi_ref[...]
    root = jnp.sqrt(1.0 - decay * decay)
    d_decay = lam * before - lam * gate_in * conv * decay / root
    d_log = d_decay * decay
    d_a = d_log * (-DECAY * soft)
    d_in = lam * conv * root
    d_logit_in = d_in * gate_in * (1.0 - gate_in)
    d_logit_a = d_a * gate_a * (1.0 - gate_a)
    d_conv = (
        lam * gate_in * root
        + split_dot(dot_nt, d_logit_in, bin_ref[...])
        + split_dot(dot_nt, d_logit_a, ba_ref[...])
    )
    low = conv.astype(HALF)
    gin_ref[...] += dot_tn(low, d_logit_in.astype(HALF))
    ga_ref[...] += dot_tn(low, d_logit_a.astype(HALF))
    lift[0:rows, :] = d_conv
    bx = bx_ref[...].astype(SINGLE)
    d_bx = jnp.zeros((rows, width), SINGLE)
    for k in range(CONV):
        if k:
            ahead, _ = positions(lens_ref, chunk * rows + k, (rows, width))
            moved = jnp.where(ahead >= k, lift[k : k + rows, :], 0.0)
        else:
            moved = d_conv
        d_bx = d_bx + moved * chan_ref[k : k + 1, :]
        gchan_ref[k : k + 1, :] += jnp.sum(moved * bx, axis=0, keepdims=True)
    dbx_ref[...] = d_bx.astype(HALF)
    lift[rows : rows + 8, :] = d_conv[0:8, :]
    sums = (d_conv, d_logit_in, d_logit_a, d_log * gate_a)
    for j, value in enumerate(sums):
        gchan_ref[CONV + j : CONV + j + 1, :] += jnp.sum(value, axis=0, keepdims=True)
    lefts = (dbx_ref[...], dby_ref[...], ob_ref[...])
    for d in range(grads.shape[0]):
        columns = slice(d * depth, (d + 1) * depth)
        rights = (n1_ref[:, columns], n1_ref[:, columns], dt_ref[0, :, columns])
        for j, (left, right) in enumerate(zip(lefts, rights)):
            grads[d, j * width : (j + 1) * width, :] += dot_tn(left, right)

    @pl.when(chunk == 0)
    def _():
        grads_ref[...] = grads[...].astype(HALF)


def backward_channels(lens, dt_all, pack, blocks_in, blocks_a, chan, saved, hidden, down, collective_id):
    bx, by, conv, gate_in, gate_a, h, ob, n1 = saved
    count, rows, model = dt_all.shape
    width = chan.shape[1]
    tokens = count * rows
    last = count - 1
    whole = lambda shape: pl.BlockSpec(shape, lambda i: (0,) * len(shape))
    part = pl.BlockSpec((rows, width), lambda i: (last - i, 0))
    before = pl.BlockSpec(
        (8, width), lambda i: (jnp.maximum((last - i) * (rows // 8) - 1, 0), 0)
    )
    full = lambda kind: jax.ShapeDtypeStruct((tokens, width), kind)
    square = jax.ShapeDtypeStruct((width, width), SINGLE)
    grads = (pack.shape[0], 3 * width, pack.shape[2])
    fused = count == PlaneSum.COUNT
    once = lambda shape, at=None: pl.BlockSpec(
        shape, lambda i: at or (0,) * len(shape), pipeline_mode=pl.Buffered(1)
    )
    tokens_kept = pl.BlockSpec(memory_space=pl.ANY)
    outs = pl.pallas_call(
        functools.partial(backward_kernel, 512),
        grid=(count,),
        out_shape=(
            full(HALF),
            full(HALF),
            square,
            square,
            jax.ShapeDtypeStruct((8, width), SINGLE),
            jax.ShapeDtypeStruct(grads, HALF),
            jax.ShapeDtypeStruct((rows, model), SINGLE),
        ),
        in_specs=[
            pl.BlockSpec(memory_space=pltpu.SMEM),
            pl.BlockSpec((1, rows, model), lambda i: (last - i, 0, 0)),
            once((pack.shape[0], width, pack.shape[2]), (0, 2, 0)),
            whole(blocks_in.shape),
            whole(blocks_a.shape),
            whole(chan.shape),
            part,
            part,
            part,
            part,
            part,
            part,
            before,
            part,
            pl.BlockSpec((rows, model), lambda i: (last - i, 0)),
            once(hidden.shape) if fused else tokens_kept,
            once(down.shape) if fused else tokens_kept,
        ],
        out_specs=(
            part,
            part,
            whole((width, width)),
            whole((width, width)),
            whole((8, width)),
            once(grads),
            once((rows, model)),
        ),
        scratch_shapes=[
            pltpu.VMEM(grads, SINGLE),
            pltpu.VMEM((rows + 8, width), SINGLE),
            pltpu.VMEM((len(lane_tiles(width)), rows, 128), SINGLE),
            pltpu.VMEM((len(lane_tiles(width)), rows, 128), SINGLE),
            pltpu.VMEM((len(lane_tiles(width)), 8, 128), SINGLE),
        ]
        + (PlaneSum.scratch(rows, model) if fused else []),
        compiler_params=pltpu.CompilerParams(
            vmem_limit_bytes=VMEM_BYTES,
            **(dict(collective_id=collective_id, has_side_effects=True) if fused else {}),
        ),
        cost_estimate=pl.CostEstimate(
            flops=8 * tokens * model * width,
            bytes_accessed=tokens * (model * 4 + width * 28),
            transcendentals=8 * tokens * width,
        ),
        name="backward_channels",
    )(
        lens, dt_all, pack, blocks_in, blocks_a, chan,
        bx, by, conv, gate_in, gate_a, h, h, ob, n1, hidden, down,
    )
    if fused:
        return outs
    summed = lax.psum_scatter(
        dot_nn(hidden, down).astype(HALF), "mp", scatter_dimension=0, tiled=True
    ).astype(SINGLE)
    return outs[:-1] + (summed,)


def diagonal(blocks):
    count, size, _ = blocks.shape
    spread = blocks[:, :, None, :] * jnp.eye(count, dtype=blocks.dtype)[:, None, :, None]
    return spread.reshape(count * size, count * size)


def on_device(
    layer_input,
    cotangent,
    norm_in,
    norm_mid,
    w_rnn_in,
    w_rnn_gate,
    w_rnn_out,
    gate_in_blocks,
    gate_a_blocks,
    channel_params,
    w_mlp_gate,
    w_mlp_up,
    w_mlp_down,
    lengths,
):
    parts = lax.axis_size("dp")
    rows, model = layer_input.shape
    depth, width = w_rnn_in.shape
    heads, bite, block = gate_in_blocks.shape
    tokens = rows * lax.axis_size("mp")

    flat = jnp.concatenate(
        [
            gate_in_blocks.astype(HALF).reshape(-1),
            gate_a_blocks.astype(HALF).reshape(-1),
            channel_params.astype(HALF).reshape(-1),
        ]
    )
    used = flat.shape[0]
    small_rows = -(-used // (16 * depth)) * 16
    flat = jnp.pad(flat, (0, small_rows * depth - used)).reshape(small_rows, depth)
    mine = jnp.concatenate(
        [
            w_rnn_in.astype(HALF).T,
            w_rnn_gate.astype(HALF).T,
            w_rnn_out.astype(HALF),
            flat,
        ],
        axis=0,
    )
    pack = lax.all_gather(mine, "dp", axis=0, tiled=False)
    down = lax.all_gather(w_mlp_down.astype(HALF), "dp", axis=1, tiled=True)
    gate_w = lax.all_gather(w_mlp_gate.astype(HALF), "dp", axis=0, tiled=True)
    up_w = lax.all_gather(w_mlp_up.astype(HALF), "dp", axis=0, tiled=True)
    bite_gain = norm_in.shape[0]
    gains = jnp.stack([norm_in, norm_mid]).astype(HALF).astype(SINGLE)
    gains = share(jnp.pad(gains, ((0, 6), (0, 128 - bite_gain))), 8)
    gain_first = gains[:, 0, :bite_gain].reshape(1, model)
    gain_second = gains[:, 1, :bite_gain].reshape(1, model)

    small = pack[:, 3 * width :, :].reshape(parts, -1)
    size = heads * bite * block
    whole_block = lambda v: diagonal(
        v.reshape(parts, heads, bite, block).transpose(1, 0, 2, 3).reshape(heads, block, block)
    )
    blocks_in = whole_block(small[:, :size])
    blocks_a = whole_block(small[:, size : 2 * size])
    channel = small[:, 2 * size : used].reshape(2 * CONV, width).astype(SINGLE)
    soft = jax.nn.softplus(-channel[2 * CONV - 1 :])
    chan = jnp.concatenate([channel, soft, jnp.zeros((7, width), SINGLE)], axis=0)

    x_all = gather_rows(layer_input, 0)
    c_all = gather_rows(cotangent, 1).reshape(tokens, model)
    n1, bx, by, conv, gate_in, gate_a, h, ob = forward_channels(
        lengths, x_all, gain_first, pack, blocks_in, blocks_a, chan
    )
    inputs = layer_input.astype(SINGLE)
    (out,) = scatter_products(
        [ob],
        [pack],
        [lambda l, r, t, cols: dot_nn(l, r[t, 2 * width : 3 * width, :])],
        lambda: jnp.einsum(
            "tc,dcm->tdm", ob, pack[:, 2 * width : 3 * width], preferred_element_type=SINGLE
        ).reshape(tokens, model),
        model,
        depth,
        2,
        2 * tokens * width * model,
    )
    residual = inputs + out
    scale_second = lax.rsqrt(jnp.mean(residual * residual, axis=-1, keepdims=True) + EPS)
    normed_mid = (residual * scale_second * gain_second).astype(HALF)
    n2 = gather_rows(normed_mid, 3).reshape(tokens, model)

    def over_dp(value, dimension):
        return lax.psum_scatter(
            value.astype(HALF), "dp", scatter_dimension=dimension, tiled=True
        )

    d_hidden = dot_nt(c_all, down)
    gate_pre = dot_nn(n2, gate_w)
    act, slope = gelu_both(gate_pre)
    d_up = (d_hidden * act).astype(HALF)
    grad_up = dot_tn(n2, d_up).astype(HALF)
    up_w, grad_up = lax.optimization_barrier((up_w, grad_up))
    grad_up = over_dp(grad_up, 0)
    up_pre = dot_nn(n2, up_w)
    hidden = (act * up_pre).astype(HALF)
    d_gate = (d_hidden * up_pre * slope).astype(HALF)
    tile = 512
    by_rows = lambda l, r, t, cols: dot_nt(l, r[cols, :])
    d_normed_mid, grad_gate, grad_down = scatter_products(
        [d_gate, d_up],
        [gate_w, up_w],
        [by_rows, by_rows],
        lambda: dot_nt(d_gate, gate_w) + dot_nt(d_up, up_w),
        model,
        tile,
        4,
        4 * tokens * model * up_w.shape[1],
        [(n2, d_gate), (c_all, hidden)],
    )
    grad_gate = over_dp(grad_gate, 0)
    grad_down = over_dp(grad_down, 0)

    weighted_second = gain_second * d_normed_mid
    grad_gain_second = jnp.sum(d_normed_mid * residual * scale_second, axis=0)
    cube_second = scale_second * scale_second * scale_second
    d_residual = (
        cotangent.astype(SINGLE)
        + scale_second * weighted_second
        - residual * cube_second * jnp.mean(weighted_second * residual, axis=-1, keepdims=True)
    )
    d_resid_low, grad_up = lax.optimization_barrier((d_residual.astype(HALF), grad_up))
    dt_all = gather_rows(d_resid_low, 6)
    dt_all, grad_gate = lax.optimization_barrier((dt_all, grad_gate))

    saved = (bx, by, conv, gate_in, gate_a, h, ob, n1)
    d_bx, d_by, gin, ga, gchan, rnn_grads, mlp_out = backward_channels(
        lengths, dt_all, pack, blocks_in, blocks_a, chan, saved, hidden, down, 5
    )
    d_bx, grad_down = lax.optimization_barrier((d_bx, grad_down))
    (d_normed,) = scatter_products(
        [d_bx, d_by],
        [pack, pack],
        [
            lambda l, r, t, cols: dot_nn(l, r[t, :width, :]),
            lambda l, r, t, cols: dot_nn(l, r[t, width : 2 * width, :]),
        ],
        lambda: jnp.einsum(
            "tc,dcm->tdm",
            jnp.concatenate([d_bx, d_by], axis=1),
            pack[:, : 2 * width],
            preferred_element_type=SINGLE,
        ).reshape(tokens, model),
        model,
        depth,
        7,
        4 * tokens * width * model,
    )
    own = lambda full: jnp.stack(
        [full[j * block : (j + 1) * block, j * block : (j + 1) * block] for j in range(heads)]
    )
    decay_row = DECAY * jax.nn.sigmoid(-channel[2 * CONV - 1 :]) * gchan[2 * CONV - 1 :]
    grad_channel = jnp.concatenate([gchan[: 2 * CONV - 1], decay_row], axis=0)
    split = lambda v: v.reshape(heads, parts, bite, block).transpose(1, 0, 2, 3).reshape(parts, -1)
    small_grads = jnp.concatenate(
        [split(own(gin)), split(own(ga)), grad_channel.reshape(parts, -1)], axis=1
    )
    small_grads = jnp.pad(small_grads, ((0, 0), (0, small_rows * depth - used)))
    small_grads = small_grads.reshape(parts, small_rows, depth).astype(HALF)
    rnn_grads = over_dp(jnp.concatenate([rnn_grads, small_grads], axis=1), 0)
    layer_output = (residual + mlp_out).astype(HALF)

    scale_first = lax.rsqrt(jnp.mean(inputs * inputs, axis=-1, keepdims=True) + EPS)
    weighted_first = gain_first * d_normed
    grad_gain_first = jnp.sum(d_normed * inputs * scale_first, axis=0)
    cube_first = scale_first * scale_first * scale_first
    grad_input = (
        d_residual
        + scale_first * weighted_first
        - inputs * cube_first * jnp.mean(weighted_first * inputs, axis=-1, keepdims=True)
    )

    rnn_grads = rnn_grads[0].astype(SINGLE)
    flat_grads = rnn_grads[3 * width :].reshape(-1)
    gain_grads = jnp.stack([grad_gain_first, grad_gain_second]).reshape(2, -1, bite_gain)
    gain_grads = jnp.pad(gain_grads.transpose(1, 0, 2), ((0, 0), (0, 6), (0, 128 - bite_gain)))
    gain_grads = total(gain_grads, 9)
    return (
        layer_output,
        grad_input,
        gain_grads[0, :bite_gain],
        gain_grads[1, :bite_gain],
        rnn_grads[:width].T,
        rnn_grads[width : 2 * width].T,
        rnn_grads[2 * width : 3 * width],
        flat_grads[:size].reshape(heads, bite, block),
        flat_grads[size : 2 * size].reshape(heads, bite, block),
        flat_grads[2 * size : used].reshape(channel_params.shape),
        grad_gate.astype(SINGLE),
        grad_up.astype(SINGLE),
        grad_down.T.astype(SINGLE),
    )


def solution(mesh):
    rows = P(("dp", "mp"), None)
    return jax.shard_map(
        on_device,
        mesh=mesh,
        in_specs=(
            rows,
            rows,
            P(("dp", "mp")),
            P(("dp", "mp")),
            P("dp", "mp"),
            P("dp", "mp"),
            P("mp", "dp"),
            P("mp", "dp", None),
            P("mp", "dp", None),
            P("dp", "mp"),
            P("dp", "mp"),
            P("dp", "mp"),
            P("mp", "dp"),
            P("dp", None),
        ),
        out_specs=(
            rows,
            rows,
            P(("dp", "mp")),
            P(("dp", "mp")),
            P("dp", "mp"),
            P("dp", "mp"),
            P("mp", "dp"),
            P("mp", "dp", None),
            P("mp", "dp", None),
            P("dp", "mp"),
            P("dp", "mp"),
            P("dp", "mp"),
            P("mp", "dp"),
        ),
        check_vma=False,
    )
```

```python
import functools
import typing

import jax
import jax.numpy as jnp
from jax import lax
from jax.experimental import pallas as pl
from jax.experimental.pallas import tpu as pltpu
from jax.sharding import PartitionSpec as P

CONV = 4
AHEAD = 2
EPS = 1e-06
DECAY = 8.0
HALF = jnp.bfloat16
SINGLE = jnp.float32
MESH = pl.DeviceIdType.MESH
VMEM_BYTES = 60 * 1024 * 1024
GELU_C = 0.7978845608028654
GELU_K = 0.044715


def dot_nn(left, right):
    return lax.dot_general(
        left, right, (((1,), (0,)), ((), ())), preferred_element_type=SINGLE
    )


def dot_nt(left, right):
    return lax.dot_general(
        left, right, (((1,), (1,)), ((), ())), preferred_element_type=SINGLE
    )


def dot_tn(left, right):
    return lax.dot_general(
        left, right, (((0,), (0,)), ((), ())), preferred_element_type=SINGLE
    )


def gelu(v):
    return 0.5 * v * (1.0 + jnp.tanh(GELU_C * (v + GELU_K * v * v * v)))


def gelu_both(v):
    square = v * v
    t = jnp.tanh(GELU_C * (v + GELU_K * v * square))
    value = 0.5 * v * (1.0 + t)
    slope = 0.5 * (1.0 + t) + 0.5 * v * (1.0 - t * t) * (GELU_C * (1.0 + 3.0 * GELU_K * square))
    return value, slope


def flip(me, mask, count):
    place = me
    bit = 1
    while bit < count:
        if mask & bit:
            place = place + (1 - 2 * ((me // bit) % 2)) * bit
        bit *= 2
    return place


def ring_peers(axis):
    me, count = lax.axis_index(axis), lax.axis_size(axis)
    return [(k, {axis: (me + k) % count}) for k in range(1, count)]


def greet(peers):
    barrier = pltpu.get_barrier_semaphore()
    for _, peer in peers:
        pl.semaphore_signal(barrier, inc=1, device_id=peer, device_id_type=MESH)
    pl.semaphore_wait(barrier, len(peers))


def exchange(peers, source, target, send, recv):
    copies = []
    for k, peer in peers:
        copy = pltpu.make_async_remote_copy(
            src_ref=source(k),
            dst_ref=target(k),
            send_sem=send.at[k],
            recv_sem=recv.at[k],
            device_id=peer,
            device_id_type=MESH,
        )
        copy.start()
        copies.append(copy)
    return copies


def gather_plan(count):
    bits = [1 << b for b in range(count.bit_length() - 1)]
    outer = bits[1:]
    orders = (outer + bits[:1], outer[::-1] + bits[:1])
    sends = []
    for half, order in enumerate(orders):
        for stage, bit in enumerate(order):
            for pick in range(1 << stage):
                mask = sum(order[j] for j in range(stage) if pick >> j & 1)
                sends.append((bin(mask).count("1"), half, mask, bit))
    sends.sort(key=lambda s: s[0])
    return bits, [s[1:] for s in sends]


class PlaneGather:
    COUNT = 8

    @staticmethod
    def scratch():
        count = PlaneGather.COUNT
        return [
            pltpu.SemaphoreType.DMA,
            pltpu.SemaphoreType.DMA((2, count)),
            pltpu.SemaphoreType.DMA((2, count)),
        ]

    def __init__(self, x_ref, o_ref, scratch):
        self.x, self.o = x_ref, o_ref
        self.own_sem, self.send, self.recv = scratch
        self.me = lax.axis_index("mp")
        self.bits, self.plan = gather_plan(self.COUNT)

    def own(self):
        rows = self.x.shape[0]
        span = pl.ds(pl.multiple_of(self.me * rows, rows), rows)
        return pltpu.make_async_copy(self.x, self.o.at[span], self.own_sem)

    def copy(self, half, mask, bit):
        rows = self.x.shape[0] // 2
        slot = 2 * flip(self.me, mask, self.COUNT) + half
        span = pl.ds(pl.multiple_of(slot * rows, rows), rows)
        return pltpu.make_async_remote_copy(
            src_ref=self.o.at[span] if mask else self.x.at[pl.ds(half * rows, rows)],
            dst_ref=self.o.at[span],
            send_sem=self.send.at[half, mask | bit],
            recv_sem=self.recv.at[half, mask | bit],
            device_id={"mp": flip(self.me, bit, self.COUNT)},
            device_id_type=MESH,
        )

    def level(self, depth):
        landed = set()
        for half, mask, bit in self.plan:
            if bin(mask).count("1") != depth:
                continue
            if mask and (half, mask) not in landed:
                landed.add((half, mask))
                self.arrived(half, mask)
            self.copy(half, mask, bit).start()

    def arrived(self, half, mask):
        for other, before, bit in self.plan:
            if other == half and before | bit == mask:
                self.copy(half, before, bit).wait_recv()

    def start(self):
        self.own().start()
        self.level(0)

    def finish(self):
        waited = {(half, mask) for half, mask, _ in self.plan}
        for half, mask, bit in self.plan:
            if (half, mask | bit) not in waited:
                self.copy(half, mask, bit).wait_recv()
        for entry in self.plan:
            self.copy(*entry).wait_send()
        self.own().wait()


class LineGather:
    COUNT = 4
    ENDS = ((0, 3), (3, 0))

    @staticmethod
    def scratch(pieces):
        shapes = ((pieces, 4), (pieces, 4), (pieces,), (pieces,))
        return [pltpu.SemaphoreType.DMA(shape) for shape in shapes]

    def __init__(self, jobs, scratch):
        self.chunks, self.of = [], []
        for source, target, pieces in jobs:
            rows = source.shape[0] // pieces
            first = len(self.chunks)
            self.chunks += [(source, target, pl.ds(p * rows, rows)) for p in range(pieces)]
            self.of.append(range(first, len(self.chunks)))
        self.send, self.recv, self.onward, self.own_sem = scratch
        self.me = lax.axis_index("dp")

    def own(self, c):
        source, target, span = self.chunks[c]
        return pltpu.make_async_copy(
            source.at[span], target.at[self.me, span], self.own_sem.at[c]
        )

    def direct(self, c, to):
        source, target, span = self.chunks[c]
        return pltpu.make_async_remote_copy(
            src_ref=source.at[span],
            dst_ref=target.at[self.me, span],
            send_sem=self.send.at[c, to],
            recv_sem=self.recv.at[c, self.me],
            device_id={"dp": to},
            device_id_type=MESH,
        )

    def handed(self, c, block, to):
        _, target, span = self.chunks[c]
        return pltpu.make_async_remote_copy(
            src_ref=target.at[block, span],
            dst_ref=target.at[block, span],
            send_sem=self.onward.at[c],
            recv_sem=self.recv.at[c, block],
            device_id={"dp": to},
            device_id_type=MESH,
        )

    def sends_to(self, to):
        senders = [z for z in range(self.COUNT) if z != to and (z, to) not in self.ENDS]
        return functools.reduce(jnp.logical_or, [self.me == z for z in senders])

    def start(self, chunks):
        for c in chunks:
            self.own(c).start()
            for to in range(self.COUNT):
                pl.when(self.sends_to(to))(lambda c=c, to=to: self.direct(c, to).start())

    def hand_on(self, chunks):
        for c in chunks:
            for first, last in self.ENDS:
                middle = 2 if last == 3 else 1

                @pl.when(self.me == middle)
                def _(c=c, first=first, last=last):
                    copy = self.handed(c, first, last)
                    copy.wait_recv()
                    copy.start()

    def begin(self, ahead):
        self.ahead, self.done = ahead, 0
        self.start(range(ahead))

    def tick(self, count=1):
        for _ in range(count):
            self.hand_on([self.done])
            if self.done + self.ahead < len(self.chunks):
                self.start([self.done + self.ahead])
            self.done += 1

    def landed(self, chunks):
        for c in chunks:
            for block in range(self.COUNT):
                early = 2 if block == 0 else 1 if block == 3 else None
                waits = self.me != block
                if early is not None:
                    waits = jnp.logical_and(waits, self.me != early)
                pl.when(waits)(lambda c=c, block=block: self.handed(c, block, 0).wait_recv())
            self.own(c).wait()

    def settle(self):
        for c in range(len(self.chunks)):
            for to in range(self.COUNT):
                pl.when(self.sends_to(to))(lambda c=c, to=to: self.direct(c, to).wait_send())
            pl.when(jnp.logical_or(self.me == 1, self.me == 2))(
                lambda c=c: self.handed(c, 0, 0).wait_send()
            )


def kernel_params(collective_id):
    return pltpu.CompilerParams(
        collective_id=collective_id, has_side_effects=True, vmem_limit_bytes=VMEM_BYTES
    )


def share(x_ref, o_ref, sems):
    send_mp, recv_mp, send_dp, recv_dp = sems
    inner, outer = ring_peers("mp"), ring_peers("dp")
    count = len(inner) + 1
    first = lax.axis_index("dp") * count
    place = first + lax.axis_index("mp")
    o_ref[place] = x_ref[...]
    mine = lambda k: o_ref.at[place]
    plane = lambda k: o_ref.at[pl.ds(first, count)]
    copies = exchange(inner, mine, mine, send_mp, recv_mp)
    for copy in copies:
        copy.wait_recv()
    later = exchange(outer, plane, plane, send_dp, recv_dp)
    return later, copies + later


def beside_products(pairs):
    for left, right, out in pairs:
        tokens, rows = left.shape
        tile = min(256, rows)

        def body(left_tile, out_tile):
            out_tile[...] = dot_tn(left_tile[...], right[...]).astype(out_tile.dtype)

        pltpu.emit_pipeline(
            body,
            grid=(rows // tile,),
            in_specs=[pl.BlockSpec((tokens, tile), lambda i: (0, i))],
            out_specs=[pl.BlockSpec((tile, right.shape[1]), lambda i: (i, 0))],
        )(left, out)


class PlaneSum:
    COUNT = 8
    ORDER = (3, 1, 2, 0)
    LINKS = ((3, 0, 2), (3, 1, 1), (1, 1, 1), (2, 0, 2), (1, 0, 1), (2, 1, 2))

    @staticmethod
    def scratch(rows, width):
        middle = rows // 2
        return [
            pltpu.VMEM((rows, width), SINGLE),
            pltpu.VMEM((2, middle, width), SINGLE),
            pltpu.VMEM((2, rows, width), HALF),
            pltpu.VMEM((4, rows, width), HALF),
            pltpu.VMEM((6, middle, width), HALF),
            pltpu.VMEM((6, middle, width), HALF),
            pltpu.SemaphoreType.DMA((4,)),
            pltpu.SemaphoreType.DMA((4,)),
            pltpu.SemaphoreType.DMA((6,)),
            pltpu.SemaphoreType.DMA((6,)),
        ]

    def __init__(self, products, tile, lefts, rights, scratch):
        self.terms = list(zip(lefts, rights, products))
        self.tile = tile
        self.acc, self.side, self.core_out, self.core_in = scratch[:4]
        self.link_out, self.link_in = scratch[4:6]
        self.core_send, self.core_recv, self.link_send, self.link_recv = scratch[6:]
        self.rows, self.width = self.acc.shape
        self.halves = (slice(0, self.rows // 2), slice(self.rows // 2, self.rows))
        self.me = lax.axis_index("mp")

    def tiles(self, step):
        def body(t, carry):
            step(t, pl.ds(pl.multiple_of(t * self.tile, self.tile), self.tile))
            return carry

        lax.fori_loop(0, self.width // self.tile, body, 0)

    def partial(self, slot, t, columns):
        span = pl.ds(pl.multiple_of(slot * self.rows, self.rows), self.rows)
        value = None
        for left, right, product in self.terms:
            term = product(left[span, :], right, t, columns)
            value = term if value is None else value + term
        return value

    def core_copy(self, c):
        return pltpu.make_async_remote_copy(
            src_ref=self.core_out.at[self.ORDER.index(c) % 2],
            dst_ref=self.core_in.at[c],
            send_sem=self.core_send.at[c],
            recv_sem=self.core_recv.at[c],
            device_id={"mp": flip(self.me, 1, self.COUNT)},
            device_id_type=MESH,
        )

    def link_copy(self, index):
        return pltpu.make_async_remote_copy(
            src_ref=self.link_out.at[index],
            dst_ref=self.link_in.at[index],
            send_sem=self.link_send.at[index],
            recv_sem=self.link_recv.at[index],
            device_id={"mp": flip(self.me, 2 * self.LINKS[index][2], self.COUNT)},
            device_id_type=MESH,
        )

    def send(self, c):
        place = self.ORDER.index(c)
        if place >= 2:
            self.core_copy(self.ORDER[place - 2]).wait_send()
        slot = flip(self.me, 2 * c + 1, self.COUNT)

        def step(t, columns):
            self.core_out[place % 2, :, columns] = self.partial(slot, t, columns).astype(HALF)

        self.tiles(step)
        self.core_copy(c).start()

    def take(self, c):
        self.core_copy(c).wait_recv()
        slot = flip(self.me, 2 * c, self.COUNT)
        ways = [i for i in range(4) if self.LINKS[i][0] == c]
        kept = [h for h in (0, 1) if c and h not in [self.LINKS[i][1] for i in ways]]

        def step(t, columns):
            value = self.partial(slot, t, columns) + self.core_in[c, :, columns].astype(SINGLE)
            if c == 0:
                self.acc[:, columns] = value
            for i in ways:
                self.link_out[i, :, columns] = value[self.halves[self.LINKS[i][1]]].astype(HALF)
            for h in kept:
                self.side[h, :, columns] = value[self.halves[h]]

        self.tiles(step)
        for i in ways:
            self.link_copy(i).start()

    def spread(self, between=lambda: None):
        self.send(3)
        self.send(1)
        self.take(3)
        self.send(2)
        self.take(1)
        between()
        self.send(0)
        self.take(2)
        self.take(0)
        self.relay()

    def relay(self):
        for index, landed, half in ((4, 0, 0), (5, 1, 1)):
            self.link_copy(landed).wait_recv()

            def step(t, columns):
                value = self.side[half, :, columns]
                value = value + self.link_in[landed, :, columns].astype(SINGLE)
                self.link_out[index, :, columns] = value.astype(HALF)

            self.tiles(step)
            self.link_copy(index).start()

    def finish(self, out_ref):
        for index in (2, 3, 4, 5):
            self.link_copy(index).wait_recv()

        def step(t, columns):
            for half, (one, two) in enumerate(((3, 4), (2, 5))):
                value = self.acc[self.halves[half], columns]
                value = value + self.link_in[one, :, columns].astype(SINGLE)
                value = value + self.link_in[two, :, columns].astype(SINGLE)
                out_ref[self.halves[half], columns] = value

        self.tiles(step)
        for c in self.ORDER[2:]:
            self.core_copy(c).wait_send()
        for index in range(6):
            self.link_copy(index).wait_send()


class LineSum:
    COUNT = 4

    @staticmethod
    def scratch(pieces):
        shapes = ((pieces, 4), (pieces, 4), (pieces,), (pieces,))
        return [pltpu.SemaphoreType.DMA(shape) for shape in shapes] + [pltpu.SemaphoreType.DMA]

    def __init__(self, jobs, scratch):
        self.jobs, self.chunks, self.of = jobs, [], []
        for job in jobs:
            _, landed, _, pieces, _, _ = job
            rows = landed.shape[1] // pieces
            first = len(self.chunks)
            self.chunks += [(job, p, rows) for p in range(pieces)]
            self.of.append(range(first, len(self.chunks)))
        self.send, self.recv, self.relay_send, self.relay_recv, self.load_sem = scratch
        self.me = lax.axis_index("dp")

    def part(self, c, block):
        (source, landed, *_), p, rows = self.chunks[c]
        return source.at[pl.ds(pl.multiple_of(block * landed.shape[1] + p * rows, 16), rows)]

    def place(self, c, sender):
        (_, landed, *_), p, rows = self.chunks[c]
        return landed.at[sender, pl.ds(p * rows, rows)]

    def relay(self, c):
        (*_, relay, _), p, _ = self.chunks[c]
        return relay.at[p]

    def direct(self, c, to, source=None):
        return pltpu.make_async_remote_copy(
            src_ref=self.part(c, to) if source is None else source,
            dst_ref=self.place(c, self.me),
            send_sem=self.send.at[c, to],
            recv_sem=self.recv.at[c, self.me],
            device_id={"dp": to},
            device_id_type=MESH,
        )

    def by_middle(self, c, block, to):
        return pltpu.make_async_remote_copy(
            src_ref=self.part(c, block),
            dst_ref=self.relay(c),
            send_sem=self.relay_send.at[c],
            recv_sem=self.relay_recv.at[c],
            device_id={"dp": to},
            device_id_type=MESH,
        )

    def among(self, places):
        return functools.reduce(jnp.logical_or, [self.me == z for z in places])

    DIRECT = ((1,), (0, 2, 3), (0, 1, 3), (2,))
    ROUND = ((0, 3, 1), (3, 0, 2))

    def start(self, chunks):
        for c in chunks:
            for end, block, middle in self.ROUND:
                pl.when(self.me == end)(
                    lambda c=c, block=block, middle=middle: self.by_middle(c, block, middle).start()
                )
            for to, senders in enumerate(self.DIRECT):
                pl.when(self.among(senders))(lambda c=c, to=to: self.direct(c, to).start())

    def hand_on(self, chunks):
        for c in chunks:
            *_, other = self.chunks[c][0]
            for _, block, middle in self.ROUND:

                @pl.when(self.me == middle)
                def _(c=c, block=block, middle=middle, other=other):
                    mine = pltpu.make_async_copy(self.part(c, block), other, self.load_sem)
                    mine.start()
                    self.by_middle(c, block, middle).wait_recv()
                    mine.wait()
                    relay = self.relay(c)
                    value = relay[...].astype(SINGLE) + other[...].astype(SINGLE)
                    relay[...] = value.astype(HALF)
                    self.direct(c, block, relay).start()

    def begin(self, ahead):
        self.ahead, self.done = ahead, 0
        self.start(range(ahead))

    def tick(self, count=1):
        for _ in range(count):
            self.hand_on([self.done])
            if self.done + self.ahead < len(self.chunks):
                self.start([self.done + self.ahead])
            self.done += 1

    SENDERS = ((1, 2), (0, 2, 3), (0, 1, 3), (1, 2))

    def collect(self, j):
        source, landed, target, _, _, _ = self.jobs[j]
        for c in self.of[j]:
            for sender in range(self.COUNT):
                takers = [z for z in range(self.COUNT) if sender in self.SENDERS[z]]
                pl.when(self.among(takers))(
                    lambda c=c, sender=sender: self.wait_from(c, sender)
                )
        rows, columns = target.shape
        tile = rows // 2 if rows >= 256 else rows

        def add(*refs):
            value = refs[0][...].astype(SINGLE)
            for ref in refs[1:-1]:
                value = value + ref[0].astype(SINGLE)
            refs[-1][...] = value

        def run(senders):
            pltpu.emit_pipeline(
                add,
                grid=(rows // tile,),
                in_specs=[
                    pl.BlockSpec((tile, columns), lambda t: (self.me * (rows // tile) + t, 0))
                ]
                + [
                    pl.BlockSpec((1, tile, columns), lambda t, sender=sender: (sender, t, 0))
                    for sender in senders
                ],
                out_specs=[pl.BlockSpec((tile, columns), lambda t: (t, 0))],
            )(source, *[landed] * len(senders), target)

        pl.when(self.among((0, 3)))(lambda: run((1, 2)))
        pl.when(self.among((1, 2)))(lambda: run((0, 3 - self.me, 3)))

    def wait_from(self, c, sender):
        pltpu.make_async_remote_copy(
            src_ref=self.place(c, sender),
            dst_ref=self.place(c, sender),
            send_sem=self.relay_send.at[c],
            recv_sem=self.recv.at[c, sender],
            device_id={"dp": 0},
            device_id_type=MESH,
        ).wait_recv()

    def settle(self):
        for c in range(len(self.chunks)):
            for to, senders in enumerate(self.DIRECT):
                pl.when(self.among(senders))(lambda c=c, to=to: self.direct(c, to).wait_send())
            for end, block, middle in self.ROUND:
                pl.when(self.me == end)(
                    lambda c=c, block=block, middle=middle: self.by_middle(
                        c, block, middle
                    ).wait_send()
                )
                pl.when(self.me == middle)(
                    lambda c=c, block=block: self.direct(c, block, self.relay(c)).wait_send()
                )


def positions(lens_ref, first, shape):
    place = lax.broadcasted_iota(jnp.int32, shape, 0) + first
    begin = jnp.zeros(shape, jnp.int32)
    total = 0
    for j in range(lens_ref.shape[1]):
        total = total + lens_ref[0, j]
        begin = jnp.where(place >= total, total, begin)
    return place - begin, place < total


def split_dot(dot, left, right):
    high = left.astype(HALF)
    low = (left - high.astype(SINGLE)).astype(HALF)
    return dot(high, right) + dot(low, right)


def lane_tiles(width):
    return [(t, t * 128, min(128, width - t * 128)) for t in range(-(-width // 128))]


def put_tiles(ref, value):
    for t, first, lanes in lane_tiles(value.shape[1]):
        ref[t, :, :lanes] = value[:, first : first + lanes]


def scan_start(tiles, lanes):
    return [(jnp.zeros((lanes, 128), SINGLE), jnp.ones((lanes, 128), SINGLE)) for _ in tiles]


def sigmoid(v):
    return 1.0 / (1.0 + jnp.exp(-v))


def forward_step(
    step,
    lens_ref,
    x_ref,
    gain_ref,
    pack_ref,
    bin_ref,
    ba_ref,
    chan_ref,
    n1_ref,
    bx_ref,
    by_ref,
    conv_ref,
    gi_ref,
    ra_ref,
    h_ref,
    ob_ref,
    taps,
    coef,
    drive,
    carry,
):
    rows, width = bx_ref.shape
    depth = pack_ref.shape[2]
    lanes = 8
    span = rows // lanes

    @pl.when(step == 0)
    def _():
        taps[...] = jnp.zeros_like(taps)
        carry[...] = jnp.zeros_like(carry)
        coef[...] = jnp.zeros_like(coef)
        drive[...] = jnp.zeros_like(drive)

    x = x_ref[...].astype(SINGLE)
    scale = lax.rsqrt(jnp.mean(x * x, axis=-1, keepdims=True) + EPS)
    normed = (x * scale * gain_ref[...]).astype(HALF)
    n1_ref[...] = normed
    total = None
    for d in range(pack_ref.shape[0]):
        term = dot_nt(normed[:, d * depth : (d + 1) * depth], pack_ref[d, : 2 * width, :])
        total = term if total is None else total + term
    bx = total[:, :width].astype(HALF)
    by = total[:, width:]
    bx_ref[...] = bx
    by_ref[...] = by
    pos, live = positions(lens_ref, step * rows, (rows, width))
    taps[0:8, :] = taps[rows : rows + 8, :]
    taps[8 : rows + 8, :] = bx.astype(SINGLE)
    conv = jnp.zeros((rows, width), SINGLE) + chan_ref[CONV : CONV + 1, :]
    for k in range(CONV):
        moved = taps[8 - k : 8 - k + rows, :]
        conv = conv + jnp.where(pos >= k, moved * chan_ref[k : k + 1, :], 0.0)
    conv_ref[...] = conv
    high = conv.astype(HALF)
    low = (conv - high.astype(SINGLE)).astype(HALF)
    gate_in = sigmoid(
        dot_nn(high, bin_ref[...]) + dot_nn(low, bin_ref[...]) + chan_ref[CONV + 1 : CONV + 2, :]
    )
    gate_a = sigmoid(
        dot_nn(high, ba_ref[...]) + dot_nn(low, ba_ref[...]) + chan_ref[CONV + 2 : CONV + 3, :]
    )
    gi_ref[...] = gate_in
    ra_ref[...] = gate_a
    decay = jnp.exp(-DECAY * gate_a * chan_ref[CONV + 4 : CONV + 5, :])
    root = jnp.sqrt(1.0 - decay * decay)
    put_tiles(coef, jnp.where(pos == 0, 0.0, decay))
    put_tiles(drive, gate_in * conv * root)
    tiles = lane_tiles(width)

    def scan(i, state):
        at = pl.ds(i, lanes, stride=span)
        result = []
        for (t, _, _), (h, prod) in zip(tiles, state):
            a = coef[t, at, :]
            h = a * h + drive[t, at, :]
            prod = prod * a
            drive[t, at, :] = h
            coef[t, at, :] = prod
            result.append((h, prod))
        return result

    state = lax.fori_loop(0, span, scan, scan_start(tiles, lanes), unroll=4)
    for (t, first, used), (h, prod) in zip(tiles, state):
        running = carry[t, 0:1, :]
        for s in range(lanes):
            at = slice(s * span, (s + 1) * span)
            value = drive[t, at, :] + coef[t, at, :] * running
            h_ref[at, first : first + used] = value[:, :used]
            running = h[s : s + 1, :] + prod[s : s + 1, :] * running
        carry[t, 0:1, :] = running
    mixed = h_ref[...].astype(HALF).astype(SINGLE)
    ob_ref[...] = jnp.where(live, gelu(by) * mixed, 0.0).astype(HALF)


def forward_kernel(*refs):
    forward_step(pl.program_id(0), *refs)


def forward_scratch(rows, width):
    tiles = len(lane_tiles(width))
    return [
        pltpu.VMEM((rows + 8, width), SINGLE),
        pltpu.VMEM((tiles, rows, 128), SINGLE),
        pltpu.VMEM((tiles, rows, 128), SINGLE),
        pltpu.VMEM((tiles, 8, 128), SINGLE),
    ]


def forward_channels(lens, x_all, gain, pack, blocks_in, blocks_a, chan):
    tokens, model = x_all.shape
    width = chan.shape[1]
    count = lax.axis_size("mp")
    rows = tokens // count
    whole = lambda shape: pl.BlockSpec(shape, lambda i: (0,) * len(shape))
    part = pl.BlockSpec((rows, width), lambda i: (i, 0))
    full = lambda kind: jax.ShapeDtypeStruct((tokens, width), kind)
    return pl.pallas_call(
        forward_kernel,
        grid=(count,),
        out_shape=(
            jax.ShapeDtypeStruct((tokens, model), HALF),
            full(HALF),
            full(SINGLE),
            full(SINGLE),
            full(SINGLE),
            full(SINGLE),
            full(SINGLE),
            full(HALF),
        ),
        in_specs=[
            pl.BlockSpec(memory_space=pltpu.SMEM),
            pl.BlockSpec((rows, model), lambda i: (i, 0)),
            whole(gain.shape),
            whole(pack.shape),
            whole(blocks_in.shape),
            whole(blocks_a.shape),
            whole(chan.shape),
        ],
        out_specs=(pl.BlockSpec((rows, model), lambda i: (i, 0)),) + (part,) * 7,
        scratch_shapes=forward_scratch(rows, width),
        compiler_params=pltpu.CompilerParams(vmem_limit_bytes=VMEM_BYTES),
        cost_estimate=pl.CostEstimate(
            flops=2 * tokens * model * 2 * width,
            bytes_accessed=tokens * (model * 4 + width * 24),
            transcendentals=8 * tokens * width,
        ),
        name="forward_channels",
    )(lens, x_all, gain, pack, blocks_in, blocks_a, chan)


def by_parts(left, right, t, columns):
    return dot_nn(left, right[t])


def backward_step(
    step,
    steps,
    lens_ref,
    dt_ref,
    pack_ref,
    bin_ref,
    ba_ref,
    chan_ref,
    bx_ref,
    by_ref,
    conv_ref,
    gi_ref,
    ra_ref,
    h_ref,
    hprev_ref,
    dbx_ref,
    dby_ref,
    gin_ref,
    ga_ref,
    gchan_ref,
    lift,
    coef,
    drive,
    carry,
):
    chunk = steps - 1 - step
    rows, width = bx_ref.shape
    depth = pack_ref.shape[2]
    lanes = 8
    span = rows // lanes

    @pl.when(step == 0)
    def _():
        lift[...] = jnp.zeros_like(lift)
        carry[...] = jnp.zeros_like(carry)
        coef[...] = jnp.zeros_like(coef)
        drive[...] = jnp.zeros_like(drive)
        gin_ref[...] = jnp.zeros_like(gin_ref)
        ga_ref[...] = jnp.zeros_like(ga_ref)
        gchan_ref[...] = jnp.zeros_like(gchan_ref)

    d_out = None
    for d in range(pack_ref.shape[0]):
        term = dot_nt(dt_ref[:, d * depth : (d + 1) * depth], pack_ref[d])
        d_out = term if d_out is None else d_out + term
    pos, live = positions(lens_ref, chunk * rows, (rows, width))
    by = by_ref[...]
    h = h_ref[...]
    side, slope = gelu_both(by)
    d_out = jnp.where(live, d_out, 0.0)
    dby_ref[...] = (d_out * h.astype(HALF).astype(SINGLE) * slope).astype(HALF)
    gate_a = ra_ref[...]
    soft = chan_ref[CONV + 4 : CONV + 5, :]
    decay = jnp.exp(-DECAY * gate_a * soft)
    put_tiles(coef, jnp.where(pos == 0, 0.0, decay))
    put_tiles(drive, (d_out * side).astype(HALF).astype(SINGLE))
    tiles = lane_tiles(width)

    def scan(j, state):
        at = pl.ds(span - 1 - j, lanes, stride=span)
        result = []
        for (t, _, _), (after, prod) in zip(tiles, state):
            a = coef[t, at, :]
            lam = drive[t, at, :] + after
            drive[t, at, :] = lam
            coef[t, at, :] = prod
            result.append((a * lam, prod * a))
        return result

    state = lax.fori_loop(0, span, scan, scan_start(tiles, lanes), unroll=4)
    for (t, first, used), (after, prod) in zip(tiles, state):
        running = carry[t, 0:1, :]
        for s in reversed(range(lanes)):
            at = slice(s * span, (s + 1) * span)
            value = drive[t, at, :] + coef[t, at, :] * running
            lift[at, first : first + used] = value[:, :used]
            running = after[s : s + 1, :] + prod[s : s + 1, :] * running
        carry[t, 0:1, :] = running
    lam = lift[0:rows, :]
    last = jnp.where(chunk > 0, hprev_ref[7:8, :], 0.0)
    before = jnp.concatenate([last, h[: rows - 1, :]], axis=0)
    before = jnp.where(pos == 0, 0.0, before)
    conv = conv_ref[...]
    gate_in = gi_ref[...]
    root = jnp.sqrt(1.0 - decay * decay)
    d_decay = lam * before - lam * gate_in * conv * decay / root
    d_log = d_decay * decay
    d_a = d_log * (-DECAY * soft)
    d_in = lam * conv * root
    d_logit_in = d_in * gate_in * (1.0 - gate_in)
    d_logit_a = d_a * gate_a * (1.0 - gate_a)
    d_conv = (
        lam * gate_in * root
        + split_dot(dot_nt, d_logit_in, bin_ref[...])
        + split_dot(dot_nt, d_logit_a, ba_ref[...])
    )
    low = conv.astype(HALF)
    gin_ref[...] += dot_tn(low, d_logit_in.astype(HALF))
    ga_ref[...] += dot_tn(low, d_logit_a.astype(HALF))
    lift[0:rows, :] = d_conv
    bx = bx_ref[...].astype(SINGLE)
    d_bx = jnp.zeros((rows, width), SINGLE)
    for k in range(CONV):
        if k:
            ahead, _ = positions(lens_ref, chunk * rows + k, (rows, width))
            moved = jnp.where(ahead >= k, lift[k : k + rows, :], 0.0)
        else:
            moved = d_conv
        d_bx = d_bx + moved * chan_ref[k : k + 1, :]
        gchan_ref[k : k + 1, :] += jnp.sum(moved * bx, axis=0, keepdims=True)
    dbx_ref[...] = d_bx.astype(HALF)
    lift[rows : rows + 8, :] = d_conv[0:8, :]
    sums = (d_conv, d_logit_in, d_logit_a, d_log * gate_a)
    for j, value in enumerate(sums):
        gchan_ref[CONV + j : CONV + j + 1, :] += jnp.sum(value, axis=0, keepdims=True)


def backward_kernel(*refs):
    refs = list(refs)
    inputs, (ob_ref, n1_ref), outputs, grads_ref, grads, scratch = (
        refs[:13], refs[13:15], refs[15:20], refs[20], refs[21], refs[22:],
    )
    step, steps = pl.program_id(0), pl.num_programs(0)

    @pl.when(step == 0)
    def _():
        grads[...] = jnp.zeros_like(grads)

    backward_step(step, steps, *inputs, *outputs, *scratch)
    dt_ref, (dbx_ref, dby_ref) = inputs[1], outputs[:2]
    width, depth = dbx_ref.shape[1], grads.shape[2]
    lefts = (dbx_ref[...], dby_ref[...], ob_ref[...])
    for d in range(grads.shape[0]):
        columns = slice(d * depth, (d + 1) * depth)
        rights = (n1_ref[:, columns], n1_ref[:, columns], dt_ref[:, columns])
        for j, (left, right) in enumerate(zip(lefts, rights)):
            grads[d, j * width : (j + 1) * width, :] += dot_tn(left, right)

    @pl.when(step == steps - 1)
    def _():
        grads_ref[...] = grads[...].astype(HALF)


def backward_channels(lens, dt_all, pack, blocks_in, blocks_a, chan, saved):
    bx, by, conv, gate_in, gate_a, h, ob, n1 = saved
    tokens, model = dt_all.shape
    width = chan.shape[1]
    count = lax.axis_size("mp")
    rows = tokens // count
    last = count - 1
    whole = lambda shape: pl.BlockSpec(shape, lambda i: (0,) * len(shape))
    part = pl.BlockSpec((rows, width), lambda i: (last - i, 0))
    across = pl.BlockSpec((rows, model), lambda i: (last - i, 0))
    before = pl.BlockSpec(
        (8, width), lambda i: (jnp.maximum((last - i) * (rows // 8) - 1, 0), 0)
    )
    full = jax.ShapeDtypeStruct((tokens, width), HALF)
    square = jax.ShapeDtypeStruct((width, width), SINGLE)
    grads = (pack.shape[0], 3 * width, pack.shape[2])
    return pl.pallas_call(
        backward_kernel,
        grid=(count,),
        out_shape=(
            full,
            full,
            square,
            square,
            jax.ShapeDtypeStruct((8, width), SINGLE),
            jax.ShapeDtypeStruct(grads, HALF),
        ),
        in_specs=[
            pl.BlockSpec(memory_space=pltpu.SMEM),
            across,
            whole(pack.shape),
            whole(blocks_in.shape),
            whole(blocks_a.shape),
            whole(chan.shape),
            part,
            part,
            part,
            part,
            part,
            part,
            before,
            part,
            across,
        ],
        out_specs=(
            part,
            part,
            whole((width, width)),
            whole((width, width)),
            whole((8, width)),
            whole(grads),
        ),
        scratch_shapes=[pltpu.VMEM(grads, SINGLE)] + forward_scratch(rows, width),
        compiler_params=pltpu.CompilerParams(vmem_limit_bytes=VMEM_BYTES),
        cost_estimate=pl.CostEstimate(
            flops=8 * tokens * model * width,
            bytes_accessed=tokens * (model * 4 + width * 28),
            transcendentals=8 * tokens * width,
        ),
        name="backward_channels",
    )(
        lens, dt_all, pack, blocks_in, blocks_a, chan,
        bx, by, conv, gate_in, gate_a, h, h, ob, n1,
    )


def log_one_plus(v):
    total = 1.0 + v
    exact = total - 1.0
    return jnp.where(exact == 0.0, v, jnp.log(total) * (v / jnp.where(exact == 0.0, 1.0, exact)))


def small_weights(small, bin_ref, ba_ref, chan_ref, heads, bite):
    parts = small.shape[0]
    width = bin_ref.shape[0]
    block = width // heads
    at_row = lax.broadcasted_iota(jnp.int32, (block, width), 0)
    at_column = lax.broadcasted_iota(jnp.int32, (block, width), 1)
    each = 2 * CONV // parts
    for d in range(parts):
        value = small[d].astype(SINGLE)
        for h in range(heads):
            place = (at_column == at_row + h * block).astype(HALF)
            for lane, target in ((0, bin_ref), (256, ba_ref)):
                piece = value[h * bite : (h + 1) * bite, lane : lane + block].astype(HALF)
                first = h * block + d * bite
                target[first : first + bite, :] = dot_nn(piece, place)
        row = heads * bite
        chan_ref[d * each : (d + 1) * each, :] = value[row : row + each, :width]
    v = -chan_ref[2 * CONV - 1 : 2 * CONV, :]
    chan_ref[2 * CONV : 2 * CONV + 1, :] = jnp.maximum(v, 0.0) + log_one_plus(
        jnp.exp(-jnp.abs(v))
    )


class ForwardIn(typing.NamedTuple):
    lens: typing.Any
    gains: typing.Any
    x: typing.Any
    cot: typing.Any
    small: typing.Any
    pack: typing.Any
    out: typing.Any
    down: typing.Any
    gate: typing.Any
    up: typing.Any


class ForwardOut(typing.NamedTuple):
    gain: typing.Any
    bin: typing.Any
    ba: typing.Any
    chan: typing.Any
    x_all: typing.Any
    c_all: typing.Any
    n2_all: typing.Any
    n1: typing.Any
    residual: typing.Any
    bx: typing.Any
    by: typing.Any
    conv: typing.Any
    gi: typing.Any
    ra: typing.Any
    h: typing.Any
    ob: typing.Any
    small4: typing.Any
    pack4: typing.Any
    out4: typing.Any
    gate4: typing.Any
    up4: typing.Any
    down4: typing.Any
    act: typing.Any
    hidden: typing.Any
    d_up: typing.Any
    d_gate: typing.Any
    grad_down: typing.Any


WEIGHT_PIECES = (1, 4, 2, 4, 4, 6)


def forward_pass_kernel(heads, bite, *refs):
    refs = list(refs)
    take = lambda n: [refs.pop(0) for _ in range(n)]
    i = ForwardIn(*take(len(ForwardIn._fields)))
    o = ForwardOut(*take(len(ForwardOut._fields)))
    tiles, bin32, ba32 = take(3)
    pack, out_w, down, gate, up = take(5)
    steps_scratch = take(4)
    ob, inputs, summed, n2_own, slope, hidden = take(6)
    load_sem, store_sem = take(2)
    share_sems = take(4)
    plane_x = PlaneGather(i.x, o.x_all, take(3))
    plane_c = PlaneGather(i.cot, o.c_all, take(3))
    plane_n = PlaneGather(n2_own, o.n2_all, take(3))
    plane = PlaneSum([by_parts], out_w.shape[2], [ob], [out_w], take(10))
    line = LineGather(
        list(
            zip(
                (i.small, i.pack, i.out, i.gate, i.up, i.down),
                (o.small4, o.pack4, o.out4, o.gate4, o.up4, o.down4),
                WEIGHT_PIECES,
            )
        ),
        refs,
    )
    small_at, pack_at, out_at, gate_at, up_at, down_at = line.of
    tokens, model = o.x_all.shape
    rows, count, width = i.x.shape[0], PlaneGather.COUNT, ob.shape[1]
    parts, _, depth = pack.shape

    greet(ring_peers("mp") + ring_peers("dp"))
    line.begin(AHEAD)
    gains_way, copies = share(i.gains, tiles, share_sems)
    plane_x.start()
    own_rows = pltpu.make_async_copy(i.x, inputs, load_sem.at[0])
    own_rows.start()
    bin32[...] = jnp.zeros_like(bin32)
    ba32[...] = jnp.zeros_like(ba32)
    o.chan[...] = jnp.zeros_like(o.chan)
    line.tick(2)
    plane_x.level(1)
    line.tick()
    plane_x.level(2)
    line.tick()
    plane_x.finish()
    plane_c.start()
    line.tick()
    for copy in gains_way:
        copy.wait_recv()
    group = 128 // (model // tiles.shape[0])
    for j in range(model // 128):
        value = tiles[group * j]
        for k in range(1, group):
            value = value + tiles[group * j + k]
        o.gain[:, j * 128 : (j + 1) * 128] = value
    line.landed(small_at)
    line.landed(pack_at)
    own_rows.wait()

    def load(source, target, j):
        copy = pltpu.make_async_copy(source, target, load_sem.at[j])
        copy.start()
        return copy

    loads = [load(o.pack4, pack, 1)]

    def with_small(small):
        copy = load(o.small4, small, 2)
        copy.wait()
        small_weights(small, bin32, ba32, o.chan, heads, bite)

    pl.run_scoped(with_small, pltpu.VMEM(o.small4.shape, HALF))
    o.bin[...] = bin32[...].astype(HALF)
    o.ba[...] = ba32[...].astype(HALF)
    loads[0].wait()

    def channels(x_tile, n1, bx, by, conv, gi, ra, h, ob_tile):
        step = pl.program_id(0)
        schedule = {
            2: line.tick,
            3: lambda: plane_c.level(1),
            4: line.tick,
            6: lambda: plane_c.level(2),
            7: line.tick,
        }
        for when, act in schedule.items():
            pl.when(step == when)(lambda act=act: (act(), None)[1])
        forward_step(
            step, i.lens, x_tile, o.gain.at[0:1], pack, o.bin, o.ba, o.chan,
            n1, bx, by, conv, gi, ra, h, ob_tile, *steps_scratch,
        )
        ob[pl.ds(pl.multiple_of(step * rows, rows), rows), :] = ob_tile[...]

    part = pl.BlockSpec((rows, width), lambda t: (t, 0))
    across = pl.BlockSpec((rows, model), lambda t: (t, 0))
    pltpu.emit_pipeline(
        channels,
        grid=(count,),
        in_specs=[across],
        out_specs=[across] + [part] * 7,
    )(o.x_all, o.n1, o.bx, o.by, o.conv, o.gi, o.ra, o.h, o.ob)
    line.landed(out_at)
    load(o.out4, out_w, 1).wait()
    plane.spread(line.tick)
    line.tick()
    plane_c.finish()
    line.tick()
    plane.finish(summed)

    def norm(t, carry):
        at = pl.ds(pl.multiple_of(t * 32, 32), 32)
        value = inputs[at, :].astype(SINGLE) + summed[at, :]
        scale = lax.rsqrt(jnp.mean(value * value, axis=-1, keepdims=True) + EPS)
        summed[at, :] = value
        n2_own[at, :] = (value * scale * o.gain[1:2, :]).astype(HALF)
        return carry

    lax.fori_loop(0, rows // 32, norm, 0)
    plane_n.start()
    stores = [pltpu.make_async_copy(summed, o.residual, store_sem)]
    stores[0].start()
    line.tick(2)
    plane_n.level(1)
    line.tick()
    plane_n.level(2)
    line.tick()
    plane_n.finish()
    line.landed(gate_at)
    line.landed(up_at)
    loads = [load(o.gate4, gate, 0), load(o.up4, up, 1)]
    for copy in loads:
        copy.wait()

    units = hidden.shape[1]
    thirds = [down_at[j : j + 2] for j in range(0, len(down_at), 2)]
    third = units // len(thirds)
    along = pl.BlockSpec((rows, units), lambda t: (t, 0))
    here = lambda: pl.ds(pl.multiple_of(pl.program_id(0) * rows, rows), rows)

    def blocks(left, right):
        value = None
        for d in range(parts):
            term = right(left[:, d * depth : (d + 1) * depth], d)
            value = term if value is None else value + term
        return value

    def activations(n2, act_tile, hidden_tile):
        for when in (3, 6):
            pl.when(pl.program_id(0) == when)(line.tick)
        value, rise = gelu_both(blocks(n2, lambda v, d: dot_nn(v, gate[d])))
        act_tile[...] = value
        above = blocks(n2, lambda v, d: dot_nn(v, up[d]))
        low = (value * above).astype(HALF)
        hidden_tile[...] = low
        hidden[here(), :] = low
        slope[here(), :] = rise * above

    pltpu.emit_pipeline(
        activations, grid=(count,), in_specs=[across], out_specs=[along, along]
    )(o.n2_all, o.act, o.hidden)
    beside_products([(o.c_all, hidden, o.grad_down)])
    line.tick()

    def gradients(act, total):
        for p, pieces in enumerate(thirds):
            if p:
                line.tick(pieces[-1] + 1 - line.done)
            span = pl.ds(p * third, third)
            act_load = load(o.act.at[:, span], act, 1)
            line.landed(pieces)
            load(o.down4.at[:, span], down.at[:, span], 0).wait()
            act_load.wait()

            def backs(c_tile, d_up_tile, d_gate_tile):
                d = pl.program_id(0)
                term = dot_nt(c_tile[...], down[d, span])

                @pl.when(d == 0)
                def _():
                    total[...] = term

                @pl.when(d > 0)
                def _():
                    total[...] += term

                @pl.when(d == parts - 1)
                def _():
                    def step(t, carry):
                        at = pl.ds(pl.multiple_of(t * 128, 128), 128)
                        back = total[at, :]
                        d_up_tile[at, :] = (back * act[at, :]).astype(HALF)
                        d_gate_tile[at, :] = (back * slope[at, span]).astype(HALF)
                        return carry

                    lax.fori_loop(0, tokens // 128, step, 0)

            piece = pl.BlockSpec((tokens, third), lambda d: (0, p))
            pltpu.emit_pipeline(
                backs,
                grid=(parts,),
                in_specs=[pl.BlockSpec((tokens, depth), lambda d: (0, d))],
                out_specs=[piece, piece],
            )(o.c_all, o.d_up, o.d_gate)

    pl.run_scoped(
        gradients, pltpu.VMEM((tokens, third), SINGLE), pltpu.VMEM((tokens, third), SINGLE)
    )
    line.settle()
    stores[0].wait()
    for copy in copies:
        copy.wait_send()


def forward_pass(lens, gains, x, cot, small, pack, out, down, gate, up, heads, bite, collective_id):
    parts, count = LineGather.COUNT, PlaneGather.COUNT
    rows, model = x.shape
    tokens = rows * count
    width, depth = out.shape
    units = down.shape[0]
    shape = jax.ShapeDtypeStruct
    four = lambda v: shape((parts,) + v.shape, HALF)
    plane_rows = shape((tokens, model), HALF)
    channel = shape((tokens, width), SINGLE)
    channel_low = shape((tokens, width), HALF)
    along = shape((tokens, units), HALF)
    square = shape((width, width), HALF)
    shapes = ForwardOut(
        gain=shape((8, model), SINGLE),
        bin=square,
        ba=square,
        chan=shape((16, width), SINGLE),
        x_all=plane_rows,
        c_all=plane_rows,
        n2_all=plane_rows,
        n1=plane_rows,
        residual=shape((rows, model), SINGLE),
        bx=channel_low,
        by=channel,
        conv=channel,
        gi=channel,
        ra=channel,
        h=channel,
        ob=channel_low,
        small4=four(small),
        pack4=four(pack),
        out4=four(out),
        gate4=four(gate),
        up4=four(up),
        down4=four(down),
        act=shape((tokens, units), SINGLE),
        hidden=along,
        d_up=along,
        d_gate=along,
        grad_down=shape((model, units), HALF),
    )
    in_vmem, in_hbm = pl.BlockSpec(memory_space=pltpu.VMEM), pl.BlockSpec(memory_space=pl.ANY)
    in_specs = ForwardIn(*[in_hbm] * len(ForwardIn._fields))._replace(
        lens=pl.BlockSpec(memory_space=pltpu.SMEM), gains=in_vmem
    )
    out_specs = ForwardOut(*[in_hbm] * len(shapes))._replace(
        gain=in_vmem, bin=in_vmem, ba=in_vmem, chan=in_vmem
    )
    inner, outer = lax.axis_size("mp"), lax.axis_size("dp")
    vmem = lambda v: pltpu.VMEM(v.shape, v.dtype)
    outs = pl.pallas_call(
        functools.partial(forward_pass_kernel, heads, bite),
        out_shape=list(shapes),
        in_specs=list(in_specs),
        out_specs=list(out_specs),
        scratch_shapes=[
            pltpu.VMEM((inner * outer,) + gains.shape, SINGLE),
            pltpu.VMEM((width, width), SINGLE),
            pltpu.VMEM((width, width), SINGLE),
        ]
        + [
            vmem(v) for v in (shapes.pack4, shapes.out4, shapes.down4, shapes.gate4, shapes.up4)
        ]
        + forward_scratch(rows, width)
        + [
            pltpu.VMEM((tokens, width), HALF),
            pltpu.VMEM((rows, model), HALF),
            pltpu.VMEM((rows, model), SINGLE),
            pltpu.VMEM((rows, model), HALF),
            pltpu.VMEM((tokens, units), SINGLE),
            pltpu.VMEM((tokens, units), HALF),
            pltpu.SemaphoreType.DMA((3,)),
            pltpu.SemaphoreType.DMA,
        ]
        + [pltpu.SemaphoreType.DMA((c,)) for c in (inner, inner, outer, outer)]
        + PlaneGather.scratch() * 3
        + PlaneSum.scratch(rows, model)
        + LineGather.scratch(sum(WEIGHT_PIECES)),
        compiler_params=kernel_params(collective_id),
        cost_estimate=pl.CostEstimate(
            flops=10 * tokens * model * units,
            bytes_accessed=40 * tokens * model,
            transcendentals=tokens * units,
        ),
        name="forward_pass",
    )(lens, gains, x, cot, small, pack, out, down, gate, up)
    return ForwardOut(*outs)


class BackwardIn(typing.NamedTuple):
    lens: typing.Any
    gain: typing.Any
    bin: typing.Any
    ba: typing.Any
    chan: typing.Any
    x: typing.Any
    cot: typing.Any
    residual: typing.Any
    n2_all: typing.Any
    n1: typing.Any
    bx: typing.Any
    by: typing.Any
    conv: typing.Any
    gi: typing.Any
    ra: typing.Any
    h: typing.Any
    ob: typing.Any
    hidden: typing.Any
    d_up: typing.Any
    d_gate: typing.Any
    grad_down: typing.Any
    out4: typing.Any
    pack4: typing.Any
    gate4: typing.Any
    up4: typing.Any
    down4: typing.Any


class BackwardOut(typing.NamedTuple):
    layer_output: typing.Any
    grad_input: typing.Any
    gain_grads: typing.Any
    dt_all: typing.Any
    grad_gate: typing.Any
    grad_up: typing.Any
    grad_out: typing.Any
    grad_pack: typing.Any
    landed_down: typing.Any
    landed_gate: typing.Any
    landed_up: typing.Any
    landed_out: typing.Any
    landed_pack: typing.Any
    landed_small: typing.Any
    sum_down: typing.Any
    sum_gate: typing.Any
    sum_up: typing.Any
    sum_out: typing.Any
    sum_pack: typing.Any
    sum_small: typing.Any


SUM_PIECES = (4, 4, 4, 2, 4, 1)


def small_gradients(small, gin, ga, gchan, chan, heads, bite):
    parts = LineSum.COUNT
    width = gin.shape[0]
    block = width // heads
    each = 2 * CONV // parts
    rows = small.shape[0] // parts
    at_row = lax.broadcasted_iota(jnp.int32, (block, width), 0)
    at_column = lax.broadcasted_iota(jnp.int32, (block, width), 1)
    small[...] = jnp.zeros_like(small)
    v = chan[2 * CONV - 1 : 2 * CONV, :]
    last = 2 * CONV - 1
    gchan[last : last + 1, :] = gchan[last : last + 1, :] * (DECAY * sigmoid(-v))
    for d in range(parts):
        for h in range(heads):
            place = (at_column == at_row + h * block).astype(HALF)
            first = h * block + d * bite
            to = d * rows + h * bite
            for lane, grads in ((0, gin), (256, ga)):
                piece = grads[first : first + bite, :].astype(HALF)
                small[to : to + bite, lane : lane + block] = dot_nt(piece, place)
        to = d * rows + heads * bite
        small[to : to + each, :width] = gchan[d * each : (d + 1) * each, :]


def backward_pass_kernel(heads, bite, *refs):
    refs = list(refs)
    take = lambda n: [refs.pop(0) for _ in range(n)]
    i = BackwardIn(*take(len(BackwardIn._fields)))
    o = BackwardOut(*take(len(BackwardOut._fields)))
    x, cot, residual, d_res, summed, dt_own, gain_sum = take(7)
    steps_scratch = take(4)
    gin, ga, gchan, small32, small = take(5)
    tiles, tiles_dp, tiles_mp = take(3)
    relays, others = take(6), take(6)
    load_sem, out_sem = take(2)
    total_sems = take(4)
    outward = [
        pltpu.make_async_copy(dt_own, o.layer_output, out_sem.at[0]),
        pltpu.make_async_copy(d_res, o.grad_input, out_sem.at[1]),
    ]
    plane_t = PlaneGather(dt_own, o.dt_all, take(3))
    shared = take(10)
    (free_sem,) = take(1)
    sources = (i.grad_down, o.grad_gate, o.grad_up, o.grad_out, o.grad_pack, small)
    landed = (
        o.landed_down, o.landed_gate, o.landed_up, o.landed_out, o.landed_pack, o.landed_small,
    )
    targets = (o.sum_down, o.sum_gate, o.sum_up, o.sum_out, o.sum_pack, o.sum_small)
    line = LineSum(list(zip(sources, landed, targets, SUM_PIECES, relays, others)), refs)
    tokens, model = o.dt_all.shape
    rows, width, units = x.shape[0], i.bx.shape[1], i.hidden.shape[1]
    count = PlaneGather.COUNT
    parts, _, depth = i.pack4.shape

    greet(ring_peers("mp") + ring_peers("dp"))
    line.begin(AHEAD)

    def load(pairs):
        copies = [
            pltpu.make_async_copy(source, target, load_sem.at[j])
            for j, (source, target) in enumerate(pairs)
        ]
        for copy in copies:
            copy.start()
        for copy in copies:
            copy.wait()

    def mlp(d_gate, d_up, gate, up):
        load(
            [
                (i.d_gate, d_gate), (i.gate4, gate), (i.d_up, d_up), (i.up4, up),
                (i.x, x), (i.cot, cot), (i.residual, residual),
            ]
        )
        by_rows = lambda left, right, t, columns: dot_nt(left, right[t])
        plane = PlaneSum([by_rows, by_rows], depth, [d_gate, d_up], [gate, up], shared)
        plane.spread(line.tick)

        def grads(n2_tile, gate_tile, up_tile):
            left = n2_tile[...]
            gate_tile[...] = dot_tn(left, d_gate[...]).astype(HALF)
            up_tile[...] = dot_tn(left, d_up[...]).astype(HALF)
            pl.when(pl.program_id(0) == 3)(line.tick)

        out_tile = pl.BlockSpec((256, units), lambda t: (t, 0))
        pltpu.emit_pipeline(
            grads,
            grid=(model // 256,),
            in_specs=[pl.BlockSpec((tokens, 256), lambda t: (0, t))],
            out_specs=[out_tile, out_tile],
        )(i.n2_all, o.grad_gate, o.grad_up)
        line.tick()
        plane.finish(summed)

    pl.run_scoped(
        mlp,
        pltpu.VMEM((tokens, units), HALF),
        pltpu.VMEM((tokens, units), HALF),
        pltpu.VMEM(i.gate4.shape, HALF),
        pltpu.VMEM(i.up4.shape, HALF),
    )
    gain_sum[...] = jnp.zeros_like(gain_sum)
    block = 32

    def norm_back(value, back, gain, row):
        scale = lax.rsqrt(jnp.mean(value * value, axis=-1, keepdims=True) + EPS)
        weighted = gain * back
        gain_sum[row : row + 1, :] += jnp.sum(back * value * scale, axis=0, keepdims=True)
        inner = jnp.mean(weighted * value, axis=-1, keepdims=True)
        return scale * weighted - value * (scale * scale * scale * inner)

    def middle(t, carry):
        at = pl.ds(pl.multiple_of(t * block, block), block)
        back = norm_back(residual[at, :], summed[at, :], i.gain[1:2, :], 1)
        back = cot[at, :].astype(SINGLE) + back
        d_res[at, :] = back
        dt_own[at, :] = back.astype(HALF)
        return carry

    lax.fori_loop(0, rows // block, middle, 0)
    plane_t.start()
    line.tick(2)
    plane_t.level(1)
    line.tick()
    plane_t.level(2)
    plane_t.finish()

    tall = pl.BlockSpec((tokens, depth), lambda t: (0, t))

    def out_gradients(ob):
        load([(i.ob, ob)])

        def body(dt_tile, out_tile):
            out_tile[...] = dot_tn(ob[...], dt_tile[...]).astype(HALF)

        pltpu.emit_pipeline(
            body,
            grid=(parts,),
            in_specs=[tall],
            out_specs=[pl.BlockSpec((width, depth), lambda t: (t, 0))],
        )(o.dt_all, o.grad_out)

    pl.run_scoped(out_gradients, pltpu.VMEM((tokens, width), HALF))
    line.tick()

    def temporal(hidden, down, out_w, d_bx, d_by):
        load([(i.hidden, hidden), (i.down4, down), (i.out4, out_w)])
        plane = PlaneSum([by_parts], depth, [hidden], [down], shared)

        def channels(dt_tile, bx, by, conv, gi, ra, h, before):
            step = pl.program_id(0)
            schedule = {
                0: lambda: (plane.send(3), plane.send(1)),
                1: lambda: (plane.take(3), plane.send(2), line.tick()),
                2: lambda: (plane.take(1), plane.send(0)),
                3: lambda: (plane.take(2), plane.take(0), line.tick()),
                5: lambda: (plane.relay(), line.tick()),
                7: line.tick,
            }
            for when, act in schedule.items():
                pl.when(step == when)(lambda act=act: (act(), None)[1])
            at = pl.ds(pl.multiple_of((count - 1 - step) * rows, rows), rows)
            backward_step(
                step, count, i.lens, dt_tile, out_w, i.bin, i.ba, i.chan,
                bx, by, conv, gi, ra, h, before, d_bx.at[at], d_by.at[at], gin, ga, gchan,
                *steps_scratch,
            )

        part = pl.BlockSpec((rows, width), lambda t: (count - 1 - t, 0))
        across = pl.BlockSpec((rows, model), lambda t: (count - 1 - t, 0))
        ahead = pl.BlockSpec(
            (8, width), lambda t: (jnp.maximum((count - 1 - t) * (rows // 8) - 1, 0), 0)
        )
        pltpu.emit_pipeline(
            channels, grid=(count,), in_specs=[across] + [part] * 6 + [ahead]
        )(o.dt_all, i.bx, i.by, i.conv, i.gi, i.ra, i.h, i.h)
        plane.finish(summed)
        for bit in plane_t.bits:
            pl.semaphore_signal(
                free_sem,
                inc=1,
                device_id={"mp": flip(lax.axis_index("mp"), bit, count)},
                device_id_type=MESH,
            )
        dt_own[...] = (residual[...] + summed[...]).astype(HALF)
        outward[0].start()
        small_gradients(small32, gin, ga, gchan, i.chan, heads, bite)
        small[...] = small32[...].astype(HALF)

    def block_input(pack, d_bx, d_by):
        pack_load = pltpu.make_async_copy(i.pack4, pack, load_sem.at[0])
        pack_load.start()

        def body(n1_tile, pack_tile):
            right = n1_tile[...]
            pack_tile[:width, :] = dot_tn(d_bx[...], right).astype(HALF)
            pack_tile[width:, :] = dot_tn(d_by[...], right).astype(HALF)

        pltpu.emit_pipeline(
            body,
            grid=(parts,),
            in_specs=[tall],
            out_specs=[pl.BlockSpec((2 * width, depth), lambda t: (t, 0))],
        )(i.n1, o.grad_pack)
        line.tick()
        pack_load.wait()
        plane = PlaneSum(
            [
                lambda left, right, t, columns: dot_nn(left, right[t, :width, :]),
                lambda left, right, t, columns: dot_nn(left, right[t, width:, :]),
            ],
            depth,
            [d_bx, d_by],
            [pack, pack],
            shared,
        )
        pl.semaphore_wait(free_sem, len(plane_t.bits))
        plane.spread(line.tick)
        line.tick()
        plane.finish(summed)

    def temporal_block(d_bx, d_by):
        pl.run_scoped(
            lambda hidden, down, out_w: temporal(hidden, down, out_w, d_bx, d_by),
            pltpu.VMEM((tokens, units), HALF),
            pltpu.VMEM(i.down4.shape, HALF),
            pltpu.VMEM(i.out4.shape, HALF),
        )
        pl.run_scoped(
            lambda pack: block_input(pack, d_bx, d_by), pltpu.VMEM(i.pack4.shape, HALF)
        )

    pl.run_scoped(
        temporal_block, pltpu.VMEM((tokens, width), HALF), pltpu.VMEM((tokens, width), HALF)
    )
    line.tick()

    def last(t, carry):
        at = pl.ds(pl.multiple_of(t * block, block), block)
        back = norm_back(x[at, :].astype(SINGLE), summed[at, :], i.gain[0:1, :], 0)
        d_res[at, :] = d_res[at, :] + back
        return carry

    lax.fori_loop(0, rows // block, last, 0)
    outward[1].start()

    for j in range(tiles.shape[0]):
        tiles[j] = gain_sum[:, j * 128 : (j + 1) * 128]
    inner, outer = ring_peers("mp"), ring_peers("dp")
    level, me = lax.axis_index("dp"), lax.axis_index("mp")
    held = tiles.shape[0] // parts
    copies = exchange(
        outer,
        lambda k: tiles.at[pl.ds((level + k) % parts * held, held)],
        lambda k: tiles_dp.at[k],
        *total_sems[:2],
    )
    line.tick()
    for j in range(3):
        line.collect(j)
    for copy in copies:
        copy.wait_recv()
    first = level * held
    for k, _ in outer:
        tiles_dp[0] = (tiles[pl.ds(first, held)] if k == 1 else tiles_dp[0]) + tiles_dp[k]
    pair = count // held
    late = exchange(
        inner,
        lambda k: tiles_dp.at[0, (me + k) % count // pair],
        lambda k: tiles_mp.at[k],
        *total_sems[2:],
    )
    line.tick(len(line.of[3]) + len(line.of[4]) - 1 - (line.done - line.of[3][0]))
    line.collect(3)
    for copy in late:
        copy.wait_recv()
    value = tiles_dp[0, me // pair]
    for k, _ in inner:
        value = value + tiles_mp[k]
    o.gain_grads[...] = value
    line.tick(len(line.chunks) - line.done)
    line.collect(4)
    line.collect(5)
    line.settle()
    for copy in copies + late:
        copy.wait_send()
    for copy in outward:
        copy.wait()


def backward_pass(values, small_rows, heads, bite, collective_id):
    parts, count = LineSum.COUNT, PlaneGather.COUNT
    rows, model = values.x.shape
    tokens = rows * count
    width = values.bx.shape[1]
    units = values.hidden.shape[1]
    depth = values.pack4.shape[2]
    sizes = (
        (depth, units), (depth, units), (depth, units),
        (width, depth), (2 * width, depth), (small_rows, depth),
    )
    shape = jax.ShapeDtypeStruct
    outs = BackwardOut(
        shape((rows, model), HALF),
        shape((rows, model), SINGLE),
        shape((8, 128), SINGLE),
        shape((tokens, model), HALF),
        shape((model, units), HALF),
        shape((model, units), HALF),
        shape((parts * width, depth), HALF),
        shape((parts * 2 * width, depth), HALF),
        *[shape((parts,) + size, HALF) for size in sizes],
        *[shape(size, SINGLE) for size in sizes],
    )
    in_vmem, in_hbm = pl.BlockSpec(memory_space=pltpu.VMEM), pl.BlockSpec(memory_space=pl.ANY)
    in_specs = BackwardIn(*[in_hbm] * len(values))._replace(
        lens=pl.BlockSpec(memory_space=pltpu.SMEM),
        gain=in_vmem,
        bin=in_vmem,
        ba=in_vmem,
        chan=in_vmem,
    )
    out_specs = BackwardOut(*[in_hbm] * len(outs))._replace(gain_grads=in_vmem)
    inner, outer = lax.axis_size("mp"), lax.axis_size("dp")
    pieces = [
        (count, (size[0] // count, size[1])) for size, count in zip(sizes, SUM_PIECES)
    ]
    tile = (8, 128)
    results = pl.pallas_call(
        functools.partial(backward_pass_kernel, heads, bite),
        out_shape=list(outs),
        in_specs=list(in_specs),
        out_specs=list(out_specs),
        scratch_shapes=[
            pltpu.VMEM((rows, model), HALF),
            pltpu.VMEM((rows, model), HALF),
            pltpu.VMEM((rows, model), SINGLE),
            pltpu.VMEM((rows, model), SINGLE),
            pltpu.VMEM((rows, model), SINGLE),
            pltpu.VMEM((rows, model), HALF),
            pltpu.VMEM((8, model), SINGLE),
        ]
        + forward_scratch(rows, width)
        + [
            pltpu.VMEM((width, width), SINGLE),
            pltpu.VMEM((width, width), SINGLE),
            pltpu.VMEM((8, width), SINGLE),
            pltpu.VMEM((parts * small_rows, depth), SINGLE),
            pltpu.VMEM((parts * small_rows, depth), HALF),
            pltpu.VMEM((model // 128,) + tile, SINGLE),
            pltpu.VMEM((outer, model // 128 // parts) + tile, SINGLE),
            pltpu.VMEM((inner,) + tile, SINGLE),
        ]
        + [pltpu.VMEM((count,) + size, HALF) for count, size in pieces]
        + [pltpu.VMEM(size, HALF) for _, size in pieces]
        + [pltpu.SemaphoreType.DMA((7,)), pltpu.SemaphoreType.DMA((2,))]
        + [pltpu.SemaphoreType.DMA((c,)) for c in (outer, outer, inner, inner)]
        + PlaneGather.scratch()
        + PlaneSum.scratch(rows, model)
        + [pltpu.SemaphoreType.REGULAR]
        + LineSum.scratch(sum(SUM_PIECES)),
        compiler_params=kernel_params(collective_id),
        cost_estimate=pl.CostEstimate(
            flops=14 * tokens * model * units,
            bytes_accessed=40 * tokens * model,
            transcendentals=tokens * units,
        ),
        name="backward_pass",
    )(*values)
    return BackwardOut(*results)


def diagonal(blocks):
    count, size, _ = blocks.shape
    spread = blocks[:, :, None, :] * jnp.eye(count, dtype=blocks.dtype)[:, None, :, None]
    return spread.reshape(count * size, count * size)


def on_device(
    layer_input,
    cotangent,
    norm_in,
    norm_mid,
    w_rnn_in,
    w_rnn_gate,
    w_rnn_out,
    gate_in_blocks,
    gate_a_blocks,
    channel_params,
    w_mlp_gate,
    w_mlp_up,
    w_mlp_down,
    lengths,
):
    parts = lax.axis_size("dp")
    rows, model = layer_input.shape
    depth, width = w_rnn_in.shape
    heads, bite, block = gate_in_blocks.shape
    tokens = rows * lax.axis_size("mp")

    fused = lax.axis_size("mp") == PlaneGather.COUNT and parts == LineGather.COUNT
    small_rows = -(-(heads * bite + 2 * CONV // parts) // 16) * 16
    lane_a = 256 if fused else block

    def small_pack(blocks_in, blocks_a, channels):
        wide = lambda v, lanes: jnp.pad(v, ((0, 0), (0, lanes - v.shape[1])))
        v = jnp.concatenate(
            [
                wide(blocks_in.reshape(-1, block), lane_a),
                wide(blocks_a.reshape(-1, block), small_lanes - lane_a),
            ],
            axis=1,
        )
        v = jnp.concatenate([v, wide(channels, small_lanes)], axis=0)
        return jnp.pad(v, ((0, small_rows - v.shape[0]), (0, 0)))

    small_lanes = 512
    small_mine = small_pack(
        gate_in_blocks.astype(HALF), gate_a_blocks.astype(HALF), channel_params.astype(HALF)
    )
    mine = jnp.concatenate([w_rnn_in.astype(HALF).T, w_rnn_gate.astype(HALF).T], axis=0)
    out_mine, down_mine = w_rnn_out.astype(HALF), w_mlp_down.astype(HALF)
    gate_mine, up_mine = w_mlp_gate.astype(HALF), w_mlp_up.astype(HALF)
    bite_gain = norm_in.shape[0]
    gains = jnp.stack([norm_in, norm_mid]).astype(HALF).astype(SINGLE)
    if fused:
        group = 128 // bite_gain
        spot = (lax.axis_index("mp") % group) * bite_gain
        gains = lax.dynamic_update_slice(jnp.zeros((8, 128), SINGLE), gains, (0, spot))
        o = forward_pass(
            lengths, gains, layer_input, cotangent, small_mine, mine, out_mine,
            down_mine, gate_mine, up_mine, heads, bite, 0,
        )
        known = BackwardIn(
            lengths, o.gain, o.bin, o.ba, o.chan, layer_input, cotangent, o.residual, o.n2_all,
            o.n1, o.bx, o.by, o.conv, o.gi, o.ra, o.h, o.ob, o.hidden, o.d_up, o.d_gate,
            o.grad_down, o.out4, o.pack4, o.gate4, o.up4, o.down4,
        )
        o = backward_pass(known, small_rows, heads, bite, 1)
        gain_grads = lax.dynamic_slice(o.gain_grads, (0, spot), (2, bite_gain))
        layer_output, grad_input = o.layer_output, o.grad_input
        grad_in, grad_side = o.sum_pack[:width], o.sum_pack[width:]
        grad_out, small_grads = o.sum_out, o.sum_small
        grad_gate, grad_up, grad_down = o.sum_gate, o.sum_up, o.sum_down
    else:
        inputs = layer_input.astype(SINGLE)
        over = lambda v: lax.all_gather(v, "dp", axis=0, tiled=False)
        gains = lax.all_gather(gains, ("dp", "mp"), axis=0, tiled=False)
        gain_first = gains[:, 0].reshape(1, model)
        gain_second = gains[:, 1].reshape(1, model)
        small, pack, out_w = over(small_mine), over(mine), over(out_mine)
        down, gate_w, up_w = over(down_mine), over(gate_mine), over(up_mine)
        whole_block = lambda v: diagonal(
            v.reshape(parts, heads, bite, block)
            .transpose(1, 0, 2, 3)
            .reshape(heads, block, block)
        )
        blocks_in = whole_block(small[:, : heads * bite, :block])
        blocks_a = whole_block(small[:, : heads * bite, lane_a : lane_a + block])
        channel = small[:, heads * bite : heads * bite + 2 * CONV // parts, :width]
        channel = channel.reshape(2 * CONV, width).astype(SINGLE)
        soft = jax.nn.softplus(-channel[2 * CONV - 1 :])
        chan = jnp.concatenate([channel, soft, jnp.zeros((7, width), SINGLE)], axis=0)
        x_all = lax.all_gather(layer_input, "mp", axis=0, tiled=True)
        c_all = lax.all_gather(cotangent, "mp", axis=0, tiled=True)
        n1, bx, by, conv, gate_in, gate_a, h, ob = forward_channels(
            lengths, x_all, gain_first, pack, blocks_in, blocks_a, chan
        )
        saved = (bx, by, conv, gate_in, gate_a, h, ob, n1)
        out = jnp.einsum("tc,dcm->tdm", ob, out_w, preferred_element_type=SINGLE)
        residual = inputs + lax.psum_scatter(
            out.reshape(tokens, model).astype(HALF), "mp", scatter_dimension=0, tiled=True
        ).astype(SINGLE)
        scale = lax.rsqrt(jnp.mean(residual * residual, axis=-1, keepdims=True) + EPS)
        normed_mid = (residual * scale * gain_second).astype(HALF)
        n2 = lax.all_gather(normed_mid, "mp", axis=0, tiled=True)
        d_hidden = dot_nt(c_all, down.transpose(1, 0, 2).reshape(-1, model))
        act, slope = gelu_both(dot_nn(n2, gate_w.reshape(model, -1)))
        d_up = (d_hidden * act).astype(HALF)
        up_pre = dot_nn(n2, up_w.reshape(model, -1))
        hidden = (act * up_pre).astype(HALF)
        d_gate = (d_hidden * up_pre * slope).astype(HALF)
        gate_w, up_w = gate_w.reshape(model, -1), up_w.reshape(model, -1)
        over_dp = lambda value: lax.psum_scatter(
            value.astype(HALF), "dp", scatter_dimension=0, tiled=True
        ).astype(SINGLE)
        over_mp = lambda value: lax.psum_scatter(
            value.astype(HALF), "mp", scatter_dimension=0, tiled=True
        ).astype(SINGLE)
        grad_down = over_dp(dot_tn(c_all, hidden))
        grad_gate, grad_up = over_dp(dot_tn(n2, d_gate)), over_dp(dot_tn(n2, d_up))
        layer_output = residual + over_mp(
            dot_nn(hidden, down.transpose(1, 0, 2).reshape(-1, model))
        )
        layer_output = layer_output.astype(HALF)
        back = over_mp(dot_nt(d_gate, gate_w) + dot_nt(d_up, up_w))
        weighted = gain_second * back
        gain_mid = jnp.sum(back * residual * scale, axis=0)
        d_residual = (
            cotangent.astype(SINGLE)
            + scale * weighted
            - residual * scale**3 * jnp.mean(weighted * residual, axis=-1, keepdims=True)
        )
        dt_all = lax.all_gather(d_residual.astype(HALF), "mp", axis=0, tiled=True)
        d_bx, d_by, gin, ga, gchan, rnn_grads = backward_channels(
            lengths, dt_all, out_w, blocks_in, blocks_a, chan, saved
        )
        back = over_mp(
            jnp.einsum(
                "tc,dcm->tdm",
                jnp.concatenate([d_bx, d_by], axis=1),
                pack,
                preferred_element_type=SINGLE,
            ).reshape(tokens, model)
        )
        own = lambda full: jnp.stack(
            [full[j * block : (j + 1) * block, j * block : (j + 1) * block] for j in range(heads)]
        )
        decay_row = DECAY * jax.nn.sigmoid(-channel[2 * CONV - 1 :]) * gchan[2 * CONV - 1 :]
        grad_channel = jnp.concatenate([gchan[: 2 * CONV - 1], decay_row], axis=0)
        split = lambda v: v.reshape(heads, parts, bite, block).transpose(1, 0, 2, 3)
        small_grads = jax.vmap(small_pack)(
            split(own(gin)), split(own(ga)), grad_channel.reshape(parts, -1, width)
        )
        small_grads = over_dp(small_grads)[0]
        rnn_grads = over_dp(rnn_grads)[0]
        grad_in, grad_side, grad_out = jnp.split(rnn_grads, 3, axis=0)
        scale = lax.rsqrt(jnp.mean(inputs * inputs, axis=-1, keepdims=True) + EPS)
        weighted = gain_first * back
        gain_in = jnp.sum(back * inputs * scale, axis=0)
        grad_input = (
            d_residual
            + scale * weighted
            - inputs * scale**3 * jnp.mean(weighted * inputs, axis=-1, keepdims=True)
        )
        gain_grads = lax.psum_scatter(
            jnp.stack([gain_in, gain_mid]), ("dp", "mp"), scatter_dimension=1, tiled=True
        )
    gate_rows = small_grads[: heads * bite]
    return (
        layer_output,
        grad_input,
        gain_grads[0],
        gain_grads[1],
        grad_in.T,
        grad_side.T,
        grad_out,
        gate_rows[:, :block].reshape(heads, bite, block),
        gate_rows[:, lane_a : lane_a + block].reshape(heads, bite, block),
        small_grads[heads * bite : heads * bite + 2 * CONV // parts, :width],
        grad_gate,
        grad_up,
        grad_down.T,
    )


def solution(mesh):
    rows = P(("dp", "mp"), None)
    return jax.shard_map(
        on_device,
        mesh=mesh,
        in_specs=(
            rows,
            rows,
            P(("dp", "mp")),
            P(("dp", "mp")),
            P("dp", "mp"),
            P("dp", "mp"),
            P("mp", "dp"),
            P("mp", "dp", None),
            P("mp", "dp", None),
            P("dp", "mp"),
            P("dp", "mp"),
            P("dp", "mp"),
            P("mp", "dp"),
            P("dp", None),
        ),
        out_specs=(
            rows,
            rows,
            P(("dp", "mp")),
            P(("dp", "mp")),
            P("dp", "mp"),
            P("dp", "mp"),
            P("mp", "dp"),
            P("mp", "dp", None),
            P("mp", "dp", None),
            P("dp", "mp"),
            P("dp", "mp"),
            P("dp", "mp"),
            P("mp", "dp"),
        ),
        check_vma=False,
    )
```

```python
import functools
import typing

import jax
import jax.numpy as jnp
from jax import lax
from jax.experimental import pallas as pl
from jax.experimental.pallas import tpu as pltpu
from jax.sharding import PartitionSpec as P

CONV = 4
AHEAD = 3
SUM_AHEAD = 3
EPS = 1e-06
DECAY = 8.0
HALF = jnp.bfloat16
SINGLE = jnp.float32
MESH = pl.DeviceIdType.MESH
VMEM_BYTES = 60 * 1024 * 1024
GELU_C = 0.7978845608028654
GELU_K = 0.044715


def dot_nn(left, right):
    return lax.dot_general(
        left, right, (((1,), (0,)), ((), ())), preferred_element_type=SINGLE
    )


def dot_nt(left, right):
    return lax.dot_general(
        left, right, (((1,), (1,)), ((), ())), preferred_element_type=SINGLE
    )


def dot_tn(left, right):
    return lax.dot_general(
        left, right, (((0,), (0,)), ((), ())), preferred_element_type=SINGLE
    )


def gelu(v):
    return 0.5 * v * (1.0 + jnp.tanh(GELU_C * (v + GELU_K * v * v * v)))


def gelu_both(v):
    square = v * v
    t = jnp.tanh(GELU_C * (v + GELU_K * v * square))
    value = 0.5 * v * (1.0 + t)
    slope = 0.5 * (1.0 + t) + 0.5 * v * (1.0 - t * t) * (GELU_C * (1.0 + 3.0 * GELU_K * square))
    return value, slope


def flip(me, mask, count):
    place = me
    bit = 1
    while bit < count:
        if mask & bit:
            place = place + (1 - 2 * ((me // bit) % 2)) * bit
        bit *= 2
    return place


def ring_peers(axis):
    me, count = lax.axis_index(axis), lax.axis_size(axis)
    return [(k, {axis: (me + k) % count}) for k in range(1, count)]


def greet(peers):
    barrier = pltpu.get_barrier_semaphore()
    for _, peer in peers:
        pl.semaphore_signal(barrier, inc=1, device_id=peer, device_id_type=MESH)
    pl.semaphore_wait(barrier, len(peers))


def exchange(peers, source, target, send, recv):
    return [
        pltpu.make_async_remote_copy(
            src_ref=source(k),
            dst_ref=target(k),
            send_sem=send.at[k],
            recv_sem=recv.at[k],
            device_id=peer,
            device_id_type=MESH,
        )
        for k, peer in peers
    ]


def each(copies, act):
    for copy in copies:
        act(copy)


START, LAND, SENT = (lambda c: c.start(), lambda c: c.wait_recv(), lambda c: c.wait_send())


def gather_plan(count):
    bits = [1 << b for b in range(count.bit_length() - 1)]
    outer = bits[1:]
    orders = (outer + bits[:1], outer[::-1] + bits[:1])
    sends = []
    for half, order in enumerate(orders):
        for stage, bit in enumerate(order):
            for pick in range(1 << stage):
                mask = sum(order[j] for j in range(stage) if pick >> j & 1)
                sends.append((bin(mask).count("1"), half, mask, bit))
    sends.sort(key=lambda s: s[0])
    return bits, [s[1:] for s in sends]


class PlaneGather:
    COUNT = 8

    @staticmethod
    def scratch():
        count = PlaneGather.COUNT
        return [
            pltpu.SemaphoreType.DMA,
            pltpu.SemaphoreType.DMA((2, count)),
            pltpu.SemaphoreType.DMA((2, count)),
        ]

    def __init__(self, x_ref, o_ref, scratch):
        self.x, self.o = x_ref, o_ref
        self.own_sem, self.send, self.recv = scratch
        self.me = lax.axis_index("mp")
        self.bits, self.plan = gather_plan(self.COUNT)

    def own(self):
        rows = self.x.shape[0]
        span = pl.ds(pl.multiple_of(self.me * rows, rows), rows)
        return pltpu.make_async_copy(self.x, self.o.at[span], self.own_sem)

    def copy(self, half, mask, bit):
        rows = self.x.shape[0] // 2
        slot = 2 * flip(self.me, mask, self.COUNT) + half
        span = pl.ds(pl.multiple_of(slot * rows, rows), rows)
        return pltpu.make_async_remote_copy(
            src_ref=self.o.at[span] if mask else self.x.at[pl.ds(half * rows, rows)],
            dst_ref=self.o.at[span],
            send_sem=self.send.at[half, mask | bit],
            recv_sem=self.recv.at[half, mask | bit],
            device_id={"mp": flip(self.me, bit, self.COUNT)},
            device_id_type=MESH,
        )

    def level(self, depth):
        landed = set()
        for half, mask, bit in self.plan:
            if bin(mask).count("1") != depth:
                continue
            if mask and (half, mask) not in landed:
                landed.add((half, mask))
                self.arrived(half, mask)
            self.copy(half, mask, bit).start()

    def arrived(self, half, mask):
        for other, before, bit in self.plan:
            if other == half and before | bit == mask:
                self.copy(half, before, bit).wait_recv()

    def start(self):
        self.own().start()
        self.level(0)

    def finish(self):
        waited = {(half, mask) for half, mask, _ in self.plan}
        for half, mask, bit in self.plan:
            if (half, mask | bit) not in waited:
                self.copy(half, mask, bit).wait_recv()
        for entry in self.plan:
            self.copy(*entry).wait_send()
        self.own().wait()


class LineGather:
    COUNT = 4
    ENDS = ((0, 3), (3, 0))

    @staticmethod
    def scratch(pieces):
        shapes = ((pieces, 4), (pieces, 4), (pieces,))
        return [pltpu.SemaphoreType.DMA(shape) for shape in shapes]

    def __init__(self, targets, pieces, scratch):
        self.chunks, self.of = [], []
        for target, count in zip(targets, pieces):
            rows = target.shape[1] // count
            first = len(self.chunks)
            self.chunks += [(target, pl.ds(p * rows, rows)) for p in range(count)]
            self.of.append(range(first, len(self.chunks)))
        self.send, self.recv, self.onward = scratch
        self.me = lax.axis_index("dp")

    def direct(self, c, to):
        target, span = self.chunks[c]
        return pltpu.make_async_remote_copy(
            src_ref=target.at[self.me, span],
            dst_ref=target.at[self.me, span],
            send_sem=self.send.at[c, to],
            recv_sem=self.recv.at[c, self.me],
            device_id={"dp": to},
            device_id_type=MESH,
        )

    def handed(self, c, block, to):
        target, span = self.chunks[c]
        return pltpu.make_async_remote_copy(
            src_ref=target.at[block, span],
            dst_ref=target.at[block, span],
            send_sem=self.onward.at[c],
            recv_sem=self.recv.at[c, block],
            device_id={"dp": to},
            device_id_type=MESH,
        )

    def sends_to(self, to):
        senders = [z for z in range(self.COUNT) if z != to and (z, to) not in self.ENDS]
        return functools.reduce(jnp.logical_or, [self.me == z for z in senders])

    def start(self, chunks):
        for c in chunks:
            for to in range(self.COUNT):
                pl.when(self.sends_to(to))(lambda c=c, to=to: self.direct(c, to).start())

    def hand_on(self, chunks):
        for c in chunks:
            for first, last in self.ENDS:
                middle = 2 if last == 3 else 1

                @pl.when(self.me == middle)
                def _(c=c, first=first, last=last):
                    copy = self.handed(c, first, last)
                    copy.wait_recv()
                    copy.start()

    def begin(self, ahead):
        self.ahead, self.done = ahead, 0
        self.start(range(ahead))

    def tick(self, count=1):
        for _ in range(count):
            self.hand_on([self.done])
            if self.done + self.ahead < len(self.chunks):
                self.start([self.done + self.ahead])
            self.done += 1

    def landed(self, chunks):
        for c in chunks:
            for block in range(self.COUNT):
                early = 2 if block == 0 else 1 if block == 3 else None
                waits = self.me != block
                if early is not None:
                    waits = jnp.logical_and(waits, self.me != early)
                pl.when(waits)(lambda c=c, block=block: self.handed(c, block, 0).wait_recv())

    def settle(self):
        for c in range(len(self.chunks)):
            for to in range(self.COUNT):
                pl.when(self.sends_to(to))(lambda c=c, to=to: self.direct(c, to).wait_send())
            pl.when(jnp.logical_or(self.me == 1, self.me == 2))(
                lambda c=c: self.handed(c, 0, 0).wait_send()
            )


def kernel_params(collective_id):
    return pltpu.CompilerParams(
        collective_id=collective_id, has_side_effects=True, vmem_limit_bytes=VMEM_BYTES
    )


def sharing(o_ref, sems):
    send_mp, recv_mp, send_dp, recv_dp = sems
    count = lax.axis_size("mp")
    first = lax.axis_index("dp") * count
    place = first + lax.axis_index("mp")
    mine = lambda k: o_ref.at[place]
    plane = lambda k: o_ref.at[pl.ds(first, count)]
    return (
        exchange(ring_peers("mp"), mine, mine, send_mp, recv_mp),
        exchange(ring_peers("dp"), plane, plane, send_dp, recv_dp),
    )


def beside_products(pairs):
    for left, right, out in pairs:
        tokens, rows = left.shape
        tile = min(256, rows)

        def body(left_tile, out_tile):
            out_tile[...] = dot_tn(left_tile[...], right[...]).astype(out_tile.dtype)

        pltpu.emit_pipeline(
            body,
            grid=(rows // tile,),
            in_specs=[pl.BlockSpec((tokens, tile), lambda i: (0, i))],
            out_specs=[pl.BlockSpec((tile, right.shape[1]), lambda i: (i, 0))],
        )(left, out)


class PlaneSum:
    COUNT = 8
    ORDER = (3, 1, 2, 0)
    LINKS = ((3, 0, 2), (3, 1, 1), (1, 1, 1), (2, 0, 2), (1, 0, 1), (2, 1, 2))

    @staticmethod
    def scratch(rows, width):
        middle = rows // 2
        return [
            pltpu.VMEM((rows, width), SINGLE),
            pltpu.VMEM((2, middle, width), SINGLE),
            pltpu.VMEM((2, rows, width), HALF),
            pltpu.VMEM((4, rows, width), HALF),
            pltpu.VMEM((6, middle, width), HALF),
            pltpu.VMEM((6, middle, width), HALF),
            pltpu.SemaphoreType.DMA((4,)),
            pltpu.SemaphoreType.DMA((4,)),
            pltpu.SemaphoreType.DMA((6,)),
            pltpu.SemaphoreType.DMA((6,)),
        ]

    def __init__(self, products, tile, lefts, rights, scratch):
        self.terms = list(zip(lefts, rights, products))
        self.tile = tile
        self.acc, self.side, self.core_out, self.core_in = scratch[:4]
        self.link_out, self.link_in = scratch[4:6]
        self.core_send, self.core_recv, self.link_send, self.link_recv = scratch[6:]
        self.rows, self.width = self.acc.shape
        self.halves = (slice(0, self.rows // 2), slice(self.rows // 2, self.rows))
        self.me = lax.axis_index("mp")

    def tiles(self, step):
        def body(t, carry):
            step(t, pl.ds(pl.multiple_of(t * self.tile, self.tile), self.tile))
            return carry

        lax.fori_loop(0, self.width // self.tile, body, 0)

    def partial(self, slot, t, columns):
        span = pl.ds(pl.multiple_of(slot * self.rows, self.rows), self.rows)
        value = None
        for left, right, product in self.terms:
            term = product(left[span, :], right, t, columns)
            value = term if value is None else value + term
        return value

    def core_copy(self, c):
        return pltpu.make_async_remote_copy(
            src_ref=self.core_out.at[self.ORDER.index(c) % 2],
            dst_ref=self.core_in.at[c],
            send_sem=self.core_send.at[c],
            recv_sem=self.core_recv.at[c],
            device_id={"mp": flip(self.me, 1, self.COUNT)},
            device_id_type=MESH,
        )

    def link_copy(self, index):
        return pltpu.make_async_remote_copy(
            src_ref=self.link_out.at[index],
            dst_ref=self.link_in.at[index],
            send_sem=self.link_send.at[index],
            recv_sem=self.link_recv.at[index],
            device_id={"mp": flip(self.me, 2 * self.LINKS[index][2], self.COUNT)},
            device_id_type=MESH,
        )

    def send(self, c):
        place = self.ORDER.index(c)
        if place >= 2:
            self.core_copy(self.ORDER[place - 2]).wait_send()
        slot = flip(self.me, 2 * c + 1, self.COUNT)

        def step(t, columns):
            self.core_out[place % 2, :, columns] = self.partial(slot, t, columns).astype(HALF)

        self.tiles(step)
        self.core_copy(c).start()

    def take(self, c):
        self.core_copy(c).wait_recv()
        slot = flip(self.me, 2 * c, self.COUNT)
        ways = [i for i in range(4) if self.LINKS[i][0] == c]
        kept = [h for h in (0, 1) if c and h not in [self.LINKS[i][1] for i in ways]]

        def step(t, columns):
            value = self.partial(slot, t, columns) + self.core_in[c, :, columns].astype(SINGLE)
            if c == 0:
                self.acc[:, columns] = value
            for i in ways:
                self.link_out[i, :, columns] = value[self.halves[self.LINKS[i][1]]].astype(HALF)
            for h in kept:
                self.side[h, :, columns] = value[self.halves[h]]

        self.tiles(step)
        for i in ways:
            self.link_copy(i).start()

    def spread(self, between=lambda: None):
        self.send(3)
        self.send(1)
        self.take(3)
        self.send(2)
        self.take(1)
        between()
        self.send(0)
        self.take(2)
        self.take(0)
        self.relay()

    def relay(self):
        for index, landed, half in ((4, 0, 0), (5, 1, 1)):
            self.link_copy(landed).wait_recv()

            def step(t, columns):
                value = self.side[half, :, columns]
                value = value + self.link_in[landed, :, columns].astype(SINGLE)
                self.link_out[index, :, columns] = value.astype(HALF)

            self.tiles(step)
            self.link_copy(index).start()

    def finish(self, out_ref):
        for index in (2, 3, 4, 5):
            self.link_copy(index).wait_recv()

        def step(t, columns):
            for half, (one, two) in enumerate(((3, 4), (2, 5))):
                value = self.acc[self.halves[half], columns]
                value = value + self.link_in[one, :, columns].astype(SINGLE)
                value = value + self.link_in[two, :, columns].astype(SINGLE)
                out_ref[self.halves[half], columns] = value

        self.tiles(step)
        for c in self.ORDER[2:]:
            self.core_copy(c).wait_send()
        for index in range(6):
            self.link_copy(index).wait_send()


class LineSum:
    COUNT = 4

    @staticmethod
    def scratch(pieces):
        shapes = ((pieces, 4), (pieces, 4), (pieces,), (pieces,))
        return [pltpu.SemaphoreType.DMA(shape) for shape in shapes] + [pltpu.SemaphoreType.DMA]

    def __init__(self, jobs, scratch):
        self.jobs, self.chunks, self.of = jobs, [], []
        for job in jobs:
            _, landed, _, pieces, _, _ = job
            rows = landed.shape[1] // pieces
            first = len(self.chunks)
            self.chunks += [(job, p, rows) for p in range(pieces)]
            self.of.append(range(first, len(self.chunks)))
        self.send, self.recv, self.relay_send, self.relay_recv, self.load_sem = scratch
        self.me = lax.axis_index("dp")

    def part(self, c, block):
        (source, landed, *_), p, rows = self.chunks[c]
        return source.at[pl.ds(pl.multiple_of(block * landed.shape[1] + p * rows, 16), rows)]

    def place(self, c, sender):
        (_, landed, *_), p, rows = self.chunks[c]
        return landed.at[sender, pl.ds(p * rows, rows)]

    def relay(self, c):
        (*_, relay, _), p, _ = self.chunks[c]
        return relay.at[p]

    def direct(self, c, to, source=None):
        return pltpu.make_async_remote_copy(
            src_ref=self.part(c, to) if source is None else source,
            dst_ref=self.place(c, self.me),
            send_sem=self.send.at[c, to],
            recv_sem=self.recv.at[c, self.me],
            device_id={"dp": to},
            device_id_type=MESH,
        )

    def by_middle(self, c, block, to):
        return pltpu.make_async_remote_copy(
            src_ref=self.part(c, block),
            dst_ref=self.relay(c),
            send_sem=self.relay_send.at[c],
            recv_sem=self.relay_recv.at[c],
            device_id={"dp": to},
            device_id_type=MESH,
        )

    def among(self, places):
        return functools.reduce(jnp.logical_or, [self.me == z for z in places])

    DIRECT = ((1,), (0, 2, 3), (0, 1, 3), (2,))
    ROUND = ((0, 3, 1), (3, 0, 2))

    def start(self, chunks):
        for c in chunks:
            for end, block, middle in self.ROUND:
                pl.when(self.me == end)(
                    lambda c=c, block=block, middle=middle: self.by_middle(c, block, middle).start()
                )
            for to, senders in enumerate(self.DIRECT):
                pl.when(self.among(senders))(lambda c=c, to=to: self.direct(c, to).start())

    def hand_on(self, chunks):
        for c in chunks:
            *_, other = self.chunks[c][0]
            for _, block, middle in self.ROUND:

                @pl.when(self.me == middle)
                def _(c=c, block=block, middle=middle, other=other):
                    mine = pltpu.make_async_copy(self.part(c, block), other, self.load_sem)
                    mine.start()
                    self.by_middle(c, block, middle).wait_recv()
                    mine.wait()
                    relay = self.relay(c)
                    value = relay[...].astype(SINGLE) + other[...].astype(SINGLE)
                    relay[...] = value.astype(HALF)
                    self.direct(c, block, relay).start()

    def begin(self, ahead):
        self.ahead, self.done = ahead, 0
        self.start(range(ahead))

    def tick(self, count=1):
        for _ in range(count):
            self.hand_on([self.done])
            if self.done + self.ahead < len(self.chunks):
                self.start([self.done + self.ahead])
            self.done += 1

    SENDERS = ((1, 2), (0, 2, 3), (0, 1, 3), (1, 2))

    def collect(self, j):
        source, landed, target, _, _, _ = self.jobs[j]
        turned = target.shape[-1] != landed.shape[-1]
        split = len(target.shape) == 3
        for c in self.of[j]:
            for sender in range(self.COUNT):
                takers = [z for z in range(self.COUNT) if sender in self.SENDERS[z]]
                pl.when(self.among(takers))(
                    lambda c=c, sender=sender: self.wait_from(c, sender)
                )
        _, rows, columns = landed.shape
        tile = rows // 2 if rows >= 256 else rows
        out_spec = pl.BlockSpec((tile, columns), lambda t: (t, 0))
        if split:
            shape = (1, columns, tile) if turned else (1, tile, columns)
            out_spec = pl.BlockSpec(shape, lambda t: (t, 0, 0))

        def add(*refs):
            value = refs[0][...].astype(SINGLE)
            for ref in refs[1:-1]:
                value = value + ref[0].astype(SINGLE)
            if split:
                refs[-1][0] = value.T if turned else value
            else:
                refs[-1][...] = value

        def run(senders):
            pltpu.emit_pipeline(
                add,
                grid=(rows // tile,),
                in_specs=[
                    pl.BlockSpec((tile, columns), lambda t: (self.me * (rows // tile) + t, 0))
                ]
                + [
                    pl.BlockSpec((1, tile, columns), lambda t, sender=sender: (sender, t, 0))
                    for sender in senders
                ],
                out_specs=[out_spec],
            )(source, *[landed] * len(senders), target)

        pl.when(self.among((0, 3)))(lambda: run((1, 2)))
        pl.when(self.among((1, 2)))(lambda: run((0, 3 - self.me, 3)))

    def wait_from(self, c, sender):
        pltpu.make_async_remote_copy(
            src_ref=self.place(c, sender),
            dst_ref=self.place(c, sender),
            send_sem=self.relay_send.at[c],
            recv_sem=self.recv.at[c, sender],
            device_id={"dp": 0},
            device_id_type=MESH,
        ).wait_recv()

    def settle(self):
        for c in range(len(self.chunks)):
            for to, senders in enumerate(self.DIRECT):
                pl.when(self.among(senders))(lambda c=c, to=to: self.direct(c, to).wait_send())
            for end, block, middle in self.ROUND:
                pl.when(self.me == end)(
                    lambda c=c, block=block, middle=middle: self.by_middle(
                        c, block, middle
                    ).wait_send()
                )
                pl.when(self.me == middle)(
                    lambda c=c, block=block: self.direct(c, block, self.relay(c)).wait_send()
                )


def positions(lens_ref, first, shape):
    place = lax.broadcasted_iota(jnp.int32, shape, 0) + first
    begin = jnp.zeros(shape, jnp.int32)
    total = 0
    for j in range(lens_ref.shape[1]):
        total = total + lens_ref[0, j]
        begin = jnp.where(place >= total, total, begin)
    return place - begin, place < total


def split_dot(dot, left, right):
    high = left.astype(HALF)
    low = (left - high.astype(SINGLE)).astype(HALF)
    return dot(high, right) + dot(low, right)


def lane_tiles(width):
    return [(t, t * 128, min(128, width - t * 128)) for t in range(-(-width // 128))]


def put_tiles(ref, value):
    for t, first, lanes in lane_tiles(value.shape[1]):
        ref[t, :, :lanes] = value[:, first : first + lanes]


def scan_start(tiles, lanes):
    return [(jnp.zeros((lanes, 128), SINGLE), jnp.ones((lanes, 128), SINGLE)) for _ in tiles]


def sigmoid(v):
    return 1.0 / (1.0 + jnp.exp(-v))


def forward_step(
    step,
    lens_ref,
    x_ref,
    gain_ref,
    pack_ref,
    bin_ref,
    ba_ref,
    chan_ref,
    n1_ref,
    bx_ref,
    by_ref,
    conv_ref,
    gi_ref,
    ra_ref,
    h_ref,
    ob_ref,
    taps,
    coef,
    drive,
    carry,
):
    rows, width = bx_ref.shape
    depth = pack_ref.shape[2]
    lanes = 8
    span = rows // lanes

    @pl.when(step == 0)
    def _():
        taps[...] = jnp.zeros_like(taps)
        carry[...] = jnp.zeros_like(carry)
        coef[...] = jnp.zeros_like(coef)
        drive[...] = jnp.zeros_like(drive)

    x = x_ref[...].astype(SINGLE)
    scale = lax.rsqrt(jnp.mean(x * x, axis=-1, keepdims=True) + EPS)
    normed = (x * scale * gain_ref[...]).astype(HALF)
    n1_ref[...] = normed
    total = None
    for d in range(pack_ref.shape[0]):
        term = dot_nt(normed[:, d * depth : (d + 1) * depth], pack_ref[d, : 2 * width, :])
        total = term if total is None else total + term
    bx = total[:, :width].astype(HALF)
    by = total[:, width:]
    bx_ref[...] = bx
    by_ref[...] = by
    pos, live = positions(lens_ref, step * rows, (rows, width))
    taps[0:8, :] = taps[rows : rows + 8, :]
    taps[8 : rows + 8, :] = bx.astype(SINGLE)
    conv = jnp.zeros((rows, width), SINGLE) + chan_ref[CONV : CONV + 1, :]
    for k in range(CONV):
        moved = taps[8 - k : 8 - k + rows, :]
        conv = conv + jnp.where(pos >= k, moved * chan_ref[k : k + 1, :], 0.0)
    conv_ref[...] = conv
    high = conv.astype(HALF)
    low = (conv - high.astype(SINGLE)).astype(HALF)
    gate_in = sigmoid(
        dot_nn(high, bin_ref[...]) + dot_nn(low, bin_ref[...]) + chan_ref[CONV + 1 : CONV + 2, :]
    )
    gate_a = sigmoid(
        dot_nn(high, ba_ref[...]) + dot_nn(low, ba_ref[...]) + chan_ref[CONV + 2 : CONV + 3, :]
    )
    gi_ref[...] = gate_in
    ra_ref[...] = gate_a
    decay = jnp.exp(-DECAY * gate_a * chan_ref[CONV + 4 : CONV + 5, :])
    root = jnp.sqrt(1.0 - decay * decay)
    put_tiles(coef, jnp.where(pos == 0, 0.0, decay))
    put_tiles(drive, gate_in * conv * root)
    tiles = lane_tiles(width)

    def scan(i, state):
        at = pl.ds(i, lanes, stride=span)
        result = []
        for (t, _, _), (h, prod) in zip(tiles, state):
            a = coef[t, at, :]
            h = a * h + drive[t, at, :]
            prod = prod * a
            drive[t, at, :] = h
            coef[t, at, :] = prod
            result.append((h, prod))
        return result

    state = lax.fori_loop(0, span, scan, scan_start(tiles, lanes), unroll=4)
    for (t, first, used), (h, prod) in zip(tiles, state):
        running = carry[t, 0:1, :]
        for s in range(lanes):
            at = slice(s * span, (s + 1) * span)
            value = drive[t, at, :] + coef[t, at, :] * running
            h_ref[at, first : first + used] = value[:, :used]
            running = h[s : s + 1, :] + prod[s : s + 1, :] * running
        carry[t, 0:1, :] = running
    mixed = h_ref[...].astype(HALF).astype(SINGLE)
    ob_ref[...] = jnp.where(live, gelu(by) * mixed, 0.0).astype(HALF)


def forward_kernel(*refs):
    forward_step(pl.program_id(0), *refs)


def forward_scratch(rows, width):
    tiles = len(lane_tiles(width))
    return [
        pltpu.VMEM((rows + 8, width), SINGLE),
        pltpu.VMEM((tiles, rows, 128), SINGLE),
        pltpu.VMEM((tiles, rows, 128), SINGLE),
        pltpu.VMEM((tiles, 8, 128), SINGLE),
    ]


def forward_channels(lens, x_all, gain, pack, blocks_in, blocks_a, chan):
    tokens, model = x_all.shape
    width = chan.shape[1]
    count = lax.axis_size("mp")
    rows = tokens // count
    whole = lambda shape: pl.BlockSpec(shape, lambda i: (0,) * len(shape))
    part = pl.BlockSpec((rows, width), lambda i: (i, 0))
    full = lambda kind: jax.ShapeDtypeStruct((tokens, width), kind)
    return pl.pallas_call(
        forward_kernel,
        grid=(count,),
        out_shape=(
            jax.ShapeDtypeStruct((tokens, model), HALF),
            full(HALF),
            full(SINGLE),
            full(SINGLE),
            full(SINGLE),
            full(SINGLE),
            full(SINGLE),
            full(HALF),
        ),
        in_specs=[
            pl.BlockSpec(memory_space=pltpu.SMEM),
            pl.BlockSpec((rows, model), lambda i: (i, 0)),
            whole(gain.shape),
            whole(pack.shape),
            whole(blocks_in.shape),
            whole(blocks_a.shape),
            whole(chan.shape),
        ],
        out_specs=(pl.BlockSpec((rows, model), lambda i: (i, 0)),) + (part,) * 7,
        scratch_shapes=forward_scratch(rows, width),
        compiler_params=pltpu.CompilerParams(vmem_limit_bytes=VMEM_BYTES),
        cost_estimate=pl.CostEstimate(
            flops=2 * tokens * model * 2 * width,
            bytes_accessed=tokens * (model * 4 + width * 24),
            transcendentals=8 * tokens * width,
        ),
        name="forward_channels",
    )(lens, x_all, gain, pack, blocks_in, blocks_a, chan)


def by_parts(left, right, t, columns):
    return dot_nn(left, right[t])


def backward_step(
    step,
    steps,
    lens_ref,
    dt_ref,
    pack_ref,
    bin_ref,
    ba_ref,
    chan_ref,
    bx_ref,
    by_ref,
    conv_ref,
    gi_ref,
    ra_ref,
    h_ref,
    hprev_ref,
    dbx_ref,
    dby_ref,
    gin_ref,
    ga_ref,
    gchan_ref,
    lift,
    coef,
    drive,
    carry,
):
    chunk = steps - 1 - step
    rows, width = bx_ref.shape
    depth = pack_ref.shape[2]
    lanes = 8
    span = rows // lanes

    @pl.when(step == 0)
    def _():
        lift[...] = jnp.zeros_like(lift)
        carry[...] = jnp.zeros_like(carry)
        coef[...] = jnp.zeros_like(coef)
        drive[...] = jnp.zeros_like(drive)
        gin_ref[...] = jnp.zeros_like(gin_ref)
        ga_ref[...] = jnp.zeros_like(ga_ref)
        gchan_ref[...] = jnp.zeros_like(gchan_ref)

    d_out = None
    for d in range(pack_ref.shape[0]):
        term = dot_nt(dt_ref[:, d * depth : (d + 1) * depth], pack_ref[d])
        d_out = term if d_out is None else d_out + term
    pos, live = positions(lens_ref, chunk * rows, (rows, width))
    by = by_ref[...]
    h = h_ref[...]
    side, slope = gelu_both(by)
    d_out = jnp.where(live, d_out, 0.0)
    dby_ref[...] = (d_out * h.astype(HALF).astype(SINGLE) * slope).astype(HALF)
    gate_a = ra_ref[...]
    soft = chan_ref[CONV + 4 : CONV + 5, :]
    decay = jnp.exp(-DECAY * gate_a * soft)
    put_tiles(coef, jnp.where(pos == 0, 0.0, decay))
    put_tiles(drive, (d_out * side).astype(HALF).astype(SINGLE))
    tiles = lane_tiles(width)

    def scan(j, state):
        at = pl.ds(span - 1 - j, lanes, stride=span)
        result = []
        for (t, _, _), (after, prod) in zip(tiles, state):
            a = coef[t, at, :]
            lam = drive[t, at, :] + after
            drive[t, at, :] = lam
            coef[t, at, :] = prod
            result.append((a * lam, prod * a))
        return result

    state = lax.fori_loop(0, span, scan, scan_start(tiles, lanes), unroll=4)
    for (t, first, used), (after, prod) in zip(tiles, state):
        running = carry[t, 0:1, :]
        for s in reversed(range(lanes)):
            at = slice(s * span, (s + 1) * span)
            value = drive[t, at, :] + coef[t, at, :] * running
            lift[at, first : first + used] = value[:, :used]
            running = after[s : s + 1, :] + prod[s : s + 1, :] * running
        carry[t, 0:1, :] = running
    lam = lift[0:rows, :]
    last = jnp.where(chunk > 0, hprev_ref[7:8, :], 0.0)
    before = jnp.concatenate([last, h[: rows - 1, :]], axis=0)
    before = jnp.where(pos == 0, 0.0, before)
    conv = conv_ref[...]
    gate_in = gi_ref[...]
    root = jnp.sqrt(1.0 - decay * decay)
    d_decay = lam * before - lam * gate_in * conv * decay / root
    d_log = d_decay * decay
    d_a = d_log * (-DECAY * soft)
    d_in = lam * conv * root
    d_logit_in = d_in * gate_in * (1.0 - gate_in)
    d_logit_a = d_a * gate_a * (1.0 - gate_a)
    d_conv = (
        lam * gate_in * root
        + split_dot(dot_nt, d_logit_in, bin_ref[...])
        + split_dot(dot_nt, d_logit_a, ba_ref[...])
    )
    low = conv.astype(HALF)
    gin_ref[...] += dot_tn(low, d_logit_in.astype(HALF))
    ga_ref[...] += dot_tn(low, d_logit_a.astype(HALF))
    lift[0:rows, :] = d_conv
    bx = bx_ref[...].astype(SINGLE)
    d_bx = jnp.zeros((rows, width), SINGLE)
    for k in range(CONV):
        if k:
            ahead, _ = positions(lens_ref, chunk * rows + k, (rows, width))
            moved = jnp.where(ahead >= k, lift[k : k + rows, :], 0.0)
        else:
            moved = d_conv
        d_bx = d_bx + moved * chan_ref[k : k + 1, :]
        gchan_ref[k : k + 1, :] += jnp.sum(moved * bx, axis=0, keepdims=True)
    dbx_ref[...] = d_bx.astype(HALF)
    lift[rows : rows + 8, :] = d_conv[0:8, :]
    sums = (d_conv, d_logit_in, d_logit_a, d_log * gate_a)
    for j, value in enumerate(sums):
        gchan_ref[CONV + j : CONV + j + 1, :] += jnp.sum(value, axis=0, keepdims=True)


def backward_kernel(*refs):
    refs = list(refs)
    inputs, (ob_ref, n1_ref), outputs, grads_ref, grads, scratch = (
        refs[:13], refs[13:15], refs[15:20], refs[20], refs[21], refs[22:],
    )
    step, steps = pl.program_id(0), pl.num_programs(0)

    @pl.when(step == 0)
    def _():
        grads[...] = jnp.zeros_like(grads)

    backward_step(step, steps, *inputs, *outputs, *scratch)
    dt_ref, (dbx_ref, dby_ref) = inputs[1], outputs[:2]
    width, depth = dbx_ref.shape[1], grads.shape[2]
    lefts = (dbx_ref[...], dby_ref[...], ob_ref[...])
    for d in range(grads.shape[0]):
        columns = slice(d * depth, (d + 1) * depth)
        rights = (n1_ref[:, columns], n1_ref[:, columns], dt_ref[:, columns])
        for j, (left, right) in enumerate(zip(lefts, rights)):
            grads[d, j * width : (j + 1) * width, :] += dot_tn(left, right)

    @pl.when(step == steps - 1)
    def _():
        grads_ref[...] = grads[...].astype(HALF)


def backward_channels(lens, dt_all, pack, blocks_in, blocks_a, chan, saved):
    bx, by, conv, gate_in, gate_a, h, ob, n1 = saved
    tokens, model = dt_all.shape
    width = chan.shape[1]
    count = lax.axis_size("mp")
    rows = tokens // count
    last = count - 1
    whole = lambda shape: pl.BlockSpec(shape, lambda i: (0,) * len(shape))
    part = pl.BlockSpec((rows, width), lambda i: (last - i, 0))
    across = pl.BlockSpec((rows, model), lambda i: (last - i, 0))
    before = pl.BlockSpec(
        (8, width), lambda i: (jnp.maximum((last - i) * (rows // 8) - 1, 0), 0)
    )
    full = jax.ShapeDtypeStruct((tokens, width), HALF)
    square = jax.ShapeDtypeStruct((width, width), SINGLE)
    grads = (pack.shape[0], 3 * width, pack.shape[2])
    return pl.pallas_call(
        backward_kernel,
        grid=(count,),
        out_shape=(
            full,
            full,
            square,
            square,
            jax.ShapeDtypeStruct((8, width), SINGLE),
            jax.ShapeDtypeStruct(grads, HALF),
        ),
        in_specs=[
            pl.BlockSpec(memory_space=pltpu.SMEM),
            across,
            whole(pack.shape),
            whole(blocks_in.shape),
            whole(blocks_a.shape),
            whole(chan.shape),
            part,
            part,
            part,
            part,
            part,
            part,
            before,
            part,
            across,
        ],
        out_specs=(
            part,
            part,
            whole((width, width)),
            whole((width, width)),
            whole((8, width)),
            whole(grads),
        ),
        scratch_shapes=[pltpu.VMEM(grads, SINGLE)] + forward_scratch(rows, width),
        compiler_params=pltpu.CompilerParams(vmem_limit_bytes=VMEM_BYTES),
        cost_estimate=pl.CostEstimate(
            flops=8 * tokens * model * width,
            bytes_accessed=tokens * (model * 4 + width * 28),
            transcendentals=8 * tokens * width,
        ),
        name="backward_channels",
    )(
        lens, dt_all, pack, blocks_in, blocks_a, chan,
        bx, by, conv, gate_in, gate_a, h, h, ob, n1,
    )


def log_one_plus(v):
    total = 1.0 + v
    exact = total - 1.0
    return jnp.where(exact == 0.0, v, jnp.log(total) * (v / jnp.where(exact == 0.0, 1.0, exact)))


def small_weights(small, bin_ref, ba_ref, chan_ref, heads, bite):
    parts = small.shape[0]
    width = bin_ref.shape[0]
    block = width // heads
    at_row = lax.broadcasted_iota(jnp.int32, (block, width), 0)
    at_column = lax.broadcasted_iota(jnp.int32, (block, width), 1)
    each = 2 * CONV // parts
    for d in range(parts):
        value = small[d].astype(SINGLE)
        for h in range(heads):
            place = (at_column == at_row + h * block).astype(HALF)
            for lane, target in ((0, bin_ref), (256, ba_ref)):
                piece = value[h * bite : (h + 1) * bite, lane : lane + block].astype(HALF)
                first = h * block + d * bite
                target[first : first + bite, :] = dot_nn(piece, place)
        row = heads * bite
        chan_ref[d * each : (d + 1) * each, :] = value[row : row + each, :width]
    v = -chan_ref[2 * CONV - 1 : 2 * CONV, :]
    chan_ref[2 * CONV : 2 * CONV + 1, :] = jnp.maximum(v, 0.0) + log_one_plus(
        jnp.exp(-jnp.abs(v))
    )


class LayerIn(typing.NamedTuple):
    lens: typing.Any
    norm_in: typing.Any
    norm_mid: typing.Any
    x: typing.Any
    cot: typing.Any
    blocks_in: typing.Any
    blocks_a: typing.Any
    channels: typing.Any
    w_in: typing.Any
    w_gate: typing.Any
    w_out: typing.Any
    gate: typing.Any
    up: typing.Any
    down: typing.Any


class LayerOut(typing.NamedTuple):
    layer_output: typing.Any
    grad_input: typing.Any
    gain_grads: typing.Any
    x_all: typing.Any
    c_all: typing.Any
    n2_all: typing.Any
    dt_all: typing.Any
    n1: typing.Any
    bx: typing.Any
    by: typing.Any
    conv: typing.Any
    gi: typing.Any
    ra: typing.Any
    h: typing.Any
    ob: typing.Any
    act: typing.Any
    slope: typing.Any
    grad_down: typing.Any
    grad_gate: typing.Any
    grad_up: typing.Any
    grad_out: typing.Any
    grad_pack: typing.Any
    pack4: typing.Any
    small4: typing.Any
    out4: typing.Any
    gate4: typing.Any
    up4: typing.Any
    down4: typing.Any
    landed_down: typing.Any
    landed_gate: typing.Any
    landed_up: typing.Any
    landed_out: typing.Any
    landed_pack: typing.Any
    landed_small: typing.Any
    sum_down: typing.Any
    sum_gate: typing.Any
    sum_up: typing.Any
    sum_out: typing.Any
    sum_pack: typing.Any
    sum_small: typing.Any


WEIGHT_PIECES = (4, 1, 2, 4, 4, 6)
SUM_PIECES = (4, 4, 4, 2, 4, 1)


def small_gradients(small, gin, ga, gchan, chan, heads, bite):
    parts = LineSum.COUNT
    width = gin.shape[0]
    block = width // heads
    each = 2 * CONV // parts
    rows = small.shape[0] // parts
    at_row = lax.broadcasted_iota(jnp.int32, (block, width), 0)
    at_column = lax.broadcasted_iota(jnp.int32, (block, width), 1)
    small[...] = jnp.zeros_like(small)
    v = chan[2 * CONV - 1 : 2 * CONV, :]
    last = 2 * CONV - 1
    gchan[last : last + 1, :] = gchan[last : last + 1, :] * (DECAY * sigmoid(-v))
    for d in range(parts):
        for h in range(heads):
            place = (at_column == at_row + h * block).astype(HALF)
            first = h * block + d * bite
            to = d * rows + h * bite
            for lane, grads in ((0, gin), (256, ga)):
                piece = grads[first : first + bite, :].astype(HALF)
                small[to : to + bite, lane : lane + block] = dot_nt(piece, place)
        to = d * rows + heads * bite
        small[to : to + each, :width] = gchan[d * each : (d + 1) * each, :]


def layer_kernel(*refs):
    refs = list(refs)
    take = lambda n: [refs.pop(0) for _ in range(n)]
    i = LayerIn(*take(len(LayerIn._fields)))
    o = LayerOut(*take(len(LayerOut._fields)))
    tiles, gain, gain_sum, bin_low, ba_low, chan = take(6)
    inputs, own_low, residual, d_res, summed = take(5)
    steps_scratch = take(4)
    gin, ga, gchan, small, turns, turns_dp, turns_mp = take(7)
    relays, others = take(6), take(3)
    load_sem, out_sem, free_sem = take(3)
    share_sems, total_sems = take(4), take(4)
    plane_x = PlaneGather(i.x, o.x_all, take(3))
    plane_c = PlaneGather(i.cot, o.c_all, take(3))
    plane_n = PlaneGather(own_low, o.n2_all, take(3))
    plane_t = PlaneGather(own_low, o.dt_all, take(3))
    shared = take(10)
    line = LineGather(
        (o.pack4, o.small4, o.out4, o.gate4, o.up4, o.down4), WEIGHT_PIECES, take(3)
    )
    pack_at, small_at, out_at, gate_at, up_at, down_at = line.of
    sources = (o.grad_down, o.grad_gate, o.grad_up, o.grad_out, o.grad_pack, small)
    landed = (
        o.landed_down, o.landed_gate, o.landed_up, o.landed_out, o.landed_pack, o.landed_small,
    )
    targets = (o.sum_down, o.sum_gate, o.sum_up, o.sum_out, o.sum_pack, o.sum_small)
    other = [others[j] for j in (0, 0, 0, 1, 1, 2)]
    sums = LineSum(list(zip(sources, landed, targets, SUM_PIECES, relays, other)), take(5))
    outward = [
        pltpu.make_async_copy(own_low, o.layer_output, out_sem.at[0]),
        pltpu.make_async_copy(d_res, o.grad_input, out_sem.at[1]),
    ]
    tokens, model = o.x_all.shape
    rows, count = i.x.shape[0], PlaneGather.COUNT
    width, units = o.bx.shape[1], o.act.shape[1]
    parts, _, depth = o.pack4.shape
    heads = width // i.blocks_in.shape[1]
    bite = i.blocks_in.shape[0] // heads
    level, me = lax.axis_index("dp"), lax.axis_index("mp")

    def copy_of(source, target, j):
        return pltpu.make_async_copy(source, target, load_sem.at[j])

    def load(pairs):
        copies = [copy_of(source, target, j) for j, (source, target) in enumerate(pairs)]
        for copy in copies:
            copy.start()
        for copy in copies:
            copy.wait()

    def stage(w_in, w_gate, w_out, gate, up, down, pack_low, out_low, gate_low, down_low, small_own):
        arrivals = [
            copy_of(source, target, j)
            for j, (source, target) in enumerate(
                (
                    (i.w_in, w_in), (i.w_gate, w_gate), (i.w_out, w_out), (i.gate, gate),
                    (i.up, up), (i.down, down), (i.x, inputs),
                )
            )
        ]
        for copy in arrivals:
            copy.start()
        greet(ring_peers("mp") + ring_peers("dp"))
        plane_x.start()
        for j, ref in enumerate((w_in, w_gate)):
            arrivals[j].wait()
            pack_low[j * width : (j + 1) * width, :] = ref[...].astype(HALF)
        load([(pack_low, o.pack4.at[level])])
        line.begin(AHEAD)
        tiles[level * count + me] = norm_tile()
        within, across_dp = sharing(tiles, share_sems)
        each(within, START)
        each(within, LAND)
        each(across_dp, START)
        small_own[...] = jnp.zeros_like(small_own)
        gate_rows, block = i.blocks_in.shape
        small_own[:gate_rows, :block] = i.blocks_in[...]
        small_own[:gate_rows, 256 : 256 + block] = i.blocks_a[...]
        small_own[gate_rows : gate_rows + i.channels.shape[0], :width] = i.channels[...]
        small[: small_own.shape[0], :] = small_own[...].astype(HALF)
        arrivals[2].wait()
        out_low[...] = w_out[...].astype(HALF)
        load([(small.at[: small_own.shape[0]], o.small4.at[level]), (out_low, o.out4.at[level])])
        for j, ref, low, target in (
            (3, gate, gate_low, o.gate4), (4, up, gate_low, o.up4), (5, down, down_low, o.down4),
        ):
            arrivals[j].wait()
            low[...] = ref[...].astype(HALF)
            load([(low, target.at[level])])
        arrivals[6].wait()

    def norm_tile():
        bits = i.norm_in.shape[1]
        spot = me % (128 // bits) * bits
        at_column = lax.broadcasted_iota(jnp.int32, (bits, 128), 1)
        place = lax.broadcasted_iota(jnp.int32, (bits, 128), 0) + spot == at_column
        both = jnp.concatenate(
            [i.norm_in[...], i.norm_mid[...], jnp.zeros((6, bits), SINGLE)], axis=0
        )
        return dot_nn(both.astype(HALF), place.astype(HALF))

    pl.run_scoped(
        stage,
        pltpu.VMEM(i.w_in.shape, SINGLE),
        pltpu.VMEM(i.w_gate.shape, SINGLE),
        pltpu.VMEM(i.w_out.shape, SINGLE),
        pltpu.VMEM(i.gate.shape, SINGLE),
        pltpu.VMEM(i.up.shape, SINGLE),
        pltpu.VMEM(i.down.shape, SINGLE),
        pltpu.VMEM(o.pack4.shape[1:], HALF),
        pltpu.VMEM(o.out4.shape[1:], HALF),
        pltpu.VMEM(o.gate4.shape[1:], HALF),
        pltpu.VMEM(o.down4.shape[1:], HALF),
        pltpu.VMEM(o.small4.shape[1:], SINGLE),
    )
    gin[...] = jnp.zeros_like(gin)
    ga[...] = jnp.zeros_like(ga)
    chan[...] = jnp.zeros_like(chan)
    line.tick()
    plane_x.level(1)
    line.tick()
    plane_x.level(2)
    line.tick()
    plane_x.finish()
    plane_c.start()
    within, across_dp = sharing(tiles, share_sems)
    each(across_dp, LAND)
    group = 128 // (model // tiles.shape[0])
    for j in range(model // 128):
        value = tiles[group * j]
        for k in range(1, group):
            value = value + tiles[group * j + k]
        gain[:, j * 128 : (j + 1) * 128] = value
    line.tick(2)
    line.landed(pack_at)
    line.landed(small_at)

    part = pl.BlockSpec((rows, width), lambda t: (t, 0))
    across = pl.BlockSpec((rows, model), lambda t: (t, 0))
    tall = pl.BlockSpec((tokens, depth), lambda t: (0, t))

    def temporal(pack, out_w, ob, small4):
        load([(o.pack4, pack), (o.small4, small4)])
        small_weights(small4, gin, ga, chan, heads, bite)
        bin_low[...] = gin[...].astype(HALF)
        ba_low[...] = ga[...].astype(HALF)

        def channels(x_tile, n1, bx, by, conv, gi, ra, h, ob_tile):
            step = pl.program_id(0)
            schedule = {
                2: line.tick,
                3: lambda: plane_c.level(1),
                4: line.tick,
                6: lambda: plane_c.level(2),
                7: line.tick,
            }
            for when, act in schedule.items():
                pl.when(step == when)(lambda act=act: (act(), None)[1])
            forward_step(
                step, i.lens, x_tile, gain.at[0:1], pack, bin_low, ba_low, chan,
                n1, bx, by, conv, gi, ra, h, ob_tile, *steps_scratch,
            )
            ob[pl.ds(pl.multiple_of(step * rows, rows), rows), :] = ob_tile[...]

        pltpu.emit_pipeline(
            channels,
            grid=(count,),
            in_specs=[across],
            out_specs=[across] + [part] * 7,
        )(o.x_all, o.n1, o.bx, o.by, o.conv, o.gi, o.ra, o.h, o.ob)
        line.landed(out_at)
        load([(o.out4, out_w)])
        plane = PlaneSum([by_parts], depth, [ob], [out_w], shared)
        plane.spread(line.tick)
        line.tick()
        plane_c.finish()
        line.tick()
        plane.finish(summed)

    pl.run_scoped(
        temporal,
        pltpu.VMEM(o.pack4.shape, HALF),
        pltpu.VMEM(o.out4.shape, HALF),
        pltpu.VMEM((tokens, width), HALF),
        pltpu.VMEM(o.small4.shape, HALF),
    )
    block = 32

    def norm(t, carry):
        at = pl.ds(pl.multiple_of(t * block, block), block)
        value = inputs[at, :].astype(SINGLE) + summed[at, :]
        scale = lax.rsqrt(jnp.mean(value * value, axis=-1, keepdims=True) + EPS)
        residual[at, :] = value
        own_low[at, :] = (value * scale * gain[1:2, :]).astype(HALF)
        return carry

    lax.fori_loop(0, rows // block, norm, 0)
    plane_n.start()
    line.tick(2)
    plane_n.level(1)
    line.tick()
    plane_n.level(2)
    line.tick()
    plane_n.finish()
    line.landed(gate_at)
    line.landed(up_at)

    def blocks(left, right):
        value = None
        for d in range(parts):
            term = right(left[:, d * depth : (d + 1) * depth], d)
            value = term if value is None else value + term
        return value

    def mlp(hidden, down, gate, up, d_up, d_gate):
        load([(o.gate4, gate), (o.up4, up), (i.cot, own_low)])
        thirds = [down_at[j : j + 2] for j in range(0, len(down_at), 2)]
        third = units // len(thirds)
        along = pl.BlockSpec((rows, units), lambda t: (t, 0))

        def activations(n2, act_tile, slope_tile):
            for when in (3, 6):
                pl.when(pl.program_id(0) == when)(line.tick)
            value, rise = gelu_both(blocks(n2, lambda v, d: dot_nn(v, gate[d])))
            act_tile[...] = value
            above = blocks(n2, lambda v, d: dot_nn(v, up[d]))
            at = pl.ds(pl.multiple_of(pl.program_id(0) * rows, rows), rows)
            hidden[at, :] = (value * above).astype(HALF)
            slope_tile[...] = rise * above

        pltpu.emit_pipeline(
            activations, grid=(count,), in_specs=[across], out_specs=[along, along]
        )(o.n2_all, o.act, o.slope)
        beside_products([(o.c_all, hidden, o.grad_down)])
        line.tick()
        whole, act_part, slope_part = summed, d_res, shared[0]

        for p, pieces in enumerate(thirds):
            if p:
                line.tick(pieces[-1] + 1 - line.done)
            if p == len(thirds) - 1:
                sums.begin(SUM_AHEAD)
            span = pl.ds(p * third, third)
            parts_in = []
            for t in range(count):
                at = pl.ds(t * rows, rows)
                columns = pl.ds(t * third, third)
                parts_in.append((o.act.at[at, span], act_part.at[:, columns]))
                parts_in.append((o.slope.at[at, span], slope_part.at[:, columns]))
            arrivals = [copy_of(a, b, 1 + j) for j, (a, b) in enumerate(parts_in)]
            for copy in arrivals:
                copy.start()
            line.landed(pieces)
            load([(o.down4.at[:, span], down.at[:, span])])
            for copy in arrivals:
                copy.wait()

            def backs(c_tile):
                d = pl.program_id(0)
                term = dot_nt(c_tile[...], down[d, span])
                pieces_of = [
                    (t, slice(t * rows, (t + 1) * rows), slice(t * third, (t + 1) * third))
                    for t in range(count)
                ]

                @pl.when(d == 0)
                def _():
                    for _, at, columns in pieces_of:
                        whole[:, columns] = term[at]

                @pl.when(d > 0)
                def _():
                    for _, at, columns in pieces_of:
                        whole[:, columns] += term[at]

                @pl.when(d == parts - 1)
                def _():
                    for _, at, columns in pieces_of:
                        back = whole[:, columns]
                        d_up[at, span] = (back * act_part[:, columns]).astype(HALF)
                        d_gate[at, span] = (back * slope_part[:, columns]).astype(HALF)

            pltpu.emit_pipeline(backs, grid=(parts,), in_specs=[tall])(o.c_all)

        by_rows = lambda left, right, t, columns: dot_nt(left, right[t])
        plane = PlaneSum([by_rows, by_rows], depth, [d_gate, d_up], [gate, up], shared)
        plane.spread(sums.tick)

        beside_products([(o.n2_all, d_gate, o.grad_gate)])
        sums.tick()
        beside_products([(o.n2_all, d_up, o.grad_up)])
        sums.tick()
        plane.finish(summed)

    gain_sum[...] = jnp.zeros_like(gain_sum)

    def norm_back(value, back, row):
        scale = lax.rsqrt(jnp.mean(value * value, axis=-1, keepdims=True) + EPS)
        weighted = gain[row : row + 1, :] * back
        gain_sum[row : row + 1, :] += jnp.sum(back * value * scale, axis=0, keepdims=True)
        inner = jnp.mean(weighted * value, axis=-1, keepdims=True)
        return scale * weighted - value * (scale * scale * scale * inner)

    def middle(t, carry):
        at = pl.ds(pl.multiple_of(t * block, block), block)
        back = norm_back(residual[at, :], summed[at, :], 1)
        back = own_low[at, :].astype(SINGLE) + back
        d_res[at, :] = back
        own_low[at, :] = back.astype(HALF)
        return carry

    def out_gradients(ob):
        load([(o.ob, ob)])

        def body(dt_tile, out_tile):
            out_tile[...] = dot_tn(ob[...], dt_tile[...]).astype(HALF)

        pltpu.emit_pipeline(
            body,
            grid=(parts,),
            in_specs=[tall],
            out_specs=[pl.BlockSpec((width, depth), lambda t: (t, 0))],
        )(o.dt_all, o.grad_out)

    def temporal_back(hidden, down, out_w, d_bx, d_by):
        load([(o.out4, out_w)])
        plane = PlaneSum([by_parts], depth, [hidden], [down], shared)

        def channels(dt_tile, bx, by, conv, gi, ra, h, before):
            step = pl.program_id(0)
            schedule = {
                0: lambda: (plane.send(3), plane.send(1)),
                1: lambda: (plane.take(3), plane.send(2), sums.tick()),
                2: lambda: (plane.take(1), plane.send(0)),
                3: lambda: (plane.take(2), plane.take(0), sums.tick()),
                5: lambda: (plane.relay(), sums.tick()),
                7: sums.tick,
            }
            for when, act in schedule.items():
                pl.when(step == when)(lambda act=act: (act(), None)[1])
            at = pl.ds(pl.multiple_of((count - 1 - step) * rows, rows), rows)
            backward_step(
                step, count, i.lens, dt_tile, out_w, bin_low, ba_low, chan,
                bx, by, conv, gi, ra, h, before, d_bx.at[at], d_by.at[at], gin, ga, gchan,
                *steps_scratch,
            )

        late = pl.BlockSpec((rows, width), lambda t: (count - 1 - t, 0))
        late_across = pl.BlockSpec((rows, model), lambda t: (count - 1 - t, 0))
        ahead = pl.BlockSpec(
            (8, width), lambda t: (jnp.maximum((count - 1 - t) * (rows // 8) - 1, 0), 0)
        )
        pltpu.emit_pipeline(
            channels, grid=(count,), in_specs=[late_across] + [late] * 6 + [ahead]
        )(o.dt_all, o.bx, o.by, o.conv, o.gi, o.ra, o.h, o.h)
        plane.finish(summed)
        for bit in plane_t.bits:
            pl.semaphore_signal(
                free_sem, inc=1, device_id={"mp": flip(me, bit, count)}, device_id_type=MESH
            )
        own_low[...] = (residual[...] + summed[...]).astype(HALF)
        outward[0].start()

    def block_input(pack, d_bx, d_by):
        pack_load = copy_of(o.pack4, pack, 0)
        pack_load.start()

        def body(n1_tile, pack_tile):
            right = n1_tile[...]
            pack_tile[:width, :] = dot_tn(d_bx[...], right).astype(HALF)
            pack_tile[width:, :] = dot_tn(d_by[...], right).astype(HALF)

        pltpu.emit_pipeline(
            body,
            grid=(parts,),
            in_specs=[tall],
            out_specs=[pl.BlockSpec((2 * width, depth), lambda t: (t, 0))],
        )(o.n1, o.grad_pack)
        sums.tick()
        pack_load.wait()
        plane = PlaneSum(
            [
                lambda left, right, t, columns: dot_nn(left, right[t, :width, :]),
                lambda left, right, t, columns: dot_nn(left, right[t, width:, :]),
            ],
            depth,
            [d_bx, d_by],
            [pack, pack],
            shared,
        )
        pl.semaphore_wait(free_sem, len(plane_t.bits))
        plane.spread(sums.tick)
        sums.tick()
        plane.finish(summed)

    def with_hidden(hidden, down):
        pl.run_scoped(
            lambda *more: mlp(hidden, down, *more),
            pltpu.VMEM(o.gate4.shape, HALF),
            pltpu.VMEM(o.up4.shape, HALF),
            pltpu.VMEM((tokens, units), HALF),
            pltpu.VMEM((tokens, units), HALF),
        )
        lax.fori_loop(0, rows // block, middle, 0)
        plane_t.start()
        sums.tick(2)
        plane_t.level(1)
        sums.tick()
        plane_t.level(2)
        plane_t.finish()
        pl.run_scoped(out_gradients, pltpu.VMEM((tokens, width), HALF))
        sums.tick()

        def with_gradients(d_bx, d_by):
            pl.run_scoped(
                lambda out_w: temporal_back(hidden, down, out_w, d_bx, d_by),
                pltpu.VMEM(o.out4.shape, HALF),
            )
            pl.run_scoped(
                lambda small32: (
                    small_gradients(small32, gin, ga, gchan, chan, heads, bite),
                    small.__setitem__(Ellipsis, small32[...].astype(HALF)),
                    None,
                )[2],
                pltpu.VMEM(small.shape, SINGLE),
            )
            pl.run_scoped(
                lambda pack: block_input(pack, d_bx, d_by), pltpu.VMEM(o.pack4.shape, HALF)
            )

        pl.run_scoped(
            with_gradients, pltpu.VMEM((tokens, width), HALF), pltpu.VMEM((tokens, width), HALF)
        )

    pl.run_scoped(
        with_hidden, pltpu.VMEM((tokens, units), HALF), pltpu.VMEM(o.down4.shape, HALF)
    )
    sums.tick()

    def last(t, carry):
        at = pl.ds(pl.multiple_of(t * block, block), block)
        back = norm_back(inputs[at, :].astype(SINGLE), summed[at, :], 0)
        d_res[at, :] = d_res[at, :] + back
        return carry

    lax.fori_loop(0, rows // block, last, 0)
    outward[1].start()

    for j in range(turns.shape[0]):
        turns[j] = gain_sum[:, j * 128 : (j + 1) * 128]
    inner, outer = ring_peers("mp"), ring_peers("dp")
    held = turns.shape[0] // parts
    early = exchange(
        outer,
        lambda k: turns.at[pl.ds((level + k) % parts * held, held)],
        lambda k: turns_dp.at[k],
        *total_sems[:2],
    )
    each(early, START)
    sums.tick()
    for j in range(3):
        sums.collect(j)
    each(early, LAND)
    first = level * held
    for k, _ in outer:
        turns_dp[0] = (turns[pl.ds(first, held)] if k == 1 else turns_dp[0]) + turns_dp[k]
    pair = count // held
    late = exchange(
        inner,
        lambda k: turns_dp.at[0, (me + k) % count // pair],
        lambda k: turns_mp.at[k],
        *total_sems[2:],
    )
    each(late, START)
    sums.tick(len(sums.of[3]) + len(sums.of[4]) - 1 - (sums.done - sums.of[3][0]))
    sums.collect(3)
    each(late, LAND)
    value = turns_dp[0, me // pair]
    for k, _ in inner:
        value = value + turns_mp[k]
    o.gain_grads[...] = value
    sums.tick(len(sums.chunks) - sums.done)
    sums.collect(4)
    sums.collect(5)
    line.settle()
    sums.settle()
    each(within + across_dp + early + late, SENT)
    for copy in outward:
        copy.wait()


def fused_layer(values, collective_id):
    parts, count = LineSum.COUNT, PlaneGather.COUNT
    rows, model = values.x.shape
    tokens = rows * count
    width, depth = values.w_in.shape
    units = values.gate.shape[1]
    small_rows = -(-(values.blocks_in.shape[0] + values.channels.shape[0]) // 16) * 16
    shape = jax.ShapeDtypeStruct
    plane_rows = shape((tokens, model), HALF)
    channel = shape((tokens, width), SINGLE)
    channel_low = shape((tokens, width), HALF)
    hidden_wide = shape((tokens, units), SINGLE)
    hidden_grads = shape((model, units), HALF)
    sizes = (
        (depth, units), (depth, units), (depth, units),
        (width, depth), (2 * width, depth), (small_rows, depth),
    )
    outs = LayerOut(
        shape((rows, model), HALF),
        shape((rows, model), SINGLE),
        shape((8, 128), SINGLE),
        *[plane_rows] * 5,
        channel_low,
        *[channel] * 5,
        channel_low,
        hidden_wide,
        hidden_wide,
        hidden_grads,
        hidden_grads,
        hidden_grads,
        shape((parts * width, depth), HALF),
        shape((parts * 2 * width, depth), HALF),
        shape((parts, 2 * width, depth), HALF),
        shape((parts, small_rows, depth), HALF),
        shape((parts, width, depth), HALF),
        shape((parts, depth, units), HALF),
        shape((parts, depth, units), HALF),
        shape((parts, units, depth), HALF),
        *[shape((parts,) + size, HALF) for size in sizes],
        *[shape(size, SINGLE) for size in sizes],
    )
    outs = outs._replace(
        sum_down=shape((2, units, depth // 2), SINGLE), sum_pack=shape((2, width, depth), SINGLE)
    )
    in_vmem, in_hbm = pl.BlockSpec(memory_space=pltpu.VMEM), pl.BlockSpec(memory_space=pl.ANY)
    in_specs = LayerIn(*[in_hbm] * len(values))._replace(
        lens=pl.BlockSpec(memory_space=pltpu.SMEM),
        norm_in=in_vmem,
        norm_mid=in_vmem,
        blocks_in=in_vmem,
        blocks_a=in_vmem,
        channels=in_vmem,
    )
    out_specs = LayerOut(*[in_hbm] * len(outs))._replace(gain_grads=in_vmem)
    inner, outer = lax.axis_size("mp"), lax.axis_size("dp")
    pieces = [(n, (size[0] // n, size[1])) for size, n in zip(sizes, SUM_PIECES)]
    tile = (8, 128)
    vmem, sem = pltpu.VMEM, pltpu.SemaphoreType.DMA
    results = pl.pallas_call(
        layer_kernel,
        out_shape=list(outs),
        in_specs=list(in_specs),
        out_specs=list(out_specs),
        scratch_shapes=[
            vmem((inner * outer,) + tile, SINGLE),
            vmem((8, model), SINGLE),
            vmem((8, model), SINGLE),
            vmem((width, width), HALF),
            vmem((width, width), HALF),
            vmem((16, width), SINGLE),
            vmem((rows, model), HALF),
            vmem((rows, model), HALF),
            vmem((rows, model), SINGLE),
            vmem((rows, model), SINGLE),
            vmem((rows, model), SINGLE),
        ]
        + forward_scratch(rows, width)
        + [
            vmem((width, width), SINGLE),
            vmem((width, width), SINGLE),
            vmem((8, width), SINGLE),
            vmem((parts * small_rows, depth), HALF),
            vmem((model // 128,) + tile, SINGLE),
            vmem((outer, model // 128 // parts) + tile, SINGLE),
            vmem((inner,) + tile, SINGLE),
        ]
        + [vmem((n,) + size, HALF) for n, size in pieces]
        + [vmem(pieces[j][1], HALF) for j in (0, 3, 5)]
        + [sem((1 + 2 * count,)), sem((2,)), pltpu.SemaphoreType.REGULAR]
        + [sem((c,)) for c in (inner, inner, outer, outer)]
        + [sem((c,)) for c in (outer, outer, inner, inner)]
        + PlaneGather.scratch() * 4
        + PlaneSum.scratch(rows, model)
        + LineGather.scratch(sum(WEIGHT_PIECES))
        + LineSum.scratch(sum(SUM_PIECES)),
        compiler_params=kernel_params(collective_id),
        cost_estimate=pl.CostEstimate(
            flops=24 * tokens * model * units,
            bytes_accessed=80 * tokens * model,
            transcendentals=2 * tokens * units,
        ),
        name="layer",
    )(*values)
    return LayerOut(*results)


def diagonal(blocks):
    count, size, _ = blocks.shape
    spread = blocks[:, :, None, :] * jnp.eye(count, dtype=blocks.dtype)[:, None, :, None]
    return spread.reshape(count * size, count * size)


def on_device(
    layer_input,
    cotangent,
    norm_in,
    norm_mid,
    w_rnn_in,
    w_rnn_gate,
    w_rnn_out,
    gate_in_blocks,
    gate_a_blocks,
    channel_params,
    w_mlp_gate,
    w_mlp_up,
    w_mlp_down,
    lengths,
):
    parts = lax.axis_size("dp")
    rows, model = layer_input.shape
    depth, width = w_rnn_in.shape
    heads, bite, block = gate_in_blocks.shape
    tokens = rows * lax.axis_size("mp")

    fused = lax.axis_size("mp") == PlaneGather.COUNT and parts == LineGather.COUNT
    small_rows = -(-(heads * bite + 2 * CONV // parts) // 16) * 16
    small_lanes = 512
    lane_a = 256 if fused else block

    def small_pack(blocks_in, blocks_a, channels):
        wide = lambda v, lanes: jnp.pad(v, ((0, 0), (0, lanes - v.shape[1])))
        v = jnp.concatenate(
            [
                wide(blocks_in.reshape(-1, block), lane_a),
                wide(blocks_a.reshape(-1, block), small_lanes - lane_a),
            ],
            axis=1,
        )
        v = jnp.concatenate([v, wide(channels, small_lanes)], axis=0)
        return jnp.pad(v, ((0, small_rows - v.shape[0]), (0, 0)))

    bite_gain = norm_in.shape[0]
    if fused:
        o = fused_layer(
            LayerIn(
                lengths, norm_in.reshape(1, -1), norm_mid.reshape(1, -1), layer_input, cotangent,
                gate_in_blocks.reshape(-1, block), gate_a_blocks.reshape(-1, block),
                channel_params, w_rnn_in.T, w_rnn_gate.T, w_rnn_out, w_mlp_gate, w_mlp_up, w_mlp_down,
            ),
            0,
        )
        spot = (lax.axis_index("mp") % (128 // bite_gain)) * bite_gain
        gain_grads = lax.dynamic_slice(o.gain_grads, (0, spot), (2, bite_gain))
        layer_output, grad_input = o.layer_output, o.grad_input
        grad_in, grad_side = o.sum_pack[0].T, o.sum_pack[1].T
        grad_out, small_grads = o.sum_out, o.sum_small
        grad_gate, grad_up = o.sum_gate, o.sum_up
        grad_down = jnp.concatenate([o.sum_down[0], o.sum_down[1]], axis=1)
    else:
        inputs = layer_input.astype(SINGLE)
        small_mine = small_pack(
            gate_in_blocks.astype(HALF), gate_a_blocks.astype(HALF), channel_params.astype(HALF)
        )
        mine = jnp.concatenate([w_rnn_in.astype(HALF).T, w_rnn_gate.astype(HALF).T], axis=0)
        out_mine, down_mine = w_rnn_out.astype(HALF), w_mlp_down.astype(HALF)
        gate_mine, up_mine = w_mlp_gate.astype(HALF), w_mlp_up.astype(HALF)
        gains = jnp.stack([norm_in, norm_mid]).astype(HALF).astype(SINGLE)
        over = lambda v: lax.all_gather(v, "dp", axis=0, tiled=False)
        gains = lax.all_gather(gains, ("dp", "mp"), axis=0, tiled=False)
        gain_first = gains[:, 0].reshape(1, model)
        gain_second = gains[:, 1].reshape(1, model)
        small, pack, out_w = over(small_mine), over(mine), over(out_mine)
        down, gate_w, up_w = over(down_mine), over(gate_mine), over(up_mine)
        whole_block = lambda v: diagonal(
            v.reshape(parts, heads, bite, block)
            .transpose(1, 0, 2, 3)
            .reshape(heads, block, block)
        )
        blocks_in = whole_block(small[:, : heads * bite, :block])
        blocks_a = whole_block(small[:, : heads * bite, lane_a : lane_a + block])
        channel = small[:, heads * bite : heads * bite + 2 * CONV // parts, :width]
        channel = channel.reshape(2 * CONV, width).astype(SINGLE)
        soft = jax.nn.softplus(-channel[2 * CONV - 1 :])
        chan = jnp.concatenate([channel, soft, jnp.zeros((7, width), SINGLE)], axis=0)
        x_all = lax.all_gather(layer_input, "mp", axis=0, tiled=True)
        c_all = lax.all_gather(cotangent, "mp", axis=0, tiled=True)
        n1, bx, by, conv, gate_in, gate_a, h, ob = forward_channels(
            lengths, x_all, gain_first, pack, blocks_in, blocks_a, chan
        )
        saved = (bx, by, conv, gate_in, gate_a, h, ob, n1)
        out = jnp.einsum("tc,dcm->tdm", ob, out_w, preferred_element_type=SINGLE)
        residual = inputs + lax.psum_scatter(
            out.reshape(tokens, model).astype(HALF), "mp", scatter_dimension=0, tiled=True
        ).astype(SINGLE)
        scale = lax.rsqrt(jnp.mean(residual * residual, axis=-1, keepdims=True) + EPS)
        normed_mid = (residual * scale * gain_second).astype(HALF)
        n2 = lax.all_gather(normed_mid, "mp", axis=0, tiled=True)
        d_hidden = dot_nt(c_all, down.transpose(1, 0, 2).reshape(-1, model))
        act, slope = gelu_both(dot_nn(n2, gate_w.reshape(model, -1)))
        d_up = (d_hidden * act).astype(HALF)
        up_pre = dot_nn(n2, up_w.reshape(model, -1))
        hidden = (act * up_pre).astype(HALF)
        d_gate = (d_hidden * up_pre * slope).astype(HALF)
        gate_w, up_w = gate_w.reshape(model, -1), up_w.reshape(model, -1)
        over_dp = lambda value: lax.psum_scatter(
            value.astype(HALF), "dp", scatter_dimension=0, tiled=True
        ).astype(SINGLE)
        over_mp = lambda value: lax.psum_scatter(
            value.astype(HALF), "mp", scatter_dimension=0, tiled=True
        ).astype(SINGLE)
        grad_down = over_dp(dot_tn(c_all, hidden))
        grad_gate, grad_up = over_dp(dot_tn(n2, d_gate)), over_dp(dot_tn(n2, d_up))
        layer_output = residual + over_mp(
            dot_nn(hidden, down.transpose(1, 0, 2).reshape(-1, model))
        )
        layer_output = layer_output.astype(HALF)
        back = over_mp(dot_nt(d_gate, gate_w) + dot_nt(d_up, up_w))
        weighted = gain_second * back
        gain_mid = jnp.sum(back * residual * scale, axis=0)
        d_residual = (
            cotangent.astype(SINGLE)
            + scale * weighted
            - residual * scale**3 * jnp.mean(weighted * residual, axis=-1, keepdims=True)
        )
        dt_all = lax.all_gather(d_residual.astype(HALF), "mp", axis=0, tiled=True)
        d_bx, d_by, gin, ga, gchan, rnn_grads = backward_channels(
            lengths, dt_all, out_w, blocks_in, blocks_a, chan, saved
        )
        back = over_mp(
            jnp.einsum(
                "tc,dcm->tdm",
                jnp.concatenate([d_bx, d_by], axis=1),
                pack,
                preferred_element_type=SINGLE,
            ).reshape(tokens, model)
        )
        own = lambda full: jnp.stack(
            [full[j * block : (j + 1) * block, j * block : (j + 1) * block] for j in range(heads)]
        )
        decay_row = DECAY * jax.nn.sigmoid(-channel[2 * CONV - 1 :]) * gchan[2 * CONV - 1 :]
        grad_channel = jnp.concatenate([gchan[: 2 * CONV - 1], decay_row], axis=0)
        split = lambda v: v.reshape(heads, parts, bite, block).transpose(1, 0, 2, 3)
        small_grads = jax.vmap(small_pack)(
            split(own(gin)), split(own(ga)), grad_channel.reshape(parts, -1, width)
        )
        small_grads = over_dp(small_grads)[0]
        rnn_grads = over_dp(rnn_grads)[0]
        grad_in, grad_side, grad_out = jnp.split(rnn_grads, 3, axis=0)
        grad_in, grad_side, grad_down = grad_in.T, grad_side.T, grad_down.T
        scale = lax.rsqrt(jnp.mean(inputs * inputs, axis=-1, keepdims=True) + EPS)
        weighted = gain_first * back
        gain_in = jnp.sum(back * inputs * scale, axis=0)
        grad_input = (
            d_residual
            + scale * weighted
            - inputs * scale**3 * jnp.mean(weighted * inputs, axis=-1, keepdims=True)
        )
        gain_grads = lax.psum_scatter(
            jnp.stack([gain_in, gain_mid]), ("dp", "mp"), scatter_dimension=1, tiled=True
        )
    gate_rows = small_grads[: heads * bite]
    return (
        layer_output,
        grad_input,
        gain_grads[0],
        gain_grads[1],
        grad_in,
        grad_side,
        grad_out,
        gate_rows[:, :block].reshape(heads, bite, block),
        gate_rows[:, lane_a : lane_a + block].reshape(heads, bite, block),
        small_grads[heads * bite : heads * bite + 2 * CONV // parts, :width],
        grad_gate,
        grad_up,
        grad_down,
    )


def solution(mesh):
    rows = P(("dp", "mp"), None)
    return jax.shard_map(
        on_device,
        mesh=mesh,
        in_specs=(
            rows,
            rows,
            P(("dp", "mp")),
            P(("dp", "mp")),
            P("dp", "mp"),
            P("dp", "mp"),
            P("mp", "dp"),
            P("mp", "dp", None),
            P("mp", "dp", None),
            P("dp", "mp"),
            P("dp", "mp"),
            P("dp", "mp"),
            P("mp", "dp"),
            P("dp", None),
        ),
        out_specs=(
            rows,
            rows,
            P(("dp", "mp")),
            P(("dp", "mp")),
            P("dp", "mp"),
            P("dp", "mp"),
            P("mp", "dp"),
            P("mp", "dp", None),
            P("mp", "dp", None),
            P("dp", "mp"),
            P("dp", "mp"),
            P("dp", "mp"),
            P("mp", "dp"),
        ),
        check_vma=False,
    )
```

```python
import functools
import typing

import jax
import jax.numpy as jnp
from jax import lax
from jax.experimental import pallas as pl
from jax.experimental.pallas import tpu as pltpu
from jax.sharding import PartitionSpec as P

CONV = 4
AHEAD = 3
SUM_AHEAD = 3
EPS = 1e-06
DECAY = 8.0
HALF = jnp.bfloat16
SINGLE = jnp.float32
MESH = pl.DeviceIdType.MESH
VMEM_BYTES = 60 * 1024 * 1024
GELU_C = 0.7978845608028654
GELU_K = 0.044715


def dot_nn(left, right):
    return lax.dot_general(
        left, right, (((1,), (0,)), ((), ())), preferred_element_type=SINGLE
    )


def dot_nt(left, right):
    return lax.dot_general(
        left, right, (((1,), (1,)), ((), ())), preferred_element_type=SINGLE
    )


def dot_tn(left, right):
    return lax.dot_general(
        left, right, (((0,), (0,)), ((), ())), preferred_element_type=SINGLE
    )


def gelu(v):
    return 0.5 * v * (1.0 + jnp.tanh(GELU_C * (v + GELU_K * v * v * v)))


def gelu_both(v):
    square = v * v
    t = jnp.tanh(GELU_C * (v + GELU_K * v * square))
    value = 0.5 * v * (1.0 + t)
    slope = 0.5 * (1.0 + t) + 0.5 * v * (1.0 - t * t) * (GELU_C * (1.0 + 3.0 * GELU_K * square))
    return value, slope


def flip(me, mask, count):
    place = me
    bit = 1
    while bit < count:
        if mask & bit:
            place = place + (1 - 2 * ((me // bit) % 2)) * bit
        bit *= 2
    return place


def ring_peers(axis):
    me, count = lax.axis_index(axis), lax.axis_size(axis)
    return [(k, {axis: (me + k) % count}) for k in range(1, count)]


def greet(peers):
    barrier = pltpu.get_barrier_semaphore()
    for _, peer in peers:
        pl.semaphore_signal(barrier, inc=1, device_id=peer, device_id_type=MESH)
    pl.semaphore_wait(barrier, len(peers))


def exchange(peers, source, target, send, recv):
    return [
        pltpu.make_async_remote_copy(
            src_ref=source(k),
            dst_ref=target(k),
            send_sem=send.at[k],
            recv_sem=recv.at[k],
            device_id=peer,
            device_id_type=MESH,
        )
        for k, peer in peers
    ]


def each(copies, act):
    for copy in copies:
        act(copy)


START, LAND, SENT = (lambda c: c.start(), lambda c: c.wait_recv(), lambda c: c.wait_send())


def gather_plan(count):
    bits = [1 << b for b in range(count.bit_length() - 1)]
    outer = bits[1:]
    orders = (outer + bits[:1], outer[::-1] + bits[:1])
    sends = []
    for half, order in enumerate(orders):
        for stage, bit in enumerate(order):
            for pick in range(1 << stage):
                mask = sum(order[j] for j in range(stage) if pick >> j & 1)
                sends.append((bin(mask).count("1"), half, mask, bit))
    sends.sort(key=lambda s: s[0])
    return bits, [s[1:] for s in sends]


class PlaneGather:
    COUNT = 8

    @staticmethod
    def scratch():
        count = PlaneGather.COUNT
        return [
            pltpu.SemaphoreType.DMA,
            pltpu.SemaphoreType.DMA((2, count)),
            pltpu.SemaphoreType.DMA((2, count)),
        ]

    def __init__(self, x_ref, o_ref, scratch):
        self.x, self.o = x_ref, o_ref
        self.own_sem, self.send, self.recv = scratch
        self.me = lax.axis_index("mp")
        self.bits, self.plan = gather_plan(self.COUNT)

    def own(self):
        rows = self.x.shape[0]
        span = pl.ds(pl.multiple_of(self.me * rows, rows), rows)
        return pltpu.make_async_copy(self.x, self.o.at[span], self.own_sem)

    def copy(self, half, mask, bit):
        rows = self.x.shape[0] // 2
        slot = 2 * flip(self.me, mask, self.COUNT) + half
        span = pl.ds(pl.multiple_of(slot * rows, rows), rows)
        return pltpu.make_async_remote_copy(
            src_ref=self.o.at[span] if mask else self.x.at[pl.ds(half * rows, rows)],
            dst_ref=self.o.at[span],
            send_sem=self.send.at[half, mask | bit],
            recv_sem=self.recv.at[half, mask | bit],
            device_id={"mp": flip(self.me, bit, self.COUNT)},
            device_id_type=MESH,
        )

    def level(self, depth):
        landed = set()
        for half, mask, bit in self.plan:
            if bin(mask).count("1") != depth:
                continue
            if mask and (half, mask) not in landed:
                landed.add((half, mask))
                self.arrived(half, mask)
            self.copy(half, mask, bit).start()

    def arrived(self, half, mask):
        for other, before, bit in self.plan:
            if other == half and before | bit == mask:
                self.copy(half, before, bit).wait_recv()

    def start(self):
        self.own().start()
        self.level(0)

    def finish(self):
        waited = {(half, mask) for half, mask, _ in self.plan}
        for half, mask, bit in self.plan:
            if (half, mask | bit) not in waited:
                self.copy(half, mask, bit).wait_recv()
        for entry in self.plan:
            self.copy(*entry).wait_send()
        self.own().wait()


class LineGather:
    COUNT = 4
    ENDS = ((0, 3), (3, 0))

    @staticmethod
    def scratch(pieces):
        shapes = ((pieces, 4), (pieces, 4), (pieces,))
        return [pltpu.SemaphoreType.DMA(shape) for shape in shapes]

    def __init__(self, targets, pieces, scratch):
        self.chunks, self.of = [], []
        for target, count in zip(targets, pieces):
            rows = target.shape[1] // count
            first = len(self.chunks)
            self.chunks += [(target, pl.ds(p * rows, rows)) for p in range(count)]
            self.of.append(range(first, len(self.chunks)))
        self.send, self.recv, self.onward = scratch
        self.me = lax.axis_index("dp")

    def direct(self, c, to):
        target, span = self.chunks[c]
        return pltpu.make_async_remote_copy(
            src_ref=target.at[self.me, span],
            dst_ref=target.at[self.me, span],
            send_sem=self.send.at[c, to],
            recv_sem=self.recv.at[c, self.me],
            device_id={"dp": to},
            device_id_type=MESH,
        )

    def handed(self, c, block, to):
        target, span = self.chunks[c]
        return pltpu.make_async_remote_copy(
            src_ref=target.at[block, span],
            dst_ref=target.at[block, span],
            send_sem=self.onward.at[c],
            recv_sem=self.recv.at[c, block],
            device_id={"dp": to},
            device_id_type=MESH,
        )

    def sends_to(self, to):
        senders = [z for z in range(self.COUNT) if z != to and (z, to) not in self.ENDS]
        return functools.reduce(jnp.logical_or, [self.me == z for z in senders])

    def start(self, chunks):
        for c in chunks:
            for to in range(self.COUNT):
                pl.when(self.sends_to(to))(lambda c=c, to=to: self.direct(c, to).start())

    def hand_on(self, chunks):
        for c in chunks:
            for first, last in self.ENDS:
                middle = 2 if last == 3 else 1

                @pl.when(self.me == middle)
                def _(c=c, first=first, last=last):
                    copy = self.handed(c, first, last)
                    copy.wait_recv()
                    copy.start()

    def begin(self, ahead):
        self.ahead, self.done = ahead, 0
        self.start(range(ahead))

    def tick(self, count=1):
        for _ in range(count):
            self.hand_on([self.done])
            if self.done + self.ahead < len(self.chunks):
                self.start([self.done + self.ahead])
            self.done += 1

    def landed(self, chunks):
        for c in chunks:
            for block in range(self.COUNT):
                early = 2 if block == 0 else 1 if block == 3 else None
                waits = self.me != block
                if early is not None:
                    waits = jnp.logical_and(waits, self.me != early)
                pl.when(waits)(lambda c=c, block=block: self.handed(c, block, 0).wait_recv())

    def settle(self):
        for c in range(len(self.chunks)):
            for to in range(self.COUNT):
                pl.when(self.sends_to(to))(lambda c=c, to=to: self.direct(c, to).wait_send())
            pl.when(jnp.logical_or(self.me == 1, self.me == 2))(
                lambda c=c: self.handed(c, 0, 0).wait_send()
            )


def kernel_params(collective_id):
    return pltpu.CompilerParams(
        collective_id=collective_id, has_side_effects=True, vmem_limit_bytes=VMEM_BYTES
    )


def sharing(o_ref, sems):
    send_mp, recv_mp, send_dp, recv_dp = sems
    count = lax.axis_size("mp")
    first = lax.axis_index("dp") * count
    place = first + lax.axis_index("mp")
    mine = lambda k: o_ref.at[place]
    plane = lambda k: o_ref.at[pl.ds(first, count)]
    return (
        exchange(ring_peers("mp"), mine, mine, send_mp, recv_mp),
        exchange(ring_peers("dp"), plane, plane, send_dp, recv_dp),
    )


def beside_products(pairs, when=None, act=None):
    for left, right, out in pairs:
        tokens, rows = left.shape
        tile = min(256, rows)

        def body(left_tile, out_tile):
            if act is not None:
                pl.when(pl.program_id(0) == when)(act)
            out_tile[...] = dot_tn(left_tile[...], right[...]).astype(out_tile.dtype)

        pltpu.emit_pipeline(
            body,
            grid=(rows // tile,),
            in_specs=[pl.BlockSpec((tokens, tile), lambda i: (0, i))],
            out_specs=[pl.BlockSpec((tile, right.shape[1]), lambda i: (i, 0))],
        )(left, out)


class PlaneSum:
    COUNT = 8
    ORDER = (3, 1, 2, 0)
    LINKS = ((3, 0, 2), (3, 1, 1), (1, 1, 1), (2, 0, 2), (1, 0, 1), (2, 1, 2))

    @staticmethod
    def scratch(rows, width):
        middle = rows // 2
        return [
            pltpu.VMEM((rows, width), SINGLE),
            pltpu.VMEM((2, middle, width), SINGLE),
            pltpu.VMEM((2, rows, width), HALF),
            pltpu.VMEM((4, rows, width), HALF),
            pltpu.VMEM((6, middle, width), HALF),
            pltpu.VMEM((6, middle, width), HALF),
            pltpu.SemaphoreType.DMA((4,)),
            pltpu.SemaphoreType.DMA((4,)),
            pltpu.SemaphoreType.DMA((6,)),
            pltpu.SemaphoreType.DMA((6,)),
        ]

    def __init__(self, products, tile, lefts, rights, scratch):
        self.terms = list(zip(lefts, rights, products))
        self.tile = tile
        self.acc, self.side, self.core_out, self.core_in = scratch[:4]
        self.link_out, self.link_in = scratch[4:6]
        self.core_send, self.core_recv, self.link_send, self.link_recv = scratch[6:]
        self.rows, self.width = self.acc.shape
        self.halves = (slice(0, self.rows // 2), slice(self.rows // 2, self.rows))
        self.me = lax.axis_index("mp")

    def tiles(self, step):
        def body(t, carry):
            step(t, pl.ds(pl.multiple_of(t * self.tile, self.tile), self.tile))
            return carry

        lax.fori_loop(0, self.width // self.tile, body, 0)

    def partial(self, slot, t, columns):
        span = pl.ds(pl.multiple_of(slot * self.rows, self.rows), self.rows)
        value = None
        for left, right, product in self.terms:
            term = product(left[span, :], right, t, columns)
            value = term if value is None else value + term
        return value

    def core_copy(self, c):
        return pltpu.make_async_remote_copy(
            src_ref=self.core_out.at[self.ORDER.index(c) % 2],
            dst_ref=self.core_in.at[c],
            send_sem=self.core_send.at[c],
            recv_sem=self.core_recv.at[c],
            device_id={"mp": flip(self.me, 1, self.COUNT)},
            device_id_type=MESH,
        )

    def link_copy(self, index):
        return pltpu.make_async_remote_copy(
            src_ref=self.link_out.at[index],
            dst_ref=self.link_in.at[index],
            send_sem=self.link_send.at[index],
            recv_sem=self.link_recv.at[index],
            device_id={"mp": flip(self.me, 2 * self.LINKS[index][2], self.COUNT)},
            device_id_type=MESH,
        )

    def send(self, c):
        place = self.ORDER.index(c)
        if place >= 2:
            self.core_copy(self.ORDER[place - 2]).wait_send()
        slot = flip(self.me, 2 * c + 1, self.COUNT)

        def step(t, columns):
            self.core_out[place % 2, :, columns] = self.partial(slot, t, columns).astype(HALF)

        self.tiles(step)
        self.core_copy(c).start()

    def take(self, c):
        self.core_copy(c).wait_recv()
        slot = flip(self.me, 2 * c, self.COUNT)
        ways = [i for i in range(4) if self.LINKS[i][0] == c]
        kept = [h for h in (0, 1) if c and h not in [self.LINKS[i][1] for i in ways]]

        def step(t, columns):
            value = self.partial(slot, t, columns) + self.core_in[c, :, columns].astype(SINGLE)
            if c == 0:
                self.acc[:, columns] = value
            for i in ways:
                self.link_out[i, :, columns] = value[self.halves[self.LINKS[i][1]]].astype(HALF)
            for h in kept:
                self.side[h, :, columns] = value[self.halves[h]]

        self.tiles(step)
        for i in ways:
            self.link_copy(i).start()

    def spread(self, between=lambda: None):
        self.send(3)
        self.send(1)
        self.take(3)
        self.send(2)
        self.take(1)
        between()
        self.send(0)
        self.take(2)
        self.take(0)
        self.relay()

    def relay(self):
        for index, landed, half in ((4, 0, 0), (5, 1, 1)):
            self.link_copy(landed).wait_recv()

            def step(t, columns):
                value = self.side[half, :, columns]
                value = value + self.link_in[landed, :, columns].astype(SINGLE)
                self.link_out[index, :, columns] = value.astype(HALF)

            self.tiles(step)
            self.link_copy(index).start()

    def finish(self, out_ref):
        for index in (2, 3, 4, 5):
            self.link_copy(index).wait_recv()

        def step(t, columns):
            for half, (one, two) in enumerate(((3, 4), (2, 5))):
                value = self.acc[self.halves[half], columns]
                value = value + self.link_in[one, :, columns].astype(SINGLE)
                value = value + self.link_in[two, :, columns].astype(SINGLE)
                out_ref[self.halves[half], columns] = value

        self.tiles(step)
        for c in self.ORDER[2:]:
            self.core_copy(c).wait_send()
        for index in range(6):
            self.link_copy(index).wait_send()


class LineSum:
    COUNT = 4

    @staticmethod
    def scratch(pieces):
        shapes = ((pieces, 4), (pieces, 4), (pieces,), (pieces,))
        return [pltpu.SemaphoreType.DMA(shape) for shape in shapes] + [pltpu.SemaphoreType.DMA]

    def __init__(self, jobs, scratch):
        self.jobs, self.chunks, self.of = jobs, [], []
        for job in jobs:
            _, landed, _, pieces, _, _ = job
            rows = landed.shape[1] // pieces
            first = len(self.chunks)
            self.chunks += [(job, p, rows) for p in range(pieces)]
            self.of.append(range(first, len(self.chunks)))
        self.send, self.recv, self.relay_send, self.relay_recv, self.load_sem = scratch
        self.me = lax.axis_index("dp")

    def part(self, c, block):
        (source, landed, *_), p, rows = self.chunks[c]
        return source.at[pl.ds(pl.multiple_of(block * landed.shape[1] + p * rows, 16), rows)]

    def place(self, c, sender):
        (_, landed, *_), p, rows = self.chunks[c]
        return landed.at[sender, pl.ds(p * rows, rows)]

    def relay(self, c):
        (*_, relay, _), p, _ = self.chunks[c]
        return relay.at[p]

    def direct(self, c, to, source=None):
        return pltpu.make_async_remote_copy(
            src_ref=self.part(c, to) if source is None else source,
            dst_ref=self.place(c, self.me),
            send_sem=self.send.at[c, to],
            recv_sem=self.recv.at[c, self.me],
            device_id={"dp": to},
            device_id_type=MESH,
        )

    def by_middle(self, c, block, to):
        return pltpu.make_async_remote_copy(
            src_ref=self.part(c, block),
            dst_ref=self.relay(c),
            send_sem=self.relay_send.at[c],
            recv_sem=self.relay_recv.at[c],
            device_id={"dp": to},
            device_id_type=MESH,
        )

    def among(self, places):
        return functools.reduce(jnp.logical_or, [self.me == z for z in places])

    DIRECT = ((1,), (0, 2, 3), (0, 1, 3), (2,))
    ROUND = ((0, 3, 1), (3, 0, 2))

    def start(self, chunks, places=(0, 1, 2, 3)):
        for c in chunks:
            for end, block, middle in self.ROUND:
                if end in places:
                    pl.when(self.me == end)(
                        lambda c=c, block=block, middle=middle: self.by_middle(
                            c, block, middle
                        ).start()
                    )
            for to, senders in enumerate(self.DIRECT):
                senders = [z for z in senders if z in places]
                if senders:
                    pl.when(self.among(senders))(lambda c=c, to=to: self.direct(c, to).start())

    def hand_on(self, chunks):
        for c in chunks:
            *_, other = self.chunks[c][0]
            for _, block, middle in self.ROUND:

                @pl.when(self.me == middle)
                def _(c=c, block=block, middle=middle, other=other):
                    mine = pltpu.make_async_copy(self.part(c, block), other, self.load_sem)
                    mine.start()
                    self.by_middle(c, block, middle).wait_recv()
                    mine.wait()
                    relay = self.relay(c)
                    value = relay[...].astype(SINGLE) + other[...].astype(SINGLE)
                    relay[...] = value.astype(HALF)
                    self.direct(c, block, relay).start()

    def begin(self, ahead, places):
        self.ahead, self.done = ahead, 0
        self.start(range(ahead), places)

    def tick(self, count=1):
        for _ in range(count):
            self.hand_on([self.done])
            if self.done + self.ahead < len(self.chunks):
                self.start([self.done + self.ahead])
            self.done += 1

    SENDERS = ((1, 2), (0, 2, 3), (0, 1, 3), (1, 2))

    def collect(self, j):
        source, landed, target, _, _, _ = self.jobs[j]
        turned = target.shape[-1] != landed.shape[-1]
        split = len(target.shape) == 3
        for c in self.of[j]:
            for sender in range(self.COUNT):
                takers = [z for z in range(self.COUNT) if sender in self.SENDERS[z]]
                pl.when(self.among(takers))(
                    lambda c=c, sender=sender: self.wait_from(c, sender)
                )
        _, rows, columns = landed.shape
        tile = rows // 2 if rows >= 256 else rows
        out_spec = pl.BlockSpec((tile, columns), lambda t: (t, 0))
        if split:
            shape = (1, columns, tile) if turned else (1, tile, columns)
            out_spec = pl.BlockSpec(shape, lambda t: (t, 0, 0))

        def add(*refs):
            value = refs[0][...].astype(SINGLE)
            for ref in refs[1:-1]:
                value = value + ref[0].astype(SINGLE)
            if split:
                refs[-1][0] = value.T if turned else value
            else:
                refs[-1][...] = value

        def run(senders):
            pltpu.emit_pipeline(
                add,
                grid=(rows // tile,),
                in_specs=[
                    pl.BlockSpec((tile, columns), lambda t: (self.me * (rows // tile) + t, 0))
                ]
                + [
                    pl.BlockSpec((1, tile, columns), lambda t, sender=sender: (sender, t, 0))
                    for sender in senders
                ],
                out_specs=[out_spec],
            )(source, *[landed] * len(senders), target)

        pl.when(self.among((0, 3)))(lambda: run((1, 2)))
        pl.when(self.among((1, 2)))(lambda: run((0, 3 - self.me, 3)))

    def wait_from(self, c, sender):
        pltpu.make_async_remote_copy(
            src_ref=self.place(c, sender),
            dst_ref=self.place(c, sender),
            send_sem=self.relay_send.at[c],
            recv_sem=self.recv.at[c, sender],
            device_id={"dp": 0},
            device_id_type=MESH,
        ).wait_recv()

    def settle(self):
        for c in range(len(self.chunks)):
            for to, senders in enumerate(self.DIRECT):
                pl.when(self.among(senders))(lambda c=c, to=to: self.direct(c, to).wait_send())
            for end, block, middle in self.ROUND:
                pl.when(self.me == end)(
                    lambda c=c, block=block, middle=middle: self.by_middle(
                        c, block, middle
                    ).wait_send()
                )
                pl.when(self.me == middle)(
                    lambda c=c, block=block: self.direct(c, block, self.relay(c)).wait_send()
                )


def positions(lens_ref, first, shape):
    place = lax.broadcasted_iota(jnp.int32, shape, 0) + first
    begin = jnp.zeros(shape, jnp.int32)
    total = 0
    for j in range(lens_ref.shape[1]):
        total = total + lens_ref[0, j]
        begin = jnp.where(place >= total, total, begin)
    return place - begin, place < total


def split_dot(dot, left, right):
    high = left.astype(HALF)
    low = (left - high.astype(SINGLE)).astype(HALF)
    return dot(high, right) + dot(low, right)


def lane_tiles(width):
    return [(t, t * 128, min(128, width - t * 128)) for t in range(-(-width // 128))]


def put_tiles(ref, value):
    for t, first, lanes in lane_tiles(value.shape[1]):
        ref[t, :, :lanes] = value[:, first : first + lanes]


def scan_start(tiles, lanes):
    return [(jnp.zeros((lanes, 128), SINGLE), jnp.ones((lanes, 128), SINGLE)) for _ in tiles]


def sigmoid(v):
    return 1.0 / (1.0 + jnp.exp(-v))


def forward_step(
    step,
    lens_ref,
    x_ref,
    gain_ref,
    pack_ref,
    bin_ref,
    ba_ref,
    chan_ref,
    n1_ref,
    bx_ref,
    by_ref,
    conv_ref,
    gi_ref,
    ra_ref,
    h_ref,
    ob_ref,
    taps,
    coef,
    drive,
    carry,
):
    rows, width = bx_ref.shape
    depth = pack_ref.shape[2]
    lanes = 8
    span = rows // lanes

    @pl.when(step == 0)
    def _():
        taps[...] = jnp.zeros_like(taps)
        carry[...] = jnp.zeros_like(carry)
        coef[...] = jnp.zeros_like(coef)
        drive[...] = jnp.zeros_like(drive)

    x = x_ref[...].astype(SINGLE)
    scale = lax.rsqrt(jnp.mean(x * x, axis=-1, keepdims=True) + EPS)
    normed = (x * scale * gain_ref[...]).astype(HALF)
    n1_ref[...] = normed
    total = None
    for d in range(pack_ref.shape[0]):
        term = dot_nt(normed[:, d * depth : (d + 1) * depth], pack_ref[d, : 2 * width, :])
        total = term if total is None else total + term
    bx = total[:, :width].astype(HALF)
    by = total[:, width:]
    bx_ref[...] = bx
    by_ref[...] = by
    pos, live = positions(lens_ref, step * rows, (rows, width))
    taps[0:8, :] = taps[rows : rows + 8, :]
    taps[8 : rows + 8, :] = bx.astype(SINGLE)
    conv = jnp.zeros((rows, width), SINGLE) + chan_ref[CONV : CONV + 1, :]
    for k in range(CONV):
        moved = taps[8 - k : 8 - k + rows, :]
        conv = conv + jnp.where(pos >= k, moved * chan_ref[k : k + 1, :], 0.0)
    conv_ref[...] = conv
    high = conv.astype(HALF)
    low = (conv - high.astype(SINGLE)).astype(HALF)
    gate_in = sigmoid(
        dot_nn(high, bin_ref[...]) + dot_nn(low, bin_ref[...]) + chan_ref[CONV + 1 : CONV + 2, :]
    )
    gate_a = sigmoid(
        dot_nn(high, ba_ref[...]) + dot_nn(low, ba_ref[...]) + chan_ref[CONV + 2 : CONV + 3, :]
    )
    gi_ref[...] = gate_in
    ra_ref[...] = gate_a
    decay = jnp.exp(-DECAY * gate_a * chan_ref[CONV + 4 : CONV + 5, :])
    root = jnp.sqrt(1.0 - decay * decay)
    put_tiles(coef, jnp.where(pos == 0, 0.0, decay))
    put_tiles(drive, gate_in * conv * root)
    tiles = lane_tiles(width)

    def scan(i, state):
        at = pl.ds(i, lanes, stride=span)
        result = []
        for (t, _, _), (h, prod) in zip(tiles, state):
            a = coef[t, at, :]
            h = a * h + drive[t, at, :]
            prod = prod * a
            drive[t, at, :] = h
            coef[t, at, :] = prod
            result.append((h, prod))
        return result

    state = lax.fori_loop(0, span, scan, scan_start(tiles, lanes), unroll=4)
    for (t, first, used), (h, prod) in zip(tiles, state):
        running = carry[t, 0:1, :]
        for s in range(lanes):
            at = slice(s * span, (s + 1) * span)
            value = drive[t, at, :] + coef[t, at, :] * running
            h_ref[at, first : first + used] = value[:, :used]
            running = h[s : s + 1, :] + prod[s : s + 1, :] * running
        carry[t, 0:1, :] = running
    mixed = h_ref[...].astype(HALF).astype(SINGLE)
    ob_ref[...] = jnp.where(live, gelu(by) * mixed, 0.0).astype(HALF)


def forward_kernel(*refs):
    forward_step(pl.program_id(0), *refs)


def forward_scratch(rows, width):
    tiles = len(lane_tiles(width))
    return [
        pltpu.VMEM((rows + 8, width), SINGLE),
        pltpu.VMEM((tiles, rows, 128), SINGLE),
        pltpu.VMEM((tiles, rows, 128), SINGLE),
        pltpu.VMEM((tiles, 8, 128), SINGLE),
    ]


def forward_channels(lens, x_all, gain, pack, blocks_in, blocks_a, chan):
    tokens, model = x_all.shape
    width = chan.shape[1]
    count = lax.axis_size("mp")
    rows = tokens // count
    whole = lambda shape: pl.BlockSpec(shape, lambda i: (0,) * len(shape))
    part = pl.BlockSpec((rows, width), lambda i: (i, 0))
    full = lambda kind: jax.ShapeDtypeStruct((tokens, width), kind)
    return pl.pallas_call(
        forward_kernel,
        grid=(count,),
        out_shape=(
            jax.ShapeDtypeStruct((tokens, model), HALF),
            full(HALF),
            full(SINGLE),
            full(SINGLE),
            full(SINGLE),
            full(SINGLE),
            full(SINGLE),
            full(HALF),
        ),
        in_specs=[
            pl.BlockSpec(memory_space=pltpu.SMEM),
            pl.BlockSpec((rows, model), lambda i: (i, 0)),
            whole(gain.shape),
            whole(pack.shape),
            whole(blocks_in.shape),
            whole(blocks_a.shape),
            whole(chan.shape),
        ],
        out_specs=(pl.BlockSpec((rows, model), lambda i: (i, 0)),) + (part,) * 7,
        scratch_shapes=forward_scratch(rows, width),
        compiler_params=pltpu.CompilerParams(vmem_limit_bytes=VMEM_BYTES),
        cost_estimate=pl.CostEstimate(
            flops=2 * tokens * model * 2 * width,
            bytes_accessed=tokens * (model * 4 + width * 24),
            transcendentals=8 * tokens * width,
        ),
        name="forward_channels",
    )(lens, x_all, gain, pack, blocks_in, blocks_a, chan)


def by_parts(left, right, t, columns):
    return dot_nn(left, right[t])


def backward_step(
    step,
    steps,
    lens_ref,
    dt_ref,
    pack_ref,
    bin_ref,
    ba_ref,
    chan_ref,
    bx_ref,
    by_ref,
    conv_ref,
    gi_ref,
    ra_ref,
    h_ref,
    hprev_ref,
    dbx_ref,
    dby_ref,
    gin_ref,
    ga_ref,
    gchan_ref,
    lift,
    coef,
    drive,
    carry,
):
    chunk = steps - 1 - step
    rows, width = bx_ref.shape
    depth = pack_ref.shape[2]
    lanes = 8
    span = rows // lanes

    @pl.when(step == 0)
    def _():
        lift[...] = jnp.zeros_like(lift)
        carry[...] = jnp.zeros_like(carry)
        coef[...] = jnp.zeros_like(coef)
        drive[...] = jnp.zeros_like(drive)
        gin_ref[...] = jnp.zeros_like(gin_ref)
        ga_ref[...] = jnp.zeros_like(ga_ref)
        gchan_ref[...] = jnp.zeros_like(gchan_ref)

    d_out = None
    for d in range(pack_ref.shape[0]):
        term = dot_nt(dt_ref[:, d * depth : (d + 1) * depth], pack_ref[d])
        d_out = term if d_out is None else d_out + term
    pos, live = positions(lens_ref, chunk * rows, (rows, width))
    by = by_ref[...]
    h = h_ref[...]
    side, slope = gelu_both(by)
    d_out = jnp.where(live, d_out, 0.0)
    dby_ref[...] = (d_out * h.astype(HALF).astype(SINGLE) * slope).astype(HALF)
    gate_a = ra_ref[...]
    soft = chan_ref[CONV + 4 : CONV + 5, :]
    decay = jnp.exp(-DECAY * gate_a * soft)
    put_tiles(coef, jnp.where(pos == 0, 0.0, decay))
    put_tiles(drive, (d_out * side).astype(HALF).astype(SINGLE))
    tiles = lane_tiles(width)

    def scan(j, state):
        at = pl.ds(span - 1 - j, lanes, stride=span)
        result = []
        for (t, _, _), (after, prod) in zip(tiles, state):
            a = coef[t, at, :]
            lam = drive[t, at, :] + after
            drive[t, at, :] = lam
            coef[t, at, :] = prod
            result.append((a * lam, prod * a))
        return result

    state = lax.fori_loop(0, span, scan, scan_start(tiles, lanes), unroll=4)
    for (t, first, used), (after, prod) in zip(tiles, state):
        running = carry[t, 0:1, :]
        for s in reversed(range(lanes)):
            at = slice(s * span, (s + 1) * span)
            value = drive[t, at, :] + coef[t, at, :] * running
            lift[at, first : first + used] = value[:, :used]
            running = after[s : s + 1, :] + prod[s : s + 1, :] * running
        carry[t, 0:1, :] = running
    lam = lift[0:rows, :]
    last = jnp.where(chunk > 0, hprev_ref[7:8, :], 0.0)
    before = jnp.concatenate([last, h[: rows - 1, :]], axis=0)
    before = jnp.where(pos == 0, 0.0, before)
    conv = conv_ref[...]
    gate_in = gi_ref[...]
    root = jnp.sqrt(1.0 - decay * decay)
    d_decay = lam * before - lam * gate_in * conv * decay / root
    d_log = d_decay * decay
    d_a = d_log * (-DECAY * soft)
    d_in = lam * conv * root
    d_logit_in = d_in * gate_in * (1.0 - gate_in)
    d_logit_a = d_a * gate_a * (1.0 - gate_a)
    d_conv = (
        lam * gate_in * root
        + split_dot(dot_nt, d_logit_in, bin_ref[...])
        + split_dot(dot_nt, d_logit_a, ba_ref[...])
    )
    low = conv.astype(HALF)
    gin_ref[...] += dot_tn(low, d_logit_in.astype(HALF))
    ga_ref[...] += dot_tn(low, d_logit_a.astype(HALF))
    lift[0:rows, :] = d_conv
    bx = bx_ref[...].astype(SINGLE)
    d_bx = jnp.zeros((rows, width), SINGLE)
    for k in range(CONV):
        if k:
            ahead, _ = positions(lens_ref, chunk * rows + k, (rows, width))
            moved = jnp.where(ahead >= k, lift[k : k + rows, :], 0.0)
        else:
            moved = d_conv
        d_bx = d_bx + moved * chan_ref[k : k + 1, :]
        gchan_ref[k : k + 1, :] += jnp.sum(moved * bx, axis=0, keepdims=True)
    dbx_ref[...] = d_bx.astype(HALF)
    lift[rows : rows + 8, :] = d_conv[0:8, :]
    sums = (d_conv, d_logit_in, d_logit_a, d_log * gate_a)
    for j, value in enumerate(sums):
        gchan_ref[CONV + j : CONV + j + 1, :] += jnp.sum(value, axis=0, keepdims=True)


def backward_kernel(*refs):
    refs = list(refs)
    inputs, (ob_ref, n1_ref), outputs, grads_ref, grads, scratch = (
        refs[:13], refs[13:15], refs[15:20], refs[20], refs[21], refs[22:],
    )
    step, steps = pl.program_id(0), pl.num_programs(0)

    @pl.when(step == 0)
    def _():
        grads[...] = jnp.zeros_like(grads)

    backward_step(step, steps, *inputs, *outputs, *scratch)
    dt_ref, (dbx_ref, dby_ref) = inputs[1], outputs[:2]
    width, depth = dbx_ref.shape[1], grads.shape[2]
    lefts = (dbx_ref[...], dby_ref[...], ob_ref[...])
    for d in range(grads.shape[0]):
        columns = slice(d * depth, (d + 1) * depth)
        rights = (n1_ref[:, columns], n1_ref[:, columns], dt_ref[:, columns])
        for j, (left, right) in enumerate(zip(lefts, rights)):
            grads[d, j * width : (j + 1) * width, :] += dot_tn(left, right)

    @pl.when(step == steps - 1)
    def _():
        grads_ref[...] = grads[...].astype(HALF)


def backward_channels(lens, dt_all, pack, blocks_in, blocks_a, chan, saved):
    bx, by, conv, gate_in, gate_a, h, ob, n1 = saved
    tokens, model = dt_all.shape
    width = chan.shape[1]
    count = lax.axis_size("mp")
    rows = tokens // count
    last = count - 1
    whole = lambda shape: pl.BlockSpec(shape, lambda i: (0,) * len(shape))
    part = pl.BlockSpec((rows, width), lambda i: (last - i, 0))
    across = pl.BlockSpec((rows, model), lambda i: (last - i, 0))
    before = pl.BlockSpec(
        (8, width), lambda i: (jnp.maximum((last - i) * (rows // 8) - 1, 0), 0)
    )
    full = jax.ShapeDtypeStruct((tokens, width), HALF)
    square = jax.ShapeDtypeStruct((width, width), SINGLE)
    grads = (pack.shape[0], 3 * width, pack.shape[2])
    return pl.pallas_call(
        backward_kernel,
        grid=(count,),
        out_shape=(
            full,
            full,
            square,
            square,
            jax.ShapeDtypeStruct((8, width), SINGLE),
            jax.ShapeDtypeStruct(grads, HALF),
        ),
        in_specs=[
            pl.BlockSpec(memory_space=pltpu.SMEM),
            across,
            whole(pack.shape),
            whole(blocks_in.shape),
            whole(blocks_a.shape),
            whole(chan.shape),
            part,
            part,
            part,
            part,
            part,
            part,
            before,
            part,
            across,
        ],
        out_specs=(
            part,
            part,
            whole((width, width)),
            whole((width, width)),
            whole((8, width)),
            whole(grads),
        ),
        scratch_shapes=[pltpu.VMEM(grads, SINGLE)] + forward_scratch(rows, width),
        compiler_params=pltpu.CompilerParams(vmem_limit_bytes=VMEM_BYTES),
        cost_estimate=pl.CostEstimate(
            flops=8 * tokens * model * width,
            bytes_accessed=tokens * (model * 4 + width * 28),
            transcendentals=8 * tokens * width,
        ),
        name="backward_channels",
    )(
        lens, dt_all, pack, blocks_in, blocks_a, chan,
        bx, by, conv, gate_in, gate_a, h, h, ob, n1,
    )


def log_one_plus(v):
    total = 1.0 + v
    exact = total - 1.0
    return jnp.where(exact == 0.0, v, jnp.log(total) * (v / jnp.where(exact == 0.0, 1.0, exact)))


def small_weights(small, bin_ref, ba_ref, chan_ref, heads, bite):
    parts = small.shape[0]
    width = bin_ref.shape[0]
    block = width // heads
    at_row = lax.broadcasted_iota(jnp.int32, (block, width), 0)
    at_column = lax.broadcasted_iota(jnp.int32, (block, width), 1)
    each = 2 * CONV // parts
    for d in range(parts):
        value = small[d].astype(SINGLE)
        for h in range(heads):
            place = (at_column == at_row + h * block).astype(HALF)
            for lane, target in ((0, bin_ref), (256, ba_ref)):
                piece = value[h * bite : (h + 1) * bite, lane : lane + block].astype(HALF)
                first = h * block + d * bite
                target[first : first + bite, :] = dot_nn(piece, place)
        row = heads * bite
        chan_ref[d * each : (d + 1) * each, :] = value[row : row + each, :width]
    v = -chan_ref[2 * CONV - 1 : 2 * CONV, :]
    chan_ref[2 * CONV : 2 * CONV + 1, :] = jnp.maximum(v, 0.0) + log_one_plus(
        jnp.exp(-jnp.abs(v))
    )


class LayerIn(typing.NamedTuple):
    lens: typing.Any
    norm_in: typing.Any
    norm_mid: typing.Any
    x: typing.Any
    cot: typing.Any
    blocks_in: typing.Any
    blocks_a: typing.Any
    channels: typing.Any
    w_in: typing.Any
    w_gate: typing.Any
    w_out: typing.Any
    gate: typing.Any
    up: typing.Any
    down: typing.Any


class LayerOut(typing.NamedTuple):
    layer_output: typing.Any
    grad_input: typing.Any
    gain_grads: typing.Any
    x_all: typing.Any
    c_all: typing.Any
    n2_all: typing.Any
    dt_all: typing.Any
    n1: typing.Any
    bx: typing.Any
    by: typing.Any
    conv: typing.Any
    gi: typing.Any
    ra: typing.Any
    h: typing.Any
    ob: typing.Any
    act: typing.Any
    slope: typing.Any
    grad_down: typing.Any
    grad_gate: typing.Any
    grad_up: typing.Any
    grad_out: typing.Any
    grad_pack: typing.Any
    pack4: typing.Any
    small4: typing.Any
    out4: typing.Any
    gate4: typing.Any
    up4: typing.Any
    down4: typing.Any
    landed_down: typing.Any
    landed_gate: typing.Any
    landed_up: typing.Any
    landed_out: typing.Any
    landed_small: typing.Any
    landed_pack: typing.Any
    sum_down: typing.Any
    sum_gate: typing.Any
    sum_up: typing.Any
    sum_out: typing.Any
    sum_small: typing.Any
    sum_pack: typing.Any


WEIGHT_PIECES = (4, 1, 2, 4, 4, 6)
SUM_PIECES = (4, 4, 4, 2, 1, 4)


def small_gradients(small, gin, ga, gchan, chan, heads, bite):
    parts = LineSum.COUNT
    width = gin.shape[0]
    block = width // heads
    each = 2 * CONV // parts
    rows = small.shape[0] // parts
    at_row = lax.broadcasted_iota(jnp.int32, (block, width), 0)
    at_column = lax.broadcasted_iota(jnp.int32, (block, width), 1)
    small[...] = jnp.zeros_like(small)
    v = chan[2 * CONV - 1 : 2 * CONV, :]
    last = 2 * CONV - 1
    gchan[last : last + 1, :] = gchan[last : last + 1, :] * (DECAY * sigmoid(-v))
    for d in range(parts):
        for h in range(heads):
            place = (at_column == at_row + h * block).astype(HALF)
            first = h * block + d * bite
            to = d * rows + h * bite
            for lane, grads in ((0, gin), (256, ga)):
                piece = grads[first : first + bite, :].astype(HALF)
                small[to : to + bite, lane : lane + block] = dot_nt(piece, place)
        to = d * rows + heads * bite
        small[to : to + each, :width] = gchan[d * each : (d + 1) * each, :]


def layer_kernel(*refs):
    refs = list(refs)
    take = lambda n: [refs.pop(0) for _ in range(n)]
    i = LayerIn(*take(len(LayerIn._fields)))
    o = LayerOut(*take(len(LayerOut._fields)))
    tiles, gain, gain_sum, bin_low, ba_low, chan = take(6)
    inputs, own_low, residual, d_res, summed = take(5)
    steps_scratch = take(4)
    gin, ga, gchan, small, turns, turns_dp, turns_mp = take(7)
    relays, others = take(6), take(3)
    load_sem, out_sem, free_sem = take(3)
    share_sems, total_sems = take(4), take(4)
    plane_x = PlaneGather(i.x, o.x_all, take(3))
    plane_c = PlaneGather(i.cot, o.c_all, take(3))
    plane_n = PlaneGather(own_low, o.n2_all, take(3))
    plane_t = PlaneGather(own_low, o.dt_all, take(3))
    shared = take(10)
    line = LineGather(
        (o.pack4, o.small4, o.out4, o.gate4, o.up4, o.down4), WEIGHT_PIECES, take(3)
    )
    pack_at, small_at, out_at, gate_at, up_at, down_at = line.of
    sources = (o.grad_down, o.grad_gate, o.grad_up, o.grad_out, small, o.grad_pack)
    landed = (
        o.landed_down, o.landed_gate, o.landed_up, o.landed_out, o.landed_small, o.landed_pack,
    )
    targets = (o.sum_down, o.sum_gate, o.sum_up, o.sum_out, o.sum_small, o.sum_pack)
    other = [others[j] for j in (0, 0, 0, 1, 2, 1)]
    sums = LineSum(list(zip(sources, landed, targets, SUM_PIECES, relays, other)), take(5))
    outward = [
        pltpu.make_async_copy(own_low, o.layer_output, out_sem.at[0]),
        pltpu.make_async_copy(d_res, o.grad_input, out_sem.at[1]),
    ]
    tokens, model = o.x_all.shape
    rows, count = i.x.shape[0], PlaneGather.COUNT
    width, units = o.bx.shape[1], o.act.shape[1]
    parts, _, depth = o.pack4.shape
    heads = width // i.blocks_in.shape[1]
    bite = i.blocks_in.shape[0] // heads
    level, me = lax.axis_index("dp"), lax.axis_index("mp")

    def copy_of(source, target, j):
        return pltpu.make_async_copy(source, target, load_sem.at[j])

    def load(pairs):
        copies = [copy_of(source, target, j) for j, (source, target) in enumerate(pairs)]
        for copy in copies:
            copy.start()
        for copy in copies:
            copy.wait()

    def stage(w_in, w_gate, w_out, gate, up, down, pack_low, out_low, gate_low, down_low, small_own):
        arrivals = [
            copy_of(source, target, j)
            for j, (source, target) in enumerate(
                (
                    (i.w_in, w_in), (i.w_gate, w_gate), (i.w_out, w_out), (i.gate, gate),
                    (i.up, up), (i.down, down), (i.x, inputs),
                )
            )
        ]
        for copy in arrivals:
            copy.start()
        greet(ring_peers("mp") + ring_peers("dp"))
        plane_x.start()
        for j, ref in enumerate((w_in, w_gate)):
            arrivals[j].wait()
            pack_low[j * width : (j + 1) * width, :] = ref[...].astype(HALF)
        load([(pack_low, o.pack4.at[level])])
        line.begin(AHEAD)
        tiles[level * count + me] = norm_tile()
        within, across_dp = sharing(tiles, share_sems)
        each(within, START)
        each(within, LAND)
        each(across_dp, START)
        small_own[...] = jnp.zeros_like(small_own)
        gate_rows, block = i.blocks_in.shape
        small_own[:gate_rows, :block] = i.blocks_in[...]
        small_own[:gate_rows, 256 : 256 + block] = i.blocks_a[...]
        small_own[gate_rows : gate_rows + i.channels.shape[0], :width] = i.channels[...]
        small[: small_own.shape[0], :] = small_own[...].astype(HALF)
        arrivals[2].wait()
        out_low[...] = w_out[...].astype(HALF)
        load([(small.at[: small_own.shape[0]], o.small4.at[level]), (out_low, o.out4.at[level])])
        line.tick()
        for j, ref, low, target in (
            (3, gate, gate_low, o.gate4), (4, up, gate_low, o.up4), (5, down, down_low, o.down4),
        ):
            arrivals[j].wait()
            low[...] = ref[...].astype(HALF)
            load([(low, target.at[level])])
        arrivals[6].wait()

    def norm_tile():
        bits = i.norm_in.shape[1]
        spot = me % (128 // bits) * bits
        at_column = lax.broadcasted_iota(jnp.int32, (bits, 128), 1)
        place = lax.broadcasted_iota(jnp.int32, (bits, 128), 0) + spot == at_column
        both = jnp.concatenate(
            [i.norm_in[...], i.norm_mid[...], jnp.zeros((6, bits), SINGLE)], axis=0
        )
        return dot_nn(both.astype(HALF), place.astype(HALF))

    pl.run_scoped(
        stage,
        pltpu.VMEM(i.w_in.shape, SINGLE),
        pltpu.VMEM(i.w_gate.shape, SINGLE),
        pltpu.VMEM(i.w_out.shape, SINGLE),
        pltpu.VMEM(i.gate.shape, SINGLE),
        pltpu.VMEM(i.up.shape, SINGLE),
        pltpu.VMEM(i.down.shape, SINGLE),
        pltpu.VMEM(o.pack4.shape[1:], HALF),
        pltpu.VMEM(o.out4.shape[1:], HALF),
        pltpu.VMEM(o.gate4.shape[1:], HALF),
        pltpu.VMEM(o.down4.shape[1:], HALF),
        pltpu.VMEM(o.small4.shape[1:], SINGLE),
    )
    gin[...] = jnp.zeros_like(gin)
    ga[...] = jnp.zeros_like(ga)
    chan[...] = jnp.zeros_like(chan)
    line.tick()
    plane_x.level(1)
    line.tick()
    plane_x.level(2)
    plane_x.finish()
    plane_c.start()
    within, across_dp = sharing(tiles, share_sems)
    each(across_dp, LAND)
    group = 128 // (model // tiles.shape[0])
    for j in range(model // 128):
        value = tiles[group * j]
        for k in range(1, group):
            value = value + tiles[group * j + k]
        gain[:, j * 128 : (j + 1) * 128] = value
    line.tick(2)
    line.landed(pack_at)
    line.landed(small_at)

    part = pl.BlockSpec((rows, width), lambda t: (t, 0))
    across = pl.BlockSpec((rows, model), lambda t: (t, 0))
    tall = pl.BlockSpec((tokens, depth), lambda t: (0, t))

    def temporal(pack, out_w, ob, small4):
        load([(o.pack4, pack), (o.small4, small4)])
        small_weights(small4, gin, ga, chan, heads, bite)
        bin_low[...] = gin[...].astype(HALF)
        ba_low[...] = ga[...].astype(HALF)

        def channels(x_tile, n1, bx, by, conv, gi, ra, h, ob_tile):
            step = pl.program_id(0)
            schedule = {
                1: line.tick,
                3: lambda: (plane_c.level(1), line.tick()),
                6: lambda: (plane_c.level(2), line.tick()),
            }
            for when, act in schedule.items():
                pl.when(step == when)(lambda act=act: (act(), None)[1])
            forward_step(
                step, i.lens, x_tile, gain.at[0:1], pack, bin_low, ba_low, chan,
                n1, bx, by, conv, gi, ra, h, ob_tile, *steps_scratch,
            )
            ob[pl.ds(pl.multiple_of(step * rows, rows), rows), :] = ob_tile[...]

        pltpu.emit_pipeline(
            channels,
            grid=(count,),
            in_specs=[across],
            out_specs=[across] + [part] * 7,
        )(o.x_all, o.n1, o.bx, o.by, o.conv, o.gi, o.ra, o.h, o.ob)
        line.landed(out_at)
        load([(o.out4, out_w)])
        plane = PlaneSum([by_parts], depth, [ob], [out_w], shared)
        plane.spread(line.tick)
        line.tick()
        plane_c.finish()
        line.tick()
        plane.finish(summed)

    pl.run_scoped(
        temporal,
        pltpu.VMEM(o.pack4.shape, HALF),
        pltpu.VMEM(o.out4.shape, HALF),
        pltpu.VMEM((tokens, width), HALF),
        pltpu.VMEM(o.small4.shape, HALF),
    )
    block = 32

    def norm(t, carry):
        at = pl.ds(pl.multiple_of(t * block, block), block)
        value = inputs[at, :].astype(SINGLE) + summed[at, :]
        scale = lax.rsqrt(jnp.mean(value * value, axis=-1, keepdims=True) + EPS)
        residual[at, :] = value
        own_low[at, :] = (value * scale * gain[1:2, :]).astype(HALF)
        return carry

    lax.fori_loop(0, rows // block, norm, 0)
    plane_n.start()
    line.tick(2)
    plane_n.level(1)
    line.tick()
    plane_n.level(2)
    line.tick()
    plane_n.finish()
    line.landed(gate_at)
    line.landed(up_at)

    def blocks(left, right):
        value = None
        for d in range(parts):
            term = right(left[:, d * depth : (d + 1) * depth], d)
            value = term if value is None else value + term
        return value

    def mlp(hidden, down, gate, up, d_up, d_gate):
        load([(o.gate4, gate), (o.up4, up), (i.cot, own_low)])
        thirds = [down_at[j : j + 2] for j in range(0, len(down_at), 2)]
        third = units // len(thirds)
        along = pl.BlockSpec((rows, units), lambda t: (t, 0))

        def activations(n2, act_tile, slope_tile):
            for when in (2, 4):
                pl.when(pl.program_id(0) == when)(line.tick)
            value, rise = gelu_both(blocks(n2, lambda v, d: dot_nn(v, gate[d])))
            act_tile[...] = value
            above = blocks(n2, lambda v, d: dot_nn(v, up[d]))
            at = pl.ds(pl.multiple_of(pl.program_id(0) * rows, rows), rows)
            hidden[at, :] = (value * above).astype(HALF)
            slope_tile[...] = rise * above

        pltpu.emit_pipeline(
            activations, grid=(count,), in_specs=[across], out_specs=[along, along]
        )(o.n2_all, o.act, o.slope)
        beside_products([(o.c_all, hidden, o.grad_down)], 3, line.tick)
        sums.begin(SUM_AHEAD, (0, 3))
        whole, act_part, slope_part = summed, d_res, shared[0]

        for p, pieces in enumerate(thirds):
            if p:
                line.tick(pieces[-1] + 1 - line.done)
            if p == len(thirds) - 1:
                sums.begin(SUM_AHEAD, (1, 2))
            span = pl.ds(p * third, third)
            parts_in = []
            for t in range(count):
                at = pl.ds(t * rows, rows)
                columns = pl.ds(t * third, third)
                parts_in.append((o.act.at[at, span], act_part.at[:, columns]))
                parts_in.append((o.slope.at[at, span], slope_part.at[:, columns]))
            arrivals = [copy_of(a, b, 1 + j) for j, (a, b) in enumerate(parts_in)]
            for copy in arrivals:
                copy.start()
            line.landed(pieces)
            load([(o.down4.at[:, span], down.at[:, span])])
            for copy in arrivals:
                copy.wait()

            def backs(c_tile):
                d = pl.program_id(0)
                term = dot_nt(c_tile[...], down[d, span])
                pieces_of = [
                    (t, slice(t * rows, (t + 1) * rows), slice(t * third, (t + 1) * third))
                    for t in range(count)
                ]

                @pl.when(d == 0)
                def _():
                    for _, at, columns in pieces_of:
                        whole[:, columns] = term[at]

                @pl.when(d > 0)
                def _():
                    for _, at, columns in pieces_of:
                        whole[:, columns] += term[at]

                @pl.when(d == parts - 1)
                def _():
                    for _, at, columns in pieces_of:
                        back = whole[:, columns]
                        d_up[at, span] = (back * act_part[:, columns]).astype(HALF)
                        d_gate[at, span] = (back * slope_part[:, columns]).astype(HALF)

            pltpu.emit_pipeline(backs, grid=(parts,), in_specs=[tall])(o.c_all)

        by_rows = lambda left, right, t, columns: dot_nt(left, right[t])
        plane = PlaneSum([by_rows, by_rows], depth, [d_gate, d_up], [gate, up], shared)
        plane.spread(sums.tick)

        beside_products([(o.n2_all, d_gate, o.grad_gate)])
        sums.tick()
        beside_products([(o.n2_all, d_up, o.grad_up)])
        sums.tick()
        plane.finish(summed)

    gain_sum[...] = jnp.zeros_like(gain_sum)

    def norm_back(value, back, row):
        scale = lax.rsqrt(jnp.mean(value * value, axis=-1, keepdims=True) + EPS)
        weighted = gain[row : row + 1, :] * back
        gain_sum[row : row + 1, :] += jnp.sum(back * value * scale, axis=0, keepdims=True)
        inner = jnp.mean(weighted * value, axis=-1, keepdims=True)
        return scale * weighted - value * (scale * scale * scale * inner)

    def middle(t, carry):
        at = pl.ds(pl.multiple_of(t * block, block), block)
        back = norm_back(residual[at, :], summed[at, :], 1)
        back = own_low[at, :].astype(SINGLE) + back
        d_res[at, :] = back
        own_low[at, :] = back.astype(HALF)
        return carry

    def out_gradients(ob):
        load([(o.ob, ob)])

        def body(dt_tile, out_tile):
            out_tile[...] = dot_tn(ob[...], dt_tile[...]).astype(HALF)

        pltpu.emit_pipeline(
            body,
            grid=(parts,),
            in_specs=[tall],
            out_specs=[pl.BlockSpec((width, depth), lambda t: (t, 0))],
        )(o.dt_all, o.grad_out)

    def temporal_back(hidden, down, out_w, d_bx, d_by):
        load([(o.out4, out_w)])
        plane = PlaneSum([by_parts], depth, [hidden], [down], shared)

        def channels(dt_tile, bx, by, conv, gi, ra, h, before):
            step = pl.program_id(0)
            schedule = {
                0: lambda: (plane.send(3), plane.send(1)),
                1: lambda: (plane.take(3), plane.send(2), sums.tick()),
                2: lambda: (plane.take(1), plane.send(0)),
                3: lambda: (plane.take(2), plane.take(0), sums.tick()),
                5: lambda: (plane.relay(), sums.tick()),
                7: sums.tick,
            }
            for when, act in schedule.items():
                pl.when(step == when)(lambda act=act: (act(), None)[1])
            at = pl.ds(pl.multiple_of((count - 1 - step) * rows, rows), rows)
            backward_step(
                step, count, i.lens, dt_tile, out_w, bin_low, ba_low, chan,
                bx, by, conv, gi, ra, h, before, d_bx.at[at], d_by.at[at], gin, ga, gchan,
                *steps_scratch,
            )

        late = pl.BlockSpec((rows, width), lambda t: (count - 1 - t, 0))
        late_across = pl.BlockSpec((rows, model), lambda t: (count - 1 - t, 0))
        ahead = pl.BlockSpec(
            (8, width), lambda t: (jnp.maximum((count - 1 - t) * (rows // 8) - 1, 0), 0)
        )
        pltpu.emit_pipeline(
            channels, grid=(count,), in_specs=[late_across] + [late] * 6 + [ahead]
        )(o.dt_all, o.bx, o.by, o.conv, o.gi, o.ra, o.h, o.h)
        plane.finish(summed)
        for bit in plane_t.bits:
            pl.semaphore_signal(
                free_sem, inc=1, device_id={"mp": flip(me, bit, count)}, device_id_type=MESH
            )
        own_low[...] = (residual[...] + summed[...]).astype(HALF)
        outward[0].start()

    def block_input(pack, d_bx, d_by):
        pack_load = copy_of(o.pack4, pack, 0)
        pack_load.start()

        def body(n1_tile, pack_tile):
            right = n1_tile[...]
            pack_tile[:width, :] = dot_tn(d_bx[...], right).astype(HALF)
            pack_tile[width:, :] = dot_tn(d_by[...], right).astype(HALF)

        pltpu.emit_pipeline(
            body,
            grid=(parts,),
            in_specs=[tall],
            out_specs=[pl.BlockSpec((2 * width, depth), lambda t: (t, 0))],
        )(o.n1, o.grad_pack)
        sums.tick()
        pack_load.wait()
        plane = PlaneSum(
            [
                lambda left, right, t, columns: dot_nn(left, right[t, :width, :]),
                lambda left, right, t, columns: dot_nn(left, right[t, width:, :]),
            ],
            depth,
            [d_bx, d_by],
            [pack, pack],
            shared,
        )
        pl.semaphore_wait(free_sem, len(plane_t.bits))
        plane.spread(sums.tick)
        sums.tick(3)
        plane.finish(summed)

    def with_hidden(hidden, down):
        pl.run_scoped(
            lambda *more: mlp(hidden, down, *more),
            pltpu.VMEM(o.gate4.shape, HALF),
            pltpu.VMEM(o.up4.shape, HALF),
            pltpu.VMEM((tokens, units), HALF),
            pltpu.VMEM((tokens, units), HALF),
        )
        lax.fori_loop(0, rows // block, middle, 0)
        plane_t.start()
        sums.tick(2)
        plane_t.level(1)
        sums.tick()
        plane_t.level(2)
        plane_t.finish()
        pl.run_scoped(out_gradients, pltpu.VMEM((tokens, width), HALF))
        sums.tick()

        def with_gradients(d_bx, d_by):
            pl.run_scoped(
                lambda out_w: temporal_back(hidden, down, out_w, d_bx, d_by),
                pltpu.VMEM(o.out4.shape, HALF),
            )
            pl.run_scoped(
                lambda small32: (
                    small_gradients(small32, gin, ga, gchan, chan, heads, bite),
                    small.__setitem__(Ellipsis, small32[...].astype(HALF)),
                    None,
                )[2],
                pltpu.VMEM(small.shape, SINGLE),
            )
            pl.run_scoped(
                lambda pack: block_input(pack, d_bx, d_by), pltpu.VMEM(o.pack4.shape, HALF)
            )

        pl.run_scoped(
            with_gradients, pltpu.VMEM((tokens, width), HALF), pltpu.VMEM((tokens, width), HALF)
        )

    pl.run_scoped(
        with_hidden, pltpu.VMEM((tokens, units), HALF), pltpu.VMEM(o.down4.shape, HALF)
    )

    def last(t, carry):
        at = pl.ds(pl.multiple_of(t * block, block), block)
        back = norm_back(inputs[at, :].astype(SINGLE), summed[at, :], 0)
        d_res[at, :] = d_res[at, :] + back
        return carry

    lax.fori_loop(0, rows // block, last, 0)
    outward[1].start()

    for j in range(turns.shape[0]):
        turns[j] = gain_sum[:, j * 128 : (j + 1) * 128]
    inner, outer = ring_peers("mp"), ring_peers("dp")
    held = turns.shape[0] // parts
    early = exchange(
        outer,
        lambda k: turns.at[pl.ds((level + k) % parts * held, held)],
        lambda k: turns_dp.at[k],
        *total_sems[:2],
    )
    each(early, START)
    sums.tick()
    for j in range(3):
        sums.collect(j)
    each(early, LAND)
    first = level * held
    for k, _ in outer:
        turns_dp[0] = (turns[pl.ds(first, held)] if k == 1 else turns_dp[0]) + turns_dp[k]
    pair = count // held
    late = exchange(
        inner,
        lambda k: turns_dp.at[0, (me + k) % count // pair],
        lambda k: turns_mp.at[k],
        *total_sems[2:],
    )
    each(late, START)
    sums.tick(len(sums.chunks) - 1 - sums.done)
    sums.collect(3)
    sums.collect(4)
    each(late, LAND)
    value = turns_dp[0, me // pair]
    for k, _ in inner:
        value = value + turns_mp[k]
    o.gain_grads[...] = value
    sums.tick()
    sums.collect(5)
    line.settle()
    sums.settle()
    each(within + across_dp + early + late, SENT)
    for copy in outward:
        copy.wait()


def fused_layer(values, collective_id):
    parts, count = LineSum.COUNT, PlaneGather.COUNT
    rows, model = values.x.shape
    tokens = rows * count
    width, depth = values.w_in.shape
    units = values.gate.shape[1]
    small_rows = -(-(values.blocks_in.shape[0] + values.channels.shape[0]) // 16) * 16
    shape = jax.ShapeDtypeStruct
    plane_rows = shape((tokens, model), HALF)
    channel = shape((tokens, width), SINGLE)
    channel_low = shape((tokens, width), HALF)
    hidden_wide = shape((tokens, units), SINGLE)
    hidden_grads = shape((model, units), HALF)
    sizes = (
        (depth, units), (depth, units), (depth, units),
        (width, depth), (small_rows, depth), (2 * width, depth),
    )
    outs = LayerOut(
        shape((rows, model), HALF),
        shape((rows, model), SINGLE),
        shape((8, 128), SINGLE),
        *[plane_rows] * 5,
        channel_low,
        *[channel] * 5,
        channel_low,
        hidden_wide,
        hidden_wide,
        hidden_grads,
        hidden_grads,
        hidden_grads,
        shape((parts * width, depth), HALF),
        shape((parts * 2 * width, depth), HALF),
        shape((parts, 2 * width, depth), HALF),
        shape((parts, small_rows, depth), HALF),
        shape((parts, width, depth), HALF),
        shape((parts, depth, units), HALF),
        shape((parts, depth, units), HALF),
        shape((parts, units, depth), HALF),
        *[shape((parts,) + size, HALF) for size in sizes],
        *[shape(size, SINGLE) for size in sizes],
    )
    outs = outs._replace(
        sum_down=shape((2, units, depth // 2), SINGLE), sum_pack=shape((2, width, depth), SINGLE)
    )
    in_vmem, in_hbm = pl.BlockSpec(memory_space=pltpu.VMEM), pl.BlockSpec(memory_space=pl.ANY)
    in_specs = LayerIn(*[in_hbm] * len(values))._replace(
        lens=pl.BlockSpec(memory_space=pltpu.SMEM),
        norm_in=in_vmem,
        norm_mid=in_vmem,
        blocks_in=in_vmem,
        blocks_a=in_vmem,
        channels=in_vmem,
    )
    out_specs = LayerOut(*[in_hbm] * len(outs))._replace(gain_grads=in_vmem)
    inner, outer = lax.axis_size("mp"), lax.axis_size("dp")
    pieces = [(n, (size[0] // n, size[1])) for size, n in zip(sizes, SUM_PIECES)]
    tile = (8, 128)
    vmem, sem = pltpu.VMEM, pltpu.SemaphoreType.DMA
    results = pl.pallas_call(
        layer_kernel,
        out_shape=list(outs),
        in_specs=list(in_specs),
        out_specs=list(out_specs),
        scratch_shapes=[
            vmem((inner * outer,) + tile, SINGLE),
            vmem((8, model), SINGLE),
            vmem((8, model), SINGLE),
            vmem((width, width), HALF),
            vmem((width, width), HALF),
            vmem((16, width), SINGLE),
            vmem((rows, model), HALF),
            vmem((rows, model), HALF),
            vmem((rows, model), SINGLE),
            vmem((rows, model), SINGLE),
            vmem((rows, model), SINGLE),
        ]
        + forward_scratch(rows, width)
        + [
            vmem((width, width), SINGLE),
            vmem((width, width), SINGLE),
            vmem((8, width), SINGLE),
            vmem((parts * small_rows, depth), HALF),
            vmem((model // 128,) + tile, SINGLE),
            vmem((outer, model // 128 // parts) + tile, SINGLE),
            vmem((inner,) + tile, SINGLE),
        ]
        + [vmem((n,) + size, HALF) for n, size in pieces]
        + [vmem(pieces[j][1], HALF) for j in (0, 3, 4)]
        + [sem((1 + 2 * count,)), sem((2,)), pltpu.SemaphoreType.REGULAR]
        + [sem((c,)) for c in (inner, inner, outer, outer)]
        + [sem((c,)) for c in (outer, outer, inner, inner)]
        + PlaneGather.scratch() * 4
        + PlaneSum.scratch(rows, model)
        + LineGather.scratch(sum(WEIGHT_PIECES))
        + LineSum.scratch(sum(SUM_PIECES)),
        compiler_params=kernel_params(collective_id),
        cost_estimate=pl.CostEstimate(
            flops=24 * tokens * model * units,
            bytes_accessed=80 * tokens * model,
            transcendentals=2 * tokens * units,
        ),
        name="layer",
    )(*values)
    return LayerOut(*results)


def diagonal(blocks):
    count, size, _ = blocks.shape
    spread = blocks[:, :, None, :] * jnp.eye(count, dtype=blocks.dtype)[:, None, :, None]
    return spread.reshape(count * size, count * size)


def on_device(
    layer_input,
    cotangent,
    norm_in,
    norm_mid,
    w_rnn_in,
    w_rnn_gate,
    w_rnn_out,
    gate_in_blocks,
    gate_a_blocks,
    channel_params,
    w_mlp_gate,
    w_mlp_up,
    w_mlp_down,
    lengths,
):
    parts = lax.axis_size("dp")
    rows, model = layer_input.shape
    depth, width = w_rnn_in.shape
    heads, bite, block = gate_in_blocks.shape
    tokens = rows * lax.axis_size("mp")

    fused = lax.axis_size("mp") == PlaneGather.COUNT and parts == LineGather.COUNT
    small_rows = -(-(heads * bite + 2 * CONV // parts) // 16) * 16
    small_lanes = 512
    lane_a = 256 if fused else block

    def small_pack(blocks_in, blocks_a, channels):
        wide = lambda v, lanes: jnp.pad(v, ((0, 0), (0, lanes - v.shape[1])))
        v = jnp.concatenate(
            [
                wide(blocks_in.reshape(-1, block), lane_a),
                wide(blocks_a.reshape(-1, block), small_lanes - lane_a),
            ],
            axis=1,
        )
        v = jnp.concatenate([v, wide(channels, small_lanes)], axis=0)
        return jnp.pad(v, ((0, small_rows - v.shape[0]), (0, 0)))

    bite_gain = norm_in.shape[0]
    if fused:
        o = fused_layer(
            LayerIn(
                lengths, norm_in.reshape(1, -1), norm_mid.reshape(1, -1), layer_input, cotangent,
                gate_in_blocks.reshape(-1, block), gate_a_blocks.reshape(-1, block),
                channel_params, w_rnn_in.T, w_rnn_gate.T, w_rnn_out, w_mlp_gate, w_mlp_up, w_mlp_down,
            ),
            0,
        )
        spot = (lax.axis_index("mp") % (128 // bite_gain)) * bite_gain
        gain_grads = lax.dynamic_slice(o.gain_grads, (0, spot), (2, bite_gain))
        layer_output, grad_input = o.layer_output, o.grad_input
        grad_in, grad_side = o.sum_pack[0].T, o.sum_pack[1].T
        grad_out, small_grads = o.sum_out, o.sum_small
        grad_gate, grad_up = o.sum_gate, o.sum_up
        grad_down = jnp.concatenate([o.sum_down[0], o.sum_down[1]], axis=1)
    else:
        inputs = layer_input.astype(SINGLE)
        small_mine = small_pack(
            gate_in_blocks.astype(HALF), gate_a_blocks.astype(HALF), channel_params.astype(HALF)
        )
        mine = jnp.concatenate([w_rnn_in.astype(HALF).T, w_rnn_gate.astype(HALF).T], axis=0)
        out_mine, down_mine = w_rnn_out.astype(HALF), w_mlp_down.astype(HALF)
        gate_mine, up_mine = w_mlp_gate.astype(HALF), w_mlp_up.astype(HALF)
        gains = jnp.stack([norm_in, norm_mid]).astype(HALF).astype(SINGLE)
        over = lambda v: lax.all_gather(v, "dp", axis=0, tiled=False)
        gains = lax.all_gather(gains, ("dp", "mp"), axis=0, tiled=False)
        gain_first = gains[:, 0].reshape(1, model)
        gain_second = gains[:, 1].reshape(1, model)
        small, pack, out_w = over(small_mine), over(mine), over(out_mine)
        down, gate_w, up_w = over(down_mine), over(gate_mine), over(up_mine)
        whole_block = lambda v: diagonal(
            v.reshape(parts, heads, bite, block)
            .transpose(1, 0, 2, 3)
            .reshape(heads, block, block)
        )
        blocks_in = whole_block(small[:, : heads * bite, :block])
        blocks_a = whole_block(small[:, : heads * bite, lane_a : lane_a + block])
        channel = small[:, heads * bite : heads * bite + 2 * CONV // parts, :width]
        channel = channel.reshape(2 * CONV, width).astype(SINGLE)
        soft = jax.nn.softplus(-channel[2 * CONV - 1 :])
        chan = jnp.concatenate([channel, soft, jnp.zeros((7, width), SINGLE)], axis=0)
        x_all = lax.all_gather(layer_input, "mp", axis=0, tiled=True)
        c_all = lax.all_gather(cotangent, "mp", axis=0, tiled=True)
        n1, bx, by, conv, gate_in, gate_a, h, ob = forward_channels(
            lengths, x_all, gain_first, pack, blocks_in, blocks_a, chan
        )
        saved = (bx, by, conv, gate_in, gate_a, h, ob, n1)
        out = jnp.einsum("tc,dcm->tdm", ob, out_w, preferred_element_type=SINGLE)
        residual = inputs + lax.psum_scatter(
            out.reshape(tokens, model).astype(HALF), "mp", scatter_dimension=0, tiled=True
        ).astype(SINGLE)
        scale = lax.rsqrt(jnp.mean(residual * residual, axis=-1, keepdims=True) + EPS)
        normed_mid = (residual * scale * gain_second).astype(HALF)
        n2 = lax.all_gather(normed_mid, "mp", axis=0, tiled=True)
        d_hidden = dot_nt(c_all, down.transpose(1, 0, 2).reshape(-1, model))
        act, slope = gelu_both(dot_nn(n2, gate_w.reshape(model, -1)))
        d_up = (d_hidden * act).astype(HALF)
        up_pre = dot_nn(n2, up_w.reshape(model, -1))
        hidden = (act * up_pre).astype(HALF)
        d_gate = (d_hidden * up_pre * slope).astype(HALF)
        gate_w, up_w = gate_w.reshape(model, -1), up_w.reshape(model, -1)
        over_dp = lambda value: lax.psum_scatter(
            value.astype(HALF), "dp", scatter_dimension=0, tiled=True
        ).astype(SINGLE)
        over_mp = lambda value: lax.psum_scatter(
            value.astype(HALF), "mp", scatter_dimension=0, tiled=True
        ).astype(SINGLE)
        grad_down = over_dp(dot_tn(c_all, hidden))
        grad_gate, grad_up = over_dp(dot_tn(n2, d_gate)), over_dp(dot_tn(n2, d_up))
        layer_output = residual + over_mp(
            dot_nn(hidden, down.transpose(1, 0, 2).reshape(-1, model))
        )
        layer_output = layer_output.astype(HALF)
        back = over_mp(dot_nt(d_gate, gate_w) + dot_nt(d_up, up_w))
        weighted = gain_second * back
        gain_mid = jnp.sum(back * residual * scale, axis=0)
        d_residual = (
            cotangent.astype(SINGLE)
            + scale * weighted
            - residual * scale**3 * jnp.mean(weighted * residual, axis=-1, keepdims=True)
        )
        dt_all = lax.all_gather(d_residual.astype(HALF), "mp", axis=0, tiled=True)
        d_bx, d_by, gin, ga, gchan, rnn_grads = backward_channels(
            lengths, dt_all, out_w, blocks_in, blocks_a, chan, saved
        )
        back = over_mp(
            jnp.einsum(
                "tc,dcm->tdm",
                jnp.concatenate([d_bx, d_by], axis=1),
                pack,
                preferred_element_type=SINGLE,
            ).reshape(tokens, model)
        )
        own = lambda full: jnp.stack(
            [full[j * block : (j + 1) * block, j * block : (j + 1) * block] for j in range(heads)]
        )
        decay_row = DECAY * jax.nn.sigmoid(-channel[2 * CONV - 1 :]) * gchan[2 * CONV - 1 :]
        grad_channel = jnp.concatenate([gchan[: 2 * CONV - 1], decay_row], axis=0)
        split = lambda v: v.reshape(heads, parts, bite, block).transpose(1, 0, 2, 3)
        small_grads = jax.vmap(small_pack)(
            split(own(gin)), split(own(ga)), grad_channel.reshape(parts, -1, width)
        )
        small_grads = over_dp(small_grads)[0]
        rnn_grads = over_dp(rnn_grads)[0]
        grad_in, grad_side, grad_out = jnp.split(rnn_grads, 3, axis=0)
        grad_in, grad_side, grad_down = grad_in.T, grad_side.T, grad_down.T
        scale = lax.rsqrt(jnp.mean(inputs * inputs, axis=-1, keepdims=True) + EPS)
        weighted = gain_first * back
        gain_in = jnp.sum(back * inputs * scale, axis=0)
        grad_input = (
            d_residual
            + scale * weighted
            - inputs * scale**3 * jnp.mean(weighted * inputs, axis=-1, keepdims=True)
        )
        gain_grads = lax.psum_scatter(
            jnp.stack([gain_in, gain_mid]), ("dp", "mp"), scatter_dimension=1, tiled=True
        )
    gate_rows = small_grads[: heads * bite]
    return (
        layer_output,
        grad_input,
        gain_grads[0],
        gain_grads[1],
        grad_in,
        grad_side,
        grad_out,
        gate_rows[:, :block].reshape(heads, bite, block),
        gate_rows[:, lane_a : lane_a + block].reshape(heads, bite, block),
        small_grads[heads * bite : heads * bite + 2 * CONV // parts, :width],
        grad_gate,
        grad_up,
        grad_down,
    )


def solution(mesh):
    rows = P(("dp", "mp"), None)
    return jax.shard_map(
        on_device,
        mesh=mesh,
        in_specs=(
            rows,
            rows,
            P(("dp", "mp")),
            P(("dp", "mp")),
            P("dp", "mp"),
            P("dp", "mp"),
            P("mp", "dp"),
            P("mp", "dp", None),
            P("mp", "dp", None),
            P("dp", "mp"),
            P("dp", "mp"),
            P("dp", "mp"),
            P("mp", "dp"),
            P("dp", None),
        ),
        out_specs=(
            rows,
            rows,
            P(("dp", "mp")),
            P(("dp", "mp")),
            P("dp", "mp"),
            P("dp", "mp"),
            P("mp", "dp"),
            P("mp", "dp", None),
            P("mp", "dp", None),
            P("dp", "mp"),
            P("dp", "mp"),
            P("dp", "mp"),
            P("mp", "dp"),
        ),
        check_vma=False,
    )
```

```python
import functools
import typing

import jax
import jax.numpy as jnp
from jax import lax
from jax.experimental import pallas as pl
from jax.experimental.pallas import tpu as pltpu
from jax.sharding import PartitionSpec as P

CONV = 4
AHEAD = 3
SUM_AHEAD = 3
EPS = 1e-06
DECAY = 8.0
HALF = jnp.bfloat16
SINGLE = jnp.float32
MESH = pl.DeviceIdType.MESH
VMEM_BYTES = 60 * 1024 * 1024
GELU_C = 0.7978845608028654
GELU_K = 0.044715


def dot_nn(left, right):
    return lax.dot_general(
        left, right, (((1,), (0,)), ((), ())), preferred_element_type=SINGLE
    )


def dot_nt(left, right):
    return lax.dot_general(
        left, right, (((1,), (1,)), ((), ())), preferred_element_type=SINGLE
    )


def dot_tn(left, right):
    return lax.dot_general(
        left, right, (((0,), (0,)), ((), ())), preferred_element_type=SINGLE
    )


def gelu(v):
    return 0.5 * v * (1.0 + jnp.tanh(GELU_C * (v + GELU_K * v * v * v)))


def gelu_both(v):
    square = v * v
    t = jnp.tanh(GELU_C * (v + GELU_K * v * square))
    value = 0.5 * v * (1.0 + t)
    slope = 0.5 * (1.0 + t) + 0.5 * v * (1.0 - t * t) * (GELU_C * (1.0 + 3.0 * GELU_K * square))
    return value, slope


def flip(me, mask, count):
    place = me
    bit = 1
    while bit < count:
        if mask & bit:
            place = place + (1 - 2 * ((me // bit) % 2)) * bit
        bit *= 2
    return place


def ring_peers(axis):
    me, count = lax.axis_index(axis), lax.axis_size(axis)
    return [(k, {axis: (me + k) % count}) for k in range(1, count)]


def greet(peers):
    barrier = pltpu.get_barrier_semaphore()
    for _, peer in peers:
        pl.semaphore_signal(barrier, inc=1, device_id=peer, device_id_type=MESH)
    pl.semaphore_wait(barrier, len(peers))


def exchange(peers, source, target, send, recv):
    return [
        pltpu.make_async_remote_copy(
            src_ref=source(k),
            dst_ref=target(k),
            send_sem=send.at[k],
            recv_sem=recv.at[k],
            device_id=peer,
            device_id_type=MESH,
        )
        for k, peer in peers
    ]


def each(copies, act):
    for copy in copies:
        act(copy)


START, LAND, SENT = (lambda c: c.start(), lambda c: c.wait_recv(), lambda c: c.wait_send())


def gather_plan(count):
    bits = [1 << b for b in range(count.bit_length() - 1)]
    outer = bits[1:]
    orders = (outer + bits[:1], outer[::-1] + bits[:1])
    sends = []
    for half, order in enumerate(orders):
        for stage, bit in enumerate(order):
            for pick in range(1 << stage):
                mask = sum(order[j] for j in range(stage) if pick >> j & 1)
                sends.append((bin(mask).count("1"), half, mask, bit))
    sends.sort(key=lambda s: s[0])
    return bits, [s[1:] for s in sends]


class PlaneGather:
    COUNT = 8

    @staticmethod
    def scratch():
        count = PlaneGather.COUNT
        return [
            pltpu.SemaphoreType.DMA,
            pltpu.SemaphoreType.DMA((2, count)),
            pltpu.SemaphoreType.DMA((2, count)),
        ]

    def __init__(self, x_ref, o_ref, scratch):
        self.x, self.o = x_ref, o_ref
        self.own_sem, self.send, self.recv = scratch
        self.me = lax.axis_index("mp")
        self.bits, self.plan = gather_plan(self.COUNT)

    def own(self):
        rows = self.x.shape[0]
        span = pl.ds(pl.multiple_of(self.me * rows, rows), rows)
        return pltpu.make_async_copy(self.x, self.o.at[span], self.own_sem)

    def copy(self, half, mask, bit):
        rows = self.x.shape[0] // 2
        slot = 2 * flip(self.me, mask, self.COUNT) + half
        span = pl.ds(pl.multiple_of(slot * rows, rows), rows)
        return pltpu.make_async_remote_copy(
            src_ref=self.o.at[span] if mask else self.x.at[pl.ds(half * rows, rows)],
            dst_ref=self.o.at[span],
            send_sem=self.send.at[half, mask | bit],
            recv_sem=self.recv.at[half, mask | bit],
            device_id={"mp": flip(self.me, bit, self.COUNT)},
            device_id_type=MESH,
        )

    def level(self, depth):
        landed = set()
        for half, mask, bit in self.plan:
            if bin(mask).count("1") != depth:
                continue
            if mask and (half, mask) not in landed:
                landed.add((half, mask))
                self.arrived(half, mask)
            self.copy(half, mask, bit).start()

    def arrived(self, half, mask):
        for other, before, bit in self.plan:
            if other == half and before | bit == mask:
                self.copy(half, before, bit).wait_recv()

    def start(self):
        self.own().start()
        self.level(0)

    def finish(self):
        waited = {(half, mask) for half, mask, _ in self.plan}
        for half, mask, bit in self.plan:
            if (half, mask | bit) not in waited:
                self.copy(half, mask, bit).wait_recv()
        for entry in self.plan:
            self.copy(*entry).wait_send()
        self.own().wait()


class LineGather:
    COUNT = 4
    ENDS = ((0, 3), (3, 0))

    @staticmethod
    def scratch(pieces):
        shapes = ((pieces, 4), (pieces, 4), (pieces,))
        return [pltpu.SemaphoreType.DMA(shape) for shape in shapes]

    def __init__(self, targets, pieces, scratch):
        self.chunks, self.of = [], []
        for target, count in zip(targets, pieces):
            rows = target.shape[1] // count
            first = len(self.chunks)
            self.chunks += [(target, pl.ds(p * rows, rows)) for p in range(count)]
            self.of.append(range(first, len(self.chunks)))
        self.send, self.recv, self.onward = scratch
        self.me = lax.axis_index("dp")

    def direct(self, c, to):
        target, span = self.chunks[c]
        return pltpu.make_async_remote_copy(
            src_ref=target.at[self.me, span],
            dst_ref=target.at[self.me, span],
            send_sem=self.send.at[c, to],
            recv_sem=self.recv.at[c, self.me],
            device_id={"dp": to},
            device_id_type=MESH,
        )

    def handed(self, c, block, to):
        target, span = self.chunks[c]
        return pltpu.make_async_remote_copy(
            src_ref=target.at[block, span],
            dst_ref=target.at[block, span],
            send_sem=self.onward.at[c],
            recv_sem=self.recv.at[c, block],
            device_id={"dp": to},
            device_id_type=MESH,
        )

    def sends_to(self, to):
        senders = [z for z in range(self.COUNT) if z != to and (z, to) not in self.ENDS]
        return functools.reduce(jnp.logical_or, [self.me == z for z in senders])

    def start(self, chunks):
        for c in chunks:
            for to in range(self.COUNT):
                pl.when(self.sends_to(to))(lambda c=c, to=to: self.direct(c, to).start())

    def hand_on(self, chunks):
        for c in chunks:
            for first, last in self.ENDS:
                middle = 2 if last == 3 else 1

                @pl.when(self.me == middle)
                def _(c=c, first=first, last=last):
                    copy = self.handed(c, first, last)
                    copy.wait_recv()
                    copy.start()

    def begin(self, ahead):
        self.ahead, self.done = ahead, 0
        self.start(range(ahead))

    def tick(self, count=1):
        for _ in range(count):
            self.hand_on([self.done])
            if self.done + self.ahead < len(self.chunks):
                self.start([self.done + self.ahead])
            self.done += 1

    def landed(self, chunks):
        for c in chunks:
            for block in range(self.COUNT):
                early = 2 if block == 0 else 1 if block == 3 else None
                waits = self.me != block
                if early is not None:
                    waits = jnp.logical_and(waits, self.me != early)
                pl.when(waits)(lambda c=c, block=block: self.handed(c, block, 0).wait_recv())

    def settle(self):
        for c in range(len(self.chunks)):
            for to in range(self.COUNT):
                pl.when(self.sends_to(to))(lambda c=c, to=to: self.direct(c, to).wait_send())
            pl.when(jnp.logical_or(self.me == 1, self.me == 2))(
                lambda c=c: self.handed(c, 0, 0).wait_send()
            )


def kernel_params(collective_id):
    return pltpu.CompilerParams(
        collective_id=collective_id, has_side_effects=True, vmem_limit_bytes=VMEM_BYTES
    )


def sharing(o_ref, sems):
    send_mp, recv_mp, send_dp, recv_dp = sems
    count = lax.axis_size("mp")
    first = lax.axis_index("dp") * count
    place = first + lax.axis_index("mp")
    mine = lambda k: o_ref.at[place]
    plane = lambda k: o_ref.at[pl.ds(first, count)]
    return (
        exchange(ring_peers("mp"), mine, mine, send_mp, recv_mp),
        exchange(ring_peers("dp"), plane, plane, send_dp, recv_dp),
    )


def beside_products(pairs, when=None, act=None):
    for left, right, out in pairs:
        tokens, rows = left.shape
        tile = min(256, rows)

        def body(left_tile, out_tile):
            if act is not None:
                pl.when(pl.program_id(0) == when)(act)
            out_tile[...] = dot_tn(left_tile[...], right[...]).astype(out_tile.dtype)

        pltpu.emit_pipeline(
            body,
            grid=(rows // tile,),
            in_specs=[pl.BlockSpec((tokens, tile), lambda i: (0, i))],
            out_specs=[pl.BlockSpec((tile, right.shape[1]), lambda i: (i, 0))],
        )(left, out)


class PlaneSum:
    COUNT = 8
    ORDER = (3, 1, 2, 0)
    LINKS = ((3, 0, 2), (3, 1, 1), (1, 1, 1), (2, 0, 2), (1, 0, 1), (2, 1, 2))

    @staticmethod
    def scratch(rows, width):
        middle = rows // 2
        return [
            pltpu.VMEM((rows, width), SINGLE),
            pltpu.VMEM((2, middle, width), SINGLE),
            pltpu.VMEM((2, rows, width), HALF),
            pltpu.VMEM((4, rows, width), HALF),
            pltpu.VMEM((6, middle, width), HALF),
            pltpu.VMEM((6, middle, width), HALF),
            pltpu.SemaphoreType.DMA((4,)),
            pltpu.SemaphoreType.DMA((4,)),
            pltpu.SemaphoreType.DMA((6,)),
            pltpu.SemaphoreType.DMA((6,)),
        ]

    def __init__(self, products, tile, lefts, rights, scratch):
        self.terms = list(zip(lefts, rights, products))
        self.tile = tile
        self.acc, self.side, self.core_out, self.core_in = scratch[:4]
        self.link_out, self.link_in = scratch[4:6]
        self.core_send, self.core_recv, self.link_send, self.link_recv = scratch[6:]
        self.rows, self.width = self.acc.shape
        self.halves = (slice(0, self.rows // 2), slice(self.rows // 2, self.rows))
        self.me = lax.axis_index("mp")

    def tiles(self, step):
        def body(t, carry):
            step(t, pl.ds(pl.multiple_of(t * self.tile, self.tile), self.tile))
            return carry

        lax.fori_loop(0, self.width // self.tile, body, 0)

    def partial(self, slot, t, columns):
        span = pl.ds(pl.multiple_of(slot * self.rows, self.rows), self.rows)
        value = None
        for left, right, product in self.terms:
            term = product(left[span, :], right, t, columns)
            value = term if value is None else value + term
        return value

    def core_copy(self, c):
        return pltpu.make_async_remote_copy(
            src_ref=self.core_out.at[self.ORDER.index(c) % 2],
            dst_ref=self.core_in.at[c],
            send_sem=self.core_send.at[c],
            recv_sem=self.core_recv.at[c],
            device_id={"mp": flip(self.me, 1, self.COUNT)},
            device_id_type=MESH,
        )

    def link_copy(self, index):
        return pltpu.make_async_remote_copy(
            src_ref=self.link_out.at[index],
            dst_ref=self.link_in.at[index],
            send_sem=self.link_send.at[index],
            recv_sem=self.link_recv.at[index],
            device_id={"mp": flip(self.me, 2 * self.LINKS[index][2], self.COUNT)},
            device_id_type=MESH,
        )

    def send(self, c):
        place = self.ORDER.index(c)
        if place >= 2:
            self.core_copy(self.ORDER[place - 2]).wait_send()
        slot = flip(self.me, 2 * c + 1, self.COUNT)

        def step(t, columns):
            self.core_out[place % 2, :, columns] = self.partial(slot, t, columns).astype(HALF)

        self.tiles(step)
        self.core_copy(c).start()

    def take(self, c):
        self.core_copy(c).wait_recv()
        slot = flip(self.me, 2 * c, self.COUNT)
        ways = [i for i in range(4) if self.LINKS[i][0] == c]
        kept = [h for h in (0, 1) if c and h not in [self.LINKS[i][1] for i in ways]]

        def step(t, columns):
            value = self.partial(slot, t, columns) + self.core_in[c, :, columns].astype(SINGLE)
            if c == 0:
                self.acc[:, columns] = value
            for i in ways:
                self.link_out[i, :, columns] = value[self.halves[self.LINKS[i][1]]].astype(HALF)
            for h in kept:
                self.side[h, :, columns] = value[self.halves[h]]

        self.tiles(step)
        for i in ways:
            self.link_copy(i).start()

    def spread(self, between=lambda: None):
        self.send(3)
        self.send(1)
        self.take(3)
        self.send(2)
        self.take(1)
        between()
        self.send(0)
        self.take(2)
        self.take(0)
        self.relay()

    def relay(self):
        for index, landed, half in ((4, 0, 0), (5, 1, 1)):
            self.link_copy(landed).wait_recv()

            def step(t, columns):
                value = self.side[half, :, columns]
                value = value + self.link_in[landed, :, columns].astype(SINGLE)
                self.link_out[index, :, columns] = value.astype(HALF)

            self.tiles(step)
            self.link_copy(index).start()

    def finish(self, out_ref):
        for index in (2, 3, 4, 5):
            self.link_copy(index).wait_recv()

        def step(t, columns):
            for half, (one, two) in enumerate(((3, 4), (2, 5))):
                value = self.acc[self.halves[half], columns]
                value = value + self.link_in[one, :, columns].astype(SINGLE)
                value = value + self.link_in[two, :, columns].astype(SINGLE)
                out_ref[self.halves[half], columns] = value

        self.tiles(step)
        for c in self.ORDER[2:]:
            self.core_copy(c).wait_send()
        for index in range(6):
            self.link_copy(index).wait_send()


class LineSum:
    COUNT = 4

    @staticmethod
    def scratch(pieces):
        shapes = ((pieces, 4), (pieces, 4), (pieces,), (pieces,))
        return [pltpu.SemaphoreType.DMA(shape) for shape in shapes] + [pltpu.SemaphoreType.DMA]

    def __init__(self, jobs, scratch):
        self.jobs, self.chunks, self.of = jobs, [], []
        for job in jobs:
            _, landed, _, pieces, _, _ = job
            rows = landed.shape[1] // pieces
            first = len(self.chunks)
            self.chunks += [(job, p, rows) for p in range(pieces)]
            self.of.append(range(first, len(self.chunks)))
        self.send, self.recv, self.relay_send, self.relay_recv, self.load_sem = scratch
        self.me = lax.axis_index("dp")

    def part(self, c, block):
        (source, landed, *_), p, rows = self.chunks[c]
        return source.at[pl.ds(pl.multiple_of(block * landed.shape[1] + p * rows, 16), rows)]

    def place(self, c, sender):
        (_, landed, *_), p, rows = self.chunks[c]
        return landed.at[sender, pl.ds(p * rows, rows)]

    def relay(self, c):
        (*_, relay, _), p, _ = self.chunks[c]
        return relay.at[p]

    def direct(self, c, to, source=None):
        return pltpu.make_async_remote_copy(
            src_ref=self.part(c, to) if source is None else source,
            dst_ref=self.place(c, self.me),
            send_sem=self.send.at[c, to],
            recv_sem=self.recv.at[c, self.me],
            device_id={"dp": to},
            device_id_type=MESH,
        )

    def by_middle(self, c, block, to):
        return pltpu.make_async_remote_copy(
            src_ref=self.part(c, block),
            dst_ref=self.relay(c),
            send_sem=self.relay_send.at[c],
            recv_sem=self.relay_recv.at[c],
            device_id={"dp": to},
            device_id_type=MESH,
        )

    def among(self, places):
        return functools.reduce(jnp.logical_or, [self.me == z for z in places])

    DIRECT = ((1,), (0, 2, 3), (0, 1, 3), (2,))
    ROUND = ((0, 3, 1), (3, 0, 2))

    def start(self, chunks, places=(0, 1, 2, 3)):
        for c in chunks:
            for end, block, middle in self.ROUND:
                if end in places:
                    pl.when(self.me == end)(
                        lambda c=c, block=block, middle=middle: self.by_middle(
                            c, block, middle
                        ).start()
                    )
            for to, senders in enumerate(self.DIRECT):
                senders = [z for z in senders if z in places]
                if senders:
                    pl.when(self.among(senders))(lambda c=c, to=to: self.direct(c, to).start())

    def hand_on(self, chunks):
        for c in chunks:
            *_, other = self.chunks[c][0]
            for _, block, middle in self.ROUND:

                @pl.when(self.me == middle)
                def _(c=c, block=block, middle=middle, other=other):
                    mine = pltpu.make_async_copy(self.part(c, block), other, self.load_sem)
                    mine.start()
                    self.by_middle(c, block, middle).wait_recv()
                    mine.wait()
                    relay = self.relay(c)
                    value = relay[...].astype(SINGLE) + other[...].astype(SINGLE)
                    relay[...] = value.astype(HALF)
                    self.direct(c, block, relay).start()

    def begin(self, ahead, places):
        self.ahead, self.done = ahead, 0
        self.start(range(ahead), places)

    def tick(self, count=1):
        for _ in range(count):
            self.hand_on([self.done])
            if self.done + self.ahead < len(self.chunks):
                self.start([self.done + self.ahead])
            self.done += 1

    SENDERS = ((1, 2), (0, 2, 3), (0, 1, 3), (1, 2))

    def collect(self, j):
        source, landed, target, _, _, _ = self.jobs[j]
        turned = target.shape[-1] != landed.shape[-1]
        split = len(target.shape) == 3
        for c in self.of[j]:
            for sender in range(self.COUNT):
                takers = [z for z in range(self.COUNT) if sender in self.SENDERS[z]]
                pl.when(self.among(takers))(
                    lambda c=c, sender=sender: self.wait_from(c, sender)
                )
        _, rows, columns = landed.shape
        tile = rows // 2 if rows >= 256 else rows
        out_spec = pl.BlockSpec((tile, columns), lambda t: (t, 0))
        if split:
            shape = (1, columns, tile) if turned else (1, tile, columns)
            out_spec = pl.BlockSpec(shape, lambda t: (t, 0, 0))

        def add(*refs):
            value = refs[0][...].astype(SINGLE)
            for ref in refs[1:-1]:
                value = value + ref[0].astype(SINGLE)
            if split:
                refs[-1][0] = value.T if turned else value
            else:
                refs[-1][...] = value

        def run(senders):
            pltpu.emit_pipeline(
                add,
                grid=(rows // tile,),
                in_specs=[
                    pl.BlockSpec((tile, columns), lambda t: (self.me * (rows // tile) + t, 0))
                ]
                + [
                    pl.BlockSpec((1, tile, columns), lambda t, sender=sender: (sender, t, 0))
                    for sender in senders
                ],
                out_specs=[out_spec],
            )(source, *[landed] * len(senders), target)

        pl.when(self.among((0, 3)))(lambda: run((1, 2)))
        pl.when(self.among((1, 2)))(lambda: run((0, 3 - self.me, 3)))

    def wait_from(self, c, sender):
        pltpu.make_async_remote_copy(
            src_ref=self.place(c, sender),
            dst_ref=self.place(c, sender),
            send_sem=self.relay_send.at[c],
            recv_sem=self.recv.at[c, sender],
            device_id={"dp": 0},
            device_id_type=MESH,
        ).wait_recv()

    def settle(self):
        for c in range(len(self.chunks)):
            for to, senders in enumerate(self.DIRECT):
                pl.when(self.among(senders))(lambda c=c, to=to: self.direct(c, to).wait_send())
            for end, block, middle in self.ROUND:
                pl.when(self.me == end)(
                    lambda c=c, block=block, middle=middle: self.by_middle(
                        c, block, middle
                    ).wait_send()
                )
                pl.when(self.me == middle)(
                    lambda c=c, block=block: self.direct(c, block, self.relay(c)).wait_send()
                )


def positions(lens_ref, first, shape):
    place = lax.broadcasted_iota(jnp.int32, shape, 0) + first
    begin = jnp.zeros(shape, jnp.int32)
    total = 0
    for j in range(lens_ref.shape[1]):
        total = total + lens_ref[0, j]
        begin = jnp.where(place >= total, total, begin)
    return place - begin, place < total


def split_dot(dot, left, right):
    high = left.astype(HALF)
    low = (left - high.astype(SINGLE)).astype(HALF)
    return dot(high, right) + dot(low, right)


def lane_tiles(width):
    return [(t, t * 128, min(128, width - t * 128)) for t in range(-(-width // 128))]


def put_tiles(ref, value):
    for t, first, lanes in lane_tiles(value.shape[1]):
        ref[t, :, :lanes] = value[:, first : first + lanes]


def scan_start(tiles, lanes):
    return [(jnp.zeros((lanes, 128), SINGLE), jnp.ones((lanes, 128), SINGLE)) for _ in tiles]


def sigmoid(v):
    return 1.0 / (1.0 + jnp.exp(-v))


def forward_step(
    step,
    lens_ref,
    x_ref,
    gain_ref,
    pack_ref,
    bin_ref,
    ba_ref,
    chan_ref,
    n1_ref,
    bx_ref,
    by_ref,
    conv_ref,
    gi_ref,
    ra_ref,
    h_ref,
    ob_ref,
    taps,
    coef,
    drive,
    carry,
):
    rows, width = bx_ref.shape
    depth = pack_ref.shape[2]
    lanes = 8
    span = rows // lanes

    @pl.when(step == 0)
    def _():
        taps[...] = jnp.zeros_like(taps)
        carry[...] = jnp.zeros_like(carry)
        coef[...] = jnp.zeros_like(coef)
        drive[...] = jnp.zeros_like(drive)

    x = x_ref[...].astype(SINGLE)
    scale = lax.rsqrt(jnp.mean(x * x, axis=-1, keepdims=True) + EPS)
    normed = (x * scale * gain_ref[...]).astype(HALF)
    n1_ref[...] = normed
    total = None
    for d in range(pack_ref.shape[0]):
        term = dot_nt(normed[:, d * depth : (d + 1) * depth], pack_ref[d, : 2 * width, :])
        total = term if total is None else total + term
    bx = total[:, :width].astype(HALF)
    by = total[:, width:]
    bx_ref[...] = bx
    by_ref[...] = by
    pos, live = positions(lens_ref, step * rows, (rows, width))
    taps[0:8, :] = taps[rows : rows + 8, :]
    taps[8 : rows + 8, :] = bx.astype(SINGLE)
    conv = jnp.zeros((rows, width), SINGLE) + chan_ref[CONV : CONV + 1, :]
    for k in range(CONV):
        moved = taps[8 - k : 8 - k + rows, :]
        conv = conv + jnp.where(pos >= k, moved * chan_ref[k : k + 1, :], 0.0)
    conv_ref[...] = conv
    high = conv.astype(HALF)
    low = (conv - high.astype(SINGLE)).astype(HALF)
    gate_in = sigmoid(
        dot_nn(high, bin_ref[...]) + dot_nn(low, bin_ref[...]) + chan_ref[CONV + 1 : CONV + 2, :]
    )
    gate_a = sigmoid(
        dot_nn(high, ba_ref[...]) + dot_nn(low, ba_ref[...]) + chan_ref[CONV + 2 : CONV + 3, :]
    )
    gi_ref[...] = gate_in
    ra_ref[...] = gate_a
    decay = jnp.exp(-DECAY * gate_a * chan_ref[CONV + 4 : CONV + 5, :])
    root = jnp.sqrt(1.0 - decay * decay)
    put_tiles(coef, jnp.where(pos == 0, 0.0, decay))
    put_tiles(drive, gate_in * conv * root)
    tiles = lane_tiles(width)

    def scan(i, state):
        at = pl.ds(i, lanes, stride=span)
        result = []
        for (t, _, _), (h, prod) in zip(tiles, state):
            a = coef[t, at, :]
            h = a * h + drive[t, at, :]
            prod = prod * a
            drive[t, at, :] = h
            coef[t, at, :] = prod
            result.append((h, prod))
        return result

    state = lax.fori_loop(0, span, scan, scan_start(tiles, lanes), unroll=4)
    for (t, first, used), (h, prod) in zip(tiles, state):
        running = carry[t, 0:1, :]
        for s in range(lanes):
            at = slice(s * span, (s + 1) * span)
            value = drive[t, at, :] + coef[t, at, :] * running
            h_ref[at, first : first + used] = value[:, :used]
            running = h[s : s + 1, :] + prod[s : s + 1, :] * running
        carry[t, 0:1, :] = running
    mixed = h_ref[...].astype(HALF).astype(SINGLE)
    ob_ref[...] = jnp.where(live, gelu(by) * mixed, 0.0).astype(HALF)


def forward_kernel(*refs):
    forward_step(pl.program_id(0), *refs)


def forward_scratch(rows, width):
    tiles = len(lane_tiles(width))
    return [
        pltpu.VMEM((rows + 8, width), SINGLE),
        pltpu.VMEM((tiles, rows, 128), SINGLE),
        pltpu.VMEM((tiles, rows, 128), SINGLE),
        pltpu.VMEM((tiles, 8, 128), SINGLE),
    ]


def forward_channels(lens, x_all, gain, pack, blocks_in, blocks_a, chan):
    tokens, model = x_all.shape
    width = chan.shape[1]
    count = lax.axis_size("mp")
    rows = tokens // count
    whole = lambda shape: pl.BlockSpec(shape, lambda i: (0,) * len(shape))
    part = pl.BlockSpec((rows, width), lambda i: (i, 0))
    full = lambda kind: jax.ShapeDtypeStruct((tokens, width), kind)
    return pl.pallas_call(
        forward_kernel,
        grid=(count,),
        out_shape=(
            jax.ShapeDtypeStruct((tokens, model), HALF),
            full(HALF),
            full(SINGLE),
            full(SINGLE),
            full(SINGLE),
            full(SINGLE),
            full(SINGLE),
            full(HALF),
        ),
        in_specs=[
            pl.BlockSpec(memory_space=pltpu.SMEM),
            pl.BlockSpec((rows, model), lambda i: (i, 0)),
            whole(gain.shape),
            whole(pack.shape),
            whole(blocks_in.shape),
            whole(blocks_a.shape),
            whole(chan.shape),
        ],
        out_specs=(pl.BlockSpec((rows, model), lambda i: (i, 0)),) + (part,) * 7,
        scratch_shapes=forward_scratch(rows, width),
        compiler_params=pltpu.CompilerParams(vmem_limit_bytes=VMEM_BYTES),
        cost_estimate=pl.CostEstimate(
            flops=2 * tokens * model * 2 * width,
            bytes_accessed=tokens * (model * 4 + width * 24),
            transcendentals=8 * tokens * width,
        ),
        name="forward_channels",
    )(lens, x_all, gain, pack, blocks_in, blocks_a, chan)


def by_parts(left, right, t, columns):
    return dot_nn(left, right[t])


def backward_step(
    step,
    steps,
    lens_ref,
    dt_ref,
    pack_ref,
    bin_ref,
    ba_ref,
    chan_ref,
    bx_ref,
    by_ref,
    conv_ref,
    gi_ref,
    ra_ref,
    h_ref,
    hprev_ref,
    dbx_ref,
    dby_ref,
    gin_ref,
    ga_ref,
    gchan_ref,
    lift,
    coef,
    drive,
    carry,
):
    chunk = steps - 1 - step
    rows, width = bx_ref.shape
    depth = pack_ref.shape[2]
    lanes = 8
    span = rows // lanes

    @pl.when(step == 0)
    def _():
        lift[...] = jnp.zeros_like(lift)
        carry[...] = jnp.zeros_like(carry)
        coef[...] = jnp.zeros_like(coef)
        drive[...] = jnp.zeros_like(drive)
        gin_ref[...] = jnp.zeros_like(gin_ref)
        ga_ref[...] = jnp.zeros_like(ga_ref)
        gchan_ref[...] = jnp.zeros_like(gchan_ref)

    d_out = None
    for d in range(pack_ref.shape[0]):
        term = dot_nt(dt_ref[:, d * depth : (d + 1) * depth], pack_ref[d])
        d_out = term if d_out is None else d_out + term
    pos, live = positions(lens_ref, chunk * rows, (rows, width))
    by = by_ref[...]
    h = h_ref[...]
    side, slope = gelu_both(by)
    d_out = jnp.where(live, d_out, 0.0)
    dby_ref[...] = (d_out * h.astype(HALF).astype(SINGLE) * slope).astype(HALF)
    gate_a = ra_ref[...]
    soft = chan_ref[CONV + 4 : CONV + 5, :]
    decay = jnp.exp(-DECAY * gate_a * soft)
    put_tiles(coef, jnp.where(pos == 0, 0.0, decay))
    put_tiles(drive, (d_out * side).astype(HALF).astype(SINGLE))
    tiles = lane_tiles(width)

    def scan(j, state):
        at = pl.ds(span - 1 - j, lanes, stride=span)
        result = []
        for (t, _, _), (after, prod) in zip(tiles, state):
            a = coef[t, at, :]
            lam = drive[t, at, :] + after
            drive[t, at, :] = lam
            coef[t, at, :] = prod
            result.append((a * lam, prod * a))
        return result

    state = lax.fori_loop(0, span, scan, scan_start(tiles, lanes), unroll=4)
    for (t, first, used), (after, prod) in zip(tiles, state):
        running = carry[t, 0:1, :]
        for s in reversed(range(lanes)):
            at = slice(s * span, (s + 1) * span)
            value = drive[t, at, :] + coef[t, at, :] * running
            lift[at, first : first + used] = value[:, :used]
            running = after[s : s + 1, :] + prod[s : s + 1, :] * running
        carry[t, 0:1, :] = running
    lam = lift[0:rows, :]
    last = jnp.where(chunk > 0, hprev_ref[7:8, :], 0.0)
    before = jnp.concatenate([last, h[: rows - 1, :]], axis=0)
    before = jnp.where(pos == 0, 0.0, before)
    conv = conv_ref[...]
    gate_in = gi_ref[...]
    root = jnp.sqrt(1.0 - decay * decay)
    d_decay = lam * before - lam * gate_in * conv * decay / root
    d_log = d_decay * decay
    d_a = d_log * (-DECAY * soft)
    d_in = lam * conv * root
    d_logit_in = d_in * gate_in * (1.0 - gate_in)
    d_logit_a = d_a * gate_a * (1.0 - gate_a)
    d_conv = (
        lam * gate_in * root
        + split_dot(dot_nt, d_logit_in, bin_ref[...])
        + split_dot(dot_nt, d_logit_a, ba_ref[...])
    )
    low = conv.astype(HALF)
    gin_ref[...] += dot_tn(low, d_logit_in.astype(HALF))
    ga_ref[...] += dot_tn(low, d_logit_a.astype(HALF))
    lift[0:rows, :] = d_conv
    bx = bx_ref[...].astype(SINGLE)
    d_bx = jnp.zeros((rows, width), SINGLE)
    for k in range(CONV):
        if k:
            ahead, _ = positions(lens_ref, chunk * rows + k, (rows, width))
            moved = jnp.where(ahead >= k, lift[k : k + rows, :], 0.0)
        else:
            moved = d_conv
        d_bx = d_bx + moved * chan_ref[k : k + 1, :]
        gchan_ref[k : k + 1, :] += jnp.sum(moved * bx, axis=0, keepdims=True)
    dbx_ref[...] = d_bx.astype(HALF)
    lift[rows : rows + 8, :] = d_conv[0:8, :]
    sums = (d_conv, d_logit_in, d_logit_a, d_log * gate_a)
    for j, value in enumerate(sums):
        gchan_ref[CONV + j : CONV + j + 1, :] += jnp.sum(value, axis=0, keepdims=True)


def backward_kernel(*refs):
    refs = list(refs)
    inputs, (ob_ref, n1_ref), outputs, grads_ref, grads, scratch = (
        refs[:13], refs[13:15], refs[15:20], refs[20], refs[21], refs[22:],
    )
    step, steps = pl.program_id(0), pl.num_programs(0)

    @pl.when(step == 0)
    def _():
        grads[...] = jnp.zeros_like(grads)

    backward_step(step, steps, *inputs, *outputs, *scratch)
    dt_ref, (dbx_ref, dby_ref) = inputs[1], outputs[:2]
    width, depth = dbx_ref.shape[1], grads.shape[2]
    lefts = (dbx_ref[...], dby_ref[...], ob_ref[...])
    for d in range(grads.shape[0]):
        columns = slice(d * depth, (d + 1) * depth)
        rights = (n1_ref[:, columns], n1_ref[:, columns], dt_ref[:, columns])
        for j, (left, right) in enumerate(zip(lefts, rights)):
            grads[d, j * width : (j + 1) * width, :] += dot_tn(left, right)

    @pl.when(step == steps - 1)
    def _():
        grads_ref[...] = grads[...].astype(HALF)


def backward_channels(lens, dt_all, pack, blocks_in, blocks_a, chan, saved):
    bx, by, conv, gate_in, gate_a, h, ob, n1 = saved
    tokens, model = dt_all.shape
    width = chan.shape[1]
    count = lax.axis_size("mp")
    rows = tokens // count
    last = count - 1
    whole = lambda shape: pl.BlockSpec(shape, lambda i: (0,) * len(shape))
    part = pl.BlockSpec((rows, width), lambda i: (last - i, 0))
    across = pl.BlockSpec((rows, model), lambda i: (last - i, 0))
    before = pl.BlockSpec(
        (8, width), lambda i: (jnp.maximum((last - i) * (rows // 8) - 1, 0), 0)
    )
    full = jax.ShapeDtypeStruct((tokens, width), HALF)
    square = jax.ShapeDtypeStruct((width, width), SINGLE)
    grads = (pack.shape[0], 3 * width, pack.shape[2])
    return pl.pallas_call(
        backward_kernel,
        grid=(count,),
        out_shape=(
            full,
            full,
            square,
            square,
            jax.ShapeDtypeStruct((8, width), SINGLE),
            jax.ShapeDtypeStruct(grads, HALF),
        ),
        in_specs=[
            pl.BlockSpec(memory_space=pltpu.SMEM),
            across,
            whole(pack.shape),
            whole(blocks_in.shape),
            whole(blocks_a.shape),
            whole(chan.shape),
            part,
            part,
            part,
            part,
            part,
            part,
            before,
            part,
            across,
        ],
        out_specs=(
            part,
            part,
            whole((width, width)),
            whole((width, width)),
            whole((8, width)),
            whole(grads),
        ),
        scratch_shapes=[pltpu.VMEM(grads, SINGLE)] + forward_scratch(rows, width),
        compiler_params=pltpu.CompilerParams(vmem_limit_bytes=VMEM_BYTES),
        cost_estimate=pl.CostEstimate(
            flops=8 * tokens * model * width,
            bytes_accessed=tokens * (model * 4 + width * 28),
            transcendentals=8 * tokens * width,
        ),
        name="backward_channels",
    )(
        lens, dt_all, pack, blocks_in, blocks_a, chan,
        bx, by, conv, gate_in, gate_a, h, h, ob, n1,
    )


def log_one_plus(v):
    total = 1.0 + v
    exact = total - 1.0
    return jnp.where(exact == 0.0, v, jnp.log(total) * (v / jnp.where(exact == 0.0, 1.0, exact)))


def small_weights(small, bin_ref, ba_ref, chan_ref, heads, bite):
    parts = small.shape[0]
    width = bin_ref.shape[0]
    block = width // heads
    at_row = lax.broadcasted_iota(jnp.int32, (block, width), 0)
    at_column = lax.broadcasted_iota(jnp.int32, (block, width), 1)
    each = 2 * CONV // parts
    for d in range(parts):
        value = small[d].astype(SINGLE)
        for h in range(heads):
            place = (at_column == at_row + h * block).astype(HALF)
            for lane, target in ((0, bin_ref), (256, ba_ref)):
                piece = value[h * bite : (h + 1) * bite, lane : lane + block].astype(HALF)
                first = h * block + d * bite
                target[first : first + bite, :] = dot_nn(piece, place)
        row = heads * bite
        chan_ref[d * each : (d + 1) * each, :] = value[row : row + each, :width]
    v = -chan_ref[2 * CONV - 1 : 2 * CONV, :]
    chan_ref[2 * CONV : 2 * CONV + 1, :] = jnp.maximum(v, 0.0) + log_one_plus(
        jnp.exp(-jnp.abs(v))
    )


class LayerIn(typing.NamedTuple):
    lens: typing.Any
    norm_in: typing.Any
    norm_mid: typing.Any
    x: typing.Any
    cot: typing.Any
    blocks_in: typing.Any
    blocks_a: typing.Any
    channels: typing.Any
    w_in: typing.Any
    w_gate: typing.Any
    w_out: typing.Any
    gate: typing.Any
    up: typing.Any
    down: typing.Any


class LayerOut(typing.NamedTuple):
    layer_output: typing.Any
    grad_input: typing.Any
    gain_grads: typing.Any
    x_all: typing.Any
    c_all: typing.Any
    n2_all: typing.Any
    dt_all: typing.Any
    n1: typing.Any
    bx: typing.Any
    by: typing.Any
    conv: typing.Any
    gi: typing.Any
    ra: typing.Any
    h: typing.Any
    ob: typing.Any
    act: typing.Any
    slope: typing.Any
    grad_down: typing.Any
    grad_gate: typing.Any
    grad_up: typing.Any
    grad_out: typing.Any
    grad_pack: typing.Any
    pack4: typing.Any
    small4: typing.Any
    out4: typing.Any
    gate4: typing.Any
    up4: typing.Any
    down4: typing.Any
    landed_down: typing.Any
    landed_gate: typing.Any
    landed_up: typing.Any
    landed_out: typing.Any
    landed_small: typing.Any
    landed_pack: typing.Any
    sum_down: typing.Any
    sum_gate: typing.Any
    sum_up: typing.Any
    sum_out: typing.Any
    sum_small: typing.Any
    sum_pack: typing.Any


WEIGHT_PIECES = (4, 1, 2, 4, 4, 6)
SUM_PIECES = (4, 4, 4, 2, 1, 4)


def small_gradients(small, gin, ga, gchan, chan, heads, bite):
    parts = LineSum.COUNT
    width = gin.shape[0]
    block = width // heads
    each = 2 * CONV // parts
    rows = small.shape[0] // parts
    at_row = lax.broadcasted_iota(jnp.int32, (block, width), 0)
    at_column = lax.broadcasted_iota(jnp.int32, (block, width), 1)
    small[...] = jnp.zeros_like(small)
    v = chan[2 * CONV - 1 : 2 * CONV, :]
    last = 2 * CONV - 1
    gchan[last : last + 1, :] = gchan[last : last + 1, :] * (DECAY * sigmoid(-v))
    for d in range(parts):
        for h in range(heads):
            place = (at_column == at_row + h * block).astype(HALF)
            first = h * block + d * bite
            to = d * rows + h * bite
            for lane, grads in ((0, gin), (256, ga)):
                piece = grads[first : first + bite, :].astype(HALF)
                small[to : to + bite, lane : lane + block] = dot_nt(piece, place)
        to = d * rows + heads * bite
        small[to : to + each, :width] = gchan[d * each : (d + 1) * each, :]


def layer_kernel(*refs):
    refs = list(refs)
    take = lambda n: [refs.pop(0) for _ in range(n)]
    i = LayerIn(*take(len(LayerIn._fields)))
    o = LayerOut(*take(len(LayerOut._fields)))
    tiles, gain, gain_sum, bin_low, ba_low, chan = take(6)
    inputs, own_low, residual, d_res, summed = take(5)
    steps_scratch = take(4)
    gin, ga, gchan, small, turns, turns_dp, turns_mp = take(7)
    relays, others = take(6), take(3)
    load_sem, out_sem, free_sem = take(3)
    share_sems, total_sems = take(4), take(4)
    plane_x = PlaneGather(i.x, o.x_all, take(3))
    plane_c = PlaneGather(i.cot, o.c_all, take(3))
    plane_n = PlaneGather(own_low, o.n2_all, take(3))
    plane_t = PlaneGather(own_low, o.dt_all, take(3))
    shared = take(10)
    line = LineGather(
        (o.pack4, o.small4, o.out4, o.gate4, o.up4, o.down4), WEIGHT_PIECES, take(3)
    )
    pack_at, small_at, out_at, gate_at, up_at, down_at = line.of
    sources = (o.grad_down, o.grad_gate, o.grad_up, o.grad_out, small, o.grad_pack)
    landed = (
        o.landed_down, o.landed_gate, o.landed_up, o.landed_out, o.landed_small, o.landed_pack,
    )
    targets = (o.sum_down, o.sum_gate, o.sum_up, o.sum_out, o.sum_small, o.sum_pack)
    other = [others[j] for j in (0, 0, 0, 1, 2, 1)]
    sums = LineSum(list(zip(sources, landed, targets, SUM_PIECES, relays, other)), take(5))
    outward = [
        pltpu.make_async_copy(own_low, o.layer_output, out_sem.at[0]),
        pltpu.make_async_copy(d_res, o.grad_input, out_sem.at[1]),
    ]
    tokens, model = o.x_all.shape
    rows, count = i.x.shape[0], PlaneGather.COUNT
    width, units = o.bx.shape[1], o.act.shape[1]
    parts, _, depth = o.pack4.shape
    heads = width // i.blocks_in.shape[1]
    bite = i.blocks_in.shape[0] // heads
    level, me = lax.axis_index("dp"), lax.axis_index("mp")

    def copy_of(source, target, j):
        return pltpu.make_async_copy(source, target, load_sem.at[j])

    def load(pairs):
        copies = [copy_of(source, target, j) for j, (source, target) in enumerate(pairs)]
        for copy in copies:
            copy.start()
        for copy in copies:
            copy.wait()

    def stage(w_in, w_gate, w_out, gate, up, down, pack_low, out_low, gate_low, down_low, small_own):
        arrivals = [
            copy_of(source, target, j)
            for j, (source, target) in enumerate(
                (
                    (i.w_in, w_in), (i.w_gate, w_gate), (i.w_out, w_out), (i.gate, gate),
                    (i.up, up), (i.down, down), (i.x, inputs),
                )
            )
        ]
        for copy in arrivals:
            copy.start()
        greet(ring_peers("mp") + ring_peers("dp"))
        plane_x.start()
        for j, ref in enumerate((w_in, w_gate)):
            arrivals[j].wait()
            pack_low[j * width : (j + 1) * width, :] = ref[...].astype(HALF)
        load([(pack_low, o.pack4.at[level])])
        line.begin(AHEAD)
        tiles[level * count + me] = norm_tile()
        within, across_dp = sharing(tiles, share_sems)
        each(within, START)
        each(within, LAND)
        each(across_dp, START)
        small_own[...] = jnp.zeros_like(small_own)
        gate_rows, block = i.blocks_in.shape
        small_own[:gate_rows, :block] = i.blocks_in[...]
        small_own[:gate_rows, 256 : 256 + block] = i.blocks_a[...]
        small_own[gate_rows : gate_rows + i.channels.shape[0], :width] = i.channels[...]
        small[: small_own.shape[0], :] = small_own[...].astype(HALF)
        arrivals[2].wait()
        out_low[...] = w_out[...].astype(HALF)
        load([(small.at[: small_own.shape[0]], o.small4.at[level]), (out_low, o.out4.at[level])])
        line.tick()
        for j, ref, low, target in (
            (3, gate, gate_low, o.gate4), (4, up, gate_low, o.up4), (5, down, down_low, o.down4),
        ):
            arrivals[j].wait()
            low[...] = ref[...].astype(HALF)
            load([(low, target.at[level])])
        arrivals[6].wait()

    def norm_tile():
        bits = i.norm_in.shape[1]
        spot = me % (128 // bits) * bits
        at_column = lax.broadcasted_iota(jnp.int32, (bits, 128), 1)
        place = lax.broadcasted_iota(jnp.int32, (bits, 128), 0) + spot == at_column
        both = jnp.concatenate(
            [i.norm_in[...], i.norm_mid[...], jnp.zeros((6, bits), SINGLE)], axis=0
        )
        return dot_nn(both.astype(HALF), place.astype(HALF))

    pl.run_scoped(
        stage,
        pltpu.VMEM(i.w_in.shape, SINGLE),
        pltpu.VMEM(i.w_gate.shape, SINGLE),
        pltpu.VMEM(i.w_out.shape, SINGLE),
        pltpu.VMEM(i.gate.shape, SINGLE),
        pltpu.VMEM(i.up.shape, SINGLE),
        pltpu.VMEM(i.down.shape, SINGLE),
        pltpu.VMEM(o.pack4.shape[1:], HALF),
        pltpu.VMEM(o.out4.shape[1:], HALF),
        pltpu.VMEM(o.gate4.shape[1:], HALF),
        pltpu.VMEM(o.down4.shape[1:], HALF),
        pltpu.VMEM(o.small4.shape[1:], SINGLE),
    )
    gin[...] = jnp.zeros_like(gin)
    ga[...] = jnp.zeros_like(ga)
    chan[...] = jnp.zeros_like(chan)
    line.tick()
    plane_x.level(1)
    line.tick()
    plane_x.level(2)
    plane_x.finish()
    plane_c.start()
    within, across_dp = sharing(tiles, share_sems)
    each(across_dp, LAND)
    group = 128 // (model // tiles.shape[0])
    for j in range(model // 128):
        value = tiles[group * j]
        for k in range(1, group):
            value = value + tiles[group * j + k]
        gain[:, j * 128 : (j + 1) * 128] = value
    line.tick(2)
    line.landed(pack_at)
    line.landed(small_at)

    part = pl.BlockSpec((rows, width), lambda t: (t, 0))
    across = pl.BlockSpec((rows, model), lambda t: (t, 0))
    tall = pl.BlockSpec((tokens, depth), lambda t: (0, t))

    def temporal(pack, out_w, ob, small4):
        load([(o.pack4, pack), (o.small4, small4)])
        small_weights(small4, gin, ga, chan, heads, bite)
        bin_low[...] = gin[...].astype(HALF)
        ba_low[...] = ga[...].astype(HALF)

        def channels(x_tile, n1, bx, by, conv, gi, ra, h, ob_tile):
            step = pl.program_id(0)
            schedule = {
                1: line.tick,
                3: lambda: (plane_c.level(1), line.tick()),
                6: lambda: (plane_c.level(2), line.tick()),
            }
            for when, act in schedule.items():
                pl.when(step == when)(lambda act=act: (act(), None)[1])
            forward_step(
                step, i.lens, x_tile, gain.at[0:1], pack, bin_low, ba_low, chan,
                n1, bx, by, conv, gi, ra, h, ob_tile, *steps_scratch,
            )
            ob[pl.ds(pl.multiple_of(step * rows, rows), rows), :] = ob_tile[...]

        pltpu.emit_pipeline(
            channels,
            grid=(count,),
            in_specs=[across],
            out_specs=[across] + [part] * 7,
        )(o.x_all, o.n1, o.bx, o.by, o.conv, o.gi, o.ra, o.h, o.ob)
        line.landed(out_at)
        load([(o.out4, out_w)])
        plane = PlaneSum([by_parts], depth, [ob], [out_w], shared)
        plane.spread(line.tick)
        line.tick()
        plane_c.finish()
        line.tick()
        plane.finish(summed)

    pl.run_scoped(
        temporal,
        pltpu.VMEM(o.pack4.shape, HALF),
        pltpu.VMEM(o.out4.shape, HALF),
        pltpu.VMEM((tokens, width), HALF),
        pltpu.VMEM(o.small4.shape, HALF),
    )
    block = 32

    def norm(t, carry):
        at = pl.ds(pl.multiple_of(t * block, block), block)
        value = inputs[at, :].astype(SINGLE) + summed[at, :]
        scale = lax.rsqrt(jnp.mean(value * value, axis=-1, keepdims=True) + EPS)
        residual[at, :] = value
        own_low[at, :] = (value * scale * gain[1:2, :]).astype(HALF)
        return carry

    lax.fori_loop(0, rows // block, norm, 0)
    plane_n.start()
    line.tick(2)
    plane_n.level(1)
    line.tick()
    plane_n.level(2)
    line.tick()
    plane_n.finish()
    line.landed(gate_at)
    line.landed(up_at)

    def blocks(left, right):
        value = None
        for d in range(parts):
            term = right(left[:, d * depth : (d + 1) * depth], d)
            value = term if value is None else value + term
        return value

    def mlp(hidden, down, gate, up, d_up, d_gate):
        load([(o.gate4, gate), (o.up4, up), (i.cot, own_low)])
        thirds = [down_at[j : j + 2] for j in range(0, len(down_at), 2)]
        third = units // len(thirds)
        along = pl.BlockSpec((rows, units), lambda t: (t, 0))

        def activations(n2, act_tile, slope_tile):
            for when in (2, 4):
                pl.when(pl.program_id(0) == when)(line.tick)
            value, rise = gelu_both(blocks(n2, lambda v, d: dot_nn(v, gate[d])))
            act_tile[...] = value
            above = blocks(n2, lambda v, d: dot_nn(v, up[d]))
            at = pl.ds(pl.multiple_of(pl.program_id(0) * rows, rows), rows)
            hidden[at, :] = (value * above).astype(HALF)
            slope_tile[...] = rise * above

        pltpu.emit_pipeline(
            activations, grid=(count,), in_specs=[across], out_specs=[along, along]
        )(o.n2_all, o.act, o.slope)
        beside_products([(o.c_all, hidden, o.grad_down)], 3, line.tick)
        sums.begin(SUM_AHEAD, (0, 3))
        whole, act_part, slope_part = summed, d_res, shared[0]

        for p, pieces in enumerate(thirds):
            if p:
                line.tick(pieces[-1] + 1 - line.done)
            if p == len(thirds) - 1:
                sums.begin(SUM_AHEAD, (1, 2))
            span = pl.ds(p * third, third)
            parts_in = []
            for t in range(count):
                at = pl.ds(t * rows, rows)
                columns = pl.ds(t * third, third)
                parts_in.append((o.act.at[at, span], act_part.at[:, columns]))
                parts_in.append((o.slope.at[at, span], slope_part.at[:, columns]))
            arrivals = [copy_of(a, b, 1 + j) for j, (a, b) in enumerate(parts_in)]
            for copy in arrivals:
                copy.start()
            line.landed(pieces)
            load([(o.down4.at[:, span], down.at[:, span])])
            for copy in arrivals:
                copy.wait()

            def backs(c_tile):
                d = pl.program_id(0)
                term = dot_nt(c_tile[...], down[d, span])
                pieces_of = [
                    (t, slice(t * rows, (t + 1) * rows), slice(t * third, (t + 1) * third))
                    for t in range(count)
                ]

                @pl.when(d == 0)
                def _():
                    for _, at, columns in pieces_of:
                        whole[:, columns] = term[at]

                @pl.when(d > 0)
                def _():
                    for _, at, columns in pieces_of:
                        whole[:, columns] += term[at]

                @pl.when(d == parts - 1)
                def _():
                    for _, at, columns in pieces_of:
                        back = whole[:, columns]
                        d_up[at, span] = (back * act_part[:, columns]).astype(HALF)
                        d_gate[at, span] = (back * slope_part[:, columns]).astype(HALF)

            pltpu.emit_pipeline(backs, grid=(parts,), in_specs=[tall])(o.c_all)

        by_rows = lambda left, right, t, columns: dot_nt(left, right[t])
        plane = PlaneSum([by_rows, by_rows], depth, [d_gate, d_up], [gate, up], shared)
        plane.spread(sums.tick)

        beside_products([(o.n2_all, d_gate, o.grad_gate)])
        sums.tick()
        beside_products([(o.n2_all, d_up, o.grad_up)])
        sums.tick()
        plane.finish(summed)

    gain_sum[...] = jnp.zeros_like(gain_sum)

    def norm_back(value, back, row):
        scale = lax.rsqrt(jnp.mean(value * value, axis=-1, keepdims=True) + EPS)
        weighted = gain[row : row + 1, :] * back
        gain_sum[row : row + 1, :] += jnp.sum(back * value * scale, axis=0, keepdims=True)
        inner = jnp.mean(weighted * value, axis=-1, keepdims=True)
        return scale * weighted - value * (scale * scale * scale * inner)

    def middle(t, carry):
        at = pl.ds(pl.multiple_of(t * block, block), block)
        back = norm_back(residual[at, :], summed[at, :], 1)
        back = own_low[at, :].astype(SINGLE) + back
        d_res[at, :] = back
        own_low[at, :] = back.astype(HALF)
        return carry

    def out_gradients(ob):
        load([(o.ob, ob)])

        def body(dt_tile, out_tile):
            out_tile[...] = dot_tn(ob[...], dt_tile[...]).astype(HALF)

        pltpu.emit_pipeline(
            body,
            grid=(parts,),
            in_specs=[tall],
            out_specs=[pl.BlockSpec((width, depth), lambda t: (t, 0))],
        )(o.dt_all, o.grad_out)

    def temporal_back(hidden, down, out_w, d_bx, d_by):
        load([(o.out4, out_w)])
        plane = PlaneSum([by_parts], depth, [hidden], [down], shared)

        def channels(dt_tile, bx, by, conv, gi, ra, h, before):
            step = pl.program_id(0)
            schedule = {
                0: lambda: (plane.send(3), plane.send(1)),
                1: lambda: (plane.take(3), plane.send(2), sums.tick()),
                2: lambda: (plane.take(1), plane.send(0)),
                3: lambda: (plane.take(2), plane.take(0), sums.tick()),
                5: lambda: (plane.relay(), sums.tick()),
                7: sums.tick,
            }
            for when, act in schedule.items():
                pl.when(step == when)(lambda act=act: (act(), None)[1])
            at = pl.ds(pl.multiple_of((count - 1 - step) * rows, rows), rows)
            backward_step(
                step, count, i.lens, dt_tile, out_w, bin_low, ba_low, chan,
                bx, by, conv, gi, ra, h, before, d_bx.at[at], d_by.at[at], gin, ga, gchan,
                *steps_scratch,
            )

        late = pl.BlockSpec((rows, width), lambda t: (count - 1 - t, 0))
        late_across = pl.BlockSpec((rows, model), lambda t: (count - 1 - t, 0))
        ahead = pl.BlockSpec(
            (8, width), lambda t: (jnp.maximum((count - 1 - t) * (rows // 8) - 1, 0), 0)
        )
        pltpu.emit_pipeline(
            channels, grid=(count,), in_specs=[late_across] + [late] * 6 + [ahead]
        )(o.dt_all, o.bx, o.by, o.conv, o.gi, o.ra, o.h, o.h)

    def block_input(pack, d_bx, d_by):
        pack_load = copy_of(o.pack4, pack, 0)
        pack_load.start()

        def body(n1_tile, pack_tile):
            right = n1_tile[...]
            pack_tile[:width, :] = dot_tn(d_bx[...], right).astype(HALF)
            pack_tile[width:, :] = dot_tn(d_by[...], right).astype(HALF)

        pltpu.emit_pipeline(
            body,
            grid=(parts,),
            in_specs=[tall],
            out_specs=[pl.BlockSpec((2 * width, depth), lambda t: (t, 0))],
        )(o.n1, o.grad_pack)
        pl.run_scoped(
            lambda small32: (
                small_gradients(small32, gin, ga, gchan, chan, heads, bite),
                small.__setitem__(Ellipsis, small32[...].astype(HALF)),
                None,
            )[2],
            pltpu.VMEM(small.shape, SINGLE),
        )
        sums.tick()
        PlaneSum([], depth, [], [], shared).finish(summed)
        for bit in plane_t.bits:
            pl.semaphore_signal(
                free_sem, inc=1, device_id={"mp": flip(me, bit, count)}, device_id_type=MESH
            )
        own_low[...] = (residual[...] + summed[...]).astype(HALF)
        outward[0].start()
        pack_load.wait()
        plane = PlaneSum(
            [
                lambda left, right, t, columns: dot_nn(left, right[t, :width, :]),
                lambda left, right, t, columns: dot_nn(left, right[t, width:, :]),
            ],
            depth,
            [d_bx, d_by],
            [pack, pack],
            shared,
        )
        pl.semaphore_wait(free_sem, len(plane_t.bits))
        plane.spread(sums.tick)
        sums.tick(3)
        plane.finish(summed)

    def with_hidden(hidden, down):
        pl.run_scoped(
            lambda *more: mlp(hidden, down, *more),
            pltpu.VMEM(o.gate4.shape, HALF),
            pltpu.VMEM(o.up4.shape, HALF),
            pltpu.VMEM((tokens, units), HALF),
            pltpu.VMEM((tokens, units), HALF),
        )
        lax.fori_loop(0, rows // block, middle, 0)
        plane_t.start()
        sums.tick(2)
        plane_t.level(1)
        sums.tick()
        plane_t.level(2)
        plane_t.finish()
        pl.run_scoped(out_gradients, pltpu.VMEM((tokens, width), HALF))
        sums.tick()

        def with_gradients(d_bx, d_by):
            pl.run_scoped(
                lambda out_w: temporal_back(hidden, down, out_w, d_bx, d_by),
                pltpu.VMEM(o.out4.shape, HALF),
            )
            pl.run_scoped(
                lambda pack: block_input(pack, d_bx, d_by), pltpu.VMEM(o.pack4.shape, HALF)
            )

        pl.run_scoped(
            with_gradients, pltpu.VMEM((tokens, width), HALF), pltpu.VMEM((tokens, width), HALF)
        )

    pl.run_scoped(
        with_hidden, pltpu.VMEM((tokens, units), HALF), pltpu.VMEM(o.down4.shape, HALF)
    )

    def last(t, carry):
        at = pl.ds(pl.multiple_of(t * block, block), block)
        back = norm_back(inputs[at, :].astype(SINGLE), summed[at, :], 0)
        d_res[at, :] = d_res[at, :] + back
        return carry

    lax.fori_loop(0, rows // block, last, 0)
    outward[1].start()

    for j in range(turns.shape[0]):
        turns[j] = gain_sum[:, j * 128 : (j + 1) * 128]
    inner, outer = ring_peers("mp"), ring_peers("dp")
    held = turns.shape[0] // parts
    early = exchange(
        outer,
        lambda k: turns.at[pl.ds((level + k) % parts * held, held)],
        lambda k: turns_dp.at[k],
        *total_sems[:2],
    )
    each(early, START)
    sums.tick()
    for j in range(3):
        sums.collect(j)
    each(early, LAND)
    first = level * held
    for k, _ in outer:
        turns_dp[0] = (turns[pl.ds(first, held)] if k == 1 else turns_dp[0]) + turns_dp[k]
    pair = count // held
    late = exchange(
        inner,
        lambda k: turns_dp.at[0, (me + k) % count // pair],
        lambda k: turns_mp.at[k],
        *total_sems[2:],
    )
    each(late, START)
    sums.tick(len(sums.chunks) - 1 - sums.done)
    sums.collect(3)
    sums.collect(4)
    each(late, LAND)
    value = turns_dp[0, me // pair]
    for k, _ in inner:
        value = value + turns_mp[k]
    o.gain_grads[...] = value
    sums.tick()
    sums.collect(5)
    line.settle()
    sums.settle()
    each(within + across_dp + early + late, SENT)
    for copy in outward:
        copy.wait()


def fused_layer(values, collective_id):
    parts, count = LineSum.COUNT, PlaneGather.COUNT
    rows, model = values.x.shape
    tokens = rows * count
    width, depth = values.w_in.shape
    units = values.gate.shape[1]
    small_rows = -(-(values.blocks_in.shape[0] + values.channels.shape[0]) // 16) * 16
    shape = jax.ShapeDtypeStruct
    plane_rows = shape((tokens, model), HALF)
    channel = shape((tokens, width), SINGLE)
    channel_low = shape((tokens, width), HALF)
    hidden_wide = shape((tokens, units), SINGLE)
    hidden_grads = shape((model, units), HALF)
    sizes = (
        (depth, units), (depth, units), (depth, units),
        (width, depth), (small_rows, depth), (2 * width, depth),
    )
    outs = LayerOut(
        shape((rows, model), HALF),
        shape((rows, model), SINGLE),
        shape((8, 128), SINGLE),
        *[plane_rows] * 5,
        channel_low,
        *[channel] * 5,
        channel_low,
        hidden_wide,
        hidden_wide,
        hidden_grads,
        hidden_grads,
        hidden_grads,
        shape((parts * width, depth), HALF),
        shape((parts * 2 * width, depth), HALF),
        shape((parts, 2 * width, depth), HALF),
        shape((parts, small_rows, depth), HALF),
        shape((parts, width, depth), HALF),
        shape((parts, depth, units), HALF),
        shape((parts, depth, units), HALF),
        shape((parts, units, depth), HALF),
        *[shape((parts,) + size, HALF) for size in sizes],
        *[shape(size, SINGLE) for size in sizes],
    )
    outs = outs._replace(
        sum_down=shape((2, units, depth // 2), SINGLE), sum_pack=shape((2, width, depth), SINGLE)
    )
    in_vmem, in_hbm = pl.BlockSpec(memory_space=pltpu.VMEM), pl.BlockSpec(memory_space=pl.ANY)
    in_specs = LayerIn(*[in_hbm] * len(values))._replace(
        lens=pl.BlockSpec(memory_space=pltpu.SMEM),
        norm_in=in_vmem,
        norm_mid=in_vmem,
        blocks_in=in_vmem,
        blocks_a=in_vmem,
        channels=in_vmem,
    )
    out_specs = LayerOut(*[in_hbm] * len(outs))._replace(gain_grads=in_vmem)
    inner, outer = lax.axis_size("mp"), lax.axis_size("dp")
    pieces = [(n, (size[0] // n, size[1])) for size, n in zip(sizes, SUM_PIECES)]
    tile = (8, 128)
    vmem, sem = pltpu.VMEM, pltpu.SemaphoreType.DMA
    results = pl.pallas_call(
        layer_kernel,
        out_shape=list(outs),
        in_specs=list(in_specs),
        out_specs=list(out_specs),
        scratch_shapes=[
            vmem((inner * outer,) + tile, SINGLE),
            vmem((8, model), SINGLE),
            vmem((8, model), SINGLE),
            vmem((width, width), HALF),
            vmem((width, width), HALF),
            vmem((16, width), SINGLE),
            vmem((rows, model), HALF),
            vmem((rows, model), HALF),
            vmem((rows, model), SINGLE),
            vmem((rows, model), SINGLE),
            vmem((rows, model), SINGLE),
        ]
        + forward_scratch(rows, width)
        + [
            vmem((width, width), SINGLE),
            vmem((width, width), SINGLE),
            vmem((8, width), SINGLE),
            vmem((parts * small_rows, depth), HALF),
            vmem((model // 128,) + tile, SINGLE),
            vmem((outer, model // 128 // parts) + tile, SINGLE),
            vmem((inner,) + tile, SINGLE),
        ]
        + [vmem((n,) + size, HALF) for n, size in pieces]
        + [vmem(pieces[j][1], HALF) for j in (0, 3, 4)]
        + [sem((1 + 2 * count,)), sem((2,)), pltpu.SemaphoreType.REGULAR]
        + [sem((c,)) for c in (inner, inner, outer, outer)]
        + [sem((c,)) for c in (outer, outer, inner, inner)]
        + PlaneGather.scratch() * 4
        + PlaneSum.scratch(rows, model)
        + LineGather.scratch(sum(WEIGHT_PIECES))
        + LineSum.scratch(sum(SUM_PIECES)),
        compiler_params=kernel_params(collective_id),
        cost_estimate=pl.CostEstimate(
            flops=24 * tokens * model * units,
            bytes_accessed=80 * tokens * model,
            transcendentals=2 * tokens * units,
        ),
        name="layer",
    )(*values)
    return LayerOut(*results)


def diagonal(blocks):
    count, size, _ = blocks.shape
    spread = blocks[:, :, None, :] * jnp.eye(count, dtype=blocks.dtype)[:, None, :, None]
    return spread.reshape(count * size, count * size)


def on_device(
    layer_input,
    cotangent,
    norm_in,
    norm_mid,
    w_rnn_in,
    w_rnn_gate,
    w_rnn_out,
    gate_in_blocks,
    gate_a_blocks,
    channel_params,
    w_mlp_gate,
    w_mlp_up,
    w_mlp_down,
    lengths,
):
    parts = lax.axis_size("dp")
    rows, model = layer_input.shape
    depth, width = w_rnn_in.shape
    heads, bite, block = gate_in_blocks.shape
    tokens = rows * lax.axis_size("mp")

    fused = lax.axis_size("mp") == PlaneGather.COUNT and parts == LineGather.COUNT
    small_rows = -(-(heads * bite + 2 * CONV // parts) // 16) * 16
    small_lanes = 512
    lane_a = 256 if fused else block

    def small_pack(blocks_in, blocks_a, channels):
        wide = lambda v, lanes: jnp.pad(v, ((0, 0), (0, lanes - v.shape[1])))
        v = jnp.concatenate(
            [
                wide(blocks_in.reshape(-1, block), lane_a),
                wide(blocks_a.reshape(-1, block), small_lanes - lane_a),
            ],
            axis=1,
        )
        v = jnp.concatenate([v, wide(channels, small_lanes)], axis=0)
        return jnp.pad(v, ((0, small_rows - v.shape[0]), (0, 0)))

    bite_gain = norm_in.shape[0]
    if fused:
        o = fused_layer(
            LayerIn(
                lengths, norm_in.reshape(1, -1), norm_mid.reshape(1, -1), layer_input, cotangent,
                gate_in_blocks.reshape(-1, block), gate_a_blocks.reshape(-1, block),
                channel_params, w_rnn_in.T, w_rnn_gate.T, w_rnn_out, w_mlp_gate, w_mlp_up, w_mlp_down,
            ),
            0,
        )
        spot = (lax.axis_index("mp") % (128 // bite_gain)) * bite_gain
        gain_grads = lax.dynamic_slice(o.gain_grads, (0, spot), (2, bite_gain))
        layer_output, grad_input = o.layer_output, o.grad_input
        grad_in, grad_side = o.sum_pack[0].T, o.sum_pack[1].T
        grad_out, small_grads = o.sum_out, o.sum_small
        grad_gate, grad_up = o.sum_gate, o.sum_up
        grad_down = jnp.concatenate([o.sum_down[0], o.sum_down[1]], axis=1)
    else:
        inputs = layer_input.astype(SINGLE)
        small_mine = small_pack(
            gate_in_blocks.astype(HALF), gate_a_blocks.astype(HALF), channel_params.astype(HALF)
        )
        mine = jnp.concatenate([w_rnn_in.astype(HALF).T, w_rnn_gate.astype(HALF).T], axis=0)
        out_mine, down_mine = w_rnn_out.astype(HALF), w_mlp_down.astype(HALF)
        gate_mine, up_mine = w_mlp_gate.astype(HALF), w_mlp_up.astype(HALF)
        gains = jnp.stack([norm_in, norm_mid]).astype(HALF).astype(SINGLE)
        over = lambda v: lax.all_gather(v, "dp", axis=0, tiled=False)
        gains = lax.all_gather(gains, ("dp", "mp"), axis=0, tiled=False)
        gain_first = gains[:, 0].reshape(1, model)
        gain_second = gains[:, 1].reshape(1, model)
        small, pack, out_w = over(small_mine), over(mine), over(out_mine)
        down, gate_w, up_w = over(down_mine), over(gate_mine), over(up_mine)
        whole_block = lambda v: diagonal(
            v.reshape(parts, heads, bite, block)
            .transpose(1, 0, 2, 3)
            .reshape(heads, block, block)
        )
        blocks_in = whole_block(small[:, : heads * bite, :block])
        blocks_a = whole_block(small[:, : heads * bite, lane_a : lane_a + block])
        channel = small[:, heads * bite : heads * bite + 2 * CONV // parts, :width]
        channel = channel.reshape(2 * CONV, width).astype(SINGLE)
        soft = jax.nn.softplus(-channel[2 * CONV - 1 :])
        chan = jnp.concatenate([channel, soft, jnp.zeros((7, width), SINGLE)], axis=0)
        x_all = lax.all_gather(layer_input, "mp", axis=0, tiled=True)
        c_all = lax.all_gather(cotangent, "mp", axis=0, tiled=True)
        n1, bx, by, conv, gate_in, gate_a, h, ob = forward_channels(
            lengths, x_all, gain_first, pack, blocks_in, blocks_a, chan
        )
        saved = (bx, by, conv, gate_in, gate_a, h, ob, n1)
        out = jnp.einsum("tc,dcm->tdm", ob, out_w, preferred_element_type=SINGLE)
        residual = inputs + lax.psum_scatter(
            out.reshape(tokens, model).astype(HALF), "mp", scatter_dimension=0, tiled=True
        ).astype(SINGLE)
        scale = lax.rsqrt(jnp.mean(residual * residual, axis=-1, keepdims=True) + EPS)
        normed_mid = (residual * scale * gain_second).astype(HALF)
        n2 = lax.all_gather(normed_mid, "mp", axis=0, tiled=True)
        d_hidden = dot_nt(c_all, down.transpose(1, 0, 2).reshape(-1, model))
        act, slope = gelu_both(dot_nn(n2, gate_w.reshape(model, -1)))
        d_up = (d_hidden * act).astype(HALF)
        up_pre = dot_nn(n2, up_w.reshape(model, -1))
        hidden = (act * up_pre).astype(HALF)
        d_gate = (d_hidden * up_pre * slope).astype(HALF)
        gate_w, up_w = gate_w.reshape(model, -1), up_w.reshape(model, -1)
        over_dp = lambda value: lax.psum_scatter(
            value.astype(HALF), "dp", scatter_dimension=0, tiled=True
        ).astype(SINGLE)
        over_mp = lambda value: lax.psum_scatter(
            value.astype(HALF), "mp", scatter_dimension=0, tiled=True
        ).astype(SINGLE)
        grad_down = over_dp(dot_tn(c_all, hidden))
        grad_gate, grad_up = over_dp(dot_tn(n2, d_gate)), over_dp(dot_tn(n2, d_up))
        layer_output = residual + over_mp(
            dot_nn(hidden, down.transpose(1, 0, 2).reshape(-1, model))
        )
        layer_output = layer_output.astype(HALF)
        back = over_mp(dot_nt(d_gate, gate_w) + dot_nt(d_up, up_w))
        weighted = gain_second * back
        gain_mid = jnp.sum(back * residual * scale, axis=0)
        d_residual = (
            cotangent.astype(SINGLE)
            + scale * weighted
            - residual * scale**3 * jnp.mean(weighted * residual, axis=-1, keepdims=True)
        )
        dt_all = lax.all_gather(d_residual.astype(HALF), "mp", axis=0, tiled=True)
        d_bx, d_by, gin, ga, gchan, rnn_grads = backward_channels(
            lengths, dt_all, out_w, blocks_in, blocks_a, chan, saved
        )
        back = over_mp(
            jnp.einsum(
                "tc,dcm->tdm",
                jnp.concatenate([d_bx, d_by], axis=1),
                pack,
                preferred_element_type=SINGLE,
            ).reshape(tokens, model)
        )
        own = lambda full: jnp.stack(
            [full[j * block : (j + 1) * block, j * block : (j + 1) * block] for j in range(heads)]
        )
        decay_row = DECAY * jax.nn.sigmoid(-channel[2 * CONV - 1 :]) * gchan[2 * CONV - 1 :]
        grad_channel = jnp.concatenate([gchan[: 2 * CONV - 1], decay_row], axis=0)
        split = lambda v: v.reshape(heads, parts, bite, block).transpose(1, 0, 2, 3)
        small_grads = jax.vmap(small_pack)(
            split(own(gin)), split(own(ga)), grad_channel.reshape(parts, -1, width)
        )
        small_grads = over_dp(small_grads)[0]
        rnn_grads = over_dp(rnn_grads)[0]
        grad_in, grad_side, grad_out = jnp.split(rnn_grads, 3, axis=0)
        grad_in, grad_side, grad_down = grad_in.T, grad_side.T, grad_down.T
        scale = lax.rsqrt(jnp.mean(inputs * inputs, axis=-1, keepdims=True) + EPS)
        weighted = gain_first * back
        gain_in = jnp.sum(back * inputs * scale, axis=0)
        grad_input = (
            d_residual
            + scale * weighted
            - inputs * scale**3 * jnp.mean(weighted * inputs, axis=-1, keepdims=True)
        )
        gain_grads = lax.psum_scatter(
            jnp.stack([gain_in, gain_mid]), ("dp", "mp"), scatter_dimension=1, tiled=True
        )
    gate_rows = small_grads[: heads * bite]
    return (
        layer_output,
        grad_input,
        gain_grads[0],
        gain_grads[1],
        grad_in,
        grad_side,
        grad_out,
        gate_rows[:, :block].reshape(heads, bite, block),
        gate_rows[:, lane_a : lane_a + block].reshape(heads, bite, block),
        small_grads[heads * bite : heads * bite + 2 * CONV // parts, :width],
        grad_gate,
        grad_up,
        grad_down,
    )


def solution(mesh):
    rows = P(("dp", "mp"), None)
    return jax.shard_map(
        on_device,
        mesh=mesh,
        in_specs=(
            rows,
            rows,
            P(("dp", "mp")),
            P(("dp", "mp")),
            P("dp", "mp"),
            P("dp", "mp"),
            P("mp", "dp"),
            P("mp", "dp", None),
            P("mp", "dp", None),
            P("dp", "mp"),
            P("dp", "mp"),
            P("dp", "mp"),
            P("mp", "dp"),
            P("dp", None),
        ),
        out_specs=(
            rows,
            rows,
            P(("dp", "mp")),
            P(("dp", "mp")),
            P("dp", "mp"),
            P("dp", "mp"),
            P("mp", "dp"),
            P("mp", "dp", None),
            P("mp", "dp", None),
            P("dp", "mp"),
            P("dp", "mp"),
            P("dp", "mp"),
            P("mp", "dp"),
        ),
        check_vma=False,
    )
```
